32 devices in a mesh: fib: 4 (over z), wav: 4 (over y, x), exp: 2 (over core).
Axes of the slice: x: 2, y: 2, z: 4, core: 2. Of those that a mesh axis runs over, the one named last changes fastest.
Arguments:
- pixels: float32 [8, 1920, 1024], P('exp', 'wav', 'fib'), may hold values from -6 to 6
- pixel_ivar: float32 [8, 1920, 1024], P('exp', 'wav', 'fib'), may hold values from 0.25 to 4
- clip_bits: int32 [8, 128, 1024], P('exp', 'wav', 'fib'), may hold values from 0 to 32767
- coupling: float32 [1024], P('fib'), may hold values from 0.5 to 200
- counts: int32 [1024], P('fib'), may hold values from 1 to 8
- good_flags: int32 [8, 1024], P('exp', 'fib'), may hold values 0 or 1
- owner_slot: int32 [1024], replicated, may hold values from 0 to 1023, as said below
Outputs:
- coadd_flux: float32 [1920, 1024], P(('wav', 'exp'), 'fib')
- coadd_ivar: float32 [1920, 1024], P(('wav', 'exp'), 'fib')
- coadd_res: float32 [3, 1920, 1024], P(None, ('wav', 'exp'), 'fib')
The draws below stay inside these ranges and needn't reach their ends.
Inputs may be any that keep to these rules, and one draw needn't show every extreme that they name: A permutation of the fibres; fibre f belongs to coadd index owner_slot[f] // 256 of fib, and the 256 fibres of each index of fib go 64 to every coadd index.
All inputs are finite; a program needn't handle non-finite values. No bound on the sum of `good_flags` on one device may be relied on, other than what follows from the above.
Results may differ from the reference program's by a relative error of at most 0.0001.
Values sent between devices are 32-bit elements; how exact they have to be, the bound alone decides.
No kernel may reach another device: no remote copies, remote signals or barrier semaphores. Data moves between devices by JAX's collectives and lax.ppermute only.
A program may use at most 128 MiB of HBM per device.

```python
import math
import jax
import jax.numpy as jnp
from jax import lax

F_DEV = 256
HALO = 50
FIBRES = 1024
EXPOS = 8
WAVES = 1920
N_WAV = 4


def draw_clip_bits(key, part):
    kept_pixels = (jax.random.randint(key, (EXPOS, WAVES // 15, 15, FIBRES), 0, 8) != 0).astype(jnp.int32)
    shifts = jnp.arange(15, dtype=jnp.int32)
    return jnp.sum(kept_pixels << shifts[None, None, :, None], axis=2).astype(jnp.int32)


def shuffle_slots(one_key):
    return jax.random.permutation(one_key, F_DEV)


def shuffle_row(one_key, row_values):
    return jax.random.permutation(one_key, row_values)


def draw_owner_slot(key, part):
    owners = FIBRES // F_DEV
    per_owner = F_DEV // owners
    source = jnp.arange(owners, dtype=jnp.int32)[:, None, None]
    target = jnp.arange(owners, dtype=jnp.int32)[None, :, None]
    offset = jnp.arange(per_owner, dtype=jnp.int32)[None, None, :]
    within = source * per_owner + offset + target * 0
    target_full = target + source * 0 + offset * 0
    target_keys = jax.random.split(jax.random.fold_in(key, 11), owners)
    target_perms = jax.vmap(shuffle_slots)(target_keys).astype(jnp.int32)
    slots = target_full * F_DEV + target_perms[target_full, within]
    rows_all = slots.reshape(owners, F_DEV)
    source_keys = jax.random.split(jax.random.fold_in(key, 12), owners)
    rows_all = jax.vmap(shuffle_row)(source_keys, rows_all)
    return rows_all.reshape(-1).astype(jnp.int32)


def touch_ends(values, key, smallest, largest):
    dims = values.shape
    index_at = [jax.random.randint(jax.random.fold_in(key, axis), (), 0, dims[axis]) for axis in range(len(dims))]
    values = values.at[tuple(index_at)].set(smallest)
    longest = dims.index(max(dims))
    index_at[longest] = (index_at[longest] + 1) % dims[longest]
    return values.at[tuple(index_at)].set(largest)


def levels(rng, extent, cuts, low, largest):
    factor_of = 1.0
    for axis_at, parts in cuts:
        steps = jax.random.uniform(jax.random.fold_in(jax.random.fold_in(rng, 6), axis_at), (parts,), jnp.float32, low / len(cuts), largest / len(cuts))
        factor_of = factor_of * jnp.repeat(jnp.exp(steps), extent[axis_at] // parts).reshape((-1,) + (1,) * (len(extent) - 1 - axis_at))
    return factor_of


def centred(key, shape, scale, reach, pieces=(), held_as=jnp.bfloat16):
    entries = jax.random.normal(key, shape, jnp.float32) * scale
    if len(pieces) > 0:
        entries = levels(key, shape, pieces, -0.22, 0.18) * entries
    return jnp.clip(entries, min=-reach, max=reach).astype(held_as)


def setup_inputs(seed: int = 0) -> dict:
    key_of = jax.random.split(jax.random.key(seed), 8)
    pixels = centred(key_of[0], (EXPOS, WAVES, FIBRES), 1.0, 6.0, ((0, 2), (1, 4), (2, 4)), jnp.float32)
    pixel_ivar = jnp.clip(jnp.exp(math.log(4.0) - 2.7725887 * jax.random.uniform(key_of[1], (EXPOS, WAVES, FIBRES), jnp.float32) ** levels(key_of[1], (EXPOS, WAVES, FIBRES), ((0, 2), (1, 4), (2, 4)), -0.2, 0.2)), 0.25, 4.0)
    clip_bits = draw_clip_bits(jax.random.fold_in(key_of[7], 71), 0)
    coupling = jnp.clip(jnp.exp(math.log(200.0) - 5.9914645 * jax.random.uniform(key_of[3], (FIBRES,), jnp.float32) ** levels(key_of[3], (FIBRES,), ((0, 4),), -0.2, 0.2)), 0.5, 200.0)
    counts = touch_ends(jax.random.randint(key_of[4], (FIBRES,), 1, EXPOS + 1), jax.random.fold_in(key_of[4], 1), 1, EXPOS).astype(jnp.int32)
    good_flags = touch_ends((jax.random.randint(key_of[5], (EXPOS, FIBRES), 0, 8) < 7).astype(jnp.int32), jax.random.fold_in(key_of[5], 1), 0, 1)
    owner_slot = draw_owner_slot(jax.random.fold_in(key_of[7], 71), 0)
    return {"pixels": pixels, "pixel_ivar": pixel_ivar, "clip_bits": clip_bits, "coupling": coupling, "counts": counts, "good_flags": good_flags, "owner_slot": owner_slot}


def reference(pixels, pixel_ivar, clip_bits, coupling, counts, good_flags, owner_slot):
    expos, waves, fibres = pixels.shape
    patch_width = waves // N_WAV
    length = patch_width + 2 * HALO
    padding = ((0, 0), (HALO, HALO), (0, 0))
    pad_pixels = jnp.pad(pixels, padding)
    pad_ivar = jnp.pad(pixel_ivar, padding)
    flux_parts = []
    band_parts = []
    for patch_index in range(N_WAV):
        start = patch_index * patch_width
        window_pixels = pad_pixels[:, start:start + length]
        window_ivar = pad_ivar[:, start:start + length]
        position = start - HALO + jnp.arange(length, dtype=jnp.int32)
        inside = ((position >= 0) & (position < waves)).astype(jnp.float32)
        linkage = coupling[None, :] * (inside[:-1] * inside[1:])[:, None]
        border = jnp.zeros((1, fibres), jnp.float32)
        link_left = jnp.concatenate([border, linkage], 0)[None]
        link_right = jnp.concatenate([linkage, border], 0)[None]
        middle = window_ivar * inside[None, :, None] + (1.0 - inside)[None, :, None] + link_left + link_right
        weighted = window_ivar * window_pixels
        lower_band = jnp.broadcast_to(-link_left, middle.shape)
        upper_band = jnp.broadcast_to(-link_right, middle.shape)
        solved = lax.linalg.tridiagonal_solve(jnp.transpose(lower_band, (0, 2, 1)), jnp.transpose(middle, (0, 2, 1)), jnp.transpose(upper_band, (0, 2, 1)), jnp.transpose(weighted, (0, 2, 1))[..., None])[..., 0]
        solved = jnp.transpose(solved, (0, 2, 1))
        flux_parts.append(solved[:, HALO:HALO + patch_width])
        row_total = middle + link_left + link_right
        bands = jnp.stack([link_left / row_total, middle / row_total, link_right / row_total])
        band_parts.append(bands[:, :, HALO:HALO + patch_width])
    flux = jnp.concatenate(flux_parts, 1)
    resolution = jnp.concatenate(band_parts, 2)
    shifts = jnp.arange(15, dtype=jnp.int32)
    kept_pixels = (clip_bits[:, :, None, :] >> shifts[None, None, :, None] & 1).reshape(expos, waves, fibres).astype(jnp.float32)
    exposure = jnp.arange(expos, dtype=jnp.int32)
    usable = good_flags.astype(jnp.float32) * (exposure[:, None] < counts[None, :]).astype(jnp.float32)
    weight = pixel_ivar * kept_pixels * usable[:, None, :]
    flux_sum = jnp.sum(weight * flux, 0)
    weight_sum = jnp.sum(weight, 0)
    band_sum = jnp.sum(weight[None] * resolution, 1)
    divisor = jnp.maximum(weight_sum, 1.0)
    inverse = jnp.argsort(owner_slot)
    coadd_flux = (flux_sum / divisor)[:, inverse]
    coadd_ivar = weight_sum[:, inverse]
    coadd_res = (band_sum / divisor[None])[:, :, inverse]
    return (coadd_flux, coadd_ivar, coadd_res)
```

```python
import functools

import jax
import jax.numpy as jnp
from jax import lax
from jax.experimental import pallas as pl
from jax.experimental.pallas import tpu as pltpu
from jax.sharding import PartitionSpec as P

HALO = 50
BITS = 15
LANES = 128
ROWS = 8
GROUP = 120
VMEM_BYTES = 48 * 1024 * 1024
F32 = jnp.float32
BF16 = jnp.bfloat16
NT = (((1,), (1,)), ((), ()))

in_vmem = pl.BlockSpec(memory_space=pltpu.VMEM)
in_smem = pl.BlockSpec(memory_space=pltpu.SMEM)
in_place = pl.BlockSpec(memory_space=pl.ANY)


def params():
    return pltpu.CompilerParams(vmem_limit_bytes=VMEM_BYTES)


def cost(flops, moved):
    return pl.CostEstimate(flops=int(flops), bytes_accessed=int(moved), transcendentals=0)


def shaped(shape, dtype=F32):
    return jax.ShapeDtypeStruct(shape, dtype)


def usable_rows(place_ref, counts_ref, good_ref):
    count = good_ref.shape[0]
    return [
        good_ref[e : e + 1, :].astype(F32)
        * jnp.where(place_ref[2] * count + e < counts_ref[...], 1.0, 0.0)
        for e in range(count)
    ]


def tile_bits(tile):
    first, last = (ROWS * tile) // BITS, (ROWS * tile + ROWS - 1) // BITS
    split = BITS * last - ROWS * tile
    row = lax.broadcasted_iota(jnp.int32, (ROWS, 1), 0)
    word = jnp.where(row >= split, last, first)
    return first, last, split, jnp.left_shift(1, ROWS * tile + row - BITS * word)


def tile_words(words, tile):
    first, last, split, mask = tile_bits(tile)
    picked = words[first : first + 1, :]
    if last != first:
        row = lax.broadcasted_iota(jnp.int32, (ROWS, 1), 0)
        picked = jnp.where(row >= split, words[last : last + 1, :], picked)
    return (picked & mask) != 0


def weights_kernel(total, place_ref, coupling_ref, counts_ref, good_ref, ivar_ref, bits_ref, theirs_ref, mine_ref):
    step = pl.program_id(0)
    steps = pl.num_programs(0)
    expos, group, _ = ivar_ref.shape
    at = (step + (1 - place_ref[2]) * (steps // 2)) % steps
    start = place_ref[1] * (steps * group) + at * group
    coupling = coupling_ref[...]
    usable = usable_rows(place_ref, counts_ref, good_ref)
    tiles = group // ROWS
    results = []
    for tile in range(tiles):
        links = 4.0 * coupling
        if tile in (0, tiles - 1):
            row = start + ROWS * tile + lax.broadcasted_iota(jnp.int32, (ROWS, 1), 0)
            links = jnp.where((row == 0) | (row == total - 1), 2.0, 4.0) * coupling
        weight_sum = band_sum = None
        for e in range(expos):
            ivar = ivar_ref[e, ROWS * tile : ROWS * (tile + 1), :]
            kept = tile_words(bits_ref[e], tile)
            weight = jnp.where(kept, ivar * usable[e], 0.0)
            band = weight / (ivar + links)
            weight_sum = weight if e == 0 else weight_sum + weight
            band_sum = band if e == 0 else band_sum + band
        results.append((weight_sum, band_sum * coupling))

    def store(ref):
        for tile, pair in enumerate(results):
            ref[0, ROWS * tile : ROWS * (tile + 1), :] = pair[0]
            ref[1, ROWS * tile : ROWS * (tile + 1), :] = pair[1]

    @pl.when(step < steps // 2)
    def _():
        store(theirs_ref)

    @pl.when(step >= steps // 2)
    def _():
        store(mine_ref)


def weight_sums(place, coupling, counts, good, ivar, bits, total):
    expos, width, fibres = ivar.shape
    steps = width // GROUP
    half = steps // 2

    def at(i, place):
        return (i + (1 - place[2]) * half) % steps

    row = pl.BlockSpec((1, fibres), lambda i, place: (0, 0))
    out = shaped((2, width // 2, fibres))
    return pl.pallas_call(
        functools.partial(weights_kernel, total),
        grid_spec=pltpu.PrefetchScalarGridSpec(
            num_scalar_prefetch=1,
            grid=(steps,),
            in_specs=[
                row,
                row,
                pl.BlockSpec((expos, fibres), lambda i, place: (0, 0)),
                pl.BlockSpec((expos, GROUP, fibres), lambda i, place: (0, at(i, place), 0)),
                pl.BlockSpec((expos, GROUP // BITS, fibres), lambda i, place: (0, at(i, place), 0)),
            ],
            out_specs=[
                pl.BlockSpec((2, GROUP, fibres), lambda i, place: (0, jnp.minimum(i, half - 1), 0)),
                pl.BlockSpec((2, GROUP, fibres), lambda i, place: (0, jnp.maximum(i - half, 0), 0)),
            ],
        ),
        out_shape=[out, out],
        compiler_params=params(),
        cost_estimate=cost(20 * ivar.size, 6 * ivar.size),
        name="weight_sums",
    )(place, coupling, counts, good, ivar, bits)


def stream_coupling(coupling_ref, expos):
    coupling = coupling_ref[...]
    blocks = coupling.shape[1] // LANES
    return jnp.concatenate(
        [jnp.broadcast_to(coupling[:, h * LANES : (h + 1) * LANES], (expos, LANES)) for h in range(blocks)], 0
    )


def fetch_streams(source_ref, first, count, scratch_ref, sems, sem_at):
    expos, _, fibres = source_ref.shape
    copies = []
    for h in range(fibres // LANES):
        for e in range(expos):
            stream = h * expos + e
            copy = pltpu.make_async_copy(
                source_ref.at[e, pl.ds(first, count), pl.ds(h * LANES, LANES)],
                scratch_ref.at[pl.ds(stream * count, count), :],
                sems.at[sem_at + stream],
            )
            copy.start()
            copies.append(copy)
    return copies


def advance(state, ivar, pixel, back_coupling):
    n, d, b = state
    d = d + n * back_coupling
    return (n + ivar * d, d, b + (ivar * pixel) * d)


def prep_kernel(
    fib_count, pack, per, rel, place_ref, coupling_ref, slots_ref, pixels_ref, ivar_ref,
    edges_ref, send_ref, recv_ref, ivar_s, pixel_s, sems,
):
    expos, width, fibres = pixels_ref.shape
    streams = expos * fibres // LANES
    count = ivar_s.shape[1] // streams
    waits = []
    for side, first in enumerate((width - count, 0)):
        waits += fetch_streams(ivar_ref, first, count, ivar_s.at[side], sems, (2 * side) * streams)
        waits += fetch_streams(pixels_ref, first, count, pixel_s.at[side], sems, (2 * side + 1) * streams)

    lanes = pack * per
    me = place_ref[0]
    slots = slots_ref[...].astype(F32)
    owner = jnp.floor((slots + 0.5) * (1.0 / fibres))
    slot_within = slots - owner * fibres
    sources = slots.shape[0]
    source = lax.broadcasted_iota(jnp.int32, (sources, fibres), 0)
    my_owner = jnp.sum(jnp.where(source == me, owner, 0.0), axis=0, keepdims=True).astype(jnp.int32)
    rows_i = lax.broadcasted_iota(jnp.int32, (fibres, fibres), 0)
    cols_i = lax.broadcasted_iota(jnp.int32, (fibres, fibres), 1)
    earlier = (rows_i < cols_i).astype(F32).astype(BF16)
    to_owner = (source == my_owner).astype(F32)
    counted = jnp.dot(to_owner.astype(BF16), earlier, preferred_element_type=F32)
    rank = jnp.sum(to_owner * counted, axis=0, keepdims=True).astype(jnp.int32)
    target = my_owner
    if rel:
        target = jnp.where(my_owner >= me, my_owner - me, my_owner - me + fib_count)
    base = target * lanes + rank
    place_of = jnp.concatenate([base + h * per for h in range(pack)], 1)
    total_lanes = fib_count * lanes
    wide = lax.broadcasted_iota(jnp.int32, (total_lanes, pack * fibres), 0)
    send_ref[...] = (wide == place_of).astype(F32).astype(BF16)

    mine = (owner == me.astype(F32)).astype(F32)
    rank_in = jnp.dot(mine.astype(BF16), earlier, preferred_element_type=F32).astype(jnp.int32)
    order = source
    if rel:
        order = jnp.where(me >= source, me - source, me - source + fib_count)
    arrival = jnp.where(mine > 0.0, order * lanes + rank_in, -total_lanes)
    tall = lax.broadcasted_iota(jnp.int32, (total_lanes, fibres), 0)
    landing = jnp.zeros((ROWS, total_lanes), F32)
    for s in range(fib_count):
        hit = tall == arrival[s : s + 1, :]
        for h in range(1, pack):
            hit = hit | (tall == arrival[s : s + 1, :] + h * per)
        values = jnp.broadcast_to(slot_within[s : s + 1, :], (ROWS, fibres)).astype(BF16)
        landing = landing + lax.dot_general(
            values, hit.astype(F32).astype(BF16), NT, preferred_element_type=F32
        )
    lane = lax.broadcasted_iota(jnp.int32, (1, total_lanes), 1)
    landing = landing[0:1, :].astype(jnp.int32)
    for h in range(1, pack):
        inside = (lane % lanes >= h * per) & (lane % lanes < (h + 1) * per)
        landing = jnp.where(inside, landing + h * fibres, landing)
    high = lax.broadcasted_iota(jnp.int32, (pack * fibres, total_lanes), 0)
    recv_ref[...] = (high == landing).astype(F32).astype(BF16)

    for wait in waits:
        wait.wait()
    back = 1.0 / stream_coupling(coupling_ref, expos)
    zero = jnp.zeros((streams, LANES), F32)
    states = [(zero, zero + 1.0, zero), (zero, zero + 1.0, zero)]
    for i in range(HALO):
        for side, row in enumerate((count - HALO + i, HALO - 1 - i)):
            at = pl.ds(row, streams, stride=count)
            states[side] = advance(states[side], ivar_s[side, at, :], pixel_s[side, at, :], back)
            if i % 10 == 9:
                scale = 1.0 / states[side][1]
                states[side] = tuple(part * scale for part in states[side])
    for side in range(2):
        n, d, b = states[side]
        scale = 1.0 / (d + n * back)
        edges_ref[side, 0] = n * scale
        edges_ref[side, 1] = b * scale


def prepare(place, coupling, slots, pixels, ivar, pack, per, rel):
    expos, width, fibres = pixels.shape
    fib_count = slots.shape[0]
    if fib_count % ROWS:
        slots = jnp.concatenate([slots, jnp.full((ROWS - fib_count % ROWS, fibres), -1, slots.dtype)], 0)
    streams = expos * fibres // LANES
    count = -(-HALO // ROWS) * ROWS
    total_lanes = fib_count * pack * per
    return pl.pallas_call(
        functools.partial(prep_kernel, fib_count, pack, per, rel),
        in_specs=[in_smem, in_vmem, in_vmem, in_place, in_place],
        out_specs=[in_vmem, in_vmem, in_vmem],
        out_shape=[
            shaped((2, 2, streams, LANES)),
            shaped((total_lanes, pack * fibres), BF16),
            shaped((pack * fibres, total_lanes), BF16),
        ],
        scratch_shapes=[
            pltpu.VMEM((2, streams * count, LANES), F32),
            pltpu.VMEM((2, streams * count, LANES), F32),
            pltpu.SemaphoreType.DMA((4 * streams,)),
        ],
        compiler_params=params(),
        cost_estimate=cost(1e8, 2e6),
        name="prepare",
    )(place, coupling, slots, pixels, ivar)


def solve_kernel(
    place_ref, coupling_ref, counts_ref, good_ref, left_ref, right_ref, pixels_ref, ivar_ref, bits_ref,
    theirs_ref, mine_ref, ivar_s, pixel_s, lead_s, rest_s, sems,
):
    expos, width, fibres = pixels_ref.shape
    streams = expos * fibres // LANES
    middle = width // 2
    waits = fetch_streams(ivar_ref, 0, width, ivar_s, sems, 0)
    waits += fetch_streams(pixels_ref, 0, width, pixel_s, sems, streams)
    coupling = stream_coupling(coupling_ref, expos)
    back = 1.0 / coupling
    for wait in waits:
        wait.wait()

    def row_at(i):
        return pl.ds(i, streams, stride=width)

    def begin(edge_ref):
        u = edge_ref[0]
        return (u, 1.0 - u * back, edge_ref[1])

    def keep(side, i, state):
        n, d, b = state
        inverse = 1.0 / (d + n * back)
        lead_s[side, i] = d * inverse
        rest_s[side, i] = (b * back) * inverse

    def eliminate(it, states):
        states = list(states)
        for k in range(ROWS):
            i = it * ROWS + k
            for side, row in enumerate((i, width - 1 - i)):
                keep(side, i, states[side])
                states[side] = advance(states[side], ivar_s[row_at(row), :], pixel_s[row_at(row), :], back)
        scaled = []
        for n, d, b in states:
            scale = 1.0 / d
            scaled.append((n * scale, d * scale, b * scale))
        return tuple(scaled)

    states = lax.fori_loop(0, middle // ROWS, eliminate, (begin(left_ref), begin(right_ref)))
    for side in range(2):
        keep(side, middle, states[side])
    lead, rest = lead_s[0, middle], rest_s[0, middle]
    lead_r, rest_r = lead_s[1, middle], rest_s[1, middle]
    left = (rest + lead * rest_r) / (1.0 - lead * lead_r)
    right = rest_r + lead_r * left

    def substitute(it, values):
        values = list(values)
        for k in range(ROWS):
            i = middle - 1 - (it * ROWS + k)
            for side, row in enumerate((i, width - 1 - i)):
                pixel_s[row_at(row), :] = values[side]
                values[side] = rest_s[side, i] + lead_s[side, i] * values[side]
        return tuple(values)

    lax.fori_loop(0, middle // ROWS, substitute, (left, right))

    usable = usable_rows(place_ref, counts_ref, good_ref)
    groups = width // GROUP
    blocks = fibres // LANES

    def coadd(out_ref, which):
        def body(g, carry):
            start = (which * (groups // 2) + g) * GROUP
            words_at = (which * (groups // 2) + g) * (GROUP // BITS)
            words = [bits_ref[e, pl.ds(pl.multiple_of(words_at, GROUP // BITS), GROUP // BITS), :] for e in range(expos)]
            for tile in range(GROUP // ROWS):
                kept = [tile_words(words[e], tile) for e in range(expos)]
                for h in range(blocks):
                    cut = slice(h * LANES, (h + 1) * LANES)
                    total = None
                    for e in range(expos):
                        at = pl.ds(pl.multiple_of((h * expos + e) * width + start + ROWS * tile, ROWS), ROWS)
                        weight = jnp.where(kept[e][:, cut], ivar_s[at, :] * usable[e][:, cut], 0.0)
                        term = weight * pixel_s[at, :]
                        total = term if e == 0 else total + term
                    out_ref[pl.ds(pl.multiple_of(g * GROUP + ROWS * tile, ROWS), ROWS), cut] = total
            return carry

        lax.fori_loop(0, groups // 2, body, 0)

    coadd(theirs_ref, 1 - place_ref[2])
    coadd(mine_ref, place_ref[2])


def flux_sums(place, coupling, counts, good, left, right, pixels, ivar, bits):
    expos, width, fibres = pixels.shape
    streams = expos * fibres // LANES
    out = shaped((width // 2, fibres))
    stream_scratch = pltpu.VMEM((streams * width, LANES), F32)
    factor_scratch = pltpu.VMEM((2, width // 2 + 1, streams, LANES), F32)
    return pl.pallas_call(
        solve_kernel,
        in_specs=[in_smem] + [in_vmem] * 5 + [in_place, in_place, in_vmem],
        out_specs=[in_vmem, in_vmem],
        out_shape=[out, out],
        scratch_shapes=[
            stream_scratch,
            stream_scratch,
            factor_scratch,
            factor_scratch,
            pltpu.SemaphoreType.DMA((2 * streams,)),
        ],
        compiler_params=params(),
        cost_estimate=cost(30 * pixels.size, 10 * pixels.size),
        name="flux_sums",
    )(place, coupling, counts, good, left, right, pixels, ivar, bits)


def split_dot(x, table, dims):
    top = x.astype(BF16)
    low = (x - top.astype(F32)).astype(BF16)
    both = lax.dot_general(jnp.concatenate([top, low], 0), table, dims, preferred_element_type=F32)
    return both[: x.shape[0]] + both[x.shape[0] :]


def sort_kernel(pack, theirs_ref, mine_ref, table_ref, *out_refs):
    values, rows, _ = mine_ref.shape
    part = rows // pack
    totals = [mine_ref[v] + theirs_ref[v] for v in range(values)]
    x = jnp.concatenate(
        [jnp.concatenate([t[h * part : (h + 1) * part] for h in range(pack)], 1) for t in totals], 0
    )
    moved = split_dot(x, table_ref[...], NT)
    lanes = moved.shape[1] // len(out_refs)
    for d, out_ref in enumerate(out_refs):
        for v in range(values):
            out_ref[v] = moved[v * part : (v + 1) * part, d * lanes : (d + 1) * lanes]


def sort_fibres(theirs, mine, table, pack, pieces):
    values, rows, _ = mine.shape
    lanes = table.shape[0] // pieces
    return pl.pallas_call(
        functools.partial(sort_kernel, pack),
        in_specs=[in_vmem] * 3,
        out_specs=[in_vmem] * pieces,
        out_shape=[shaped((values, rows // pack, lanes))] * pieces,
        compiler_params=params(),
        cost_estimate=cost(4 * values * rows * table.size // pack, 3 * mine.size * 4),
        name="sort_fibres",
    )(theirs, mine, table)


def exchange(pieces, fib_count):
    if len(pieces) == 1:
        return [lax.all_to_all(pieces[0], "fib", split_axis=2, concat_axis=2, tiled=True)]
    arrived = [pieces[0]]
    for d in range(1, fib_count):
        arrived.append(lax.ppermute(pieces[d], "fib", [(i, (i + d) % fib_count) for i in range(fib_count)]))
    return arrived


def landed(refs, table):
    values, part, _ = refs[0].shape
    x = jnp.concatenate(
        [jnp.concatenate([ref[v] for ref in refs], 1) if len(refs) > 1 else refs[0][v] for v in range(values)], 0
    )
    moved = split_dot(x, table, NT)
    return [moved[v * part : (v + 1) * part] for v in range(values)]


def weights_end_kernel(pack, total, place_ref, table_ref, *refs):
    *piece_refs, ivar_ref, res_ref = refs
    weight, band = landed(piece_refs, table_ref[...])
    rows, fibres = ivar_ref.shape
    part = rows // pack
    start = (place_ref[1] * 2 + place_ref[2]) * rows
    for h in range(pack):
        at = slice(h * part, (h + 1) * part)
        cut = slice(h * fibres, (h + 1) * fibres)
        row = start + h * part + lax.broadcasted_iota(jnp.int32, (part, 1), 0)
        w, b = weight[:, cut], band[:, cut]
        inverse = 1.0 / jnp.maximum(w, 1.0)
        before = jnp.where(row == 0, 0.0, b)
        after = jnp.where(row == total - 1, 0.0, b)
        ivar_ref[at, :] = w
        res_ref[0, at, :] = before * inverse
        res_ref[1, at, :] = (w - before - after) * inverse
        res_ref[2, at, :] = after * inverse


def end_weights(place, table, pieces, pack, fibres, total):
    rows = pieces[0].shape[1] * pack
    return pl.pallas_call(
        functools.partial(weights_end_kernel, pack, total),
        in_specs=[in_smem] + [in_vmem] * (1 + len(pieces)),
        out_specs=[in_vmem] * 2,
        out_shape=[shaped((rows, fibres)), shaped((3, rows, fibres))],
        compiler_params=params(),
        cost_estimate=cost(4 * rows * table.size, 6 * rows * fibres * 4),
        name="end_weights",
    )(place, table, *pieces)


def flux_end_kernel(pack, table_ref, ivar_ref, *refs):
    *piece_refs, flux_ref = refs
    (flux,) = landed(piece_refs, table_ref[...])
    rows, fibres = flux_ref.shape
    part = rows // pack
    for h in range(pack):
        at = slice(h * part, (h + 1) * part)
        flux_ref[at, :] = flux[:, h * fibres : (h + 1) * fibres] / jnp.maximum(ivar_ref[at, :], 1.0)


def end_flux(table, ivar, pieces, pack):
    rows, fibres = ivar.shape
    return pl.pallas_call(
        functools.partial(flux_end_kernel, pack),
        in_specs=[in_vmem] * (2 + len(pieces)),
        out_specs=in_vmem,
        out_shape=shaped((rows, fibres)),
        compiler_params=params(),
        cost_estimate=cost(2 * rows * table.size, 3 * rows * fibres * 4),
        name="end_flux",
    )(table, ivar, *pieces)


def per_device(pixels, pixel_ivar, clip_bits, coupling, counts, good_flags, owner_slot):
    expos, width, fibres = pixels.shape
    fib_count, wav_count = lax.axis_size("fib"), lax.axis_size("wav")
    total = width * wav_count
    per = fibres // fib_count
    rows = width // 2
    pack = max(1, LANES // per)
    while pack > 1 and rows % (pack * ROWS):
        pack //= 2
    rel = pack * per == LANES
    pieces = fib_count if rel else 1
    place = jnp.stack([lax.axis_index(axis) for axis in ("fib", "wav", "exp")]).astype(jnp.int32)
    coupling, counts = coupling[None], counts[None]
    swap = [(0, 1), (1, 0)]

    theirs, mine = weight_sums(place, coupling, counts, good_flags, pixel_ivar, clip_bits, total)
    theirs = lax.ppermute(theirs, "exp", swap)
    edges, send_table, recv_table = prepare(
        place, coupling, owner_slot.reshape(fib_count, fibres), pixels, pixel_ivar, pack, per, rel
    )
    up = [(i, i + 1) for i in range(wav_count - 1)]
    left = lax.ppermute(edges[0], "wav", up)
    right = lax.ppermute(edges[1], "wav", [(j, i) for i, j in up])
    weight_pieces = exchange(sort_fibres(theirs, mine, send_table, pack, pieces), fib_count)

    theirs, mine = flux_sums(
        place, coupling, counts, good_flags, left, right, pixels, pixel_ivar, clip_bits
    )
    theirs = lax.ppermute(theirs, "exp", swap)
    flux_pieces = exchange(sort_fibres(theirs[None], mine[None], send_table, pack, pieces), fib_count)

    ivar, res = end_weights(place, recv_table, weight_pieces, pack, fibres, total)
    flux = end_flux(recv_table, ivar, flux_pieces, pack)
    return (flux, ivar, res)


def solution(mesh):
    return jax.shard_map(
        per_device,
        mesh=mesh,
        in_specs=(
            P("exp", "wav", "fib"),
            P("exp", "wav", "fib"),
            P("exp", "wav", "fib"),
            P("fib"),
            P("fib"),
            P("exp", "fib"),
            P(),
        ),
        out_specs=(
            P(("wav", "exp"), "fib"),
            P(("wav", "exp"), "fib"),
            P(None, ("wav", "exp"), "fib"),
        ),
        check_vma=False,
    )
```

```python
import functools

import jax
import jax.numpy as jnp
from jax import lax
from jax.experimental import pallas as pl
from jax.experimental.pallas import tpu as pltpu
from jax.sharding import PartitionSpec as P

HALO = 50
BITS = 15
LANES = 128
ROWS = 8
GROUP = 120
VMEM_BYTES = 32 * 1024 * 1024
F32 = jnp.float32
BF16 = jnp.bfloat16
NT = (((1,), (1,)), ((), ()))

in_vmem = pl.BlockSpec(memory_space=pltpu.VMEM)
in_smem = pl.BlockSpec(memory_space=pltpu.SMEM)
in_hbm = pl.BlockSpec(memory_space=pltpu.HBM)


def params():
    return pltpu.CompilerParams(vmem_limit_bytes=VMEM_BYTES)


def cost(flops, moved):
    return pl.CostEstimate(flops=int(flops), bytes_accessed=int(moved), transcendentals=0)


def held_in_hbm(*arrays):
    return [pltpu.with_memory_space_constraint(array, pltpu.HBM) for array in arrays]


def shaped(shape, dtype=F32):
    return jax.ShapeDtypeStruct(shape, dtype)


def usable_rows(place_ref, counts_ref, good_ref):
    count = good_ref.shape[0]
    return [
        good_ref[e : e + 1, :].astype(F32)
        * jnp.where(place_ref[2] * count + e < counts_ref[...], 1.0, 0.0)
        for e in range(count)
    ]


def tile_bits(tile):
    first, last = (ROWS * tile) // BITS, (ROWS * tile + ROWS - 1) // BITS
    split = BITS * last - ROWS * tile
    row = lax.broadcasted_iota(jnp.int32, (ROWS, 1), 0)
    word = jnp.where(row >= split, last, first)
    return first, last, split, jnp.left_shift(1, ROWS * tile + row - BITS * word)


def tile_words(words, tile):
    first, last, split, mask = tile_bits(tile)
    picked = words[first : first + 1, :]
    if last != first:
        row = lax.broadcasted_iota(jnp.int32, (ROWS, 1), 0)
        picked = jnp.where(row >= split, words[last : last + 1, :], picked)
    return (picked & mask) != 0


def in_flight(pairs, sems, at=0):
    copies = [pltpu.make_async_copy(source, target, sems.at[at + i]) for i, (source, target) in enumerate(pairs)]
    for copy in copies:
        copy.start()
    return copies


def inverse_of(x):
    guess = pl.reciprocal(x, approx=True)
    return guess * (2.0 - x * guess)


def owners(slots_ref, fib_count, fibres):
    rows = [slots_ref[:, s * fibres : (s + 1) * fibres].astype(F32) for s in range(fib_count)]
    sources = -(-fib_count // ROWS) * ROWS
    if sources > fib_count:
        rows.append(jnp.full((sources - fib_count, fibres), -1.0, F32))
    slots = jnp.concatenate(rows, 0)
    owner = jnp.floor((slots + 0.5) * (1.0 / fibres))
    return owner, slots - owner * fibres


def earlier_fibres(fibres):
    row = lax.broadcasted_iota(jnp.int32, (fibres, fibres), 0)
    col = lax.broadcasted_iota(jnp.int32, (fibres, fibres), 1)
    return (row < col).astype(F32).astype(BF16)


def write_send_table(fib_count, pack, per, rel, me, slots_ref, table_ref):
    fibres = table_ref.shape[1] // pack
    lanes = pack * per
    owner, _ = owners(slots_ref, fib_count, fibres)
    source = lax.broadcasted_iota(jnp.int32, owner.shape, 0)
    my_owner = jnp.sum(jnp.where(source == me, owner, 0.0), axis=0, keepdims=True).astype(jnp.int32)
    to_owner = (source == my_owner).astype(F32)
    counted = jnp.dot(to_owner.astype(BF16), earlier_fibres(fibres), preferred_element_type=F32)
    rank = jnp.sum(to_owner * counted, axis=0, keepdims=True).astype(jnp.int32)
    target = my_owner
    if rel:
        target = jnp.where(my_owner >= me, my_owner - me, my_owner - me + fib_count)
    base = target * lanes + rank
    place_of = jnp.concatenate([base + h * per for h in range(pack)], 1)
    row = lax.broadcasted_iota(jnp.int32, table_ref.shape, 0)
    table_ref[...] = (row == place_of).astype(F32).astype(BF16)


def write_recv_table(fib_count, pack, per, rel, me, slots_ref, table_ref):
    fibres = table_ref.shape[0] // pack
    lanes = pack * per
    total_lanes = fib_count * lanes
    owner, column = owners(slots_ref, fib_count, fibres)
    source = lax.broadcasted_iota(jnp.int32, owner.shape, 0)
    mine = (owner == me.astype(F32)).astype(F32)
    rank_in = jnp.dot(mine.astype(BF16), earlier_fibres(fibres), preferred_element_type=F32).astype(jnp.int32)
    order = source
    if rel:
        order = jnp.where(me >= source, me - source, me - source + fib_count)
    arrival = jnp.where(mine > 0.0, order * lanes + rank_in, -total_lanes)
    tall = lax.broadcasted_iota(jnp.int32, (total_lanes, fibres), 0)
    landing = jnp.zeros((ROWS, total_lanes), F32)
    for s in range(fib_count):
        hit = tall == arrival[s : s + 1, :]
        for h in range(1, pack):
            hit = hit | (tall == arrival[s : s + 1, :] + h * per)
        values = jnp.broadcast_to(column[s : s + 1, :], (ROWS, fibres)).astype(BF16)
        landing = landing + lax.dot_general(
            values, hit.astype(F32).astype(BF16), NT, preferred_element_type=F32
        )
    lane = lax.broadcasted_iota(jnp.int32, (1, total_lanes), 1)
    landing = landing[0:1, :].astype(jnp.int32)
    for h in range(1, pack):
        inside = (lane % lanes >= h * per) & (lane % lanes < (h + 1) * per)
        landing = jnp.where(inside, landing + h * fibres, landing)
    row = lax.broadcasted_iota(jnp.int32, table_ref.shape, 0)
    table_ref[...] = (row == landing).astype(F32).astype(BF16)


def weights_kernel(
    write_table, mine, wav_count, place_ref, slots_ref, coupling_ref, counts_ref, good_ref, ivar_ref, bits_ref,
    sums_ref, weight_ref, table_ref, slots_v, coupling_v, counts_v, good_v, ivar_v, bits_v, sems,
):
    expos, width, _ = ivar_ref.shape
    half = width // 2
    groups = half // GROUP
    which = place_ref[2] if mine else 1 - place_ref[2]
    first = pl.multiple_of(which * half, ROWS)
    first_word = pl.multiple_of(which * (half // BITS), ROWS)
    waits = in_flight(
        [
            (slots_ref, slots_v),
            (coupling_ref, coupling_v),
            (counts_ref, counts_v),
            (good_ref, good_v),
            (bits_ref.at[:, pl.ds(first_word, half // BITS), :], bits_v),
        ]
        + [
            (ivar_ref.at[:, pl.ds(first + g * GROUP, GROUP), :], ivar_v.at[:, pl.ds(g * GROUP, GROUP), :])
            for g in range(groups)
        ],
        sems,
    )
    waits[0].wait()
    write_table(place_ref[0], slots_v, table_ref)
    for wait in waits[1:5]:
        wait.wait()
    coupling = coupling_v[...]
    usable = usable_rows(place_ref, counts_v, good_v)
    start = place_ref[1] * width + first
    tiles = half // ROWS
    tiles_in_group = GROUP // ROWS
    words_in_group = GROUP // BITS
    for tile in range(tiles):
        group, within = divmod(tile, tiles_in_group)
        if within == 0:
            waits[5 + group].wait()
        links = 4.0 * coupling
        if tile in (0, tiles - 1):
            row = start + ROWS * tile + lax.broadcasted_iota(jnp.int32, (ROWS, 1), 0)
            links = jnp.where((row == 0) | (row == wav_count * width - 1), 2.0, 4.0) * coupling
        at = slice(ROWS * tile, ROWS * (tile + 1))
        weight_sum = band_sum = None
        for e in range(expos):
            ivar = ivar_v[e, at, :]
            words = bits_v[e, words_in_group * group : words_in_group * (group + 1), :]
            weight = jnp.where(tile_words(words, within), ivar * usable[e], 0.0)
            weight_ref[e, at, :] = weight
            band = weight * inverse_of(ivar + links)
            weight_sum = weight if e == 0 else weight_sum + weight
            band_sum = band if e == 0 else band_sum + band
        sums_ref[0, at, :] = weight_sum
        sums_ref[1, at, :] = band_sum * coupling


def weight_sums(write_table, table_shape, mine, wav_count, place, slots, coupling, counts, good, ivar, bits):
    expos, width, fibres = ivar.shape
    half = width // 2
    return pl.pallas_call(
        functools.partial(weights_kernel, write_table, mine, wav_count),
        in_specs=[in_smem] + [in_hbm] * 6,
        out_specs=[in_vmem] * 3,
        out_shape=[shaped((2, half, fibres)), shaped((expos, half, fibres)), shaped(table_shape, BF16)],
        scratch_shapes=[
            pltpu.VMEM(slots.shape, jnp.int32),
            pltpu.VMEM(coupling.shape, F32),
            pltpu.VMEM(counts.shape, jnp.int32),
            pltpu.VMEM(good.shape, jnp.int32),
            pltpu.VMEM((expos, half, fibres), F32),
            pltpu.VMEM((expos, half // BITS, fibres), jnp.int32),
            pltpu.SemaphoreType.DMA((5 + half // GROUP,)),
        ],
        compiler_params=params(),
        cost_estimate=cost(20 * ivar.size, 6 * ivar.size),
        name="weights_kept" if mine else "weights_sent",
    )(place, *held_in_hbm(slots, coupling, counts, good, ivar, bits))


def stream_coupling(coupling_ref, expos):
    coupling = coupling_ref[...]
    blocks = coupling.shape[1] // LANES
    return jnp.concatenate(
        [jnp.broadcast_to(coupling[:, h * LANES : (h + 1) * LANES], (expos, LANES)) for h in range(blocks)], 0
    )


def advance(state, ivar, pixel, back_coupling):
    n, d, b = state
    d = d + n * back_coupling
    return (n + ivar * d, d, b + (ivar * pixel) * d)


def edges_kernel(place_ref, coupling_ref, pixels_ref, ivar_ref, edges_ref, pixel_out, ivar_out, sems):
    expos, width, fibres = pixels_ref.shape
    streams = expos * fibres // LANES
    count = -(-HALO // ROWS) * ROWS

    def copies(first, length):
        pairs = []
        for source, target in ((ivar_ref, ivar_out), (pixels_ref, pixel_out)):
            for stream in range(streams):
                h, e = divmod(stream, expos)
                pairs.append(
                    (
                        source.at[e, pl.ds(first, length), pl.ds(h * LANES, LANES)],
                        target.at[pl.ds(stream * width + first, length), :],
                    )
                )
        return pairs

    waits = in_flight(copies(0, count) + copies(width - count, count), sems)
    rest = in_flight(copies(count, width - 2 * count), sems, len(waits))
    for wait in waits:
        wait.wait()
    back = 1.0 / stream_coupling(coupling_ref, expos)
    zero = jnp.zeros((streams, LANES), F32)
    states = [(zero, zero + 1.0, zero), (zero, zero + 1.0, zero)]
    for i in range(HALO):
        for side, row in enumerate((width - HALO + i, HALO - 1 - i)):
            at = pl.ds(row, streams, stride=width)
            states[side] = advance(states[side], ivar_out[at, :], pixel_out[at, :], back)
            if i % 10 == 9:
                scale = inverse_of(states[side][1])
                states[side] = tuple(part * scale for part in states[side])
    for side in range(2):
        n, d, b = states[side]
        scale = 1.0 / (d + n * back)
        edges_ref[side, 0] = n * scale
        edges_ref[side, 1] = b * scale
    for wait in rest:
        wait.wait()


def edge_rows(place, coupling, pixels, ivar):
    expos, width, fibres = pixels.shape
    streams = expos * fibres // LANES
    laid = shaped((streams * width, LANES))
    return pl.pallas_call(
        edges_kernel,
        in_specs=[in_smem, in_vmem, in_hbm, in_hbm],
        out_specs=[in_vmem] * 3,
        out_shape=[shaped((2, 2, streams, LANES)), laid, laid],
        scratch_shapes=[pltpu.SemaphoreType.DMA((6 * streams,))],
        compiler_params=params(),
        cost_estimate=cost(0, 0),
        name="edge_rows",
    )(place, coupling, *held_in_hbm(pixels, ivar))


def solve_kernel(
    place_ref, coupling_ref, left_ref, right_ref, pixel_ref, ivar_ref, weight_t_ref, weight_m_ref,
    theirs_ref, mine_ref, solved_s, lead_s, rest_s,
):
    streams = left_ref.shape[1]
    expos, half, fibres = weight_t_ref.shape
    width = ivar_ref.shape[0] // streams
    middle = width // 2
    coupling = stream_coupling(coupling_ref, expos)
    back = 1.0 / coupling

    def row_at(i):
        return pl.ds(i, streams, stride=width)

    def begin(edge_ref):
        u = edge_ref[0]
        return (u, 1.0 - u * back, edge_ref[1])

    def keep(side, i, state):
        n, d, b = state
        inverse = inverse_of(d + n * back)
        lead_s[side, i] = d * inverse
        rest_s[side, i] = (b * back) * inverse

    def eliminate(it, states):
        states = list(states)
        for k in range(ROWS):
            i = it * ROWS + k
            for side, row in enumerate((i, width - 1 - i)):
                keep(side, i, states[side])
                states[side] = advance(states[side], ivar_ref[row_at(row), :], pixel_ref[row_at(row), :], back)
        scaled = []
        for n, d, b in states:
            scale = inverse_of(d)
            scaled.append((n * scale, d * scale, b * scale))
        return tuple(scaled)

    states = lax.fori_loop(0, middle // ROWS, eliminate, (begin(left_ref), begin(right_ref)))
    for side in range(2):
        keep(side, middle, states[side])
    lead, rest = lead_s[0, middle], rest_s[0, middle]
    lead_r, rest_r = lead_s[1, middle], rest_s[1, middle]
    left = (rest + lead * rest_r) / (1.0 - lead * lead_r)
    right = rest_r + lead_r * left

    def substitute(it, values):
        values = list(values)
        for k in range(ROWS):
            i = middle - 1 - (it * ROWS + k)
            for side, row in enumerate((i, width - 1 - i)):
                solved_s[row_at(row), :] = values[side]
                values[side] = rest_s[side, i] + lead_s[side, i] * values[side]
        return tuple(values)

    lax.fori_loop(0, middle // ROWS, substitute, (left, right))

    blocks = fibres // LANES
    unroll = 5

    def coadd(out_ref, weight_ref, which):
        start = which * half

        def body(g, carry):
            for k in range(unroll):
                row = pl.multiple_of((g * unroll + k) * ROWS, ROWS)
                for h in range(blocks):
                    cut = pl.ds(h * LANES, LANES)
                    total = None
                    for e in range(expos):
                        at = pl.ds(pl.multiple_of((h * expos + e) * width + start + row, ROWS), ROWS)
                        term = weight_ref[e, pl.ds(row, ROWS), cut] * solved_s[at, :]
                        total = term if e == 0 else total + term
                    out_ref[0, pl.ds(row, ROWS), cut] = total
            return carry

        lax.fori_loop(0, half // (unroll * ROWS), body, 0)

    coadd(theirs_ref, weight_t_ref, 1 - place_ref[2])
    coadd(mine_ref, weight_m_ref, place_ref[2])


def flux_sums(place, coupling, left, right, pixels, ivar, weight_t, weight_m):
    expos, half, fibres = weight_t.shape
    streams = left.shape[1]
    out = shaped((1, half, fibres))
    factor_scratch = pltpu.VMEM((2, half + 1, streams, LANES), F32)
    return pl.pallas_call(
        solve_kernel,
        in_specs=[in_smem] + [in_vmem] * 7,
        out_specs=[in_vmem, in_vmem],
        out_shape=[out, out],
        scratch_shapes=[pltpu.VMEM(pixels.shape, F32), factor_scratch, factor_scratch],
        compiler_params=params(),
        cost_estimate=cost(0, 0),
        name="flux_sums",
    )(place, coupling, left, right, pixels, ivar, weight_t, weight_m)


def split_dot(x, table, dims):
    top = x.astype(BF16)
    low = (x - top.astype(F32)).astype(BF16)
    both = lax.dot_general(jnp.concatenate([top, low], 0), table, dims, preferred_element_type=F32)
    return both[: x.shape[0]] + both[x.shape[0] :]


def sort_kernel(pack, scaled, theirs_ref, mine_ref, table_ref, *refs):
    values, rows, _ = mine_ref.shape
    part = rows // pack
    totals = [mine_ref[v] + theirs_ref[v] for v in range(values)]
    if scaled:
        scale_ref, *out_refs = refs
        totals = [t * scale_ref[...] for t in totals]
    else:
        *out_refs, scale_ref = refs
        scale = 1.0 / jnp.maximum(totals[0], 1.0)
        scale_ref[...] = scale
        totals[1] = totals[1] * scale
    x = jnp.concatenate(
        [jnp.concatenate([t[h * part : (h + 1) * part] for h in range(pack)], 1) for t in totals], 0
    )
    moved = split_dot(x, table_ref[...], NT)
    lanes = moved.shape[1] // len(out_refs)
    for d, out_ref in enumerate(out_refs):
        for v in range(values):
            out_ref[v] = moved[v * part : (v + 1) * part, d * lanes : (d + 1) * lanes]


def sort_fibres(theirs, mine, table, pack, pieces, scale=None):
    values, rows, fibres = mine.shape
    lanes = table.shape[0] // pieces
    scaled = scale is not None
    outs = [shaped((values, rows // pack, lanes))] * pieces + ([] if scaled else [shaped((rows, fibres))])
    args = (theirs, mine, table) + ((scale,) if scaled else ())
    return pl.pallas_call(
        functools.partial(sort_kernel, pack, scaled),
        in_specs=[in_vmem] * len(args),
        out_specs=[in_vmem] * len(outs),
        out_shape=outs,
        compiler_params=params(),
        cost_estimate=cost(0, 0),
        name="sort_flux" if scaled else "sort_weights",
    )(*args)


def exchange(pieces, fib_count):
    if len(pieces) == 1:
        return [lax.all_to_all(pieces[0], "fib", split_axis=2, concat_axis=2, tiled=True)]
    arrived = [pieces[0]]
    for d in range(1, fib_count):
        arrived.append(lax.ppermute(pieces[d], "fib", [(i, (i + d) % fib_count) for i in range(fib_count)]))
    return arrived


def landed(refs, table):
    values, part, _ = refs[0].shape
    x = jnp.concatenate(
        [jnp.concatenate([ref[v] for ref in refs], 1) if len(refs) > 1 else refs[0][v] for v in range(values)], 0
    )
    moved = split_dot(x, table, NT)
    return [moved[v * part : (v + 1) * part] for v in range(values)]


def weights_end_kernel(pack, total, place_ref, table_ref, *refs):
    *piece_refs, ivar_ref, res_ref = refs
    weight, band = landed(piece_refs, table_ref[...])
    rows, fibres = ivar_ref.shape
    part = rows // pack
    start = (place_ref[1] * 2 + place_ref[2]) * rows
    for h in range(pack):
        at = slice(h * part, (h + 1) * part)
        cut = slice(h * fibres, (h + 1) * fibres)
        row = start + h * part + lax.broadcasted_iota(jnp.int32, (part, 1), 0)
        w, b = weight[:, cut], band[:, cut]
        before = jnp.where(row == 0, 0.0, b)
        after = jnp.where(row == total - 1, 0.0, b)
        ivar_ref[at, :] = w
        res_ref[0, at, :] = before
        res_ref[1, at, :] = jnp.minimum(w, 1.0) - before - after
        res_ref[2, at, :] = after


def end_weights(place, table, pieces, pack, fibres, total):
    rows = pieces[0].shape[1] * pack
    return pl.pallas_call(
        functools.partial(weights_end_kernel, pack, total),
        in_specs=[in_smem] + [in_vmem] * (1 + len(pieces)),
        out_specs=[in_vmem] * 2,
        out_shape=[shaped((rows, fibres)), shaped((3, rows, fibres))],
        compiler_params=params(),
        cost_estimate=cost(4 * rows * table.size, 6 * rows * fibres * 4),
        name="end_weights",
    )(place, table, *pieces)


def flux_end_kernel(pack, table_ref, *refs):
    *piece_refs, flux_ref = refs
    (flux,) = landed(piece_refs, table_ref[...])
    rows, fibres = flux_ref.shape
    part = rows // pack
    for h in range(pack):
        flux_ref[h * part : (h + 1) * part, :] = flux[:, h * fibres : (h + 1) * fibres]


def end_flux(table, pieces, pack, fibres):
    rows = pieces[0].shape[1] * pack
    return pl.pallas_call(
        functools.partial(flux_end_kernel, pack),
        in_specs=[in_vmem] * (1 + len(pieces)),
        out_specs=in_vmem,
        out_shape=shaped((rows, fibres)),
        compiler_params=params(),
        cost_estimate=cost(2 * rows * table.size, 2 * rows * fibres * 4),
        name="end_flux",
    )(table, *pieces)


def after(value, done):
    return lax.optimization_barrier((value, done))[0]


def per_device(pixels, pixel_ivar, clip_bits, coupling, counts, good_flags, owner_slot):
    expos, width, fibres = pixels.shape
    fib_count, wav_count = lax.axis_size("fib"), lax.axis_size("wav")
    total = width * wav_count
    per = fibres // fib_count
    rows = width // 2
    pack = max(1, LANES // per)
    while pack > 1 and rows % (pack * ROWS):
        pack //= 2
    rel = pack * per == LANES
    pieces = fib_count if rel else 1
    place = jnp.stack([lax.axis_index(axis) for axis in ("fib", "wav", "exp")]).astype(jnp.int32)
    coupling, counts, slots = coupling[None], counts[None], owner_slot[None]
    swap = [(0, 1), (1, 0)]
    moves = (fib_count, pack, per, rel)
    send_shape = (fib_count * pack * per, pack * fibres)

    theirs, weight_t, send_table = weight_sums(
        functools.partial(write_send_table, *moves), send_shape, False, wav_count,
        place, slots, coupling, counts, good_flags, pixel_ivar, clip_bits,
    )
    arriving = lax.ppermute(theirs, "exp", swap)
    mine, weight_m, recv_table = weight_sums(
        functools.partial(write_recv_table, *moves), send_shape[::-1], True, wav_count,
        after(place, theirs), slots, coupling, counts, good_flags, pixel_ivar, clip_bits,
    )
    *sorted_pieces, scale = sort_fibres(arriving, mine, send_table, pack, pieces)
    weight_pieces = exchange(sorted_pieces, fib_count)

    edges, pixel_s, ivar_s = edge_rows(after(place, scale), coupling, pixels, pixel_ivar)
    up = [(i, i + 1) for i in range(wav_count - 1)]
    left = lax.ppermute(edges[0], "wav", up)
    right = lax.ppermute(edges[1], "wav", [(j, i) for i, j in up])
    if rel:
        left = after(left, weight_pieces[fib_count // 2])
    theirs, mine = flux_sums(place, coupling, left, right, pixel_s, ivar_s, weight_t, weight_m)
    if rel:
        theirs = after(theirs, weight_pieces[1])
    theirs = lax.ppermute(theirs, "exp", swap)
    flux_pieces = exchange(sort_fibres(theirs, mine, send_table, pack, pieces, scale), fib_count)

    ivar, res = end_weights(place, recv_table, weight_pieces, pack, fibres, total)
    flux = end_flux(recv_table, flux_pieces, pack, fibres)
    return (flux, ivar, res)


def solution(mesh):
    return jax.shard_map(
        per_device,
        mesh=mesh,
        in_specs=(
            P("exp", "wav", "fib"),
            P("exp", "wav", "fib"),
            P("exp", "wav", "fib"),
            P("fib"),
            P("fib"),
            P("exp", "fib"),
            P(),
        ),
        out_specs=(
            P(("wav", "exp"), "fib"),
            P(("wav", "exp"), "fib"),
            P(None, ("wav", "exp"), "fib"),
        ),
        check_vma=False,
    )
```

```python
import functools

import jax
import jax.numpy as jnp
from jax import lax
from jax.experimental import pallas as pl
from jax.experimental.pallas import tpu as pltpu
from jax.sharding import PartitionSpec as P

HALO = 50
BITS = 15
LANES = 128
ROWS = 8
GROUP = 120
VMEM_BYTES = 32 * 1024 * 1024
F32 = jnp.float32
BF16 = jnp.bfloat16
NT = (((1,), (1,)), ((), ()))

in_vmem = pl.BlockSpec(memory_space=pltpu.VMEM)
in_smem = pl.BlockSpec(memory_space=pltpu.SMEM)
in_hbm = pl.BlockSpec(memory_space=pltpu.HBM)


def params():
    return pltpu.CompilerParams(vmem_limit_bytes=VMEM_BYTES)


def cost(flops, moved):
    return pl.CostEstimate(flops=int(flops), bytes_accessed=int(moved), transcendentals=0)


def held_in_hbm(*arrays):
    return [pltpu.with_memory_space_constraint(array, pltpu.HBM) for array in arrays]


def shaped(shape, dtype=F32):
    return jax.ShapeDtypeStruct(shape, dtype)


def usable_rows(place_ref, counts_ref, good_ref):
    count = good_ref.shape[0]
    return [
        good_ref[e : e + 1, :].astype(F32)
        * jnp.where(place_ref[2] * count + e < counts_ref[...], 1.0, 0.0)
        for e in range(count)
    ]


def tile_bits(tile):
    first, last = (ROWS * tile) // BITS, (ROWS * tile + ROWS - 1) // BITS
    split = BITS * last - ROWS * tile
    row = lax.broadcasted_iota(jnp.int32, (ROWS, 1), 0)
    word = jnp.where(row >= split, last, first)
    return first, last, split, jnp.left_shift(1, ROWS * tile + row - BITS * word)


def tile_words(words, tile):
    first, last, split, mask = tile_bits(tile)
    picked = words[first : first + 1, :]
    if last != first:
        row = lax.broadcasted_iota(jnp.int32, (ROWS, 1), 0)
        picked = jnp.where(row >= split, words[last : last + 1, :], picked)
    return (picked & mask) != 0


def in_flight(pairs, sems, at=0):
    copies = [pltpu.make_async_copy(source, target, sems.at[at + i]) for i, (source, target) in enumerate(pairs)]
    for copy in copies:
        copy.start()
    return copies


def inverse_of(x):
    guess = pl.reciprocal(x, approx=True)
    return guess * (2.0 - x * guess)


def advance(state, ivar, pixel, back_coupling):
    n, d, b = state
    next_d = d + n * back_coupling
    return (n * (1.0 + ivar * back_coupling) + ivar * d, next_d, b + (ivar * pixel) * next_d)


def rescaled(state):
    scale = inverse_of(state[1])
    return tuple(part * scale for part in state)


def divisor_of(size, most):
    return max(k for k in range(1, most + 1) if size % k == 0)


def owners(slots_ref, fib_count, fibres):
    rows = [slots_ref[:, s * fibres : (s + 1) * fibres].astype(F32) for s in range(fib_count)]
    sources = -(-fib_count // ROWS) * ROWS
    if sources > fib_count:
        rows.append(jnp.full((sources - fib_count, fibres), -1.0, F32))
    slots = jnp.concatenate(rows, 0)
    owner = jnp.floor((slots + 0.5) * (1.0 / fibres))
    return owner, slots - owner * fibres


def earlier_fibres(fibres):
    row = lax.broadcasted_iota(jnp.int32, (fibres, fibres), 0)
    col = lax.broadcasted_iota(jnp.int32, (fibres, fibres), 1)
    return (row < col).astype(F32).astype(BF16)


def write_send_table(fib_count, pack, per, rel, me, slots_ref, table_ref):
    fibres = table_ref.shape[1] // pack
    lanes = pack * per
    owner, _ = owners(slots_ref, fib_count, fibres)
    source = lax.broadcasted_iota(jnp.int32, owner.shape, 0)
    my_owner = jnp.sum(jnp.where(source == me, owner, 0.0), axis=0, keepdims=True).astype(jnp.int32)
    to_owner = (source == my_owner).astype(F32)
    counted = jnp.dot(to_owner.astype(BF16), earlier_fibres(fibres), preferred_element_type=F32)
    rank = jnp.sum(to_owner * counted, axis=0, keepdims=True).astype(jnp.int32)
    target = my_owner
    if rel:
        target = jnp.where(my_owner >= me, my_owner - me, my_owner - me + fib_count)
    base = target * lanes + rank
    place_of = jnp.concatenate([base + h * per for h in range(pack)], 1)
    row = lax.broadcasted_iota(jnp.int32, table_ref.shape, 0)
    table_ref[...] = (row == place_of).astype(F32).astype(BF16)


def write_recv_table(fib_count, pack, per, rel, me, slots_ref, table_ref):
    fibres = table_ref.shape[0] // pack
    lanes = pack * per
    total_lanes = fib_count * lanes
    owner, column = owners(slots_ref, fib_count, fibres)
    source = lax.broadcasted_iota(jnp.int32, owner.shape, 0)
    mine = (owner == me.astype(F32)).astype(F32)
    rank_in = jnp.dot(mine.astype(BF16), earlier_fibres(fibres), preferred_element_type=F32).astype(jnp.int32)
    order = source
    if rel:
        order = jnp.where(me >= source, me - source, me - source + fib_count)
    arrival = jnp.where(mine > 0.0, order * lanes + rank_in, -total_lanes)
    tall = lax.broadcasted_iota(jnp.int32, (total_lanes, fibres), 0)
    landing = jnp.zeros((ROWS, total_lanes), F32)
    for s in range(fib_count):
        hit = tall == arrival[s : s + 1, :]
        for h in range(1, pack):
            hit = hit | (tall == arrival[s : s + 1, :] + h * per)
        values = jnp.broadcast_to(column[s : s + 1, :], (ROWS, fibres)).astype(BF16)
        landing = landing + lax.dot_general(
            values, hit.astype(F32).astype(BF16), NT, preferred_element_type=F32
        )
    lane = lax.broadcasted_iota(jnp.int32, (1, total_lanes), 1)
    landing = landing[0:1, :].astype(jnp.int32)
    for h in range(1, pack):
        inside = (lane % lanes >= h * per) & (lane % lanes < (h + 1) * per)
        landing = jnp.where(inside, landing + h * fibres, landing)
    row = lax.broadcasted_iota(jnp.int32, table_ref.shape, 0)
    table_ref[...] = (row == landing).astype(F32).astype(BF16)


def stream_coupling(coupling_ref, expos):
    coupling = coupling_ref[...]
    blocks = coupling.shape[1] // LANES
    return jnp.concatenate(
        [jnp.broadcast_to(coupling[:, h * LANES : (h + 1) * LANES], (expos, LANES)) for h in range(blocks)], 0
    )


def weight_tile(coupling, usable, words, ivars, within, scale_row):
    links = scale_row * coupling
    weights = []
    weight_sum = band_sum = None
    for e, ivar in enumerate(ivars):
        weight = jnp.where(tile_words(words[e], within), ivar * usable[e], 0.0)
        band = weight * inverse_of(ivar + links)
        weights.append(weight)
        weight_sum = weight if e == 0 else weight_sum + weight
        band_sum = band if e == 0 else band_sum + band
    return weights, weight_sum, band_sum * coupling


def half_copies(which, ivar_ref, bits_ref, ivar_v, bits_v):
    half = ivar_v.shape[1]
    first = pl.multiple_of(which * half, ROWS)
    first_word = pl.multiple_of(which * (half // BITS), ROWS)
    return [
        (bits_ref.at[:, pl.ds(first_word, half // BITS), :], bits_v),
        (ivar_ref.at[:, pl.ds(first, half), :], ivar_v),
    ]


def write_weights(place_ref, wav_count, which, coupling_v, counts_v, good_v, ivar_v, bits_v, sums_ref, weight_ref, beside):
    expos, half, _ = ivar_v.shape
    coupling = coupling_v[...]
    usable = usable_rows(place_ref, counts_v, good_v)
    start = place_ref[1] * (2 * half) + which * half
    tiles = half // ROWS
    tiles_in_group = GROUP // ROWS
    words_in_group = GROUP // BITS
    for tile in range(tiles):
        group, within = divmod(tile, tiles_in_group)
        scale_row = 4.0
        if tile in (0, tiles - 1):
            row = start + ROWS * tile + lax.broadcasted_iota(jnp.int32, (ROWS, 1), 0)
            scale_row = jnp.where((row == 0) | (row == wav_count * 2 * half - 1), 2.0, 4.0)
        at = slice(ROWS * tile, ROWS * (tile + 1))
        words = [bits_v[e, words_in_group * group : words_in_group * (group + 1), :] for e in range(expos)]
        weights, weight_sum, band_sum = weight_tile(
            coupling, usable, words, [ivar_v[e, at, :] for e in range(expos)], within, scale_row
        )
        for e in range(expos):
            weight_ref[e, at, :] = weights[e]
        sums_ref[0, at, :] = weight_sum
        sums_ref[1, at, :] = band_sum
        beside(tile, tiles)


def stream_copies(source_ref, target, first, length, pitch, offset):
    expos, _, fibres = source_ref.shape
    return [
        (
            source_ref.at[e, pl.ds(first, length), pl.ds(h * LANES, LANES)],
            target.at[pl.ds((h * expos + e) * pitch + offset, length), :],
        )
        for h in range(fibres // LANES)
        for e in range(expos)
    ]


def first_kernel(
    moves, wav_count, place_ref, slots_ref, coupling_ref, counts_ref, good_ref, pixels_ref, ivar_ref, bits_ref,
    sums_ref, weight_ref, table_ref, up_ref, down_ref,
    slots_v, coupling_v, counts_v, good_v, ivar_v, bits_v, ivar_s, pixel_s, sems,
):
    expos, width, fibres = ivar_ref.shape
    streams = expos * fibres // LANES
    count = ivar_s.shape[0] // (2 * streams)
    which = 1 - place_ref[2]
    pairs = [(slots_ref, slots_v), (coupling_ref, coupling_v), (counts_ref, counts_v), (good_ref, good_v)]
    for source, target in ((ivar_ref, ivar_s), (pixels_ref, pixel_s)):
        pairs += stream_copies(source, target, 0, count, 2 * count, 0)
        pairs += stream_copies(source, target, width - count, count, 2 * count, count)
    pairs += half_copies(which, ivar_ref, bits_ref, ivar_v, bits_v)
    waits = in_flight(pairs, sems)
    waits[0].wait()
    write_send_table(*moves, place_ref[0], slots_v, table_ref)
    for wait in waits[1:]:
        wait.wait()

    back = 1.0 / stream_coupling(coupling_v, expos)
    zero = jnp.zeros((streams, LANES), F32)
    states = [(zero, zero + 1.0, zero), (zero, zero + 1.0, zero)]

    def eliminate(tile, tiles):
        for i in range(HALO * tile // tiles, HALO * (tile + 1) // tiles):
            for side, row in enumerate((2 * count - HALO + i, HALO - 1 - i)):
                at = pl.ds(row, streams, stride=2 * count)
                states[side] = advance(states[side], ivar_s[at, :], pixel_s[at, :], back)
                if i % 24 == 23:
                    states[side] = rescaled(states[side])

    write_weights(
        place_ref, wav_count, which, coupling_v, counts_v, good_v, ivar_v, bits_v, sums_ref, weight_ref, eliminate
    )
    for (n, d, b), out_ref in zip(states, (up_ref, down_ref)):
        scale = 1.0 / (d + n * back)
        out_ref[0] = n * scale
        out_ref[1] = b * scale


def weights_scratch(slots, coupling, counts, good, ivar):
    expos, width, fibres = ivar.shape
    half = width // 2
    return [
        pltpu.VMEM(coupling.shape, F32),
        pltpu.VMEM(counts.shape, jnp.int32),
        pltpu.VMEM(good.shape, jnp.int32),
        pltpu.VMEM((expos, half, fibres), F32),
        pltpu.VMEM((expos, half // BITS, fibres), jnp.int32),
    ]


def sent_weights(moves, wav_count, place, slots, coupling, counts, good, pixels, ivar, bits):
    expos, width, fibres = ivar.shape
    half = width // 2
    streams = expos * fibres // LANES
    fib_count, pack, per, _ = moves
    count = -(-HALO // ROWS) * ROWS
    edge = shaped((2, streams, LANES))
    return pl.pallas_call(
        functools.partial(first_kernel, moves, wav_count),
        in_specs=[in_smem] + [in_hbm] * 7,
        out_specs=[in_vmem] * 5,
        out_shape=[
            shaped((2, half, fibres)),
            shaped((expos, half, fibres)),
            shaped((fib_count * pack * per, pack * fibres), BF16),
            edge,
            edge,
        ],
        scratch_shapes=[
            pltpu.VMEM(slots.shape, jnp.int32),
            *weights_scratch(slots, coupling, counts, good, ivar),
            pltpu.VMEM((streams * 2 * count, LANES), F32),
            pltpu.VMEM((streams * 2 * count, LANES), F32),
            pltpu.SemaphoreType.DMA((6 + 4 * streams,)),
        ],
        compiler_params=params(),
        cost_estimate=cost(20 * ivar.size, 6 * ivar.size),
        name="sent_weights",
    )(place, *held_in_hbm(slots, coupling, counts, good, pixels, ivar, bits))


def second_kernel(
    wav_count, place_ref, coupling_ref, counts_ref, good_ref, pixels_ref, ivar_ref, bits_ref,
    sums_ref, weight_ref, pixel_out, ivar_out, coupling_v, counts_v, good_v, ivar_v, bits_v, sems,
):
    width = ivar_ref.shape[1]
    which = place_ref[2]
    pairs = [(coupling_ref, coupling_v), (counts_ref, counts_v), (good_ref, good_v)]
    pairs += half_copies(which, ivar_ref, bits_ref, ivar_v, bits_v)
    waits = in_flight(pairs, sems)
    laid = stream_copies(ivar_ref, ivar_out, 0, width, width, 0) + stream_copies(pixels_ref, pixel_out, 0, width, width, 0)
    rest = in_flight(laid, sems, len(waits))
    for wait in waits:
        wait.wait()
    write_weights(
        place_ref, wav_count, which, coupling_v, counts_v, good_v, ivar_v, bits_v, sums_ref, weight_ref,
        lambda tile, tiles: None,
    )
    for wait in rest:
        wait.wait()


def kept_weights(wav_count, place, coupling, counts, good, pixels, ivar, bits):
    expos, width, fibres = ivar.shape
    half = width // 2
    streams = expos * fibres // LANES
    laid = shaped((streams * width, LANES))
    return pl.pallas_call(
        functools.partial(second_kernel, wav_count),
        in_specs=[in_smem] + [in_hbm] * 6,
        out_specs=[in_vmem] * 4,
        out_shape=[shaped((2, half, fibres)), shaped((expos, half, fibres)), laid, laid],
        scratch_shapes=[
            *weights_scratch(None, coupling, counts, good, ivar),
            pltpu.SemaphoreType.DMA((5 + 2 * streams,)),
        ],
        compiler_params=params(),
        cost_estimate=cost(20 * ivar.size, 6 * ivar.size),
        name="kept_weights",
    )(place, *held_in_hbm(coupling, counts, good, pixels, ivar, bits))


def recv_kernel(moves, place_ref, slots_ref, table_ref):
    write_recv_table(*moves, place_ref[0], slots_ref, table_ref)


def recv_moves(moves, place, slots, fibres):
    fib_count, pack, per, _ = moves
    return pl.pallas_call(
        functools.partial(recv_kernel, moves),
        in_specs=[in_smem, in_vmem],
        out_specs=in_vmem,
        out_shape=shaped((pack * fibres, fib_count * pack * per), BF16),
        compiler_params=params(),
        cost_estimate=cost(1e6, 1e6),
        name="recv_moves",
    )(place, slots)


def solve_kernel(
    place_ref, coupling_ref, left_ref, right_ref, pixel_ref, ivar_ref, weight_t_ref, weight_m_ref,
    theirs_ref, mine_ref, solved_s, lead_s, rest_s,
):
    streams = left_ref.shape[1]
    expos, half, fibres = weight_t_ref.shape
    width = ivar_ref.shape[0] // streams
    middle = width // 2
    coupling = stream_coupling(coupling_ref, expos)
    back = 1.0 / coupling

    def row_at(i):
        return pl.ds(i, streams, stride=width)

    def begin(edge_ref):
        u = edge_ref[0]
        return (u, 1.0 - u * back, edge_ref[1])

    def keep(side, i, state):
        n, d, b = state
        inverse = inverse_of(d + n * back)
        lead_s[side, i] = d * inverse
        rest_s[side, i] = (b * back) * inverse

    unrolled = divisor_of(middle, 24)

    def eliminate(it, states):
        states = list(states)
        for k in range(unrolled):
            i = it * unrolled + k
            for side, row in enumerate((i, width - 1 - i)):
                keep(side, i, states[side])
                states[side] = advance(states[side], ivar_ref[row_at(row), :], pixel_ref[row_at(row), :], back)
        return tuple(rescaled(state) for state in states)

    states = lax.fori_loop(0, middle // unrolled, eliminate, (begin(left_ref), begin(right_ref)))
    for side in range(2):
        keep(side, middle, states[side])
    lead, rest = lead_s[0, middle], rest_s[0, middle]
    lead_r, rest_r = lead_s[1, middle], rest_s[1, middle]
    left = (rest + lead * rest_r) / (1.0 - lead * lead_r)
    right = rest_r + lead_r * left
    several = divisor_of(middle, 48)

    def after_both(near, far):
        return far[0] * near[0], far[1] + far[0] * near[1]

    def step(factors, value):
        return factors[1] + factors[0] * value

    def substitute(it, values):
        values = list(values)
        for k in range(0, several, 4):
            for side in range(2):
                rows = [middle - 1 - (it * several + k + m) for m in range(4)]
                one, two, three, four = [(lead_s[side, i], rest_s[side, i]) for i in rows]
                first_two = after_both(one, two)
                all_four = after_both(first_two, after_both(three, four))
                value = values[side]
                third = step(first_two, value)
                solved = [value, step(one, value), third, step(three, third)]
                values[side] = step(all_four, value)
                for i, x in zip(rows, solved):
                    solved_s[row_at(i if side == 0 else width - 1 - i), :] = x
        return tuple(values)

    lax.fori_loop(0, middle // several, substitute, (left, right))

    blocks = fibres // LANES
    unroll = 5

    def coadd(out_ref, weight_ref, which):
        start = which * half

        def body(g, carry):
            for k in range(unroll):
                row = pl.multiple_of((g * unroll + k) * ROWS, ROWS)
                for h in range(blocks):
                    cut = pl.ds(h * LANES, LANES)
                    total = None
                    for e in range(expos):
                        at = pl.ds(pl.multiple_of((h * expos + e) * width + start + row, ROWS), ROWS)
                        term = weight_ref[e, pl.ds(row, ROWS), cut] * solved_s[at, :]
                        total = term if e == 0 else total + term
                    out_ref[0, pl.ds(row, ROWS), cut] = total
            return carry

        lax.fori_loop(0, half // (unroll * ROWS), body, 0)

    coadd(theirs_ref, weight_t_ref, 1 - place_ref[2])
    coadd(mine_ref, weight_m_ref, place_ref[2])


def flux_sums(place, coupling, left, right, pixels, ivar, weight_t, weight_m):
    expos, half, fibres = weight_t.shape
    streams = left.shape[1]
    out = shaped((1, half, fibres))
    factor_scratch = pltpu.VMEM((2, half + 1, streams, LANES), F32)
    return pl.pallas_call(
        solve_kernel,
        in_specs=[in_smem] + [in_vmem] * 7,
        out_specs=[in_vmem, in_vmem],
        out_shape=[out, out],
        scratch_shapes=[pltpu.VMEM(pixels.shape, F32), factor_scratch, factor_scratch],
        compiler_params=params(),
        cost_estimate=cost(0, 0),
        name="flux_sums",
    )(place, coupling, left, right, pixels, ivar, weight_t, weight_m)


def split_dot(x, table, dims):
    top = x.astype(BF16)
    low = (x - top.astype(F32)).astype(BF16)
    both = lax.dot_general(jnp.concatenate([top, low], 0), table, dims, preferred_element_type=F32)
    return both[: x.shape[0]] + both[x.shape[0] :]


def sort_kernel(pack, scaled, theirs_ref, mine_ref, table_ref, *refs):
    values, rows, _ = mine_ref.shape
    part = rows // pack
    totals = [mine_ref[v] + theirs_ref[v] for v in range(values)]
    if scaled:
        scale_ref, *out_refs = refs
        totals = [t * scale_ref[...] for t in totals]
    else:
        *out_refs, scale_ref = refs
        scale = 1.0 / jnp.maximum(totals[0], 1.0)
        scale_ref[...] = scale
        totals[1] = totals[1] * scale
    x = jnp.concatenate(
        [jnp.concatenate([t[h * part : (h + 1) * part] for h in range(pack)], 1) for t in totals], 0
    )
    moved = split_dot(x, table_ref[...], NT)
    lanes = moved.shape[1] // len(out_refs)
    for d, out_ref in enumerate(out_refs):
        for v in range(values):
            out_ref[v] = moved[v * part : (v + 1) * part, d * lanes : (d + 1) * lanes]


def sort_fibres(theirs, mine, table, pack, pieces, scale=None):
    values, rows, fibres = mine.shape
    lanes = table.shape[0] // pieces
    scaled = scale is not None
    outs = [shaped((values, rows // pack, lanes))] * pieces + ([] if scaled else [shaped((rows, fibres))])
    args = (theirs, mine, table) + ((scale,) if scaled else ())
    return pl.pallas_call(
        functools.partial(sort_kernel, pack, scaled),
        in_specs=[in_vmem] * len(args),
        out_specs=[in_vmem] * len(outs),
        out_shape=outs,
        compiler_params=params(),
        cost_estimate=cost(0, 0),
        name="sort_flux" if scaled else "sort_weights",
    )(*args)


def exchange(pieces, fib_count):
    if len(pieces) == 1:
        return [lax.all_to_all(pieces[0], "fib", split_axis=2, concat_axis=2, tiled=True)]
    arrived = [pieces[0]]
    for d in range(1, fib_count):
        arrived.append(lax.ppermute(pieces[d], "fib", [(i, (i + d) % fib_count) for i in range(fib_count)]))
    return arrived


def landed(refs, table):
    values, part, _ = refs[0].shape
    x = jnp.concatenate(
        [jnp.concatenate([ref[v] for ref in refs], 1) if len(refs) > 1 else refs[0][v] for v in range(values)], 0
    )
    moved = split_dot(x, table, NT)
    return [moved[v * part : (v + 1) * part] for v in range(values)]


def weights_end_kernel(pack, total, place_ref, table_ref, *refs):
    *piece_refs, ivar_ref, res_ref = refs
    weight, band = landed(piece_refs, table_ref[...])
    rows, fibres = ivar_ref.shape
    part = rows // pack
    start = (place_ref[1] * 2 + place_ref[2]) * rows
    for h in range(pack):
        at = slice(h * part, (h + 1) * part)
        cut = slice(h * fibres, (h + 1) * fibres)
        row = start + h * part + lax.broadcasted_iota(jnp.int32, (part, 1), 0)
        w, b = weight[:, cut], band[:, cut]
        before = jnp.where(row == 0, 0.0, b)
        after = jnp.where(row == total - 1, 0.0, b)
        ivar_ref[at, :] = w
        res_ref[0, at, :] = before
        res_ref[1, at, :] = jnp.minimum(w, 1.0) - before - after
        res_ref[2, at, :] = after


def end_weights(place, table, pieces, pack, fibres, total):
    rows = pieces[0].shape[1] * pack
    return pl.pallas_call(
        functools.partial(weights_end_kernel, pack, total),
        in_specs=[in_smem] + [in_vmem] * (1 + len(pieces)),
        out_specs=[in_vmem] * 2,
        out_shape=[shaped((rows, fibres)), shaped((3, rows, fibres))],
        compiler_params=params(),
        cost_estimate=cost(4 * rows * table.size, 6 * rows * fibres * 4),
        name="end_weights",
    )(place, table, *pieces)


def flux_end_kernel(pack, table_ref, *refs):
    *piece_refs, flux_ref = refs
    (flux,) = landed(piece_refs, table_ref[...])
    rows, fibres = flux_ref.shape
    part = rows // pack
    for h in range(pack):
        flux_ref[h * part : (h + 1) * part, :] = flux[:, h * fibres : (h + 1) * fibres]


def end_flux(table, pieces, pack, fibres):
    rows = pieces[0].shape[1] * pack
    return pl.pallas_call(
        functools.partial(flux_end_kernel, pack),
        in_specs=[in_vmem] * (1 + len(pieces)),
        out_specs=in_vmem,
        out_shape=shaped((rows, fibres)),
        compiler_params=params(),
        cost_estimate=cost(2 * rows * table.size, 2 * rows * fibres * 4),
        name="end_flux",
    )(table, *pieces)


def after(value, done):
    return lax.optimization_barrier((value, done))[0]


def per_device(pixels, pixel_ivar, clip_bits, coupling, counts, good_flags, owner_slot):
    expos, width, fibres = pixels.shape
    fib_count, wav_count = lax.axis_size("fib"), lax.axis_size("wav")
    total = width * wav_count
    per = fibres // fib_count
    rows = width // 2
    pack = max(1, LANES // per)
    while pack > 1 and rows % (pack * ROWS):
        pack //= 2
    rel = pack * per == LANES
    pieces = fib_count if rel else 1
    place = jnp.stack([lax.axis_index(axis) for axis in ("fib", "wav", "exp")]).astype(jnp.int32)
    coupling, counts, slots = coupling[None], counts[None], owner_slot[None]
    swap = [(0, 1), (1, 0)]
    moves = (fib_count, pack, per, rel)

    theirs, weight_t, send_table, up, down = sent_weights(
        moves, wav_count, place, slots, coupling, counts, good_flags, pixels, pixel_ivar, clip_bits
    )
    arriving = lax.ppermute(theirs, "exp", swap)
    upward = [(i, i + 1) for i in range(wav_count - 1)]
    left = lax.ppermute(up, "wav", upward)
    right = lax.ppermute(down, "wav", [(j, i) for i, j in upward])
    mine, weight_m, pixel_s, ivar_s = kept_weights(
        wav_count, after(place, theirs), coupling, counts, good_flags, pixels, pixel_ivar, clip_bits
    )
    *sorted_pieces, scale = sort_fibres(arriving, mine, send_table, pack, pieces)
    if rel:
        sorted_pieces[1] = after(sorted_pieces[1], (left, right))
    weight_pieces = exchange(sorted_pieces, fib_count)

    theirs, mine = flux_sums(place, coupling, left, right, pixel_s, ivar_s, weight_t, weight_m)
    recv_table = recv_moves(moves, after(place, theirs), slots, fibres)
    if rel:
        theirs = after(theirs, (weight_pieces[1], weight_pieces[-1]))
    theirs = lax.ppermute(theirs, "exp", swap)
    flux_pieces = exchange(sort_fibres(theirs, mine, send_table, pack, pieces, scale), fib_count)

    ivar, res = end_weights(place, recv_table, weight_pieces, pack, fibres, total)
    flux = end_flux(recv_table, flux_pieces, pack, fibres)
    return (flux, ivar, res)


def solution(mesh):
    return jax.shard_map(
        per_device,
        mesh=mesh,
        in_specs=(
            P("exp", "wav", "fib"),
            P("exp", "wav", "fib"),
            P("exp", "wav", "fib"),
            P("fib"),
            P("fib"),
            P("exp", "fib"),
            P(),
        ),
        out_specs=(
            P(("wav", "exp"), "fib"),
            P(("wav", "exp"), "fib"),
            P(None, ("wav", "exp"), "fib"),
        ),
        check_vma=False,
    )
```

```python
import functools

import jax
import jax.numpy as jnp
from jax import lax
from jax.experimental import pallas as pl
from jax.experimental.pallas import tpu as pltpu
from jax.sharding import PartitionSpec as P

HALO = 50
BITS = 15
LANES = 128
ROWS = 8
GROUP = 120
VMEM_BYTES = 32 * 1024 * 1024
F32 = jnp.float32
BF16 = jnp.bfloat16
NT = (((1,), (1,)), ((), ()))

in_vmem = pl.BlockSpec(memory_space=pltpu.VMEM)
in_smem = pl.BlockSpec(memory_space=pltpu.SMEM)
in_hbm = pl.BlockSpec(memory_space=pltpu.HBM)


def params():
    return pltpu.CompilerParams(vmem_limit_bytes=VMEM_BYTES)


def cost(flops, moved):
    return pl.CostEstimate(flops=int(flops), bytes_accessed=int(moved), transcendentals=0)


def held_in_hbm(*arrays):
    return [pltpu.with_memory_space_constraint(array, pltpu.HBM) for array in arrays]


def shaped(shape, dtype=F32):
    return jax.ShapeDtypeStruct(shape, dtype)


def usable_rows(place_ref, counts_ref, good_ref):
    count = good_ref.shape[0]
    return [
        good_ref[e : e + 1, :].astype(F32)
        * jnp.where(place_ref[2] * count + e < counts_ref[...], 1.0, 0.0)
        for e in range(count)
    ]


def tile_bits(tile):
    first, last = (ROWS * tile) // BITS, (ROWS * tile + ROWS - 1) // BITS
    split = BITS * last - ROWS * tile
    row = lax.broadcasted_iota(jnp.int32, (ROWS, 1), 0)
    word = jnp.where(row >= split, last, first)
    return first, last, split, jnp.left_shift(1, ROWS * tile + row - BITS * word)


def tile_words(words, tile):
    first, last, split, mask = tile_bits(tile)
    picked = words[first : first + 1, :]
    if last != first:
        row = lax.broadcasted_iota(jnp.int32, (ROWS, 1), 0)
        picked = jnp.where(row >= split, words[last : last + 1, :], picked)
    return (picked & mask) != 0


def in_flight(pairs, sems, at=0):
    copies = [pltpu.make_async_copy(source, target, sems.at[at + i]) for i, (source, target) in enumerate(pairs)]
    for copy in copies:
        copy.start()
    return copies


def inverse_of(x):
    guess = pl.reciprocal(x, approx=True)
    return guess * (2.0 - x * guess)


def advance(state, ivar, pixel, back_coupling):
    n, d, b = state
    next_d = d + n * back_coupling
    return (n * (1.0 + ivar * back_coupling) + ivar * d, next_d, b + (ivar * pixel) * next_d)


def rescaled(state):
    scale = inverse_of(state[1])
    return tuple(part * scale for part in state)


def odd(rows):
    return rows + 1 - rows % 2


def divisor_of(size, most):
    return max(k for k in range(1, most + 1) if size % k == 0)


def owners(slots_ref, fib_count, fibres):
    rows = [slots_ref[:, s * fibres : (s + 1) * fibres].astype(F32) for s in range(fib_count)]
    sources = -(-fib_count // ROWS) * ROWS
    if sources > fib_count:
        rows.append(jnp.full((sources - fib_count, fibres), -1.0, F32))
    slots = jnp.concatenate(rows, 0)
    owner = jnp.floor((slots + 0.5) * (1.0 / fibres))
    return owner, slots - owner * fibres


def earlier_fibres(fibres):
    row = lax.broadcasted_iota(jnp.int32, (fibres, fibres), 0)
    col = lax.broadcasted_iota(jnp.int32, (fibres, fibres), 1)
    return (row < col).astype(F32).astype(BF16)


def write_send_table(fib_count, pack, per, rel, me, slots_ref, table_ref):
    fibres = table_ref.shape[1] // pack
    lanes = pack * per
    owner, _ = owners(slots_ref, fib_count, fibres)
    source = lax.broadcasted_iota(jnp.int32, owner.shape, 0)
    my_owner = jnp.sum(jnp.where(source == me, owner, 0.0), axis=0, keepdims=True).astype(jnp.int32)
    to_owner = (source == my_owner).astype(F32)
    counted = jnp.dot(to_owner.astype(BF16), earlier_fibres(fibres), preferred_element_type=F32)
    rank = jnp.sum(to_owner * counted, axis=0, keepdims=True).astype(jnp.int32)
    target = my_owner
    if rel:
        target = jnp.where(my_owner >= me, my_owner - me, my_owner - me + fib_count)
    base = target * lanes + rank
    place_of = jnp.concatenate([base + h * per for h in range(pack)], 1)
    row = lax.broadcasted_iota(jnp.int32, table_ref.shape, 0)
    table_ref[...] = (row == place_of).astype(F32).astype(BF16)


def write_recv_table(fib_count, pack, per, rel, me, slots_ref, table_ref):
    fibres = table_ref.shape[0] // pack
    lanes = pack * per
    total_lanes = fib_count * lanes
    owner, column = owners(slots_ref, fib_count, fibres)
    source = lax.broadcasted_iota(jnp.int32, owner.shape, 0)
    mine = (owner == me.astype(F32)).astype(F32)
    rank_in = jnp.dot(mine.astype(BF16), earlier_fibres(fibres), preferred_element_type=F32).astype(jnp.int32)
    order = source
    if rel:
        order = jnp.where(me >= source, me - source, me - source + fib_count)
    arrival = jnp.where(mine > 0.0, order * lanes + rank_in, -total_lanes)
    tall = lax.broadcasted_iota(jnp.int32, (total_lanes, fibres), 0)
    landing = jnp.zeros((ROWS, total_lanes), F32)
    for s in range(fib_count):
        hit = tall == arrival[s : s + 1, :]
        for h in range(1, pack):
            hit = hit | (tall == arrival[s : s + 1, :] + h * per)
        values = jnp.broadcast_to(column[s : s + 1, :], (ROWS, fibres)).astype(BF16)
        landing = landing + lax.dot_general(
            values, hit.astype(F32).astype(BF16), NT, preferred_element_type=F32
        )
    lane = lax.broadcasted_iota(jnp.int32, (1, total_lanes), 1)
    landing = landing[0:1, :].astype(jnp.int32)
    for h in range(1, pack):
        inside = (lane % lanes >= h * per) & (lane % lanes < (h + 1) * per)
        landing = jnp.where(inside, landing + h * fibres, landing)
    row = lax.broadcasted_iota(jnp.int32, table_ref.shape, 0)
    table_ref[...] = (row == landing).astype(F32).astype(BF16)


def stream_coupling(coupling_ref, expos):
    coupling = coupling_ref[...]
    blocks = coupling.shape[1] // LANES
    return jnp.concatenate(
        [jnp.broadcast_to(coupling[:, h * LANES : (h + 1) * LANES], (expos, LANES)) for h in range(blocks)], 0
    )


def weight_tile(coupling, usable, words, ivars, within, scale_row):
    links = scale_row * coupling
    weights = []
    weight_sum = band_sum = None
    for e, ivar in enumerate(ivars):
        weight = jnp.where(tile_words(words[e], within), ivar * usable[e], 0.0)
        band = weight * inverse_of(ivar + links)
        weights.append(weight)
        weight_sum = weight if e == 0 else weight_sum + weight
        band_sum = band if e == 0 else band_sum + band
    return weights, weight_sum, band_sum * coupling


def half_copies(which, ivar_ref, bits_ref, ivar_v, bits_v):
    half = ivar_v.shape[1]
    first = pl.multiple_of(which * half, ROWS)
    first_word = pl.multiple_of(which * (half // BITS), ROWS)
    return [
        (bits_ref.at[:, pl.ds(first_word, half // BITS), :], bits_v),
        (ivar_ref.at[:, pl.ds(first, half), :], ivar_v),
    ]


def write_weights(place_ref, wav_count, which, coupling_v, counts_v, good_v, ivar_v, bits_v, sums_ref, weight_ref, beside):
    expos, half, _ = ivar_v.shape
    coupling = coupling_v[...]
    usable = usable_rows(place_ref, counts_v, good_v)
    start = place_ref[1] * (2 * half) + which * half
    tiles = half // ROWS
    tiles_in_group = GROUP // ROWS
    words_in_group = GROUP // BITS
    for tile in range(tiles):
        group, within = divmod(tile, tiles_in_group)
        scale_row = 4.0
        if tile in (0, tiles - 1):
            row = start + ROWS * tile + lax.broadcasted_iota(jnp.int32, (ROWS, 1), 0)
            scale_row = jnp.where((row == 0) | (row == wav_count * 2 * half - 1), 2.0, 4.0)
        at = slice(ROWS * tile, ROWS * (tile + 1))
        words = [bits_v[e, words_in_group * group : words_in_group * (group + 1), :] for e in range(expos)]
        weights, weight_sum, band_sum = weight_tile(
            coupling, usable, words, [ivar_v[e, at, :] for e in range(expos)], within, scale_row
        )
        for e in range(expos):
            weight_ref[e, at, :] = weights[e]
        sums_ref[0, at, :] = weight_sum
        sums_ref[1, at, :] = band_sum
        beside(tile, tiles)


def stream_copies(source_ref, target, first, length, pitch, offset):
    expos, _, fibres = source_ref.shape
    return [
        (
            source_ref.at[e, pl.ds(first, length), pl.ds(h * LANES, LANES)],
            target.at[pl.ds((h * expos + e) * pitch + offset, length), :],
        )
        for h in range(fibres // LANES)
        for e in range(expos)
    ]


def first_kernel(
    moves, wav_count, place_ref, slots_ref, coupling_ref, counts_ref, good_ref, pixels_ref, ivar_ref, bits_ref,
    sums_ref, weight_ref, table_ref, up_ref, down_ref,
    slots_v, coupling_v, counts_v, good_v, ivar_v, bits_v, ivar_s, pixel_s, sems,
):
    expos, width, fibres = ivar_ref.shape
    streams = expos * fibres // LANES
    count = -(-HALO // ROWS) * ROWS
    pitch = odd(2 * count)
    which = 1 - place_ref[2]
    pairs = [(slots_ref, slots_v), (coupling_ref, coupling_v), (counts_ref, counts_v), (good_ref, good_v)]
    for source, target in ((ivar_ref, ivar_s), (pixels_ref, pixel_s)):
        pairs += stream_copies(source, target, 0, count, pitch, 0)
        pairs += stream_copies(source, target, width - count, count, pitch, count)
    pairs += half_copies(which, ivar_ref, bits_ref, ivar_v, bits_v)
    waits = in_flight(pairs, sems)
    waits[0].wait()
    write_send_table(*moves, place_ref[0], slots_v, table_ref)
    for wait in waits[1:]:
        wait.wait()

    back = 1.0 / stream_coupling(coupling_v, expos)
    zero = jnp.zeros((streams, LANES), F32)
    states = [(zero, zero + 1.0, zero), (zero, zero + 1.0, zero)]

    def eliminate(tile, tiles):
        for i in range(HALO * tile // tiles, HALO * (tile + 1) // tiles):
            for side, row in enumerate((2 * count - HALO + i, HALO - 1 - i)):
                at = pl.ds(row, streams, stride=pitch)
                states[side] = advance(states[side], ivar_s[at, :], pixel_s[at, :], back)
                if i % 24 == 23:
                    states[side] = rescaled(states[side])

    write_weights(
        place_ref, wav_count, which, coupling_v, counts_v, good_v, ivar_v, bits_v, sums_ref, weight_ref, eliminate
    )
    for (n, d, b), out_ref in zip(states, (up_ref, down_ref)):
        scale = 1.0 / (d + n * back)
        out_ref[0] = n * scale
        out_ref[1] = b * scale


def weights_scratch(slots, coupling, counts, good, ivar):
    expos, width, fibres = ivar.shape
    half = width // 2
    return [
        pltpu.VMEM(coupling.shape, F32),
        pltpu.VMEM(counts.shape, jnp.int32),
        pltpu.VMEM(good.shape, jnp.int32),
        pltpu.VMEM((expos, half, fibres), F32),
        pltpu.VMEM((expos, half // BITS, fibres), jnp.int32),
    ]


def sent_weights(moves, wav_count, place, slots, coupling, counts, good, pixels, ivar, bits):
    expos, width, fibres = ivar.shape
    half = width // 2
    streams = expos * fibres // LANES
    fib_count, pack, per, _ = moves
    count = -(-HALO // ROWS) * ROWS
    edge = shaped((2, streams, LANES))
    return pl.pallas_call(
        functools.partial(first_kernel, moves, wav_count),
        in_specs=[in_smem] + [in_hbm] * 7,
        out_specs=[in_vmem] * 5,
        out_shape=[
            shaped((2, half, fibres)),
            shaped((expos, half, fibres)),
            shaped((fib_count * pack * per, pack * fibres), BF16),
            edge,
            edge,
        ],
        scratch_shapes=[
            pltpu.VMEM(slots.shape, jnp.int32),
            *weights_scratch(slots, coupling, counts, good, ivar),
            pltpu.VMEM((streams * odd(2 * count), LANES), F32),
            pltpu.VMEM((streams * odd(2 * count), LANES), F32),
            pltpu.SemaphoreType.DMA((6 + 4 * streams,)),
        ],
        compiler_params=params(),
        cost_estimate=cost(20 * ivar.size, 6 * ivar.size),
        name="sent_weights",
    )(place, *held_in_hbm(slots, coupling, counts, good, pixels, ivar, bits))


def second_kernel(
    wav_count, place_ref, coupling_ref, counts_ref, good_ref, pixels_ref, ivar_ref, bits_ref,
    sums_ref, weight_ref, pixel_out, ivar_out, coupling_v, counts_v, good_v, ivar_v, bits_v, sems,
):
    width = ivar_ref.shape[1]
    which = place_ref[2]
    pairs = [(coupling_ref, coupling_v), (counts_ref, counts_v), (good_ref, good_v)]
    pairs += half_copies(which, ivar_ref, bits_ref, ivar_v, bits_v)
    waits = in_flight(pairs, sems)
    laid = stream_copies(ivar_ref, ivar_out, 0, width, odd(width), 0)
    laid += stream_copies(pixels_ref, pixel_out, 0, width, odd(width), 0)
    rest = in_flight(laid, sems, len(waits))
    for wait in waits:
        wait.wait()
    write_weights(
        place_ref, wav_count, which, coupling_v, counts_v, good_v, ivar_v, bits_v, sums_ref, weight_ref,
        lambda tile, tiles: None,
    )
    for wait in rest:
        wait.wait()


def kept_weights(wav_count, place, coupling, counts, good, pixels, ivar, bits):
    expos, width, fibres = ivar.shape
    half = width // 2
    streams = expos * fibres // LANES
    laid = shaped((streams * odd(width), LANES))
    return pl.pallas_call(
        functools.partial(second_kernel, wav_count),
        in_specs=[in_smem] + [in_hbm] * 6,
        out_specs=[in_vmem] * 4,
        out_shape=[shaped((2, half, fibres)), shaped((expos, half, fibres)), laid, laid],
        scratch_shapes=[
            *weights_scratch(None, coupling, counts, good, ivar),
            pltpu.SemaphoreType.DMA((5 + 2 * streams,)),
        ],
        compiler_params=params(),
        cost_estimate=cost(20 * ivar.size, 6 * ivar.size),
        name="kept_weights",
    )(place, *held_in_hbm(coupling, counts, good, pixels, ivar, bits))


def recv_kernel(moves, place_ref, slots_ref, table_ref):
    write_recv_table(*moves, place_ref[0], slots_ref, table_ref)


def recv_moves(moves, place, slots, fibres):
    fib_count, pack, per, _ = moves
    return pl.pallas_call(
        functools.partial(recv_kernel, moves),
        in_specs=[in_smem, in_vmem],
        out_specs=in_vmem,
        out_shape=shaped((pack * fibres, fib_count * pack * per), BF16),
        compiler_params=params(),
        cost_estimate=cost(1e6, 1e6),
        name="recv_moves",
    )(place, slots)


def solve_kernel(
    place_ref, coupling_ref, left_ref, right_ref, pixel_ref, ivar_ref, weight_t_ref, weight_m_ref,
    theirs_ref, mine_ref, solved_s, lead_s, rest_s,
):
    streams = left_ref.shape[1]
    expos, half, fibres = weight_t_ref.shape
    width = 2 * half
    pitch = odd(width)
    middle = half
    coupling = stream_coupling(coupling_ref, expos)
    back = 1.0 / coupling

    def row_at(i):
        return pl.ds(i, streams, stride=pitch)

    def begin(edge_ref):
        u = edge_ref[0]
        return (u, 1.0 - u * back, edge_ref[1])

    def keep(side, i, state):
        n, d, b = state
        inverse = inverse_of(d + n * back)
        lead_s[side, i] = d * inverse
        rest_s[side, i] = (b * back) * inverse

    unrolled = divisor_of(middle, 24)

    def eliminate(it, states):
        states = list(states)
        for k in range(unrolled):
            i = it * unrolled + k
            for side, row in enumerate((i, width - 1 - i)):
                keep(side, i, states[side])
                states[side] = advance(states[side], ivar_ref[row_at(row), :], pixel_ref[row_at(row), :], back)
        return tuple(rescaled(state) for state in states)

    states = lax.fori_loop(0, middle // unrolled, eliminate, (begin(left_ref), begin(right_ref)))
    for side in range(2):
        keep(side, middle, states[side])
    lead, rest = lead_s[0, middle], rest_s[0, middle]
    lead_r, rest_r = lead_s[1, middle], rest_s[1, middle]
    left = (rest + lead * rest_r) / (1.0 - lead * lead_r)
    right = rest_r + lead_r * left
    several = divisor_of(middle, 48)

    def after_both(near, far):
        return far[0] * near[0], far[1] + far[0] * near[1]

    def step(factors, value):
        return factors[1] + factors[0] * value

    def substitute(it, values):
        values = list(values)
        for k in range(0, several, 4):
            for side in range(2):
                rows = [middle - 1 - (it * several + k + m) for m in range(4)]
                one, two, three, four = [(lead_s[side, i], rest_s[side, i]) for i in rows]
                first_two = after_both(one, two)
                all_four = after_both(first_two, after_both(three, four))
                value = values[side]
                third = step(first_two, value)
                solved = [value, step(one, value), third, step(three, third)]
                values[side] = step(all_four, value)
                for i, x in zip(rows, solved):
                    solved_s[row_at(i if side == 0 else width - 1 - i), :] = x
        return tuple(values)

    lax.fori_loop(0, middle // several, substitute, (left, right))

    blocks = fibres // LANES
    unroll = 5

    def coadd(out_ref, weight_ref, which):
        start = which * half

        def body(g, carry):
            for k in range(unroll):
                row = pl.multiple_of((g * unroll + k) * ROWS, ROWS)
                for h in range(blocks):
                    cut = pl.ds(h * LANES, LANES)
                    total = None
                    for e in range(expos):
                        at = pl.ds((h * expos + e) * pitch + start + row, ROWS)
                        term = weight_ref[e, pl.ds(row, ROWS), cut] * solved_s[at, :]
                        total = term if e == 0 else total + term
                    out_ref[0, pl.ds(row, ROWS), cut] = total
            return carry

        lax.fori_loop(0, half // (unroll * ROWS), body, 0)

    coadd(theirs_ref, weight_t_ref, 1 - place_ref[2])
    coadd(mine_ref, weight_m_ref, place_ref[2])


def flux_sums(place, coupling, left, right, pixels, ivar, weight_t, weight_m):
    expos, half, fibres = weight_t.shape
    streams = left.shape[1]
    out = shaped((1, half, fibres))
    factor_scratch = pltpu.VMEM((2, half + 1, streams, LANES), F32)
    return pl.pallas_call(
        solve_kernel,
        in_specs=[in_smem] + [in_vmem] * 7,
        out_specs=[in_vmem, in_vmem],
        out_shape=[out, out],
        scratch_shapes=[pltpu.VMEM(pixels.shape, F32), factor_scratch, factor_scratch],
        compiler_params=params(),
        cost_estimate=cost(0, 0),
        name="flux_sums",
    )(place, coupling, left, right, pixels, ivar, weight_t, weight_m)


def split_dot(x, table, dims):
    top = x.astype(BF16)
    low = (x - top.astype(F32)).astype(BF16)
    both = lax.dot_general(jnp.concatenate([top, low], 0), table, dims, preferred_element_type=F32)
    return both[: x.shape[0]] + both[x.shape[0] :]


def sort_kernel(pack, scaled, theirs_ref, mine_ref, table_ref, *refs):
    values, rows, _ = mine_ref.shape
    part = rows // pack
    totals = [mine_ref[v] + theirs_ref[v] for v in range(values)]
    if scaled:
        scale_ref, *out_refs = refs
        totals = [t * scale_ref[...] for t in totals]
    else:
        *out_refs, scale_ref = refs
        scale = 1.0 / jnp.maximum(totals[0], 1.0)
        scale_ref[...] = scale
        totals[1] = totals[1] * scale
    x = jnp.concatenate(
        [jnp.concatenate([t[h * part : (h + 1) * part] for h in range(pack)], 1) for t in totals], 0
    )
    moved = split_dot(x, table_ref[...], NT)
    lanes = moved.shape[1] // len(out_refs)
    for d, out_ref in enumerate(out_refs):
        for v in range(values):
            out_ref[v] = moved[v * part : (v + 1) * part, d * lanes : (d + 1) * lanes]


def sort_fibres(theirs, mine, table, pack, pieces, scale=None):
    values, rows, fibres = mine.shape
    lanes = table.shape[0] // pieces
    scaled = scale is not None
    outs = [shaped((values, rows // pack, lanes))] * pieces + ([] if scaled else [shaped((rows, fibres))])
    args = (theirs, mine, table) + ((scale,) if scaled else ())
    return pl.pallas_call(
        functools.partial(sort_kernel, pack, scaled),
        in_specs=[in_vmem] * len(args),
        out_specs=[in_vmem] * len(outs),
        out_shape=outs,
        compiler_params=params(),
        cost_estimate=cost(0, 0),
        name="sort_flux" if scaled else "sort_weights",
    )(*args)


def exchange(pieces, fib_count):
    if len(pieces) == 1:
        return [lax.all_to_all(pieces[0], "fib", split_axis=2, concat_axis=2, tiled=True)]
    arrived = [pieces[0]]
    for d in range(1, fib_count):
        arrived.append(lax.ppermute(pieces[d], "fib", [(i, (i + d) % fib_count) for i in range(fib_count)]))
    return arrived


def landed(refs, table):
    values, part, _ = refs[0].shape
    x = jnp.concatenate(
        [jnp.concatenate([ref[v] for ref in refs], 1) if len(refs) > 1 else refs[0][v] for v in range(values)], 0
    )
    moved = split_dot(x, table, NT)
    return [moved[v * part : (v + 1) * part] for v in range(values)]


def weights_end_kernel(pack, total, place_ref, table_ref, *refs):
    *piece_refs, ivar_ref, res_ref = refs
    weight, band = landed(piece_refs, table_ref[...])
    rows, fibres = ivar_ref.shape
    part = rows // pack
    start = (place_ref[1] * 2 + place_ref[2]) * rows
    for h in range(pack):
        at = slice(h * part, (h + 1) * part)
        cut = slice(h * fibres, (h + 1) * fibres)
        row = start + h * part + lax.broadcasted_iota(jnp.int32, (part, 1), 0)
        w, b = weight[:, cut], band[:, cut]
        before = jnp.where(row == 0, 0.0, b)
        after = jnp.where(row == total - 1, 0.0, b)
        ivar_ref[at, :] = w
        res_ref[0, at, :] = before
        res_ref[1, at, :] = jnp.minimum(w, 1.0) - before - after
        res_ref[2, at, :] = after


def end_weights(place, table, pieces, pack, fibres, total):
    rows = pieces[0].shape[1] * pack
    return pl.pallas_call(
        functools.partial(weights_end_kernel, pack, total),
        in_specs=[in_smem] + [in_vmem] * (1 + len(pieces)),
        out_specs=[in_vmem] * 2,
        out_shape=[shaped((rows, fibres)), shaped((3, rows, fibres))],
        compiler_params=params(),
        cost_estimate=cost(4 * rows * table.size, 6 * rows * fibres * 4),
        name="end_weights",
    )(place, table, *pieces)


def flux_end_kernel(pack, table_ref, *refs):
    *piece_refs, flux_ref = refs
    (flux,) = landed(piece_refs, table_ref[...])
    rows, fibres = flux_ref.shape
    part = rows // pack
    for h in range(pack):
        flux_ref[h * part : (h + 1) * part, :] = flux[:, h * fibres : (h + 1) * fibres]


def end_flux(table, pieces, pack, fibres):
    rows = pieces[0].shape[1] * pack
    return pl.pallas_call(
        functools.partial(flux_end_kernel, pack),
        in_specs=[in_vmem] * (1 + len(pieces)),
        out_specs=in_vmem,
        out_shape=shaped((rows, fibres)),
        compiler_params=params(),
        cost_estimate=cost(2 * rows * table.size, 2 * rows * fibres * 4),
        name="end_flux",
    )(table, *pieces)


def after(value, done):
    return lax.optimization_barrier((value, done))[0]


def per_device(pixels, pixel_ivar, clip_bits, coupling, counts, good_flags, owner_slot):
    expos, width, fibres = pixels.shape
    fib_count, wav_count = lax.axis_size("fib"), lax.axis_size("wav")
    total = width * wav_count
    per = fibres // fib_count
    rows = width // 2
    pack = max(1, LANES // per)
    while pack > 1 and rows % (pack * ROWS):
        pack //= 2
    rel = pack * per == LANES
    pieces = fib_count if rel else 1
    place = jnp.stack([lax.axis_index(axis) for axis in ("fib", "wav", "exp")]).astype(jnp.int32)
    coupling, counts, slots = coupling[None], counts[None], owner_slot[None]
    swap = [(0, 1), (1, 0)]
    moves = (fib_count, pack, per, rel)

    theirs, weight_t, send_table, up, down = sent_weights(
        moves, wav_count, place, slots, coupling, counts, good_flags, pixels, pixel_ivar, clip_bits
    )
    arriving = lax.ppermute(theirs, "exp", swap)
    upward = [(i, i + 1) for i in range(wav_count - 1)]
    left = lax.ppermute(up, "wav", upward)
    right = lax.ppermute(down, "wav", [(j, i) for i, j in upward])
    mine, weight_m, pixel_s, ivar_s = kept_weights(
        wav_count, after(place, theirs), coupling, counts, good_flags, pixels, pixel_ivar, clip_bits
    )
    *sorted_pieces, scale = sort_fibres(arriving, mine, send_table, pack, pieces)
    if rel:
        sorted_pieces[1] = after(sorted_pieces[1], (left, right))
    weight_pieces = exchange(sorted_pieces, fib_count)

    theirs, mine = flux_sums(place, coupling, left, right, pixel_s, ivar_s, weight_t, weight_m)
    recv_table = recv_moves(moves, after(place, theirs), slots, fibres)
    if rel:
        theirs = after(theirs, (weight_pieces[1], weight_pieces[-1]))
    theirs = lax.ppermute(theirs, "exp", swap)
    flux_pieces = exchange(sort_fibres(theirs, mine, send_table, pack, pieces, scale), fib_count)

    ivar, res = end_weights(place, recv_table, weight_pieces, pack, fibres, total)
    flux = end_flux(recv_table, flux_pieces, pack, fibres)
    return (flux, ivar, res)


def solution(mesh):
    return jax.shard_map(
        per_device,
        mesh=mesh,
        in_specs=(
            P("exp", "wav", "fib"),
            P("exp", "wav", "fib"),
            P("exp", "wav", "fib"),
            P("fib"),
            P("fib"),
            P("exp", "fib"),
            P(),
        ),
        out_specs=(
            P(("wav", "exp"), "fib"),
            P(("wav", "exp"), "fib"),
            P(None, ("wav", "exp"), "fib"),
        ),
        check_vma=False,
    )
```

```python
import functools

import jax
import jax.numpy as jnp
from jax import lax
from jax.experimental import pallas as pl
from jax.experimental.pallas import tpu as pltpu
from jax.sharding import PartitionSpec as P

HALO = 50
BITS = 15
LANES = 128
ROWS = 8
GROUP = 120
VMEM_BYTES = 32 * 1024 * 1024
F32 = jnp.float32
BF16 = jnp.bfloat16
NT = (((1,), (1,)), ((), ()))

in_vmem = pl.BlockSpec(memory_space=pltpu.VMEM)
in_smem = pl.BlockSpec(memory_space=pltpu.SMEM)
in_hbm = pl.BlockSpec(memory_space=pltpu.HBM)


def params():
    return pltpu.CompilerParams(vmem_limit_bytes=VMEM_BYTES)


def cost(flops, moved):
    return pl.CostEstimate(flops=int(flops), bytes_accessed=int(moved), transcendentals=0)


def held_in_hbm(*arrays):
    return [pltpu.with_memory_space_constraint(array, pltpu.HBM) for array in arrays]


def shaped(shape, dtype=F32):
    return jax.ShapeDtypeStruct(shape, dtype)


def usable_rows(place_ref, counts_ref, good_ref):
    count = good_ref.shape[0]
    return [
        good_ref[e : e + 1, :].astype(F32)
        * jnp.where(place_ref[2] * count + e < counts_ref[...], 1.0, 0.0)
        for e in range(count)
    ]


def tile_bits(tile):
    first, last = (ROWS * tile) // BITS, (ROWS * tile + ROWS - 1) // BITS
    split = BITS * last - ROWS * tile
    row = lax.broadcasted_iota(jnp.int32, (ROWS, 1), 0)
    word = jnp.where(row >= split, last, first)
    return first, last, split, jnp.left_shift(1, ROWS * tile + row - BITS * word)


def tile_words(words, tile):
    first, last, split, mask = tile_bits(tile)
    picked = words[first : first + 1, :]
    if last != first:
        row = lax.broadcasted_iota(jnp.int32, (ROWS, 1), 0)
        picked = jnp.where(row >= split, words[last : last + 1, :], picked)
    return (picked & mask) != 0


def in_flight(pairs, sems, at=0):
    copies = [pltpu.make_async_copy(source, target, sems.at[at + i]) for i, (source, target) in enumerate(pairs)]
    for copy in copies:
        copy.start()
    return copies


def inverse_of(x):
    guess = pl.reciprocal(x, approx=True)
    return guess * (2.0 - x * guess)


def advance(state, ivar, pixel, back_coupling):
    n, d, b = state
    next_d = d + n * back_coupling
    return (n * (1.0 + ivar * back_coupling) + ivar * d, next_d, b + (ivar * pixel) * next_d)


def rescaled(state):
    scale = inverse_of(state[1])
    return tuple(part * scale for part in state)


def odd(rows):
    return rows + 1 - rows % 2


def divisor_of(size, most):
    return max(k for k in range(1, most + 1) if size % k == 0)


def owners(slots_ref, fib_count, fibres):
    rows = [slots_ref[:, s * fibres : (s + 1) * fibres].astype(F32) for s in range(fib_count)]
    sources = -(-fib_count // ROWS) * ROWS
    if sources > fib_count:
        rows.append(jnp.full((sources - fib_count, fibres), -1.0, F32))
    slots = jnp.concatenate(rows, 0)
    owner = jnp.floor((slots + 0.5) * (1.0 / fibres))
    return owner, slots - owner * fibres


def earlier_fibres(fibres):
    row = lax.broadcasted_iota(jnp.int32, (fibres, fibres), 0)
    col = lax.broadcasted_iota(jnp.int32, (fibres, fibres), 1)
    return (row < col).astype(F32).astype(BF16)


def write_send_table(fib_count, pack, per, rel, me, slots_ref, table_ref):
    fibres = table_ref.shape[1] // pack
    lanes = pack * per
    owner, _ = owners(slots_ref, fib_count, fibres)
    source = lax.broadcasted_iota(jnp.int32, owner.shape, 0)
    my_owner = jnp.sum(jnp.where(source == me, owner, 0.0), axis=0, keepdims=True).astype(jnp.int32)
    to_owner = (source == my_owner).astype(F32)
    counted = jnp.dot(to_owner.astype(BF16), earlier_fibres(fibres), preferred_element_type=F32)
    rank = jnp.sum(to_owner * counted, axis=0, keepdims=True).astype(jnp.int32)
    target = my_owner
    if rel:
        target = jnp.where(my_owner >= me, my_owner - me, my_owner - me + fib_count)
    base = target * lanes + rank
    place_of = jnp.concatenate([base + h * per for h in range(pack)], 1)
    row = lax.broadcasted_iota(jnp.int32, table_ref.shape, 0)
    table_ref[...] = (row == place_of).astype(F32).astype(BF16)


def write_recv_table(fib_count, pack, per, rel, me, slots_ref, table_ref):
    fibres = table_ref.shape[0] // pack
    lanes = pack * per
    total_lanes = fib_count * lanes
    owner, column = owners(slots_ref, fib_count, fibres)
    source = lax.broadcasted_iota(jnp.int32, owner.shape, 0)
    mine = (owner == me.astype(F32)).astype(F32)
    rank_in = jnp.dot(mine.astype(BF16), earlier_fibres(fibres), preferred_element_type=F32).astype(jnp.int32)
    order = source
    if rel:
        order = jnp.where(me >= source, me - source, me - source + fib_count)
    arrival = jnp.where(mine > 0.0, order * lanes + rank_in, -total_lanes)
    tall = lax.broadcasted_iota(jnp.int32, (total_lanes, fibres), 0)
    landing = jnp.zeros((ROWS, total_lanes), F32)
    for s in range(fib_count):
        hit = tall == arrival[s : s + 1, :]
        for h in range(1, pack):
            hit = hit | (tall == arrival[s : s + 1, :] + h * per)
        values = jnp.broadcast_to(column[s : s + 1, :], (ROWS, fibres)).astype(BF16)
        landing = landing + lax.dot_general(
            values, hit.astype(F32).astype(BF16), NT, preferred_element_type=F32
        )
    lane = lax.broadcasted_iota(jnp.int32, (1, total_lanes), 1)
    landing = landing[0:1, :].astype(jnp.int32)
    for h in range(1, pack):
        inside = (lane % lanes >= h * per) & (lane % lanes < (h + 1) * per)
        landing = jnp.where(inside, landing + h * fibres, landing)
    row = lax.broadcasted_iota(jnp.int32, table_ref.shape, 0)
    table_ref[...] = (row == landing).astype(F32).astype(BF16)


def stream_coupling(coupling_ref, expos):
    coupling = coupling_ref[...]
    blocks = coupling.shape[1] // LANES
    return jnp.concatenate(
        [jnp.broadcast_to(coupling[:, h * LANES : (h + 1) * LANES], (expos, LANES)) for h in range(blocks)], 0
    )


def weight_tile(coupling, usable, words, ivars, within, scale_row):
    links = scale_row * coupling
    weights = []
    weight_sum = band_sum = None
    for e, ivar in enumerate(ivars):
        weight = jnp.where(tile_words(words[e], within), ivar * usable[e], 0.0)
        band = weight * inverse_of(ivar + links)
        weights.append(weight)
        weight_sum = weight if e == 0 else weight_sum + weight
        band_sum = band if e == 0 else band_sum + band
    return weights, weight_sum, band_sum * coupling


def half_copies(which, ivar_ref, bits_ref, ivar_v, bits_v):
    half = ivar_v.shape[1]
    first = pl.multiple_of(which * half, ROWS)
    first_word = pl.multiple_of(which * (half // BITS), ROWS)
    return [
        (bits_ref.at[:, pl.ds(first_word, half // BITS), :], bits_v),
        (ivar_ref.at[:, pl.ds(first, half), :], ivar_v),
    ]


def write_weights(place_ref, wav_count, which, coupling_v, counts_v, good_v, ivar_v, bits_v, sums_ref, weight_ref, beside):
    expos, half, _ = ivar_v.shape
    coupling = coupling_v[...]
    usable = usable_rows(place_ref, counts_v, good_v)
    start = place_ref[1] * (2 * half) + which * half
    tiles = half // ROWS
    tiles_in_group = GROUP // ROWS
    words_in_group = GROUP // BITS
    for tile in range(tiles):
        group, within = divmod(tile, tiles_in_group)
        scale_row = 4.0
        if tile in (0, tiles - 1):
            row = start + ROWS * tile + lax.broadcasted_iota(jnp.int32, (ROWS, 1), 0)
            scale_row = jnp.where((row == 0) | (row == wav_count * 2 * half - 1), 2.0, 4.0)
        at = slice(ROWS * tile, ROWS * (tile + 1))
        words = [bits_v[e, words_in_group * group : words_in_group * (group + 1), :] for e in range(expos)]
        weights, weight_sum, band_sum = weight_tile(
            coupling, usable, words, [ivar_v[e, at, :] for e in range(expos)], within, scale_row
        )
        for e in range(expos):
            weight_ref[e, at, :] = weights[e]
        sums_ref[0, at, :] = weight_sum
        sums_ref[1, at, :] = band_sum
        beside(tile, tiles)


def stream_copies(source_ref, target, first, length, pitch, offset):
    expos, _, fibres = source_ref.shape
    return [
        (
            source_ref.at[e, pl.ds(first, length), pl.ds(h * LANES, LANES)],
            target.at[pl.ds((h * expos + e) * pitch + offset, length), :],
        )
        for h in range(fibres // LANES)
        for e in range(expos)
    ]


def sent_kernel(
    moves, wav_count, place_ref, slots_ref, coupling_ref, counts_ref, good_ref, ivar_ref, bits_ref,
    sums_ref, weight_ref, table_ref, slots_v, coupling_v, counts_v, good_v, ivar_v, bits_v, sems,
):
    which = 1 - place_ref[2]
    pairs = [(slots_ref, slots_v), (coupling_ref, coupling_v), (counts_ref, counts_v), (good_ref, good_v)]
    pairs += half_copies(which, ivar_ref, bits_ref, ivar_v, bits_v)
    waits = in_flight(pairs, sems)
    waits[0].wait()
    write_send_table(*moves, place_ref[0], slots_v, table_ref)
    for wait in waits[1:]:
        wait.wait()
    write_weights(
        place_ref, wav_count, which, coupling_v, counts_v, good_v, ivar_v, bits_v, sums_ref, weight_ref,
        lambda tile, tiles: None,
    )


def weights_scratch(coupling, counts, good, ivar):
    expos, width, fibres = ivar.shape
    half = width // 2
    return [
        pltpu.VMEM(coupling.shape, F32),
        pltpu.VMEM(counts.shape, jnp.int32),
        pltpu.VMEM(good.shape, jnp.int32),
        pltpu.VMEM((expos, half, fibres), F32),
        pltpu.VMEM((expos, half // BITS, fibres), jnp.int32),
    ]


def sent_weights(moves, wav_count, place, slots, coupling, counts, good, ivar, bits):
    expos, width, fibres = ivar.shape
    half = width // 2
    fib_count, pack, per, _ = moves
    return pl.pallas_call(
        functools.partial(sent_kernel, moves, wav_count),
        in_specs=[in_smem] + [in_hbm] * 6,
        out_specs=[in_vmem] * 3,
        out_shape=[
            shaped((2, half, fibres)),
            shaped((expos, half, fibres)),
            shaped((fib_count * pack * per, pack * fibres), BF16),
        ],
        scratch_shapes=[
            pltpu.VMEM(slots.shape, jnp.int32),
            *weights_scratch(coupling, counts, good, ivar),
            pltpu.SemaphoreType.DMA((6,)),
        ],
        compiler_params=params(),
        cost_estimate=cost(20 * ivar.size, 6 * ivar.size),
        name="sent_weights",
    )(place, *held_in_hbm(slots, coupling, counts, good, ivar, bits))


def kept_kernel(
    wav_count, place_ref, coupling_ref, counts_ref, good_ref, pixels_ref, ivar_ref, bits_ref,
    sums_ref, weight_ref, up_ref, down_ref, coupling_v, counts_v, good_v, ivar_v, bits_v, ivar_s, pixel_s, sems,
):
    expos, width, fibres = ivar_ref.shape
    streams = expos * fibres // LANES
    count = -(-HALO // ROWS) * ROWS
    pitch = odd(2 * count)
    which = place_ref[2]
    pairs = [(coupling_ref, coupling_v), (counts_ref, counts_v), (good_ref, good_v)]
    pairs += half_copies(which, ivar_ref, bits_ref, ivar_v, bits_v)
    for source, target in ((ivar_ref, ivar_s), (pixels_ref, pixel_s)):
        pairs += stream_copies(source, target, 0, count, pitch, 0)
        pairs += stream_copies(source, target, width - count, count, pitch, count)
    for wait in in_flight(pairs, sems):
        wait.wait()

    back = 1.0 / stream_coupling(coupling_v, expos)
    zero = jnp.zeros((streams, LANES), F32)
    states = [(zero, zero + 1.0, zero), (zero, zero + 1.0, zero)]

    def eliminate(tile, tiles):
        for i in range(HALO * tile // tiles, HALO * (tile + 1) // tiles):
            for side, row in enumerate((2 * count - HALO + i, HALO - 1 - i)):
                at = pl.ds(row, streams, stride=pitch)
                states[side] = advance(states[side], ivar_s[at, :], pixel_s[at, :], back)
                if i % 24 == 23:
                    states[side] = rescaled(states[side])

    write_weights(
        place_ref, wav_count, which, coupling_v, counts_v, good_v, ivar_v, bits_v, sums_ref, weight_ref, eliminate
    )
    for (n, d, b), out_ref in zip(states, (up_ref, down_ref)):
        scale = 1.0 / (d + n * back)
        out_ref[0] = n * scale
        out_ref[1] = b * scale


def kept_weights(wav_count, place, coupling, counts, good, pixels, ivar, bits):
    expos, width, fibres = ivar.shape
    half = width // 2
    streams = expos * fibres // LANES
    count = -(-HALO // ROWS) * ROWS
    edge = shaped((2, streams, LANES))
    return pl.pallas_call(
        functools.partial(kept_kernel, wav_count),
        in_specs=[in_smem] + [in_hbm] * 6,
        out_specs=[in_vmem] * 4,
        out_shape=[shaped((2, half, fibres)), shaped((expos, half, fibres)), edge, edge],
        scratch_shapes=[
            *weights_scratch(coupling, counts, good, ivar),
            pltpu.VMEM((streams * odd(2 * count), LANES), F32),
            pltpu.VMEM((streams * odd(2 * count), LANES), F32),
            pltpu.SemaphoreType.DMA((5 + 4 * streams,)),
        ],
        compiler_params=params(),
        cost_estimate=cost(20 * ivar.size, 6 * ivar.size),
        name="kept_weights",
    )(place, *held_in_hbm(coupling, counts, good, pixels, ivar, bits))


def layout_kernel(place_ref, pixels_ref, ivar_ref, pixel_out, ivar_out, sems):
    width = ivar_ref.shape[1]
    pairs = stream_copies(ivar_ref, ivar_out, 0, width, odd(width), 0)
    pairs += stream_copies(pixels_ref, pixel_out, 0, width, odd(width), 0)
    for wait in in_flight(pairs, sems):
        wait.wait()


def stream_layout(place, pixels, ivar):
    expos, width, fibres = ivar.shape
    streams = expos * fibres // LANES
    laid = shaped((streams * odd(width), LANES))
    return pl.pallas_call(
        layout_kernel,
        in_specs=[in_smem] + [in_hbm] * 2,
        out_specs=[in_vmem] * 2,
        out_shape=[laid, laid],
        scratch_shapes=[pltpu.SemaphoreType.DMA((2 * streams,))],
        compiler_params=params(),
        cost_estimate=cost(0, 16 * ivar.size),
        name="stream_layout",
    )(place, *held_in_hbm(pixels, ivar))


def recv_kernel(moves, place_ref, slots_ref, table_ref):
    write_recv_table(*moves, place_ref[0], slots_ref, table_ref)


def recv_moves(moves, place, slots, fibres):
    fib_count, pack, per, _ = moves
    return pl.pallas_call(
        functools.partial(recv_kernel, moves),
        in_specs=[in_smem, in_vmem],
        out_specs=in_vmem,
        out_shape=shaped((pack * fibres, fib_count * pack * per), BF16),
        compiler_params=params(),
        cost_estimate=cost(1e6, 1e6),
        name="recv_moves",
    )(place, slots)


def solve_kernel(
    place_ref, coupling_ref, left_ref, right_ref, pixel_ref, ivar_ref, weight_t_ref, weight_m_ref,
    theirs_ref, mine_ref, solved_s, lead_s, rest_s,
):
    streams = left_ref.shape[1]
    expos, half, fibres = weight_t_ref.shape
    width = 2 * half
    pitch = odd(width)
    middle = half
    coupling = stream_coupling(coupling_ref, expos)
    back = 1.0 / coupling

    def row_at(i):
        return pl.ds(i, streams, stride=pitch)

    def begin(edge_ref):
        u = edge_ref[0]
        return (u, 1.0 - u * back, edge_ref[1])

    def keep(side, i, state):
        n, d, b = state
        inverse = inverse_of(d + n * back)
        lead_s[side, i] = d * inverse
        rest_s[side, i] = (b * back) * inverse

    unrolled = divisor_of(middle, 24)

    def eliminate(it, states):
        states = list(states)
        for k in range(unrolled):
            i = it * unrolled + k
            for side, row in enumerate((i, width - 1 - i)):
                keep(side, i, states[side])
                states[side] = advance(states[side], ivar_ref[row_at(row), :], pixel_ref[row_at(row), :], back)
        return tuple(rescaled(state) for state in states)

    states = lax.fori_loop(0, middle // unrolled, eliminate, (begin(left_ref), begin(right_ref)))
    for side in range(2):
        keep(side, middle, states[side])
    lead, rest = lead_s[0, middle], rest_s[0, middle]
    lead_r, rest_r = lead_s[1, middle], rest_s[1, middle]
    left = (rest + lead * rest_r) / (1.0 - lead * lead_r)
    right = rest_r + lead_r * left
    several = divisor_of(middle, 48)

    def after_both(near, far):
        return far[0] * near[0], far[1] + far[0] * near[1]

    def step(factors, value):
        return factors[1] + factors[0] * value

    def substitute(it, values):
        values = list(values)
        for k in range(0, several, 4):
            for side in range(2):
                rows = [middle - 1 - (it * several + k + m) for m in range(4)]
                one, two, three, four = [(lead_s[side, i], rest_s[side, i]) for i in rows]
                first_two = after_both(one, two)
                all_four = after_both(first_two, after_both(three, four))
                value = values[side]
                third = step(first_two, value)
                solved = [value, step(one, value), third, step(three, third)]
                values[side] = step(all_four, value)
                for i, x in zip(rows, solved):
                    solved_s[row_at(i if side == 0 else width - 1 - i), :] = x
        return tuple(values)

    lax.fori_loop(0, middle // several, substitute, (left, right))

    blocks = fibres // LANES
    unroll = 5

    def coadd(out_ref, weight_ref, which):
        start = which * half

        def body(g, carry):
            for k in range(unroll):
                row = pl.multiple_of((g * unroll + k) * ROWS, ROWS)
                for h in range(blocks):
                    cut = pl.ds(h * LANES, LANES)
                    total = None
                    for e in range(expos):
                        at = pl.ds((h * expos + e) * pitch + start + row, ROWS)
                        term = weight_ref[e, pl.ds(row, ROWS), cut] * solved_s[at, :]
                        total = term if e == 0 else total + term
                    out_ref[0, pl.ds(row, ROWS), cut] = total
            return carry

        lax.fori_loop(0, half // (unroll * ROWS), body, 0)

    coadd(theirs_ref, weight_t_ref, 1 - place_ref[2])
    coadd(mine_ref, weight_m_ref, place_ref[2])


def flux_sums(place, coupling, left, right, pixels, ivar, weight_t, weight_m):
    expos, half, fibres = weight_t.shape
    streams = left.shape[1]
    out = shaped((1, half, fibres))
    factor_scratch = pltpu.VMEM((2, half + 1, streams, LANES), F32)
    return pl.pallas_call(
        solve_kernel,
        in_specs=[in_smem] + [in_vmem] * 7,
        out_specs=[in_vmem, in_vmem],
        out_shape=[out, out],
        scratch_shapes=[pltpu.VMEM(pixels.shape, F32), factor_scratch, factor_scratch],
        compiler_params=params(),
        cost_estimate=cost(0, 0),
        name="flux_sums",
    )(place, coupling, left, right, pixels, ivar, weight_t, weight_m)


def split_dot(x, table, dims):
    top = x.astype(BF16)
    low = (x - top.astype(F32)).astype(BF16)
    both = lax.dot_general(jnp.concatenate([top, low], 0), table, dims, preferred_element_type=F32)
    return both[: x.shape[0]] + both[x.shape[0] :]


def sort_kernel(pack, scaled, theirs_ref, mine_ref, table_ref, *refs):
    values, rows, _ = mine_ref.shape
    part = rows // pack
    totals = [mine_ref[v] + theirs_ref[v] for v in range(values)]
    if scaled:
        scale_ref, *out_refs = refs
        totals = [t * scale_ref[...] for t in totals]
    else:
        *out_refs, scale_ref = refs
        scale = 1.0 / jnp.maximum(totals[0], 1.0)
        scale_ref[...] = scale
        totals[1] = totals[1] * scale
    x = jnp.concatenate(
        [jnp.concatenate([t[h * part : (h + 1) * part] for h in range(pack)], 1) for t in totals], 0
    )
    moved = split_dot(x, table_ref[...], NT)
    lanes = moved.shape[1] // len(out_refs)
    for d, out_ref in enumerate(out_refs):
        for v in range(values):
            out_ref[v] = moved[v * part : (v + 1) * part, d * lanes : (d + 1) * lanes]


def sort_fibres(theirs, mine, table, pack, pieces, scale=None):
    values, rows, fibres = mine.shape
    lanes = table.shape[0] // pieces
    scaled = scale is not None
    outs = [shaped((values, rows // pack, lanes))] * pieces + ([] if scaled else [shaped((rows, fibres))])
    args = (theirs, mine, table) + ((scale,) if scaled else ())
    return pl.pallas_call(
        functools.partial(sort_kernel, pack, scaled),
        in_specs=[in_vmem] * len(args),
        out_specs=[in_vmem] * len(outs),
        out_shape=outs,
        compiler_params=params(),
        cost_estimate=cost(0, 0),
        name="sort_flux" if scaled else "sort_weights",
    )(*args)


def exchange(pieces, fib_count):
    if len(pieces) == 1:
        return [lax.all_to_all(pieces[0], "fib", split_axis=2, concat_axis=2, tiled=True)]
    arrived = [pieces[0]]
    for d in range(1, fib_count):
        arrived.append(lax.ppermute(pieces[d], "fib", [(i, (i + d) % fib_count) for i in range(fib_count)]))
    return arrived


def landed(refs, table):
    values, part, _ = refs[0].shape
    x = jnp.concatenate(
        [jnp.concatenate([ref[v] for ref in refs], 1) if len(refs) > 1 else refs[0][v] for v in range(values)], 0
    )
    moved = split_dot(x, table, NT)
    return [moved[v * part : (v + 1) * part] for v in range(values)]


def weights_end_kernel(pack, total, place_ref, table_ref, *refs):
    *piece_refs, ivar_ref, res_ref = refs
    weight, band = landed(piece_refs, table_ref[...])
    rows, fibres = ivar_ref.shape
    part = rows // pack
    start = (place_ref[1] * 2 + place_ref[2]) * rows
    for h in range(pack):
        at = slice(h * part, (h + 1) * part)
        cut = slice(h * fibres, (h + 1) * fibres)
        row = start + h * part + lax.broadcasted_iota(jnp.int32, (part, 1), 0)
        w, b = weight[:, cut], band[:, cut]
        before = jnp.where(row == 0, 0.0, b)
        after = jnp.where(row == total - 1, 0.0, b)
        ivar_ref[at, :] = w
        res_ref[0, at, :] = before
        res_ref[1, at, :] = jnp.minimum(w, 1.0) - before - after
        res_ref[2, at, :] = after


def end_weights(place, table, pieces, pack, fibres, total):
    rows = pieces[0].shape[1] * pack
    return pl.pallas_call(
        functools.partial(weights_end_kernel, pack, total),
        in_specs=[in_smem] + [in_vmem] * (1 + len(pieces)),
        out_specs=[in_vmem] * 2,
        out_shape=[shaped((rows, fibres)), shaped((3, rows, fibres))],
        compiler_params=params(),
        cost_estimate=cost(4 * rows * table.size, 6 * rows * fibres * 4),
        name="end_weights",
    )(place, table, *pieces)


def flux_end_kernel(pack, table_ref, *refs):
    *piece_refs, flux_ref = refs
    (flux,) = landed(piece_refs, table_ref[...])
    rows, fibres = flux_ref.shape
    part = rows // pack
    for h in range(pack):
        flux_ref[h * part : (h + 1) * part, :] = flux[:, h * fibres : (h + 1) * fibres]


def end_flux(table, pieces, pack, fibres):
    rows = pieces[0].shape[1] * pack
    return pl.pallas_call(
        functools.partial(flux_end_kernel, pack),
        in_specs=[in_vmem] * (1 + len(pieces)),
        out_specs=in_vmem,
        out_shape=shaped((rows, fibres)),
        compiler_params=params(),
        cost_estimate=cost(2 * rows * table.size, 2 * rows * fibres * 4),
        name="end_flux",
    )(table, *pieces)


def after(value, done):
    return lax.optimization_barrier((value, done))[0]


def per_device(pixels, pixel_ivar, clip_bits, coupling, counts, good_flags, owner_slot):
    expos, width, fibres = pixels.shape
    fib_count, wav_count = lax.axis_size("fib"), lax.axis_size("wav")
    total = width * wav_count
    per = fibres // fib_count
    rows = width // 2
    pack = max(1, LANES // per)
    while pack > 1 and rows % (pack * ROWS):
        pack //= 2
    rel = pack * per == LANES
    pieces = fib_count if rel else 1
    place = jnp.stack([lax.axis_index(axis) for axis in ("fib", "wav", "exp")]).astype(jnp.int32)
    coupling, counts, slots = coupling[None], counts[None], owner_slot[None]
    swap = [(0, 1), (1, 0)]
    moves = (fib_count, pack, per, rel)

    theirs, weight_t, send_table = sent_weights(
        moves, wav_count, place, slots, coupling, counts, good_flags, pixel_ivar, clip_bits
    )
    arriving = lax.ppermute(theirs, "exp", swap)
    mine, weight_m, up, down = kept_weights(
        wav_count, after(place, theirs), coupling, counts, good_flags, pixels, pixel_ivar, clip_bits
    )
    *sorted_pieces, scale = sort_fibres(arriving, mine, send_table, pack, pieces)
    weight_pieces = exchange(sorted_pieces, fib_count)

    up, down = after((up, down), scale)
    upward = [(i, i + 1) for i in range(wav_count - 1)]
    left = lax.ppermute(up, "wav", upward)
    right = lax.ppermute(down, "wav", [(j, i) for i, j in upward])
    pixel_s, ivar_s = stream_layout(after(place, scale), pixels, pixel_ivar)
    theirs, mine = flux_sums(place, coupling, left, right, pixel_s, ivar_s, weight_t, weight_m)
    recv_table = recv_moves(moves, after(place, theirs), slots, fibres)
    if rel:
        theirs = after(theirs, (weight_pieces[1], weight_pieces[2]))
    theirs = lax.ppermute(theirs, "exp", swap)
    flux_pieces = exchange(sort_fibres(theirs, mine, send_table, pack, pieces, scale), fib_count)

    ivar, res = end_weights(place, recv_table, weight_pieces, pack, fibres, total)
    flux = end_flux(recv_table, flux_pieces, pack, fibres)
    return (flux, ivar, res)


def solution(mesh):
    return jax.shard_map(
        per_device,
        mesh=mesh,
        in_specs=(
            P("exp", "wav", "fib"),
            P("exp", "wav", "fib"),
            P("exp", "wav", "fib"),
            P("fib"),
            P("fib"),
            P("exp", "fib"),
            P(),
        ),
        out_specs=(
            P(("wav", "exp"), "fib"),
            P(("wav", "exp"), "fib"),
            P(None, ("wav", "exp"), "fib"),
        ),
        check_vma=False,
    )
```

```python
import functools

import jax
import jax.numpy as jnp
from jax import lax
from jax.experimental import pallas as pl
from jax.experimental.pallas import tpu as pltpu
from jax.sharding import PartitionSpec as P

HALO = 50
BITS = 15
LANES = 128
ROWS = 8
GROUP = 120
VMEM_BYTES = 32 * 1024 * 1024
F32 = jnp.float32
BF16 = jnp.bfloat16
NT = (((1,), (1,)), ((), ()))

in_vmem = pl.BlockSpec(memory_space=pltpu.VMEM)
in_smem = pl.BlockSpec(memory_space=pltpu.SMEM)
in_hbm = pl.BlockSpec(memory_space=pltpu.HBM)


def params():
    return pltpu.CompilerParams(vmem_limit_bytes=VMEM_BYTES)


def cost(flops, moved):
    return pl.CostEstimate(flops=int(flops), bytes_accessed=int(moved), transcendentals=0)


def held_in_hbm(*arrays):
    return [pltpu.with_memory_space_constraint(array, pltpu.HBM) for array in arrays]


def shaped(shape, dtype=F32):
    return jax.ShapeDtypeStruct(shape, dtype)


def usable_rows(place_ref, counts_ref, good_ref):
    count = good_ref.shape[0]
    return [
        good_ref[e : e + 1, :].astype(F32)
        * jnp.where(place_ref[2] * count + e < counts_ref[...], 1.0, 0.0)
        for e in range(count)
    ]


def tile_bits(tile):
    first, last = (ROWS * tile) // BITS, (ROWS * tile + ROWS - 1) // BITS
    split = BITS * last - ROWS * tile
    row = lax.broadcasted_iota(jnp.int32, (ROWS, 1), 0)
    word = jnp.where(row >= split, last, first)
    return first, last, split, jnp.left_shift(1, ROWS * tile + row - BITS * word)


def tile_words(words, tile):
    first, last, split, mask = tile_bits(tile)
    picked = words[first : first + 1, :]
    if last != first:
        row = lax.broadcasted_iota(jnp.int32, (ROWS, 1), 0)
        picked = jnp.where(row >= split, words[last : last + 1, :], picked)
    return (picked & mask) != 0


def in_flight(pairs, sems, at=0):
    copies = [pltpu.make_async_copy(source, target, sems.at[at + i]) for i, (source, target) in enumerate(pairs)]
    for copy in copies:
        copy.start()
    return copies


def inverse_of(x):
    guess = pl.reciprocal(x, approx=True)
    return guess * (2.0 - x * guess)


def advance(state, ivar, pixel, back_coupling):
    n, d, b = state
    next_d = d + n * back_coupling
    return (n * (1.0 + ivar * back_coupling) + ivar * d, next_d, b + (ivar * pixel) * next_d)


def rescaled(state):
    scale = inverse_of(state[1])
    return tuple(part * scale for part in state)


def odd(rows):
    return rows + 1 - rows % 2


def divisor_of(size, most):
    return max(k for k in range(1, most + 1) if size % k == 0)


def owners(slots_ref, fib_count, fibres):
    rows = [slots_ref[:, s * fibres : (s + 1) * fibres].astype(F32) for s in range(fib_count)]
    sources = -(-fib_count // ROWS) * ROWS
    if sources > fib_count:
        rows.append(jnp.full((sources - fib_count, fibres), -1.0, F32))
    slots = jnp.concatenate(rows, 0)
    owner = jnp.floor((slots + 0.5) * (1.0 / fibres))
    return owner, slots - owner * fibres


def earlier_fibres(fibres):
    row = lax.broadcasted_iota(jnp.int32, (fibres, fibres), 0)
    col = lax.broadcasted_iota(jnp.int32, (fibres, fibres), 1)
    return (row < col).astype(F32).astype(BF16)


def write_send_table(fib_count, pack, per, rel, me, slots_ref, table_ref):
    fibres = table_ref.shape[1] // pack
    lanes = pack * per
    owner, _ = owners(slots_ref, fib_count, fibres)
    source = lax.broadcasted_iota(jnp.int32, owner.shape, 0)
    my_owner = jnp.sum(jnp.where(source == me, owner, 0.0), axis=0, keepdims=True).astype(jnp.int32)
    to_owner = (source == my_owner).astype(F32)
    counted = jnp.dot(to_owner.astype(BF16), earlier_fibres(fibres), preferred_element_type=F32)
    rank = jnp.sum(to_owner * counted, axis=0, keepdims=True).astype(jnp.int32)
    target = my_owner
    if rel:
        target = jnp.where(my_owner >= me, my_owner - me, my_owner - me + fib_count)
    base = target * lanes + rank
    place_of = jnp.concatenate([base + h * per for h in range(pack)], 1)
    row = lax.broadcasted_iota(jnp.int32, table_ref.shape, 0)
    table_ref[...] = (row == place_of).astype(F32).astype(BF16)


def write_recv_table(fib_count, pack, per, rel, me, slots_ref, table_ref):
    fibres = table_ref.shape[0] // pack
    lanes = pack * per
    total_lanes = fib_count * lanes
    owner, column = owners(slots_ref, fib_count, fibres)
    source = lax.broadcasted_iota(jnp.int32, owner.shape, 0)
    mine = (owner == me.astype(F32)).astype(F32)
    rank_in = jnp.dot(mine.astype(BF16), earlier_fibres(fibres), preferred_element_type=F32).astype(jnp.int32)
    order = source
    if rel:
        order = jnp.where(me >= source, me - source, me - source + fib_count)
    arrival = jnp.where(mine > 0.0, order * lanes + rank_in, -total_lanes)
    tall = lax.broadcasted_iota(jnp.int32, (total_lanes, fibres), 0)
    landing = jnp.zeros((ROWS, total_lanes), F32)
    for s in range(fib_count):
        hit = tall == arrival[s : s + 1, :]
        for h in range(1, pack):
            hit = hit | (tall == arrival[s : s + 1, :] + h * per)
        values = jnp.broadcast_to(column[s : s + 1, :], (ROWS, fibres)).astype(BF16)
        landing = landing + lax.dot_general(
            values, hit.astype(F32).astype(BF16), NT, preferred_element_type=F32
        )
    lane = lax.broadcasted_iota(jnp.int32, (1, total_lanes), 1)
    landing = landing[0:1, :].astype(jnp.int32)
    for h in range(1, pack):
        inside = (lane % lanes >= h * per) & (lane % lanes < (h + 1) * per)
        landing = jnp.where(inside, landing + h * fibres, landing)
    row = lax.broadcasted_iota(jnp.int32, table_ref.shape, 0)
    table_ref[...] = (row == landing).astype(F32).astype(BF16)


def stream_coupling(coupling_ref, expos):
    coupling = coupling_ref[...]
    blocks = coupling.shape[1] // LANES
    return jnp.concatenate(
        [jnp.broadcast_to(coupling[:, h * LANES : (h + 1) * LANES], (expos, LANES)) for h in range(blocks)], 0
    )


def weight_tile(coupling, usable, words, ivars, within, scale_row):
    links = scale_row * coupling
    weights = []
    weight_sum = band_sum = None
    for e, ivar in enumerate(ivars):
        weight = jnp.where(tile_words(words[e], within), ivar * usable[e], 0.0)
        band = weight * inverse_of(ivar + links)
        weights.append(weight)
        weight_sum = weight if e == 0 else weight_sum + weight
        band_sum = band if e == 0 else band_sum + band
    return weights, weight_sum, band_sum * coupling


def write_weights(place_ref, wav_count, which, coupling_v, counts_v, good_v, ivar_of, words_of, sums_ref, weight_ref, beside):
    expos, half, _ = weight_ref.shape
    coupling = coupling_v[...]
    usable = usable_rows(place_ref, counts_v, good_v)
    start = place_ref[1] * (2 * half) + which * half
    tiles = half // ROWS
    tiles_in_group = GROUP // ROWS
    for tile in range(tiles):
        beside(tile, tiles)
        group, within = divmod(tile, tiles_in_group)
        scale_row = 4.0
        if tile in (0, tiles - 1):
            row = start + ROWS * tile + lax.broadcasted_iota(jnp.int32, (ROWS, 1), 0)
            scale_row = jnp.where((row == 0) | (row == wav_count * 2 * half - 1), 2.0, 4.0)
        at = slice(ROWS * tile, ROWS * (tile + 1))
        weights, weight_sum, band_sum = weight_tile(
            coupling,
            usable,
            [words_of(e, group) for e in range(expos)],
            [ivar_of(e, tile) for e in range(expos)],
            within,
            scale_row,
        )
        for e in range(expos):
            weight_ref[e, at, :] = weights[e]
        sums_ref[0, at, :] = weight_sum
        sums_ref[1, at, :] = band_sum


def sent_kernel(
    moves, wav_count, place_ref, slots_ref, coupling_ref, counts_ref, good_ref, bits_ref, ivar_ref, pixels_ref,
    sums_ref, weight_ref, table_ref, slots_v, coupling_v, counts_v, good_v, bits_v, ivar_v, pixels_v, sems,
):
    expos, width, _ = ivar_ref.shape
    half = width // 2
    which = 1 - place_ref[2]
    words = GROUP // BITS

    def part(source, target, first):
        at = pl.ds(pl.multiple_of(first, ROWS), GROUP)
        return source.at[:, at, :], target.at[:, at, :]

    waits = in_flight(
        [
            (slots_ref, slots_v),
            (coupling_ref, coupling_v),
            (counts_ref, counts_v),
            (good_ref, good_v),
            (bits_ref, bits_v),
        ]
        + [part(ivar_ref, ivar_v, which * half + g) for g in range(0, half, GROUP)]
        + [part(ivar_ref, ivar_v, (1 - which) * half + g) for g in range(0, half, GROUP)]
        + [(pixels_ref, pixels_v)],
        sems,
    )
    waits[0].wait()
    write_send_table(*moves, place_ref[0], slots_v, table_ref)
    for wait in waits[1:5]:
        wait.wait()

    def arrive(tile, tiles):
        if ROWS * tile % GROUP == 0:
            waits[5 + ROWS * tile // GROUP].wait()

    write_weights(
        place_ref, wav_count, which, coupling_v, counts_v, good_v,
        lambda e, tile: ivar_v[e, pl.ds(pl.multiple_of(which * half + ROWS * tile, ROWS), ROWS), :],
        lambda e, group: bits_v[e, pl.ds(pl.multiple_of(which * (half // BITS) + words * group, words), words), :],
        sums_ref, weight_ref, arrive,
    )
    for wait in waits[5 + half // GROUP :]:
        wait.wait()


def sent_weights(moves, wav_count, place, slots, coupling, counts, good, bits, ivar, pixels):
    expos, width, fibres = ivar.shape
    half = width // 2
    fib_count, pack, per, _ = moves
    inputs = (slots, coupling, counts, good, bits, ivar, pixels)
    return pl.pallas_call(
        functools.partial(sent_kernel, moves, wav_count),
        in_specs=[in_smem] + [in_hbm] * 7,
        out_specs=[in_vmem] * 10,
        out_shape=[
            shaped((2, half, fibres)),
            shaped((expos, half, fibres)),
            shaped((fib_count * pack * per, pack * fibres), BF16),
        ]
        + [shaped(x.shape, x.dtype) for x in inputs],
        scratch_shapes=[pltpu.SemaphoreType.DMA((6 + width // GROUP,))],
        compiler_params=params(),
        cost_estimate=cost(20 * ivar.size, 6 * ivar.size),
        name="sent_weights",
    )(place, *held_in_hbm(*inputs))


def lay_out(source_ref, target_ref, pieces, pitch):
    expos, _, fibres = source_ref.shape
    for h in range(fibres // LANES):
        for e in range(expos):
            for first, length, at in pieces:
                target_ref[pl.ds((h * expos + e) * pitch + at, length), :] = source_ref[
                    e, pl.ds(first, length), pl.ds(h * LANES, LANES)
                ]


def kept_kernel(
    wav_count, place_ref, coupling_ref, counts_ref, good_ref, pixels_ref, ivar_ref, bits_ref,
    sums_ref, weight_ref, up_ref, down_ref, ivar_s, pixel_s,
):
    expos, width, fibres = ivar_ref.shape
    half = width // 2
    streams = expos * fibres // LANES
    count = -(-HALO // ROWS) * ROWS
    pitch = odd(2 * count)
    which = place_ref[2]
    words = GROUP // BITS
    edges = [(0, count, 0), (width - count, count, count)]
    lay_out(ivar_ref, ivar_s, edges, pitch)
    lay_out(pixels_ref, pixel_s, edges, pitch)
    back = 1.0 / stream_coupling(coupling_ref, expos)
    zero = jnp.zeros((streams, LANES), F32)
    states = [(zero, zero + 1.0, zero), (zero, zero + 1.0, zero)]

    def eliminate(tile, tiles):
        for i in range(HALO * tile // tiles, HALO * (tile + 1) // tiles):
            for side, row in enumerate((2 * count - HALO + i, HALO - 1 - i)):
                at = pl.ds(row, streams, stride=pitch)
                states[side] = advance(states[side], ivar_s[at, :], pixel_s[at, :], back)
                if i % 24 == 23:
                    states[side] = rescaled(states[side])

    write_weights(
        place_ref, wav_count, which, coupling_ref, counts_ref, good_ref,
        lambda e, tile: ivar_ref[e, pl.ds(pl.multiple_of(which * half + ROWS * tile, ROWS), ROWS), :],
        lambda e, group: bits_ref[e, pl.ds(pl.multiple_of(which * (half // BITS) + words * group, words), words), :],
        sums_ref, weight_ref, eliminate,
    )
    for (n, d, b), out_ref in zip(states, (up_ref, down_ref)):
        scale = 1.0 / (d + n * back)
        out_ref[0] = n * scale
        out_ref[1] = b * scale


def kept_weights(wav_count, place, coupling, counts, good, pixels, ivar, bits):
    expos, width, fibres = ivar.shape
    half = width // 2
    streams = expos * fibres // LANES
    count = -(-HALO // ROWS) * ROWS
    edge = shaped((2, streams, LANES))
    edge_scratch = pltpu.VMEM((streams * odd(2 * count), LANES), F32)
    return pl.pallas_call(
        functools.partial(kept_kernel, wav_count),
        in_specs=[in_smem] + [in_vmem] * 6,
        out_specs=[in_vmem] * 4,
        out_shape=[shaped((2, half, fibres)), shaped((expos, half, fibres)), edge, edge],
        scratch_shapes=[edge_scratch, edge_scratch],
        compiler_params=params(),
        cost_estimate=cost(20 * ivar.size, 6 * ivar.size),
        name="kept_weights",
    )(place, coupling, counts, good, pixels, ivar, bits)


def layout_kernel(moves, place_ref, slots_ref, pixels_ref, ivar_ref, table_ref, pixel_out, ivar_out):
    width = ivar_ref.shape[1]
    lay_out(ivar_ref, ivar_out, [(0, width, 0)], odd(width))
    lay_out(pixels_ref, pixel_out, [(0, width, 0)], odd(width))
    write_recv_table(*moves, place_ref[0], slots_ref, table_ref)


def stream_layout(moves, place, slots, pixels, ivar):
    expos, width, fibres = ivar.shape
    streams = expos * fibres // LANES
    fib_count, pack, per, _ = moves
    laid = shaped((streams * odd(width), LANES))
    return pl.pallas_call(
        functools.partial(layout_kernel, moves),
        in_specs=[in_smem] + [in_vmem] * 3,
        out_specs=[in_vmem] * 3,
        out_shape=[shaped((pack * fibres, fib_count * pack * per), BF16), laid, laid],
        compiler_params=params(),
        cost_estimate=cost(0, 16 * ivar.size),
        name="stream_layout",
    )(place, slots, pixels, ivar)


def solve_kernel(
    wav_count, place_ref, coupling_ref, left_ref, right_ref, pixel_ref, ivar_ref, weight_t_ref, weight_m_ref,
    theirs_ref, mine_ref, solved_s, lead_s, rest_s,
):
    streams = left_ref.shape[1]
    expos, half, fibres = weight_t_ref.shape
    width = 2 * half
    pitch = odd(width)
    middle = half
    coupling = stream_coupling(coupling_ref, expos)
    back = 1.0 / coupling

    def row_at(i):
        return pl.ds(i, streams, stride=pitch)

    def begin(edge_ref, outermost):
        u = jnp.where(place_ref[1] == outermost, 0.0, edge_ref[0])
        return (u, 1.0 - u * back, jnp.where(place_ref[1] == outermost, 0.0, edge_ref[1]))

    def keep(side, i, state):
        n, d, b = state
        inverse = inverse_of(d + n * back)
        lead_s[side, i] = d * inverse
        rest_s[side, i] = (b * back) * inverse

    unrolled = divisor_of(middle, 24)

    def eliminate(it, states):
        states = list(states)
        for k in range(unrolled):
            i = it * unrolled + k
            for side, row in enumerate((i, width - 1 - i)):
                keep(side, i, states[side])
                states[side] = advance(states[side], ivar_ref[row_at(row), :], pixel_ref[row_at(row), :], back)
        return tuple(rescaled(state) for state in states)

    states = lax.fori_loop(0, middle // unrolled, eliminate, (begin(left_ref, 0), begin(right_ref, wav_count - 1)))
    for side in range(2):
        keep(side, middle, states[side])
    lead, rest = lead_s[0, middle], rest_s[0, middle]
    lead_r, rest_r = lead_s[1, middle], rest_s[1, middle]
    left = (rest + lead * rest_r) / (1.0 - lead * lead_r)
    right = rest_r + lead_r * left
    several = divisor_of(middle, 48)

    def after_both(near, far):
        return far[0] * near[0], far[1] + far[0] * near[1]

    def step(factors, value):
        return factors[1] + factors[0] * value

    def substitute(it, values):
        values = list(values)
        for k in range(0, several, 4):
            for side in range(2):
                rows = [middle - 1 - (it * several + k + m) for m in range(4)]
                one, two, three, four = [(lead_s[side, i], rest_s[side, i]) for i in rows]
                first_two = after_both(one, two)
                all_four = after_both(first_two, after_both(three, four))
                value = values[side]
                third = step(first_two, value)
                solved = [value, step(one, value), third, step(three, third)]
                values[side] = step(all_four, value)
                for i, x in zip(rows, solved):
                    solved_s[row_at(i if side == 0 else width - 1 - i), :] = x
        return tuple(values)

    lax.fori_loop(0, middle // several, substitute, (left, right))

    blocks = fibres // LANES
    unroll = 5

    def coadd(out_ref, weight_ref, which):
        start = which * half

        def body(g, carry):
            for k in range(unroll):
                row = pl.multiple_of((g * unroll + k) * ROWS, ROWS)
                for h in range(blocks):
                    cut = pl.ds(h * LANES, LANES)
                    total = None
                    for e in range(expos):
                        at = pl.ds((h * expos + e) * pitch + start + row, ROWS)
                        term = weight_ref[e, pl.ds(row, ROWS), cut] * solved_s[at, :]
                        total = term if e == 0 else total + term
                    out_ref[0, pl.ds(row, ROWS), cut] = total
            return carry

        lax.fori_loop(0, half // (unroll * ROWS), body, 0)

    coadd(theirs_ref, weight_t_ref, 1 - place_ref[2])
    coadd(mine_ref, weight_m_ref, place_ref[2])


def flux_sums(wav_count, place, coupling, left, right, pixels, ivar, weight_t, weight_m):
    expos, half, fibres = weight_t.shape
    streams = left.shape[1]
    out = shaped((1, half, fibres))
    factor_scratch = pltpu.VMEM((2, half + 1, streams, LANES), F32)
    return pl.pallas_call(
        functools.partial(solve_kernel, wav_count),
        in_specs=[in_smem] + [in_vmem] * 7,
        out_specs=[in_vmem, in_vmem],
        out_shape=[out, out],
        scratch_shapes=[pltpu.VMEM(pixels.shape, F32), factor_scratch, factor_scratch],
        compiler_params=params(),
        cost_estimate=cost(0, 0),
        name="flux_sums",
    )(place, coupling, left, right, pixels, ivar, weight_t, weight_m)


def split_dot(x, table, dims):
    top = x.astype(BF16)
    low = (x - top.astype(F32)).astype(BF16)
    both = lax.dot_general(jnp.concatenate([top, low], 0), table, dims, preferred_element_type=F32)
    return both[: x.shape[0]] + both[x.shape[0] :]


def sort_kernel(pack, scaled, theirs_ref, mine_ref, table_ref, *refs):
    values, rows, _ = mine_ref.shape
    part = rows // pack
    totals = [mine_ref[v] + theirs_ref[v] for v in range(values)]
    if scaled:
        scale_ref, *out_refs = refs
        totals = [t * scale_ref[...] for t in totals]
    else:
        *out_refs, scale_ref = refs
        scale = 1.0 / jnp.maximum(totals[0], 1.0)
        scale_ref[...] = scale
        totals[1] = totals[1] * scale
    x = jnp.concatenate(
        [jnp.concatenate([t[h * part : (h + 1) * part] for h in range(pack)], 1) for t in totals], 0
    )
    moved = split_dot(x, table_ref[...], NT)
    lanes = moved.shape[1] // len(out_refs)
    for d, out_ref in enumerate(out_refs):
        for v in range(values):
            out_ref[v] = moved[v * part : (v + 1) * part, d * lanes : (d + 1) * lanes]


def sort_fibres(theirs, mine, table, pack, pieces, scale=None):
    values, rows, fibres = mine.shape
    lanes = table.shape[0] // pieces
    scaled = scale is not None
    outs = [shaped((values, rows // pack, lanes))] * pieces + ([] if scaled else [shaped((rows, fibres))])
    args = (theirs, mine, table) + ((scale,) if scaled else ())
    return pl.pallas_call(
        functools.partial(sort_kernel, pack, scaled),
        in_specs=[in_vmem] * len(args),
        out_specs=[in_vmem] * len(outs),
        out_shape=outs,
        compiler_params=params(),
        cost_estimate=cost(0, 0),
        name="sort_flux" if scaled else "sort_weights",
    )(*args)


def exchange(pieces, fib_count):
    if len(pieces) == 1:
        return [lax.all_to_all(pieces[0], "fib", split_axis=2, concat_axis=2, tiled=True)]
    arrived = [pieces[0]]
    for d in range(1, fib_count):
        arrived.append(lax.ppermute(pieces[d], "fib", [(i, (i + d) % fib_count) for i in range(fib_count)]))
    return arrived


def landed(refs, table):
    values, part, _ = refs[0].shape
    x = jnp.concatenate(
        [jnp.concatenate([ref[v] for ref in refs], 1) if len(refs) > 1 else refs[0][v] for v in range(values)], 0
    )
    moved = split_dot(x, table, NT)
    return [moved[v * part : (v + 1) * part] for v in range(values)]


def weights_end_kernel(pack, total, place_ref, table_ref, *refs):
    *piece_refs, ivar_ref, res_ref = refs
    weight, band = landed(piece_refs, table_ref[...])
    rows, fibres = ivar_ref.shape
    part = rows // pack
    start = (place_ref[1] * 2 + place_ref[2]) * rows
    for h in range(pack):
        at = slice(h * part, (h + 1) * part)
        cut = slice(h * fibres, (h + 1) * fibres)
        row = start + h * part + lax.broadcasted_iota(jnp.int32, (part, 1), 0)
        w, b = weight[:, cut], band[:, cut]
        before = jnp.where(row == 0, 0.0, b)
        after = jnp.where(row == total - 1, 0.0, b)
        ivar_ref[at, :] = w
        res_ref[0, at, :] = before
        res_ref[1, at, :] = jnp.minimum(w, 1.0) - before - after
        res_ref[2, at, :] = after


def end_weights(place, table, pieces, pack, fibres, total):
    rows = pieces[0].shape[1] * pack
    return pl.pallas_call(
        functools.partial(weights_end_kernel, pack, total),
        in_specs=[in_smem] + [in_vmem] * (1 + len(pieces)),
        out_specs=[in_vmem] * 2,
        out_shape=[shaped((rows, fibres)), shaped((3, rows, fibres))],
        compiler_params=params(),
        cost_estimate=cost(4 * rows * table.size, 6 * rows * fibres * 4),
        name="end_weights",
    )(place, table, *pieces)


def flux_end_kernel(pack, table_ref, *refs):
    *piece_refs, flux_ref = refs
    (flux,) = landed(piece_refs, table_ref[...])
    rows, fibres = flux_ref.shape
    part = rows // pack
    for h in range(pack):
        flux_ref[h * part : (h + 1) * part, :] = flux[:, h * fibres : (h + 1) * fibres]


def end_flux(table, pieces, pack, fibres):
    rows = pieces[0].shape[1] * pack
    return pl.pallas_call(
        functools.partial(flux_end_kernel, pack),
        in_specs=[in_vmem] * (1 + len(pieces)),
        out_specs=in_vmem,
        out_shape=shaped((rows, fibres)),
        compiler_params=params(),
        cost_estimate=cost(2 * rows * table.size, 2 * rows * fibres * 4),
        name="end_flux",
    )(table, *pieces)


def after(value, done):
    return lax.optimization_barrier((value, done))[0]


def per_device(pixels, pixel_ivar, clip_bits, coupling, counts, good_flags, owner_slot):
    expos, width, fibres = pixels.shape
    fib_count, wav_count = lax.axis_size("fib"), lax.axis_size("wav")
    total = width * wav_count
    per = fibres // fib_count
    rows = width // 2
    pack = max(1, LANES // per)
    while pack > 1 and rows % (pack * ROWS):
        pack //= 2
    rel = pack * per == LANES
    pieces = fib_count if rel else 1
    place = jnp.stack([lax.axis_index(axis) for axis in ("fib", "wav", "exp")]).astype(jnp.int32)
    coupling, counts, slots = coupling[None], counts[None], owner_slot[None]
    swap = [(0, 1), (1, 0)]
    moves = (fib_count, pack, per, rel)

    theirs, weight_t, send_table, slots, coupling, counts, good, bits, ivar, counted = sent_weights(
        moves, wav_count, place, slots, coupling, counts, good_flags, clip_bits, pixel_ivar, pixels
    )
    arriving = lax.ppermute(theirs, "exp", swap)
    mine, weight_m, up, down = kept_weights(
        wav_count, place, coupling, counts, good, counted, ivar, bits
    )
    *sorted_pieces, scale = sort_fibres(arriving, mine, send_table, pack, pieces)
    weight_pieces = exchange(sorted_pieces, fib_count)

    up, down = after((up, down), scale)
    upward = [(i, (i + 1) % wav_count) for i in range(wav_count)]
    left = lax.ppermute(up, "wav", upward)
    right = lax.ppermute(down, "wav", [(j, i) for i, j in upward])
    recv_table, pixel_s, ivar_s = stream_layout(moves, after(place, scale), slots, counted, ivar)
    theirs, mine = flux_sums(wav_count, place, coupling, left, right, pixel_s, ivar_s, weight_t, weight_m)
    if rel:
        theirs = after(theirs, weight_pieces[1:])
    theirs = lax.ppermute(theirs, "exp", swap)
    flux_pieces = exchange(sort_fibres(theirs, mine, send_table, pack, pieces, scale), fib_count)

    ivar, res = end_weights(place, recv_table, weight_pieces, pack, fibres, total)
    flux = end_flux(recv_table, flux_pieces, pack, fibres)
    return (flux, ivar, res)


def solution(mesh):
    return jax.shard_map(
        per_device,
        mesh=mesh,
        in_specs=(
            P("exp", "wav", "fib"),
            P("exp", "wav", "fib"),
            P("exp", "wav", "fib"),
            P("fib"),
            P("fib"),
            P("exp", "fib"),
            P(),
        ),
        out_specs=(
            P(("wav", "exp"), "fib"),
            P(("wav", "exp"), "fib"),
            P(None, ("wav", "exp"), "fib"),
        ),
        check_vma=False,
    )
```

```python
import functools

import jax
import jax.numpy as jnp
from jax import lax
from jax.experimental import pallas as pl
from jax.experimental.pallas import tpu as pltpu
from jax.sharding import PartitionSpec as P

HALO = 50
BITS = 15
LANES = 128
ROWS = 8
GROUP = 120
VMEM_BYTES = 32 * 1024 * 1024
F32 = jnp.float32
BF16 = jnp.bfloat16
NT = (((1,), (1,)), ((), ()))

in_vmem = pl.BlockSpec(memory_space=pltpu.VMEM)
in_smem = pl.BlockSpec(memory_space=pltpu.SMEM)
in_hbm = pl.BlockSpec(memory_space=pltpu.HBM)


def params():
    return pltpu.CompilerParams(vmem_limit_bytes=VMEM_BYTES)


def cost(flops, moved):
    return pl.CostEstimate(flops=int(flops), bytes_accessed=int(moved), transcendentals=0)


def held_in_hbm(*arrays):
    return [pltpu.with_memory_space_constraint(array, pltpu.HBM) for array in arrays]


def shaped(shape, dtype=F32):
    return jax.ShapeDtypeStruct(shape, dtype)


def usable_rows(place_ref, counts_ref, good_ref):
    count = good_ref.shape[0]
    return [
        good_ref[e : e + 1, :].astype(F32)
        * jnp.where(place_ref[2] * count + e < counts_ref[...], 1.0, 0.0)
        for e in range(count)
    ]


def tile_bits(tile):
    first, last = (ROWS * tile) // BITS, (ROWS * tile + ROWS - 1) // BITS
    split = BITS * last - ROWS * tile
    row = lax.broadcasted_iota(jnp.int32, (ROWS, 1), 0)
    word = jnp.where(row >= split, last, first)
    return first, last, split, jnp.left_shift(1, ROWS * tile + row - BITS * word)


def tile_words(words, tile):
    first, last, split, mask = tile_bits(tile)
    picked = words[first : first + 1, :]
    if last != first:
        row = lax.broadcasted_iota(jnp.int32, (ROWS, 1), 0)
        picked = jnp.where(row >= split, words[last : last + 1, :], picked)
    return (picked & mask) != 0


def in_flight(pairs, sems, at=0):
    copies = [pltpu.make_async_copy(source, target, sems.at[at + i]) for i, (source, target) in enumerate(pairs)]
    for copy in copies:
        copy.start()
    return copies


def inverse_of(x):
    guess = pl.reciprocal(x, approx=True)
    return guess * (2.0 - x * guess)


def advance(state, ivar, pixel, back_coupling):
    n, d, b = state
    ratio = ivar * back_coupling
    next_d = d + n
    return (n * (1.0 + ratio) + ratio * d, next_d, b + (ivar * pixel) * next_d)


def rescaled(state):
    scale = inverse_of(state[1])
    return tuple(part * scale for part in state)


def odd(rows):
    return rows + 1 - rows % 2


def divisor_of(size, most):
    return max(k for k in range(1, most + 1) if size % k == 0)


def owners(slots_ref, fib_count, fibres):
    rows = [slots_ref[:, s * fibres : (s + 1) * fibres].astype(F32) for s in range(fib_count)]
    sources = -(-fib_count // ROWS) * ROWS
    if sources > fib_count:
        rows.append(jnp.full((sources - fib_count, fibres), -1.0, F32))
    slots = jnp.concatenate(rows, 0)
    owner = jnp.floor((slots + 0.5) * (1.0 / fibres))
    return owner, slots - owner * fibres


def earlier_fibres(fibres):
    row = lax.broadcasted_iota(jnp.int32, (fibres, fibres), 0)
    col = lax.broadcasted_iota(jnp.int32, (fibres, fibres), 1)
    return (row < col).astype(F32).astype(BF16)


def write_send_table(fib_count, pack, per, rel, me, slots_ref, table_ref):
    fibres = table_ref.shape[1] // pack
    lanes = pack * per
    owner, _ = owners(slots_ref, fib_count, fibres)
    source = lax.broadcasted_iota(jnp.int32, owner.shape, 0)
    my_owner = jnp.sum(jnp.where(source == me, owner, 0.0), axis=0, keepdims=True).astype(jnp.int32)
    to_owner = (source == my_owner).astype(F32)
    counted = jnp.dot(to_owner.astype(BF16), earlier_fibres(fibres), preferred_element_type=F32)
    rank = jnp.sum(to_owner * counted, axis=0, keepdims=True).astype(jnp.int32)
    target = my_owner
    if rel:
        target = jnp.where(my_owner >= me, my_owner - me, my_owner - me + fib_count)
    base = target * lanes + rank
    place_of = jnp.concatenate([base + h * per for h in range(pack)], 1)
    row = lax.broadcasted_iota(jnp.int32, table_ref.shape, 0)
    table_ref[...] = (row == place_of).astype(F32).astype(BF16)


def write_recv_table(fib_count, pack, per, rel, me, slots_ref, table_ref):
    fibres = table_ref.shape[0] // pack
    lanes = pack * per
    total_lanes = fib_count * lanes
    owner, column = owners(slots_ref, fib_count, fibres)
    source = lax.broadcasted_iota(jnp.int32, owner.shape, 0)
    mine = (owner == me.astype(F32)).astype(F32)
    rank_in = jnp.dot(mine.astype(BF16), earlier_fibres(fibres), preferred_element_type=F32).astype(jnp.int32)
    order = source
    if rel:
        order = jnp.where(me >= source, me - source, me - source + fib_count)
    arrival = jnp.where(mine > 0.0, order * lanes + rank_in, -total_lanes)
    tall = lax.broadcasted_iota(jnp.int32, (total_lanes, fibres), 0)
    landing = jnp.zeros((ROWS, total_lanes), F32)
    for s in range(fib_count):
        hit = tall == arrival[s : s + 1, :]
        for h in range(1, pack):
            hit = hit | (tall == arrival[s : s + 1, :] + h * per)
        values = jnp.broadcast_to(column[s : s + 1, :], (ROWS, fibres)).astype(BF16)
        landing = landing + lax.dot_general(
            values, hit.astype(F32).astype(BF16), NT, preferred_element_type=F32
        )
    lane = lax.broadcasted_iota(jnp.int32, (1, total_lanes), 1)
    landing = landing[0:1, :].astype(jnp.int32)
    for h in range(1, pack):
        inside = (lane % lanes >= h * per) & (lane % lanes < (h + 1) * per)
        landing = jnp.where(inside, landing + h * fibres, landing)
    row = lax.broadcasted_iota(jnp.int32, table_ref.shape, 0)
    table_ref[...] = (row == landing).astype(F32).astype(BF16)


def stream_coupling(coupling_ref, expos):
    coupling = coupling_ref[...]
    blocks = coupling.shape[1] // LANES
    return jnp.concatenate(
        [jnp.broadcast_to(coupling[:, h * LANES : (h + 1) * LANES], (expos, LANES)) for h in range(blocks)], 0
    )


def weight_tile(coupling, usable, words, ivars, within, scale_row):
    links = scale_row * coupling
    weights = []
    weight_sum = band_sum = None
    for e, ivar in enumerate(ivars):
        weight = jnp.where(tile_words(words[e], within), ivar * usable[e], 0.0)
        band = weight * inverse_of(ivar + links)
        weights.append(weight)
        weight_sum = weight if e == 0 else weight_sum + weight
        band_sum = band if e == 0 else band_sum + band
    return weights, weight_sum, band_sum * coupling


def write_weights(place_ref, wav_count, which, coupling_v, counts_v, good_v, ivar_of, words_of, sums_ref, weight_ref, beside):
    expos, half, _ = weight_ref.shape
    coupling = coupling_v[...]
    usable = usable_rows(place_ref, counts_v, good_v)
    start = place_ref[1] * (2 * half) + which * half
    tiles = half // ROWS
    tiles_in_group = GROUP // ROWS
    for tile in range(tiles):
        beside(tile, tiles)
        group, within = divmod(tile, tiles_in_group)
        scale_row = 4.0
        if tile in (0, tiles - 1):
            row = start + ROWS * tile + lax.broadcasted_iota(jnp.int32, (ROWS, 1), 0)
            scale_row = jnp.where((row == 0) | (row == wav_count * 2 * half - 1), 2.0, 4.0)
        at = slice(ROWS * tile, ROWS * (tile + 1))
        weights, weight_sum, band_sum = weight_tile(
            coupling,
            usable,
            [words_of(e, group) for e in range(expos)],
            [ivar_of(e, tile) for e in range(expos)],
            within,
            scale_row,
        )
        for e in range(expos):
            weight_ref[e, at, :] = weights[e]
        sums_ref[0, at, :] = weight_sum
        sums_ref[1, at, :] = band_sum


def sent_kernel(
    moves, wav_count, place_ref, slots_ref, coupling_ref, counts_ref, good_ref, bits_ref, ivar_ref,
    sums_ref, weight_ref, table_ref, slots_v, coupling_v, counts_v, good_v, bits_v, ivar_v, sems,
):
    expos, width, _ = ivar_ref.shape
    half = width // 2
    which = 1 - place_ref[2]
    words = GROUP // BITS

    def part(source, target, first):
        at = pl.ds(pl.multiple_of(first, ROWS), GROUP)
        return source.at[:, at, :], target.at[:, at, :]

    waits = in_flight(
        [
            (slots_ref, slots_v),
            (coupling_ref, coupling_v),
            (counts_ref, counts_v),
            (good_ref, good_v),
            (bits_ref, bits_v),
        ]
        + [part(ivar_ref, ivar_v, which * half + g) for g in range(0, half, GROUP)]
        + [part(ivar_ref, ivar_v, (1 - which) * half + g) for g in range(0, half, GROUP)],
        sems,
    )
    waits[0].wait()
    write_send_table(*moves, place_ref[0], slots_v, table_ref)
    for wait in waits[1:5]:
        wait.wait()

    def arrive(tile, tiles):
        if ROWS * tile % GROUP == 0:
            waits[5 + ROWS * tile // GROUP].wait()

    write_weights(
        place_ref, wav_count, which, coupling_v, counts_v, good_v,
        lambda e, tile: ivar_v[e, pl.ds(pl.multiple_of(which * half + ROWS * tile, ROWS), ROWS), :],
        lambda e, group: bits_v[e, pl.ds(pl.multiple_of(which * (half // BITS) + words * group, words), words), :],
        sums_ref, weight_ref, arrive,
    )
    for wait in waits[5 + half // GROUP :]:
        wait.wait()


def sent_weights(moves, wav_count, place, slots, coupling, counts, good, bits, ivar):
    expos, width, fibres = ivar.shape
    half = width // 2
    fib_count, pack, per, _ = moves
    inputs = (slots, coupling, counts, good, bits, ivar)
    return pl.pallas_call(
        functools.partial(sent_kernel, moves, wav_count),
        in_specs=[in_smem] + [in_hbm] * 6,
        out_specs=[in_vmem] * 9,
        out_shape=[
            shaped((2, half, fibres)),
            shaped((expos, half, fibres)),
            shaped((fib_count * pack * per, pack * fibres), BF16),
        ]
        + [shaped(x.shape, x.dtype) for x in inputs],
        scratch_shapes=[pltpu.SemaphoreType.DMA((5 + width // GROUP,))],
        compiler_params=params(),
        cost_estimate=cost(20 * ivar.size, 6 * ivar.size),
        name="sent_weights",
    )(place, *held_in_hbm(*inputs))


def lay_out(source_ref, target_ref, pieces, pitch):
    expos, _, fibres = source_ref.shape
    for h in range(fibres // LANES):
        for e in range(expos):
            for first, length, at in pieces:
                target_ref[pl.ds((h * expos + e) * pitch + at, length), :] = source_ref[
                    e, pl.ds(first, length), pl.ds(h * LANES, LANES)
                ]


def kept_kernel(
    wav_count, place_ref, coupling_ref, counts_ref, good_ref, pixels_ref, ivar_ref, bits_ref,
    sums_ref, weight_ref, up_ref, down_ref, ivar_s, pixel_s,
):
    expos, width, fibres = ivar_ref.shape
    half = width // 2
    streams = expos * fibres // LANES
    count = -(-HALO // ROWS) * ROWS
    pitch = odd(2 * count)
    which = place_ref[2]
    words = GROUP // BITS
    edges = [(0, count, 0), (width - count, count, count)]
    lay_out(ivar_ref, ivar_s, edges, pitch)
    lay_out(pixels_ref, pixel_s, edges, pitch)
    coupling = stream_coupling(coupling_ref, expos)
    back = 1.0 / coupling
    zero = jnp.zeros((streams, LANES), F32)
    states = [(zero, zero + 1.0, zero), (zero, zero + 1.0, zero)]

    def eliminate(tile, tiles):
        for i in range(HALO * tile // tiles, HALO * (tile + 1) // tiles):
            for side, row in enumerate((2 * count - HALO + i, HALO - 1 - i)):
                at = pl.ds(row, streams, stride=pitch)
                states[side] = advance(states[side], ivar_s[at, :], pixel_s[at, :], back)
                if i % 24 == 23:
                    states[side] = rescaled(states[side])

    write_weights(
        place_ref, wav_count, which, coupling_ref, counts_ref, good_ref,
        lambda e, tile: ivar_ref[e, pl.ds(pl.multiple_of(which * half + ROWS * tile, ROWS), ROWS), :],
        lambda e, group: bits_ref[e, pl.ds(pl.multiple_of(which * (half // BITS) + words * group, words), words), :],
        sums_ref, weight_ref, eliminate,
    )
    for (n, d, b), out_ref in zip(states, (up_ref, down_ref)):
        scale = 1.0 / (d + n)
        out_ref[0] = coupling * (n * scale)
        out_ref[1] = b * scale


def kept_weights(wav_count, place, coupling, counts, good, pixels, ivar, bits):
    expos, width, fibres = ivar.shape
    half = width // 2
    streams = expos * fibres // LANES
    count = -(-HALO // ROWS) * ROWS
    edge = shaped((2, streams, LANES))
    edge_scratch = pltpu.VMEM((streams * odd(2 * count), LANES), F32)
    return pl.pallas_call(
        functools.partial(kept_kernel, wav_count),
        in_specs=[in_smem] + [in_vmem] * 6,
        out_specs=[in_vmem] * 4,
        out_shape=[shaped((2, half, fibres)), shaped((expos, half, fibres)), edge, edge],
        scratch_shapes=[edge_scratch, edge_scratch],
        compiler_params=params(),
        cost_estimate=cost(20 * ivar.size, 6 * ivar.size),
        name="kept_weights",
    )(place, coupling, counts, good, pixels, ivar, bits)


def layout_kernel(moves, place_ref, slots_ref, pixels_ref, ivar_ref, table_ref, pixel_out, ivar_out):
    width = ivar_ref.shape[1]
    lay_out(ivar_ref, ivar_out, [(0, width, 0)], odd(width))
    lay_out(pixels_ref, pixel_out, [(0, width, 0)], odd(width))
    write_recv_table(*moves, place_ref[0], slots_ref, table_ref)


def stream_layout(moves, place, slots, pixels, ivar):
    expos, width, fibres = ivar.shape
    streams = expos * fibres // LANES
    fib_count, pack, per, _ = moves
    laid = shaped((streams * odd(width), LANES))
    return pl.pallas_call(
        functools.partial(layout_kernel, moves),
        in_specs=[in_smem] + [in_vmem] * 3,
        out_specs=[in_vmem] * 3,
        out_shape=[shaped((pack * fibres, fib_count * pack * per), BF16), laid, laid],
        compiler_params=params(),
        cost_estimate=cost(0, 16 * ivar.size),
        name="stream_layout",
    )(place, slots, pixels, ivar)


def solve_kernel(
    wav_count, place_ref, coupling_ref, left_ref, right_ref, pixel_ref, ivar_ref, weight_ref,
    theirs_ref, solved_s, lead_s, rest_s,
):
    streams = left_ref.shape[1]
    expos, half, fibres = weight_ref.shape
    width = 2 * half
    pitch = odd(width)
    middle = half
    coupling = stream_coupling(coupling_ref, expos)
    back = 1.0 / coupling

    def row_at(i):
        return pl.ds(i, streams, stride=pitch)

    def begin(edge_ref, outermost):
        n = jnp.where(place_ref[1] == outermost, 0.0, edge_ref[0]) * back
        return (n, 1.0 - n, jnp.where(place_ref[1] == outermost, 0.0, edge_ref[1]))

    def keep(side, i, state):
        n, d, b = state
        inverse = inverse_of(d + n)
        lead_s[side, i] = d * inverse
        rest_s[side, i] = b * inverse

    unrolled = divisor_of(middle, 24)

    def eliminate(it, states):
        states = list(states)
        for k in range(unrolled):
            i = it * unrolled + k
            for side, row in enumerate((i, width - 1 - i)):
                keep(side, i, states[side])
                states[side] = advance(states[side], ivar_ref[row_at(row), :], pixel_ref[row_at(row), :], back)
        return tuple(rescaled(state) for state in states)

    states = lax.fori_loop(0, middle // unrolled, eliminate, (begin(left_ref, 0), begin(right_ref, wav_count - 1)))
    for side in range(2):
        keep(side, middle, states[side])
    lead, rest = lead_s[0, middle], rest_s[0, middle]
    lead_r, rest_r = lead_s[1, middle], rest_s[1, middle]
    left = (rest + lead * rest_r) / (1.0 - lead * lead_r)
    right = rest_r + lead_r * left
    several = divisor_of(middle, 48)

    def after_both(near, far):
        return far[0] * near[0], far[1] + far[0] * near[1]

    def step(factors, value):
        return factors[1] + factors[0] * value

    def substitute(it, values):
        values = list(values)
        for k in range(0, several, 4):
            for side in range(2):
                rows = [middle - 1 - (it * several + k + m) for m in range(4)]
                one, two, three, four = [(lead_s[side, i], rest_s[side, i]) for i in rows]
                first_two = after_both(one, two)
                all_four = after_both(first_two, after_both(three, four))
                value = values[side]
                third = step(first_two, value)
                solved = [value, step(one, value), third, step(three, third)]
                values[side] = step(all_four, value)
                for i, x in zip(rows, solved):
                    solved_s[row_at(i if side == 0 else width - 1 - i), :] = x
        return tuple(values)

    lax.fori_loop(0, middle // several, substitute, (left, right))

    add_up(theirs_ref, weight_ref, solved_s, coupling_ref, 1 - place_ref[2])


def add_up(out_ref, weight_ref, solved_ref, coupling_ref, which):
    expos, half, fibres = weight_ref.shape
    pitch = odd(2 * half)
    start = which * half
    back = 1.0 / coupling_ref[...]
    unrolled = divisor_of(half // ROWS, 5)

    def body(g, carry):
        for k in range(unrolled):
            row = pl.multiple_of((g * unrolled + k) * ROWS, ROWS)
            for h in range(fibres // LANES):
                total = None
                for e in range(expos):
                    at = pl.ds((h * expos + e) * pitch + start + row, ROWS)
                    term = weight_ref[e, pl.ds(row, ROWS), pl.ds(h * LANES, LANES)] * solved_ref[at, :]
                    total = term if e == 0 else total + term
                out_ref[0, pl.ds(row, ROWS), pl.ds(h * LANES, LANES)] = total * back[:, h * LANES : (h + 1) * LANES]
        return carry

    lax.fori_loop(0, half // ROWS // unrolled, body, 0)


def flux_sums(wav_count, place, coupling, left, right, pixels, ivar, weight):
    expos, half, fibres = weight.shape
    streams = left.shape[1]
    factor_scratch = pltpu.VMEM((2, half + 1, streams, LANES), F32)
    return pl.pallas_call(
        functools.partial(solve_kernel, wav_count),
        in_specs=[in_smem] + [in_vmem] * 6,
        out_specs=[in_vmem, in_vmem],
        out_shape=[shaped((1, half, fibres)), shaped(pixels.shape)],
        scratch_shapes=[factor_scratch, factor_scratch],
        compiler_params=params(),
        cost_estimate=cost(0, 0),
        name="flux_sums",
    )(place, coupling, left, right, pixels, ivar, weight)


def kept_flux_kernel(place_ref, coupling_ref, solved_ref, weight_ref, out_ref):
    add_up(out_ref, weight_ref, solved_ref, coupling_ref, place_ref[2])


def kept_flux(place, coupling, solved, weight):
    expos, half, fibres = weight.shape
    return pl.pallas_call(
        kept_flux_kernel,
        in_specs=[in_smem] + [in_vmem] * 3,
        out_specs=in_vmem,
        out_shape=shaped((1, half, fibres)),
        compiler_params=params(),
        cost_estimate=cost(2 * weight.size, 8 * weight.size),
        name="kept_flux",
    )(place, coupling, solved, weight)


def split_dot(x, table, dims):
    top = x.astype(BF16)
    low = (x - top.astype(F32)).astype(BF16)
    both = lax.dot_general(jnp.concatenate([top, low], 0), table, dims, preferred_element_type=F32)
    return both[: x.shape[0]] + both[x.shape[0] :]


def sort_kernel(pack, scaled, theirs_ref, mine_ref, table_ref, *refs):
    values, rows, _ = mine_ref.shape
    part = rows // pack
    totals = [mine_ref[v] + theirs_ref[v] for v in range(values)]
    if scaled:
        scale_ref, *out_refs = refs
        totals = [t * scale_ref[...] for t in totals]
    else:
        *out_refs, scale_ref = refs
        scale = 1.0 / jnp.maximum(totals[0], 1.0)
        scale_ref[...] = scale
        totals[1] = totals[1] * scale
    x = jnp.concatenate(
        [jnp.concatenate([t[h * part : (h + 1) * part] for h in range(pack)], 1) for t in totals], 0
    )
    moved = split_dot(x, table_ref[...], NT)
    lanes = moved.shape[1] // len(out_refs)
    for d, out_ref in enumerate(out_refs):
        for v in range(values):
            out_ref[v] = moved[v * part : (v + 1) * part, d * lanes : (d + 1) * lanes]


def sort_fibres(theirs, mine, table, pack, pieces, scale=None):
    values, rows, fibres = mine.shape
    lanes = table.shape[0] // pieces
    scaled = scale is not None
    outs = [shaped((values, rows // pack, lanes))] * pieces + ([] if scaled else [shaped((rows, fibres))])
    args = (theirs, mine, table) + ((scale,) if scaled else ())
    return pl.pallas_call(
        functools.partial(sort_kernel, pack, scaled),
        in_specs=[in_vmem] * len(args),
        out_specs=[in_vmem] * len(outs),
        out_shape=outs,
        compiler_params=params(),
        cost_estimate=cost(0, 0),
        name="sort_flux" if scaled else "sort_weights",
    )(*args)


def exchange(pieces, fib_count):
    if len(pieces) == 1:
        return [lax.all_to_all(pieces[0], "fib", split_axis=2, concat_axis=2, tiled=True)]
    arrived = [pieces[0]]
    for d in range(1, fib_count):
        arrived.append(lax.ppermute(pieces[d], "fib", [(i, (i + d) % fib_count) for i in range(fib_count)]))
    return arrived


def landed(refs, table):
    values, part, _ = refs[0].shape
    x = jnp.concatenate(
        [jnp.concatenate([ref[v] for ref in refs], 1) if len(refs) > 1 else refs[0][v] for v in range(values)], 0
    )
    moved = split_dot(x, table, NT)
    return [moved[v * part : (v + 1) * part] for v in range(values)]


def weights_end_kernel(pack, total, place_ref, table_ref, *refs):
    *piece_refs, ivar_ref, res_ref = refs
    weight, band = landed(piece_refs, table_ref[...])
    rows, fibres = ivar_ref.shape
    part = rows // pack
    start = (place_ref[1] * 2 + place_ref[2]) * rows
    for h in range(pack):
        at = slice(h * part, (h + 1) * part)
        cut = slice(h * fibres, (h + 1) * fibres)
        row = start + h * part + lax.broadcasted_iota(jnp.int32, (part, 1), 0)
        w, b = weight[:, cut], band[:, cut]
        before = jnp.where(row == 0, 0.0, b)
        after = jnp.where(row == total - 1, 0.0, b)
        ivar_ref[at, :] = w
        res_ref[0, at, :] = before
        res_ref[1, at, :] = jnp.minimum(w, 1.0) - before - after
        res_ref[2, at, :] = after


def end_weights(place, table, pieces, pack, fibres, total):
    rows = pieces[0].shape[1] * pack
    return pl.pallas_call(
        functools.partial(weights_end_kernel, pack, total),
        in_specs=[in_smem] + [in_vmem] * (1 + len(pieces)),
        out_specs=[in_vmem] * 2,
        out_shape=[shaped((rows, fibres)), shaped((3, rows, fibres))],
        compiler_params=params(),
        cost_estimate=cost(4 * rows * table.size, 6 * rows * fibres * 4),
        name="end_weights",
    )(place, table, *pieces)


def flux_end_kernel(pack, table_ref, *refs):
    *piece_refs, flux_ref = refs
    (flux,) = landed(piece_refs, table_ref[...])
    rows, fibres = flux_ref.shape
    part = rows // pack
    for h in range(pack):
        flux_ref[h * part : (h + 1) * part, :] = flux[:, h * fibres : (h + 1) * fibres]


def end_flux(table, pieces, pack, fibres):
    rows = pieces[0].shape[1] * pack
    return pl.pallas_call(
        functools.partial(flux_end_kernel, pack),
        in_specs=[in_vmem] * (1 + len(pieces)),
        out_specs=in_vmem,
        out_shape=shaped((rows, fibres)),
        compiler_params=params(),
        cost_estimate=cost(2 * rows * table.size, 2 * rows * fibres * 4),
        name="end_flux",
    )(table, *pieces)


def after(value, done):
    return lax.optimization_barrier((value, done))[0]


def per_device(pixels, pixel_ivar, clip_bits, coupling, counts, good_flags, owner_slot):
    expos, width, fibres = pixels.shape
    fib_count, wav_count = lax.axis_size("fib"), lax.axis_size("wav")
    total = width * wav_count
    per = fibres // fib_count
    rows = width // 2
    pack = max(1, LANES // per)
    while pack > 1 and rows % (pack * ROWS):
        pack //= 2
    rel = pack * per == LANES
    pieces = fib_count if rel else 1
    place = jnp.stack([lax.axis_index(axis) for axis in ("fib", "wav", "exp")]).astype(jnp.int32)
    coupling, counts, slots = coupling[None], counts[None], owner_slot[None]
    swap = [(0, 1), (1, 0)]
    moves = (fib_count, pack, per, rel)

    theirs, weight_t, send_table, slots, coupling, counts, good, bits, ivar = sent_weights(
        moves, wav_count, place, slots, coupling, counts, good_flags, clip_bits, pixel_ivar
    )
    arriving = lax.ppermute(theirs, "exp", swap)
    mine, weight_m, up, down = kept_weights(
        wav_count, place, coupling, counts, good, pixels, ivar, bits
    )
    *sorted_pieces, scale = sort_fibres(arriving, mine, send_table, pack, pieces)
    weight_pieces = exchange(sorted_pieces, fib_count)

    up, down = after((up, down), scale)
    upward = [(i, (i + 1) % wav_count) for i in range(wav_count)]
    left = lax.ppermute(up, "wav", upward)
    right = lax.ppermute(down, "wav", [(j, i) for i, j in upward])
    recv_table, pixel_s, ivar_s = stream_layout(moves, after(place, scale), slots, pixels, ivar)
    theirs, solved = flux_sums(wav_count, place, coupling, left, right, pixel_s, ivar_s, weight_t)
    if rel:
        theirs = after(theirs, weight_pieces[1:-1])
    arriving = lax.ppermute(theirs, "exp", swap)
    mine = kept_flux(after(place, theirs), coupling, solved, weight_m)
    flux_pieces = exchange(sort_fibres(arriving, mine, send_table, pack, pieces, scale), fib_count)

    ivar, res = end_weights(place, recv_table, weight_pieces, pack, fibres, total)
    flux = end_flux(recv_table, flux_pieces, pack, fibres)
    return (flux, ivar, res)


def solution(mesh):
    return jax.shard_map(
        per_device,
        mesh=mesh,
        in_specs=(
            P("exp", "wav", "fib"),
            P("exp", "wav", "fib"),
            P("exp", "wav", "fib"),
            P("fib"),
            P("fib"),
            P("exp", "fib"),
            P(),
        ),
        out_specs=(
            P(("wav", "exp"), "fib"),
            P(("wav", "exp"), "fib"),
            P(None, ("wav", "exp"), "fib"),
        ),
        check_vma=False,
    )
```

```python
import functools

import jax
import jax.numpy as jnp
from jax import lax
from jax.experimental import pallas as pl
from jax.experimental.pallas import tpu as pltpu
from jax.sharding import PartitionSpec as P

HALO = 50
BITS = 15
LANES = 128
ROWS = 8
GROUP = 120
VMEM_BYTES = 32 * 1024 * 1024
F32 = jnp.float32
BF16 = jnp.bfloat16
NT = (((1,), (1,)), ((), ()))

in_vmem = pl.BlockSpec(memory_space=pltpu.VMEM)
in_smem = pl.BlockSpec(memory_space=pltpu.SMEM)
in_hbm = pl.BlockSpec(memory_space=pltpu.HBM)


def params():
    return pltpu.CompilerParams(vmem_limit_bytes=VMEM_BYTES)


def cost(flops, moved):
    return pl.CostEstimate(flops=int(flops), bytes_accessed=int(moved), transcendentals=0)


def held_in_hbm(*arrays):
    return [pltpu.with_memory_space_constraint(array, pltpu.HBM) for array in arrays]


def shaped(shape, dtype=F32):
    return jax.ShapeDtypeStruct(shape, dtype)


def usable_rows(place_ref, counts_ref, good_ref):
    count = good_ref.shape[0]
    return [
        good_ref[e : e + 1, :].astype(F32)
        * jnp.where(place_ref[2] * count + e < counts_ref[...], 1.0, 0.0)
        for e in range(count)
    ]


def tile_bits(tile):
    first, last = (ROWS * tile) // BITS, (ROWS * tile + ROWS - 1) // BITS
    split = BITS * last - ROWS * tile
    row = lax.broadcasted_iota(jnp.int32, (ROWS, 1), 0)
    word = jnp.where(row >= split, last, first)
    return first, last, split, jnp.left_shift(1, ROWS * tile + row - BITS * word)


def tile_words(words, tile):
    first, last, split, mask = tile_bits(tile)
    picked = words[first : first + 1, :]
    if last != first:
        row = lax.broadcasted_iota(jnp.int32, (ROWS, 1), 0)
        picked = jnp.where(row >= split, words[last : last + 1, :], picked)
    return (picked & mask) != 0


def in_flight(pairs, sems, at=0):
    copies = [pltpu.make_async_copy(source, target, sems.at[at + i]) for i, (source, target) in enumerate(pairs)]
    for copy in copies:
        copy.start()
    return copies


def inverse_of(x):
    guess = pl.reciprocal(x, approx=True)
    return guess * (2.0 - x * guess)


def advance(state, ivar, pixel, back_coupling):
    n, d, b = state
    ratio = ivar * back_coupling
    next_d = d + n
    return (n * (1.0 + ratio) + ratio * d, next_d, b + (ivar * pixel) * next_d)


def rescaled(state):
    scale = inverse_of(state[1])
    return tuple(part * scale for part in state)


def odd(rows):
    return rows + 1 - rows % 2


def divisor_of(size, most):
    return max(k for k in range(1, most + 1) if size % k == 0)


def owners(slots_ref, fib_count, fibres):
    rows = [slots_ref[:, s * fibres : (s + 1) * fibres].astype(F32) for s in range(fib_count)]
    sources = -(-fib_count // ROWS) * ROWS
    if sources > fib_count:
        rows.append(jnp.full((sources - fib_count, fibres), -1.0, F32))
    slots = jnp.concatenate(rows, 0)
    owner = jnp.floor((slots + 0.5) * (1.0 / fibres))
    return owner, slots - owner * fibres


def earlier_fibres(fibres):
    row = lax.broadcasted_iota(jnp.int32, (fibres, fibres), 0)
    col = lax.broadcasted_iota(jnp.int32, (fibres, fibres), 1)
    return (row < col).astype(F32).astype(BF16)


def write_send_table(fib_count, pack, per, rel, me, slots_ref, table_ref):
    fibres = table_ref.shape[1] // pack
    lanes = pack * per
    owner, _ = owners(slots_ref, fib_count, fibres)
    source = lax.broadcasted_iota(jnp.int32, owner.shape, 0)
    my_owner = jnp.sum(jnp.where(source == me, owner, 0.0), axis=0, keepdims=True).astype(jnp.int32)
    to_owner = (source == my_owner).astype(F32)
    counted = jnp.dot(to_owner.astype(BF16), earlier_fibres(fibres), preferred_element_type=F32)
    rank = jnp.sum(to_owner * counted, axis=0, keepdims=True).astype(jnp.int32)
    target = my_owner
    if rel:
        target = jnp.where(my_owner >= me, my_owner - me, my_owner - me + fib_count)
    base = target * lanes + rank
    place_of = jnp.concatenate([base + h * per for h in range(pack)], 1)
    row = lax.broadcasted_iota(jnp.int32, table_ref.shape, 0)
    table_ref[...] = (row == place_of).astype(F32).astype(BF16)


def write_recv_table(fib_count, pack, per, rel, me, slots_ref, table_ref):
    fibres = table_ref.shape[0] // pack
    lanes = pack * per
    total_lanes = fib_count * lanes
    owner, column = owners(slots_ref, fib_count, fibres)
    source = lax.broadcasted_iota(jnp.int32, owner.shape, 0)
    mine = (owner == me.astype(F32)).astype(F32)
    rank_in = jnp.dot(mine.astype(BF16), earlier_fibres(fibres), preferred_element_type=F32).astype(jnp.int32)
    order = source
    if rel:
        order = jnp.where(me >= source, me - source, me - source + fib_count)
    arrival = jnp.where(mine > 0.0, order * lanes + rank_in, -total_lanes)
    tall = lax.broadcasted_iota(jnp.int32, (total_lanes, fibres), 0)
    landing = jnp.zeros((ROWS, total_lanes), F32)
    for s in range(fib_count):
        hit = tall == arrival[s : s + 1, :]
        for h in range(1, pack):
            hit = hit | (tall == arrival[s : s + 1, :] + h * per)
        values = jnp.broadcast_to(column[s : s + 1, :], (ROWS, fibres)).astype(BF16)
        landing = landing + lax.dot_general(
            values, hit.astype(F32).astype(BF16), NT, preferred_element_type=F32
        )
    lane = lax.broadcasted_iota(jnp.int32, (1, total_lanes), 1)
    landing = landing[0:1, :].astype(jnp.int32)
    for h in range(1, pack):
        inside = (lane % lanes >= h * per) & (lane % lanes < (h + 1) * per)
        landing = jnp.where(inside, landing + h * fibres, landing)
    row = lax.broadcasted_iota(jnp.int32, table_ref.shape, 0)
    table_ref[...] = (row == landing).astype(F32).astype(BF16)


def stream_coupling(coupling_ref, expos):
    coupling = coupling_ref[...]
    blocks = coupling.shape[1] // LANES
    return jnp.concatenate(
        [jnp.broadcast_to(coupling[:, h * LANES : (h + 1) * LANES], (expos, LANES)) for h in range(blocks)], 0
    )


def weight_tile(coupling, usable, words, ivars, within, scale_row):
    links = scale_row * coupling
    weights = []
    weight_sum = band_sum = None
    for e, ivar in enumerate(ivars):
        weight = jnp.where(tile_words(words[e], within), ivar * usable[e], 0.0)
        band = weight * inverse_of(ivar + links)
        weights.append(weight)
        weight_sum = weight if e == 0 else weight_sum + weight
        band_sum = band if e == 0 else band_sum + band
    return weights, weight_sum, band_sum * coupling


def write_weights(place_ref, wav_count, which, coupling_v, counts_v, good_v, ivar_of, words_of, sums_ref, weight_ref, beside):
    expos, half, _ = weight_ref.shape
    coupling = coupling_v[...]
    usable = usable_rows(place_ref, counts_v, good_v)
    start = place_ref[1] * (2 * half) + which * half
    tiles = half // ROWS
    tiles_in_group = GROUP // ROWS
    for tile in range(tiles):
        beside(tile, tiles)
        group, within = divmod(tile, tiles_in_group)
        scale_row = 4.0
        if tile in (0, tiles - 1):
            row = start + ROWS * tile + lax.broadcasted_iota(jnp.int32, (ROWS, 1), 0)
            scale_row = jnp.where((row == 0) | (row == wav_count * 2 * half - 1), 2.0, 4.0)
        at = slice(ROWS * tile, ROWS * (tile + 1))
        weights, weight_sum, band_sum = weight_tile(
            coupling,
            usable,
            [words_of(e, group) for e in range(expos)],
            [ivar_of(e, tile) for e in range(expos)],
            within,
            scale_row,
        )
        for e in range(expos):
            weight_ref[e, at, :] = weights[e]
        sums_ref[0, at, :] = weight_sum
        sums_ref[1, at, :] = band_sum


def sent_kernel(
    moves, wav_count, place_ref, slots_ref, coupling_ref, counts_ref, good_ref, bits_ref, ivar_ref,
    sums_ref, weight_ref, table_ref, slots_v, coupling_v, counts_v, good_v, bits_v, ivar_v, sems,
):
    expos, width, _ = ivar_ref.shape
    half = width // 2
    which = 1 - place_ref[2]
    words = GROUP // BITS

    def part(source, target, first):
        at = pl.ds(pl.multiple_of(first, ROWS), GROUP)
        return source.at[:, at, :], target.at[:, at, :]

    waits = in_flight(
        [
            (slots_ref, slots_v),
            (coupling_ref, coupling_v),
            (counts_ref, counts_v),
            (good_ref, good_v),
            (bits_ref, bits_v),
        ]
        + [part(ivar_ref, ivar_v, which * half + g) for g in range(0, half, GROUP)]
        + [part(ivar_ref, ivar_v, (1 - which) * half + g) for g in range(0, half, GROUP)],
        sems,
    )
    waits[0].wait()
    write_send_table(*moves, place_ref[0], slots_v, table_ref)
    for wait in waits[1:5]:
        wait.wait()

    def arrive(tile, tiles):
        if ROWS * tile % GROUP == 0:
            waits[5 + ROWS * tile // GROUP].wait()

    write_weights(
        place_ref, wav_count, which, coupling_v, counts_v, good_v,
        lambda e, tile: ivar_v[e, pl.ds(pl.multiple_of(which * half + ROWS * tile, ROWS), ROWS), :],
        lambda e, group: bits_v[e, pl.ds(pl.multiple_of(which * (half // BITS) + words * group, words), words), :],
        sums_ref, weight_ref, arrive,
    )
    for wait in waits[5 + half // GROUP :]:
        wait.wait()


def sent_weights(moves, wav_count, place, slots, coupling, counts, good, bits, ivar):
    expos, width, fibres = ivar.shape
    half = width // 2
    fib_count, pack, per, _ = moves
    inputs = (slots, coupling, counts, good, bits, ivar)
    return pl.pallas_call(
        functools.partial(sent_kernel, moves, wav_count),
        in_specs=[in_smem] + [in_hbm] * 6,
        out_specs=[in_vmem] * 9,
        out_shape=[
            shaped((2, half, fibres)),
            shaped((expos, half, fibres)),
            shaped((fib_count * pack * per, pack * fibres), BF16),
        ]
        + [shaped(x.shape, x.dtype) for x in inputs],
        scratch_shapes=[pltpu.SemaphoreType.DMA((5 + width // GROUP,))],
        compiler_params=params(),
        cost_estimate=cost(20 * ivar.size, 6 * ivar.size),
        name="sent_weights",
    )(place, *held_in_hbm(*inputs))


def lay_out(source_ref, target_ref, pieces, pitch):
    expos, _, fibres = source_ref.shape
    for h in range(fibres // LANES):
        for e in range(expos):
            for first, length, at in pieces:
                target_ref[pl.ds((h * expos + e) * pitch + at, length), :] = source_ref[
                    e, pl.ds(first, length), pl.ds(h * LANES, LANES)
                ]


def kept_kernel(
    wav_count, place_ref, coupling_ref, counts_ref, good_ref, pixels_ref, ivar_ref, bits_ref,
    sums_ref, weight_ref, up_ref, down_ref, ivar_s, pixel_s,
):
    expos, width, fibres = ivar_ref.shape
    half = width // 2
    streams = expos * fibres // LANES
    count = -(-HALO // ROWS) * ROWS
    pitch = odd(2 * count)
    which = place_ref[2]
    words = GROUP // BITS
    edges = [(0, count, 0), (width - count, count, count)]
    lay_out(ivar_ref, ivar_s, edges, pitch)
    lay_out(pixels_ref, pixel_s, edges, pitch)
    coupling = stream_coupling(coupling_ref, expos)
    back = 1.0 / coupling
    zero = jnp.zeros((streams, LANES), F32)
    states = [(zero, zero + 1.0, zero), (zero, zero + 1.0, zero)]

    def eliminate(tile, tiles):
        for i in range(HALO * tile // tiles, HALO * (tile + 1) // tiles):
            for side, row in enumerate((2 * count - HALO + i, HALO - 1 - i)):
                at = pl.ds(row, streams, stride=pitch)
                states[side] = advance(states[side], ivar_s[at, :], pixel_s[at, :], back)
                if i % 24 == 23:
                    states[side] = rescaled(states[side])

    write_weights(
        place_ref, wav_count, which, coupling_ref, counts_ref, good_ref,
        lambda e, tile: ivar_ref[e, pl.ds(pl.multiple_of(which * half + ROWS * tile, ROWS), ROWS), :],
        lambda e, group: bits_ref[e, pl.ds(pl.multiple_of(which * (half // BITS) + words * group, words), words), :],
        sums_ref, weight_ref, eliminate,
    )
    for (n, d, b), out_ref in zip(states, (up_ref, down_ref)):
        scale = 1.0 / (d + n)
        out_ref[0] = coupling * (n * scale)
        out_ref[1] = b * scale


def kept_weights(wav_count, place, coupling, counts, good, pixels, ivar, bits):
    expos, width, fibres = ivar.shape
    half = width // 2
    streams = expos * fibres // LANES
    count = -(-HALO // ROWS) * ROWS
    edge = shaped((2, streams, LANES))
    edge_scratch = pltpu.VMEM((streams * odd(2 * count), LANES), F32)
    return pl.pallas_call(
        functools.partial(kept_kernel, wav_count),
        in_specs=[in_smem] + [in_vmem] * 6,
        out_specs=[in_vmem] * 4,
        out_shape=[shaped((2, half, fibres)), shaped((expos, half, fibres)), edge, edge],
        scratch_shapes=[edge_scratch, edge_scratch],
        compiler_params=params(),
        cost_estimate=cost(20 * ivar.size, 6 * ivar.size),
        name="kept_weights",
    )(place, coupling, counts, good, pixels, ivar, bits)


def layout_kernel(moves, place_ref, slots_ref, pixels_ref, ivar_ref, table_ref, pixel_out, ivar_out):
    width = ivar_ref.shape[1]
    lay_out(ivar_ref, ivar_out, [(0, width, 0)], odd(width))
    lay_out(pixels_ref, pixel_out, [(0, width, 0)], odd(width))
    write_recv_table(*moves, place_ref[0], slots_ref, table_ref)


def stream_layout(moves, place, slots, pixels, ivar):
    expos, width, fibres = ivar.shape
    streams = expos * fibres // LANES
    fib_count, pack, per, _ = moves
    laid = shaped((streams * odd(width), LANES))
    return pl.pallas_call(
        functools.partial(layout_kernel, moves),
        in_specs=[in_smem] + [in_vmem] * 3,
        out_specs=[in_vmem] * 3,
        out_shape=[shaped((pack * fibres, fib_count * pack * per), BF16), laid, laid],
        compiler_params=params(),
        cost_estimate=cost(0, 16 * ivar.size),
        name="stream_layout",
    )(place, slots, pixels, ivar)


def solve_kernel(
    wav_count, place_ref, coupling_ref, left_ref, right_ref, pixel_ref, ivar_ref, weight_ref,
    theirs_ref, solved_s, lead_s, rest_s,
):
    streams = left_ref.shape[1]
    expos, half, fibres = weight_ref.shape
    width = 2 * half
    pitch = odd(width)
    middle = half
    coupling = stream_coupling(coupling_ref, expos)
    back = 1.0 / coupling

    def row_at(i):
        return pl.ds(i, streams, stride=pitch)

    def begin(edge_ref, outermost):
        n = jnp.where(place_ref[1] == outermost, 0.0, edge_ref[0]) * back
        return (n, 1.0 - n, jnp.where(place_ref[1] == outermost, 0.0, edge_ref[1]))

    def keep(side, i, state):
        n, d, b = state
        inverse = inverse_of(d + n)
        lead_s[side, i] = d * inverse
        rest_s[side, i] = b * inverse

    unrolled = divisor_of(middle, 24)

    def eliminate(it, states):
        states = list(states)
        for k in range(unrolled):
            i = it * unrolled + k
            for side, row in enumerate((i, width - 1 - i)):
                keep(side, i, states[side])
                states[side] = advance(states[side], ivar_ref[row_at(row), :], pixel_ref[row_at(row), :], back)
        return tuple(rescaled(state) for state in states)

    states = lax.fori_loop(0, middle // unrolled, eliminate, (begin(left_ref, 0), begin(right_ref, wav_count - 1)))
    for side in range(2):
        keep(side, middle, states[side])
    lead, rest = lead_s[0, middle], rest_s[0, middle]
    lead_r, rest_r = lead_s[1, middle], rest_s[1, middle]
    left = (rest + lead * rest_r) / (1.0 - lead * lead_r)
    right = rest_r + lead_r * left
    several = divisor_of(middle, 48)

    def after_both(near, far):
        return far[0] * near[0], far[1] + far[0] * near[1]

    def step(factors, value):
        return factors[1] + factors[0] * value

    def substitute(it, values):
        values = list(values)
        for k in range(0, several, 4):
            for side in range(2):
                rows = [middle - 1 - (it * several + k + m) for m in range(4)]
                one, two, three, four = [(lead_s[side, i], rest_s[side, i]) for i in rows]
                first_two = after_both(one, two)
                all_four = after_both(first_two, after_both(three, four))
                value = values[side]
                third = step(first_two, value)
                solved = [value, step(one, value), third, step(three, third)]
                values[side] = step(all_four, value)
                for i, x in zip(rows, solved):
                    solved_s[row_at(i if side == 0 else width - 1 - i), :] = x
        return tuple(values)

    lax.fori_loop(0, middle // several, substitute, (left, right))

    add_up(theirs_ref, weight_ref, solved_s, coupling_ref, 1 - place_ref[2])


def add_up(out_ref, weight_ref, solved_ref, coupling_ref, which):
    expos, half, fibres = weight_ref.shape
    pitch = odd(2 * half)
    start = which * half
    back = 1.0 / coupling_ref[...]
    unrolled = divisor_of(half // ROWS, 5)

    def body(g, carry):
        for k in range(unrolled):
            row = pl.multiple_of((g * unrolled + k) * ROWS, ROWS)
            for h in range(fibres // LANES):
                total = None
                for e in range(expos):
                    at = pl.ds((h * expos + e) * pitch + start + row, ROWS)
                    term = weight_ref[e, pl.ds(row, ROWS), pl.ds(h * LANES, LANES)] * solved_ref[at, :]
                    total = term if e == 0 else total + term
                out_ref[0, pl.ds(row, ROWS), pl.ds(h * LANES, LANES)] = total * back[:, h * LANES : (h + 1) * LANES]
        return carry

    lax.fori_loop(0, half // ROWS // unrolled, body, 0)


def flux_sums(wav_count, place, coupling, left, right, pixels, ivar, weight):
    expos, half, fibres = weight.shape
    streams = left.shape[1]
    factor_scratch = pltpu.VMEM((2, half + 1, streams, LANES), F32)
    return pl.pallas_call(
        functools.partial(solve_kernel, wav_count),
        in_specs=[in_smem] + [in_vmem] * 6,
        out_specs=[in_vmem, in_vmem],
        out_shape=[shaped((1, half, fibres)), shaped(pixels.shape)],
        scratch_shapes=[factor_scratch, factor_scratch],
        compiler_params=params(),
        cost_estimate=cost(0, 0),
        name="flux_sums",
    )(place, coupling, left, right, pixels, ivar, weight)


def kept_flux_kernel(place_ref, coupling_ref, solved_ref, weight_ref, out_ref):
    add_up(out_ref, weight_ref, solved_ref, coupling_ref, place_ref[2])


def kept_flux(place, coupling, solved, weight):
    expos, half, fibres = weight.shape
    return pl.pallas_call(
        kept_flux_kernel,
        in_specs=[in_smem] + [in_vmem] * 3,
        out_specs=in_vmem,
        out_shape=shaped((1, half, fibres)),
        compiler_params=params(),
        cost_estimate=cost(2 * weight.size, 8 * weight.size),
        name="kept_flux",
    )(place, coupling, solved, weight)


def split_dot(x, table, dims):
    top = x.astype(BF16)
    low = (x - top.astype(F32)).astype(BF16)
    both = lax.dot_general(jnp.concatenate([top, low], 0), table, dims, preferred_element_type=F32)
    return both[: x.shape[0]] + both[x.shape[0] :]


def sort_kernel(pack, scaled, theirs_ref, mine_ref, table_ref, *refs):
    values, rows, _ = mine_ref.shape
    part = rows // pack
    totals = [mine_ref[v] + theirs_ref[v] for v in range(values)]
    if scaled:
        scale_ref, _, *out_refs = refs
        totals = [t * scale_ref[...] for t in totals]
    else:
        *out_refs, scale_ref = refs
        scale = 1.0 / jnp.maximum(totals[0], 1.0)
        scale_ref[...] = scale
        totals[1] = totals[1] * scale
    x = jnp.concatenate(
        [jnp.concatenate([t[h * part : (h + 1) * part] for h in range(pack)], 1) for t in totals], 0
    )
    moved = split_dot(x, table_ref[...], NT)
    lanes = moved.shape[1] // len(out_refs)
    for d, out_ref in enumerate(out_refs):
        for v in range(values):
            out_ref[v] = moved[v * part : (v + 1) * part, d * lanes : (d + 1) * lanes]


def sort_fibres(theirs, mine, table, pack, pieces, scale=None, ahead=None):
    values, rows, fibres = mine.shape
    lanes = table.shape[0] // pieces
    scaled = scale is not None
    outs = [shaped((values, rows // pack, lanes))] * pieces + ([] if scaled else [shaped((rows, fibres))])
    args = (theirs, mine, table) + ((scale, ahead) if scaled else ())
    return pl.pallas_call(
        functools.partial(sort_kernel, pack, scaled),
        in_specs=[in_vmem] * len(args),
        out_specs=[in_vmem] * len(outs),
        out_shape=outs,
        compiler_params=params(),
        cost_estimate=cost(0, 0),
        name="sort_flux" if scaled else "sort_weights",
    )(*args)


def exchange(pieces, fib_count):
    if len(pieces) == 1:
        return [lax.all_to_all(pieces[0], "fib", split_axis=2, concat_axis=2, tiled=True)]
    arrived = [pieces[0]]
    for d in range(1, fib_count):
        arrived.append(lax.ppermute(pieces[d], "fib", [(i, (i + d) % fib_count) for i in range(fib_count)]))
    return arrived


def landed(refs, table):
    values, part, _ = refs[0].shape
    x = jnp.concatenate(
        [jnp.concatenate([ref[v] for ref in refs], 1) if len(refs) > 1 else refs[0][v] for v in range(values)], 0
    )
    moved = split_dot(x, table, NT)
    return [moved[v * part : (v + 1) * part] for v in range(values)]


def weights_end_kernel(pack, total, place_ref, table_ref, *refs):
    *piece_refs, ivar_ref, res_ref = refs
    weight, band = landed(piece_refs, table_ref[...])
    rows, fibres = ivar_ref.shape
    part = rows // pack
    start = (place_ref[1] * 2 + place_ref[2]) * rows
    for h in range(pack):
        at = slice(h * part, (h + 1) * part)
        cut = slice(h * fibres, (h + 1) * fibres)
        row = start + h * part + lax.broadcasted_iota(jnp.int32, (part, 1), 0)
        w, b = weight[:, cut], band[:, cut]
        before = jnp.where(row == 0, 0.0, b)
        after = jnp.where(row == total - 1, 0.0, b)
        ivar_ref[at, :] = w
        res_ref[0, at, :] = before
        res_ref[1, at, :] = jnp.minimum(w, 1.0) - before - after
        res_ref[2, at, :] = after


def end_weights(place, table, pieces, pack, fibres, total):
    rows = pieces[0].shape[1] * pack
    return pl.pallas_call(
        functools.partial(weights_end_kernel, pack, total),
        in_specs=[in_smem] + [in_vmem] * (1 + len(pieces)),
        out_specs=[in_vmem] * 2,
        out_shape=[shaped((rows, fibres)), shaped((3, rows, fibres))],
        compiler_params=params(),
        cost_estimate=cost(4 * rows * table.size, 6 * rows * fibres * 4),
        name="end_weights",
    )(place, table, *pieces)


def flux_end_kernel(pack, table_ref, *refs):
    *piece_refs, flux_ref = refs
    (flux,) = landed(piece_refs, table_ref[...])
    rows, fibres = flux_ref.shape
    part = rows // pack
    for h in range(pack):
        flux_ref[h * part : (h + 1) * part, :] = flux[:, h * fibres : (h + 1) * fibres]


def end_flux(table, pieces, pack, fibres):
    rows = pieces[0].shape[1] * pack
    return pl.pallas_call(
        functools.partial(flux_end_kernel, pack),
        in_specs=[in_vmem] * (1 + len(pieces)),
        out_specs=in_vmem,
        out_shape=shaped((rows, fibres)),
        compiler_params=params(),
        cost_estimate=cost(2 * rows * table.size, 2 * rows * fibres * 4),
        name="end_flux",
    )(table, *pieces)


def after(value, done):
    return lax.optimization_barrier((value, done))[0]


def per_device(pixels, pixel_ivar, clip_bits, coupling, counts, good_flags, owner_slot):
    expos, width, fibres = pixels.shape
    fib_count, wav_count = lax.axis_size("fib"), lax.axis_size("wav")
    total = width * wav_count
    per = fibres // fib_count
    rows = width // 2
    pack = max(1, LANES // per)
    while pack > 1 and rows % (pack * ROWS):
        pack //= 2
    rel = pack * per == LANES
    pieces = fib_count if rel else 1
    place = jnp.stack([lax.axis_index(axis) for axis in ("fib", "wav", "exp")]).astype(jnp.int32)
    coupling, counts, slots = coupling[None], counts[None], owner_slot[None]
    swap = [(0, 1), (1, 0)]
    moves = (fib_count, pack, per, rel)

    theirs, weight_t, send_table, slots, coupling, counts, good, bits, ivar = sent_weights(
        moves, wav_count, place, slots, coupling, counts, good_flags, clip_bits, pixel_ivar
    )
    arriving = lax.ppermute(theirs, "exp", swap)
    mine, weight_m, up, down = kept_weights(
        wav_count, place, coupling, counts, good, pixels, ivar, bits
    )
    upward = [(i, (i + 1) % wav_count) for i in range(wav_count)]
    left = lax.ppermute(up, "wav", upward)
    right = lax.ppermute(down, "wav", [(j, i) for i, j in upward])
    *sorted_pieces, scale = sort_fibres(arriving, mine, send_table, pack, pieces)
    weight_pieces = exchange(sorted_pieces, fib_count)

    recv_table, pixel_s, ivar_s = stream_layout(moves, after(place, scale), slots, pixels, ivar)
    theirs, solved = flux_sums(wav_count, place, coupling, left, right, pixel_s, ivar_s, weight_t)
    ahead = sum(piece[0, :ROWS, :] for piece in weight_pieces[1:] or weight_pieces)
    arriving = lax.ppermute(theirs, "exp", swap)
    mine = kept_flux(after(place, theirs), coupling, solved, weight_m)
    flux_pieces = exchange(sort_fibres(arriving, mine, send_table, pack, pieces, scale, ahead), fib_count)

    ivar, res = end_weights(place, recv_table, weight_pieces, pack, fibres, total)
    flux = end_flux(recv_table, flux_pieces, pack, fibres)
    return (flux, ivar, res)


def solution(mesh):
    return jax.shard_map(
        per_device,
        mesh=mesh,
        in_specs=(
            P("exp", "wav", "fib"),
            P("exp", "wav", "fib"),
            P("exp", "wav", "fib"),
            P("fib"),
            P("fib"),
            P("exp", "fib"),
            P(),
        ),
        out_specs=(
            P(("wav", "exp"), "fib"),
            P(("wav", "exp"), "fib"),
            P(None, ("wav", "exp"), "fib"),
        ),
        check_vma=False,
    )
```

```python
import functools

import jax
import jax.numpy as jnp
from jax import lax
from jax.experimental import pallas as pl
from jax.experimental.pallas import tpu as pltpu
from jax.sharding import PartitionSpec as P

HALO = 50
BITS = 15
LANES = 128
ROWS = 8
GROUP = 120
VMEM_BYTES = 32 * 1024 * 1024
F32 = jnp.float32
BF16 = jnp.bfloat16
NT = (((1,), (1,)), ((), ()))

in_vmem = pl.BlockSpec(memory_space=pltpu.VMEM)
in_smem = pl.BlockSpec(memory_space=pltpu.SMEM)
in_hbm = pl.BlockSpec(memory_space=pltpu.HBM)


def params():
    return pltpu.CompilerParams(vmem_limit_bytes=VMEM_BYTES)


def cost(flops, moved):
    return pl.CostEstimate(flops=int(flops), bytes_accessed=int(moved), transcendentals=0)


def held_in_hbm(*arrays):
    return [pltpu.with_memory_space_constraint(array, pltpu.HBM) for array in arrays]


def shaped(shape, dtype=F32):
    return jax.ShapeDtypeStruct(shape, dtype)


def usable_rows(place_ref, counts_ref, good_ref):
    count = good_ref.shape[0]
    return [
        good_ref[e : e + 1, :].astype(F32)
        * jnp.where(place_ref[2] * count + e < counts_ref[...], 1.0, 0.0)
        for e in range(count)
    ]


def tile_bits(tile):
    first, last = (ROWS * tile) // BITS, (ROWS * tile + ROWS - 1) // BITS
    split = BITS * last - ROWS * tile
    row = lax.broadcasted_iota(jnp.int32, (ROWS, 1), 0)
    word = jnp.where(row >= split, last, first)
    return first, last, split, jnp.left_shift(1, ROWS * tile + row - BITS * word)


def tile_words(words, tile):
    first, last, split, mask = tile_bits(tile)
    picked = words[first : first + 1, :]
    if last != first:
        row = lax.broadcasted_iota(jnp.int32, (ROWS, 1), 0)
        picked = jnp.where(row >= split, words[last : last + 1, :], picked)
    return (picked & mask) != 0


def in_flight(pairs, sems, at=0):
    copies = [pltpu.make_async_copy(source, target, sems.at[at + i]) for i, (source, target) in enumerate(pairs)]
    for copy in copies:
        copy.start()
    return copies


def inverse_of(x):
    guess = pl.reciprocal(x, approx=True)
    return guess * (2.0 - x * guess)


def advance(state, ivar, pixel, back_coupling):
    n, d, b = state
    ratio = ivar * back_coupling
    next_d = d + n
    return (n * (1.0 + ratio) + ratio * d, next_d, b + (ivar * pixel) * next_d)


def rescaled(state):
    scale = inverse_of(state[1])
    return tuple(part * scale for part in state)


def odd(rows):
    return rows + 1 - rows % 2


def divisor_of(size, most):
    return max(k for k in range(1, most + 1) if size % k == 0)


def owners(slots_ref, fib_count, fibres):
    rows = [slots_ref[:, s * fibres : (s + 1) * fibres].astype(F32) for s in range(fib_count)]
    sources = -(-fib_count // ROWS) * ROWS
    if sources > fib_count:
        rows.append(jnp.full((sources - fib_count, fibres), -1.0, F32))
    slots = jnp.concatenate(rows, 0)
    owner = jnp.floor((slots + 0.5) * (1.0 / fibres))
    return owner, slots - owner * fibres


def earlier_fibres(fibres):
    row = lax.broadcasted_iota(jnp.int32, (fibres, fibres), 0)
    col = lax.broadcasted_iota(jnp.int32, (fibres, fibres), 1)
    return (row < col).astype(F32).astype(BF16)


def write_send_table(fib_count, pack, per, rel, me, slots_ref, table_ref):
    fibres = table_ref.shape[1] // pack
    lanes = pack * per
    owner, _ = owners(slots_ref, fib_count, fibres)
    source = lax.broadcasted_iota(jnp.int32, owner.shape, 0)
    my_owner = jnp.sum(jnp.where(source == me, owner, 0.0), axis=0, keepdims=True).astype(jnp.int32)
    to_owner = (source == my_owner).astype(F32)
    counted = jnp.dot(to_owner.astype(BF16), earlier_fibres(fibres), preferred_element_type=F32)
    rank = jnp.sum(to_owner * counted, axis=0, keepdims=True).astype(jnp.int32)
    target = my_owner
    if rel:
        target = jnp.where(my_owner >= me, my_owner - me, my_owner - me + fib_count)
    base = target * lanes + rank
    place_of = jnp.concatenate([base + h * per for h in range(pack)], 1)
    row = lax.broadcasted_iota(jnp.int32, table_ref.shape, 0)
    table_ref[...] = (row == place_of).astype(F32).astype(BF16)


def write_recv_table(fib_count, pack, per, rel, me, slots_ref, table_ref):
    fibres = table_ref.shape[0] // pack
    lanes = pack * per
    total_lanes = fib_count * lanes
    owner, column = owners(slots_ref, fib_count, fibres)
    source = lax.broadcasted_iota(jnp.int32, owner.shape, 0)
    mine = (owner == me.astype(F32)).astype(F32)
    rank_in = jnp.dot(mine.astype(BF16), earlier_fibres(fibres), preferred_element_type=F32).astype(jnp.int32)
    order = source
    if rel:
        order = jnp.where(me >= source, me - source, me - source + fib_count)
    arrival = jnp.where(mine > 0.0, order * lanes + rank_in, -total_lanes)
    tall = lax.broadcasted_iota(jnp.int32, (total_lanes, fibres), 0)
    landing = jnp.zeros((ROWS, total_lanes), F32)
    for s in range(fib_count):
        hit = tall == arrival[s : s + 1, :]
        for h in range(1, pack):
            hit = hit | (tall == arrival[s : s + 1, :] + h * per)
        values = jnp.broadcast_to(column[s : s + 1, :], (ROWS, fibres)).astype(BF16)
        landing = landing + lax.dot_general(
            values, hit.astype(F32).astype(BF16), NT, preferred_element_type=F32
        )
    lane = lax.broadcasted_iota(jnp.int32, (1, total_lanes), 1)
    landing = landing[0:1, :].astype(jnp.int32)
    for h in range(1, pack):
        inside = (lane % lanes >= h * per) & (lane % lanes < (h + 1) * per)
        landing = jnp.where(inside, landing + h * fibres, landing)
    row = lax.broadcasted_iota(jnp.int32, table_ref.shape, 0)
    table_ref[...] = (row == landing).astype(F32).astype(BF16)


def stream_coupling(coupling_ref, expos):
    coupling = coupling_ref[...]
    blocks = coupling.shape[1] // LANES
    return jnp.concatenate(
        [jnp.broadcast_to(coupling[:, h * LANES : (h + 1) * LANES], (expos, LANES)) for h in range(blocks)], 0
    )


def weight_tile(coupling, usable, words, ivars, within, scale_row):
    links = scale_row * coupling
    weights = []
    weight_sum = band_sum = None
    for e, ivar in enumerate(ivars):
        weight = jnp.where(tile_words(words[e], within), ivar * usable[e], 0.0)
        band = weight * inverse_of(ivar + links)
        weights.append(weight)
        weight_sum = weight if e == 0 else weight_sum + weight
        band_sum = band if e == 0 else band_sum + band
    return weights, weight_sum, band_sum * coupling


def write_weights(place_ref, wav_count, which, coupling_v, counts_v, good_v, ivar_of, words_of, sums_ref, weight_ref, beside):
    expos, half, _ = weight_ref.shape
    coupling = coupling_v[...]
    usable = usable_rows(place_ref, counts_v, good_v)
    start = place_ref[1] * (2 * half) + which * half
    tiles = half // ROWS
    tiles_in_group = GROUP // ROWS
    for tile in range(tiles):
        beside(tile, tiles)
        group, within = divmod(tile, tiles_in_group)
        scale_row = 4.0
        if tile in (0, tiles - 1):
            row = start + ROWS * tile + lax.broadcasted_iota(jnp.int32, (ROWS, 1), 0)
            scale_row = jnp.where((row == 0) | (row == wav_count * 2 * half - 1), 2.0, 4.0)
        at = slice(ROWS * tile, ROWS * (tile + 1))
        weights, weight_sum, band_sum = weight_tile(
            coupling,
            usable,
            [words_of(e, group) for e in range(expos)],
            [ivar_of(e, tile) for e in range(expos)],
            within,
            scale_row,
        )
        for e in range(expos):
            weight_ref[e, at, :] = weights[e]
        sums_ref[0, at, :] = weight_sum
        sums_ref[1, at, :] = band_sum


def sent_kernel(
    moves, wav_count, place_ref, slots_ref, coupling_ref, counts_ref, good_ref, bits_ref, ivar_ref,
    sums_ref, weight_ref, table_ref, slots_v, coupling_v, counts_v, good_v, bits_v, ivar_v, sems,
):
    expos, width, _ = ivar_ref.shape
    half = width // 2
    which = 1 - place_ref[2]
    words = GROUP // BITS

    def part(source, target, first):
        at = pl.ds(pl.multiple_of(first, ROWS), GROUP)
        return source.at[:, at, :], target.at[:, at, :]

    waits = in_flight(
        [
            (slots_ref, slots_v),
            (coupling_ref, coupling_v),
            (counts_ref, counts_v),
            (good_ref, good_v),
            (bits_ref, bits_v),
        ]
        + [part(ivar_ref, ivar_v, which * half + g) for g in range(0, half, GROUP)]
        + [part(ivar_ref, ivar_v, (1 - which) * half + g) for g in range(0, half, GROUP)],
        sems,
    )
    waits[0].wait()
    write_send_table(*moves, place_ref[0], slots_v, table_ref)
    for wait in waits[1:5]:
        wait.wait()

    def arrive(tile, tiles):
        if ROWS * tile % GROUP == 0:
            waits[5 + ROWS * tile // GROUP].wait()

    write_weights(
        place_ref, wav_count, which, coupling_v, counts_v, good_v,
        lambda e, tile: ivar_v[e, pl.ds(pl.multiple_of(which * half + ROWS * tile, ROWS), ROWS), :],
        lambda e, group: bits_v[e, pl.ds(pl.multiple_of(which * (half // BITS) + words * group, words), words), :],
        sums_ref, weight_ref, arrive,
    )
    for wait in waits[5 + half // GROUP :]:
        wait.wait()


def sent_weights(moves, wav_count, place, slots, coupling, counts, good, bits, ivar):
    expos, width, fibres = ivar.shape
    half = width // 2
    fib_count, pack, per, _ = moves
    inputs = (slots, coupling, counts, good, bits, ivar)
    return pl.pallas_call(
        functools.partial(sent_kernel, moves, wav_count),
        in_specs=[in_smem] + [in_hbm] * 6,
        out_specs=[in_vmem] * 9,
        out_shape=[
            shaped((2, half, fibres)),
            shaped((expos, half, fibres)),
            shaped((fib_count * pack * per, pack * fibres), BF16),
        ]
        + [shaped(x.shape, x.dtype) for x in inputs],
        scratch_shapes=[pltpu.SemaphoreType.DMA((5 + width // GROUP,))],
        compiler_params=params(),
        cost_estimate=cost(20 * ivar.size, 6 * ivar.size),
        name="sent_weights",
    )(place, *held_in_hbm(*inputs))


def lay_out(source_ref, target_ref, pieces, pitch):
    expos, _, fibres = source_ref.shape
    for h in range(fibres // LANES):
        for e in range(expos):
            for first, length, at in pieces:
                target_ref[pl.ds((h * expos + e) * pitch + at, length), :] = source_ref[
                    e, pl.ds(first, length), pl.ds(h * LANES, LANES)
                ]


def kept_kernel(
    wav_count, place_ref, coupling_ref, counts_ref, good_ref, pixels_ref, ivar_ref, bits_ref,
    sums_ref, weight_ref, up_ref, down_ref, ivar_s, pixel_s,
):
    expos, width, fibres = ivar_ref.shape
    half = width // 2
    streams = expos * fibres // LANES
    count = -(-HALO // ROWS) * ROWS
    pitch = odd(2 * count)
    which = place_ref[2]
    words = GROUP // BITS
    edges = [(0, count, 0), (width - count, count, count)]
    lay_out(ivar_ref, ivar_s, edges, pitch)
    lay_out(pixels_ref, pixel_s, edges, pitch)
    coupling = stream_coupling(coupling_ref, expos)
    back = 1.0 / coupling
    zero = jnp.zeros((streams, LANES), F32)
    states = [(zero, zero + 1.0, zero), (zero, zero + 1.0, zero)]

    def eliminate(tile, tiles):
        for i in range(HALO * tile // tiles, HALO * (tile + 1) // tiles):
            for side, row in enumerate((2 * count - HALO + i, HALO - 1 - i)):
                at = pl.ds(row, streams, stride=pitch)
                states[side] = advance(states[side], ivar_s[at, :], pixel_s[at, :], back)
                if i % 24 == 23:
                    states[side] = rescaled(states[side])

    write_weights(
        place_ref, wav_count, which, coupling_ref, counts_ref, good_ref,
        lambda e, tile: ivar_ref[e, pl.ds(pl.multiple_of(which * half + ROWS * tile, ROWS), ROWS), :],
        lambda e, group: bits_ref[e, pl.ds(pl.multiple_of(which * (half // BITS) + words * group, words), words), :],
        sums_ref, weight_ref, eliminate,
    )
    for (n, d, b), out_ref in zip(states, (up_ref, down_ref)):
        scale = 1.0 / (d + n)
        out_ref[0] = coupling * (n * scale)
        out_ref[1] = b * scale


def kept_weights(wav_count, place, coupling, counts, good, pixels, ivar, bits):
    expos, width, fibres = ivar.shape
    half = width // 2
    streams = expos * fibres // LANES
    count = -(-HALO // ROWS) * ROWS
    edge = shaped((2, streams, LANES))
    edge_scratch = pltpu.VMEM((streams * odd(2 * count), LANES), F32)
    return pl.pallas_call(
        functools.partial(kept_kernel, wav_count),
        in_specs=[in_smem] + [in_vmem] * 6,
        out_specs=[in_vmem] * 4,
        out_shape=[shaped((2, half, fibres)), shaped((expos, half, fibres)), edge, edge],
        scratch_shapes=[edge_scratch, edge_scratch],
        compiler_params=params(),
        cost_estimate=cost(20 * ivar.size, 6 * ivar.size),
        name="kept_weights",
    )(place, coupling, counts, good, pixels, ivar, bits)


def layout_kernel(arrived_ref, pixels_ref, ivar_ref, pixel_out, ivar_out):
    width = ivar_ref.shape[1]
    lay_out(ivar_ref, ivar_out, [(0, width, 0)], odd(width))
    lay_out(pixels_ref, pixel_out, [(0, width, 0)], odd(width))


def stream_layout(arrived, pixels, ivar):
    expos, width, fibres = ivar.shape
    streams = expos * fibres // LANES
    laid = shaped((streams * odd(width), LANES))
    return pl.pallas_call(
        layout_kernel,
        in_specs=[in_vmem] * 3,
        out_specs=[in_vmem] * 2,
        out_shape=[laid, laid],
        compiler_params=params(),
        cost_estimate=cost(0, 16 * ivar.size),
        name="stream_layout",
    )(arrived, pixels, ivar)


def recv_kernel(moves, place_ref, slots_ref, table_ref):
    write_recv_table(*moves, place_ref[0], slots_ref, table_ref)


def recv_moves(moves, place, slots, fibres):
    fib_count, pack, per, _ = moves
    return pl.pallas_call(
        functools.partial(recv_kernel, moves),
        in_specs=[in_smem, in_vmem],
        out_specs=in_vmem,
        out_shape=shaped((pack * fibres, fib_count * pack * per), BF16),
        compiler_params=params(),
        cost_estimate=cost(1e6, 1e6),
        name="recv_moves",
    )(place, slots)


def solve_kernel(
    wav_count, place_ref, coupling_ref, left_ref, right_ref, pixel_ref, ivar_ref, weight_ref,
    theirs_ref, solved_s, lead_s, rest_s,
):
    streams = left_ref.shape[1]
    expos, half, fibres = weight_ref.shape
    width = 2 * half
    pitch = odd(width)
    middle = half
    coupling = stream_coupling(coupling_ref, expos)
    back = 1.0 / coupling

    def row_at(i):
        return pl.ds(i, streams, stride=pitch)

    def begin(edge_ref, outermost):
        n = jnp.where(place_ref[1] == outermost, 0.0, edge_ref[0]) * back
        return (n, 1.0 - n, jnp.where(place_ref[1] == outermost, 0.0, edge_ref[1]))

    def keep(side, i, state):
        n, d, b = state
        inverse = inverse_of(d + n)
        lead_s[side, i] = d * inverse
        rest_s[side, i] = b * inverse

    unrolled = divisor_of(middle, 24)

    def eliminate(it, states):
        states = list(states)
        for k in range(unrolled):
            i = it * unrolled + k
            for side, row in enumerate((i, width - 1 - i)):
                keep(side, i, states[side])
                states[side] = advance(states[side], ivar_ref[row_at(row), :], pixel_ref[row_at(row), :], back)
        return tuple(rescaled(state) for state in states)

    states = lax.fori_loop(0, middle // unrolled, eliminate, (begin(left_ref, 0), begin(right_ref, wav_count - 1)))
    for side in range(2):
        keep(side, middle, states[side])
    lead, rest = lead_s[0, middle], rest_s[0, middle]
    lead_r, rest_r = lead_s[1, middle], rest_s[1, middle]
    left = (rest + lead * rest_r) / (1.0 - lead * lead_r)
    right = rest_r + lead_r * left
    several = divisor_of(middle, 48)

    def after_both(near, far):
        return far[0] * near[0], far[1] + far[0] * near[1]

    def step(factors, value):
        return factors[1] + factors[0] * value

    def substitute(it, values):
        values = list(values)
        for k in range(0, several, 4):
            for side in range(2):
                rows = [middle - 1 - (it * several + k + m) for m in range(4)]
                one, two, three, four = [(lead_s[side, i], rest_s[side, i]) for i in rows]
                first_two = after_both(one, two)
                all_four = after_both(first_two, after_both(three, four))
                value = values[side]
                third = step(first_two, value)
                solved = [value, step(one, value), third, step(three, third)]
                values[side] = step(all_four, value)
                for i, x in zip(rows, solved):
                    solved_s[row_at(i if side == 0 else width - 1 - i), :] = x
        return tuple(values)

    lax.fori_loop(0, middle // several, substitute, (left, right))

    add_up(theirs_ref, weight_ref, solved_s, coupling_ref, 1 - place_ref[2])


def add_up(out_ref, weight_ref, solved_ref, coupling_ref, which):
    expos, half, fibres = weight_ref.shape
    pitch = odd(2 * half)
    start = which * half
    back = 1.0 / coupling_ref[...]
    unrolled = divisor_of(half // ROWS, 5)

    def body(g, carry):
        for k in range(unrolled):
            row = pl.multiple_of((g * unrolled + k) * ROWS, ROWS)
            for h in range(fibres // LANES):
                total = None
                for e in range(expos):
                    at = pl.ds((h * expos + e) * pitch + start + row, ROWS)
                    term = weight_ref[e, pl.ds(row, ROWS), pl.ds(h * LANES, LANES)] * solved_ref[at, :]
                    total = term if e == 0 else total + term
                out_ref[0, pl.ds(row, ROWS), pl.ds(h * LANES, LANES)] = total * back[:, h * LANES : (h + 1) * LANES]
        return carry

    lax.fori_loop(0, half // ROWS // unrolled, body, 0)


def flux_sums(wav_count, place, coupling, left, right, pixels, ivar, weight):
    expos, half, fibres = weight.shape
    streams = left.shape[1]
    factor_scratch = pltpu.VMEM((2, half + 1, streams, LANES), F32)
    return pl.pallas_call(
        functools.partial(solve_kernel, wav_count),
        in_specs=[in_smem] + [in_vmem] * 6,
        out_specs=[in_vmem, in_vmem],
        out_shape=[shaped((1, half, fibres)), shaped(pixels.shape)],
        scratch_shapes=[factor_scratch, factor_scratch],
        compiler_params=params(),
        cost_estimate=cost(0, 0),
        name="flux_sums",
    )(place, coupling, left, right, pixels, ivar, weight)


def kept_flux_kernel(place_ref, coupling_ref, solved_ref, weight_ref, out_ref):
    add_up(out_ref, weight_ref, solved_ref, coupling_ref, place_ref[2])


def kept_flux(place, coupling, solved, weight):
    expos, half, fibres = weight.shape
    return pl.pallas_call(
        kept_flux_kernel,
        in_specs=[in_smem] + [in_vmem] * 3,
        out_specs=in_vmem,
        out_shape=shaped((1, half, fibres)),
        compiler_params=params(),
        cost_estimate=cost(2 * weight.size, 8 * weight.size),
        name="kept_flux",
    )(place, coupling, solved, weight)


def split_dot(x, table, dims):
    top = x.astype(BF16)
    low = (x - top.astype(F32)).astype(BF16)
    both = lax.dot_general(jnp.concatenate([top, low], 0), table, dims, preferred_element_type=F32)
    return both[: x.shape[0]] + both[x.shape[0] :]


def sort_kernel(pack, scaled, theirs_ref, mine_ref, table_ref, *refs):
    values, rows, _ = mine_ref.shape
    part = rows // pack
    totals = [mine_ref[v] + theirs_ref[v] for v in range(values)]
    if scaled:
        scale_ref, _, *out_refs = refs
        totals = [t * scale_ref[...] for t in totals]
    else:
        *out_refs, scale_ref = refs
        scale = 1.0 / jnp.maximum(totals[0], 1.0)
        scale_ref[...] = scale
        totals[1] = totals[1] * scale
    x = jnp.concatenate(
        [jnp.concatenate([t[h * part : (h + 1) * part] for h in range(pack)], 1) for t in totals], 0
    )
    moved = split_dot(x, table_ref[...], NT)
    lanes = moved.shape[1] // len(out_refs)
    for d, out_ref in enumerate(out_refs):
        for v in range(values):
            out_ref[v] = moved[v * part : (v + 1) * part, d * lanes : (d + 1) * lanes]


def sort_fibres(theirs, mine, table, pack, pieces, scale=None, ahead=None):
    values, rows, fibres = mine.shape
    lanes = table.shape[0] // pieces
    scaled = scale is not None
    outs = [shaped((values, rows // pack, lanes))] * pieces + ([] if scaled else [shaped((rows, fibres))])
    args = (theirs, mine, table) + ((scale, ahead) if scaled else ())
    return pl.pallas_call(
        functools.partial(sort_kernel, pack, scaled),
        in_specs=[in_vmem] * len(args),
        out_specs=[in_vmem] * len(outs),
        out_shape=outs,
        compiler_params=params(),
        cost_estimate=cost(0, 0),
        name="sort_flux" if scaled else "sort_weights",
    )(*args)


def exchange(pieces, fib_count):
    if len(pieces) == 1:
        return [lax.all_to_all(pieces[0], "fib", split_axis=2, concat_axis=2, tiled=True)]
    arrived = [pieces[0]]
    for d in range(1, fib_count):
        arrived.append(lax.ppermute(pieces[d], "fib", [(i, (i + d) % fib_count) for i in range(fib_count)]))
    return arrived


def landed(refs, table):
    values, part, _ = refs[0].shape
    x = jnp.concatenate(
        [jnp.concatenate([ref[v] for ref in refs], 1) if len(refs) > 1 else refs[0][v] for v in range(values)], 0
    )
    moved = split_dot(x, table, NT)
    return [moved[v * part : (v + 1) * part] for v in range(values)]


def weights_end_kernel(pack, total, place_ref, table_ref, *refs):
    *piece_refs, ivar_ref, res_ref = refs
    weight, band = landed(piece_refs, table_ref[...])
    rows, fibres = ivar_ref.shape
    part = rows // pack
    start = (place_ref[1] * 2 + place_ref[2]) * rows
    for h in range(pack):
        at = slice(h * part, (h + 1) * part)
        cut = slice(h * fibres, (h + 1) * fibres)
        row = start + h * part + lax.broadcasted_iota(jnp.int32, (part, 1), 0)
        w, b = weight[:, cut], band[:, cut]
        before = jnp.where(row == 0, 0.0, b)
        after = jnp.where(row == total - 1, 0.0, b)
        ivar_ref[at, :] = w
        res_ref[0, at, :] = before
        res_ref[1, at, :] = jnp.minimum(w, 1.0) - before - after
        res_ref[2, at, :] = after


def end_weights(place, table, pieces, pack, fibres, total):
    rows = pieces[0].shape[1] * pack
    return pl.pallas_call(
        functools.partial(weights_end_kernel, pack, total),
        in_specs=[in_smem] + [in_vmem] * (1 + len(pieces)),
        out_specs=[in_vmem] * 2,
        out_shape=[shaped((rows, fibres)), shaped((3, rows, fibres))],
        compiler_params=params(),
        cost_estimate=cost(4 * rows * table.size, 6 * rows * fibres * 4),
        name="end_weights",
    )(place, table, *pieces)


def flux_end_kernel(pack, table_ref, *refs):
    *piece_refs, flux_ref = refs
    (flux,) = landed(piece_refs, table_ref[...])
    rows, fibres = flux_ref.shape
    part = rows // pack
    for h in range(pack):
        flux_ref[h * part : (h + 1) * part, :] = flux[:, h * fibres : (h + 1) * fibres]


def end_flux(table, pieces, pack, fibres):
    rows = pieces[0].shape[1] * pack
    return pl.pallas_call(
        functools.partial(flux_end_kernel, pack),
        in_specs=[in_vmem] * (1 + len(pieces)),
        out_specs=in_vmem,
        out_shape=shaped((rows, fibres)),
        compiler_params=params(),
        cost_estimate=cost(2 * rows * table.size, 2 * rows * fibres * 4),
        name="end_flux",
    )(table, *pieces)


def after(value, done):
    return lax.optimization_barrier((value, done))[0]


def per_device(pixels, pixel_ivar, clip_bits, coupling, counts, good_flags, owner_slot):
    expos, width, fibres = pixels.shape
    fib_count, wav_count = lax.axis_size("fib"), lax.axis_size("wav")
    total = width * wav_count
    per = fibres // fib_count
    rows = width // 2
    pack = max(1, LANES // per)
    while pack > 1 and rows % (pack * ROWS):
        pack //= 2
    rel = pack * per == LANES
    pieces = fib_count if rel else 1
    place = jnp.stack([lax.axis_index(axis) for axis in ("fib", "wav", "exp")]).astype(jnp.int32)
    coupling, counts, slots = coupling[None], counts[None], owner_slot[None]
    swap = [(0, 1), (1, 0)]
    moves = (fib_count, pack, per, rel)

    theirs, weight_t, send_table, slots, coupling, counts, good, bits, ivar = sent_weights(
        moves, wav_count, place, slots, coupling, counts, good_flags, clip_bits, pixel_ivar
    )
    arriving = lax.ppermute(theirs, "exp", swap)
    mine, weight_m, up, down = kept_weights(
        wav_count, place, coupling, counts, good, pixels, ivar, bits
    )
    upward = [(i, (i + 1) % wav_count) for i in range(wav_count)]
    left = lax.ppermute(up, "wav", upward)
    right = lax.ppermute(down, "wav", [(j, i) for i, j in upward])
    *sorted_pieces, scale = sort_fibres(arriving, mine, send_table, pack, pieces)
    weight_pieces = exchange(sorted_pieces, fib_count)

    pixel_s, ivar_s = stream_layout(left[0] + right[0], pixels, ivar)
    theirs, solved = flux_sums(wav_count, place, coupling, left, right, pixel_s, ivar_s, weight_t)
    ahead = sum(piece[0, :ROWS, :] for piece in weight_pieces[1:-1] or weight_pieces)
    arriving = lax.ppermute(theirs, "exp", swap)
    mine = kept_flux(after(place, theirs), coupling, solved, weight_m)
    sorted_pieces = sort_fibres(arriving, mine, send_table, pack, pieces, scale, ahead)
    flux_pieces = exchange(sorted_pieces, fib_count)
    recv_table = recv_moves(moves, after(place, sorted_pieces[0]), slots, fibres)

    ivar, res = end_weights(place, recv_table, weight_pieces, pack, fibres, total)
    flux = end_flux(recv_table, flux_pieces, pack, fibres)
    return (flux, ivar, res)


def solution(mesh):
    return jax.shard_map(
        per_device,
        mesh=mesh,
        in_specs=(
            P("exp", "wav", "fib"),
            P("exp", "wav", "fib"),
            P("exp", "wav", "fib"),
            P("fib"),
            P("fib"),
            P("exp", "fib"),
            P(),
        ),
        out_specs=(
            P(("wav", "exp"), "fib"),
            P(("wav", "exp"), "fib"),
            P(None, ("wav", "exp"), "fib"),
        ),
        check_vma=False,
    )
```

```python
import functools

import jax
import jax.numpy as jnp
from jax import lax
from jax.experimental import pallas as pl
from jax.experimental.pallas import tpu as pltpu
from jax.sharding import PartitionSpec as P

HALO = 50
BITS = 15
LANES = 128
ROWS = 8
GROUP = 120
VMEM_BYTES = 32 * 1024 * 1024
F32 = jnp.float32
BF16 = jnp.bfloat16
NT = (((1,), (1,)), ((), ()))

in_vmem = pl.BlockSpec(memory_space=pltpu.VMEM)
in_smem = pl.BlockSpec(memory_space=pltpu.SMEM)
in_hbm = pl.BlockSpec(memory_space=pltpu.HBM)


def params():
    return pltpu.CompilerParams(vmem_limit_bytes=VMEM_BYTES)


def cost(flops, moved):
    return pl.CostEstimate(flops=int(flops), bytes_accessed=int(moved), transcendentals=0)


def held_in_hbm(*arrays):
    return [pltpu.with_memory_space_constraint(array, pltpu.HBM) for array in arrays]


def shaped(shape, dtype=F32):
    return jax.ShapeDtypeStruct(shape, dtype)


def usable_rows(place_ref, counts_ref, good_ref):
    count = good_ref.shape[0]
    return [
        good_ref[e : e + 1, :].astype(F32)
        * jnp.where(place_ref[2] * count + e < counts_ref[...], 1.0, 0.0)
        for e in range(count)
    ]


def tile_bits(tile):
    first, last = (ROWS * tile) // BITS, (ROWS * tile + ROWS - 1) // BITS
    split = BITS * last - ROWS * tile
    row = lax.broadcasted_iota(jnp.int32, (ROWS, 1), 0)
    word = jnp.where(row >= split, last, first)
    return first, last, split, jnp.left_shift(1, ROWS * tile + row - BITS * word)


def tile_words(words, tile):
    first, last, split, mask = tile_bits(tile)
    picked = words[first : first + 1, :]
    if last != first:
        row = lax.broadcasted_iota(jnp.int32, (ROWS, 1), 0)
        picked = jnp.where(row >= split, words[last : last + 1, :], picked)
    return (picked & mask) != 0


def in_flight(pairs, sems, at=0):
    copies = [pltpu.make_async_copy(source, target, sems.at[at + i]) for i, (source, target) in enumerate(pairs)]
    for copy in copies:
        copy.start()
    return copies


def inverse_of(x):
    guess = pl.reciprocal(x, approx=True)
    return guess * (2.0 - x * guess)


def advance(state, ivar, pixel, back_coupling):
    n, d, b = state
    ratio = ivar * back_coupling
    next_d = d + n
    return (n * (1.0 + ratio) + ratio * d, next_d, b + (ivar * pixel) * next_d)


def rescaled(state):
    scale = inverse_of(state[1])
    return tuple(part * scale for part in state)


def odd(rows):
    return rows + 1 - rows % 2


def divisor_of(size, most):
    return max(k for k in range(1, most + 1) if size % k == 0)


def owners(slots_ref, fib_count, fibres):
    rows = [slots_ref[:, s * fibres : (s + 1) * fibres].astype(F32) for s in range(fib_count)]
    sources = -(-fib_count // ROWS) * ROWS
    if sources > fib_count:
        rows.append(jnp.full((sources - fib_count, fibres), -1.0, F32))
    slots = jnp.concatenate(rows, 0)
    owner = jnp.floor((slots + 0.5) * (1.0 / fibres))
    return owner, slots - owner * fibres


def earlier_fibres(fibres):
    row = lax.broadcasted_iota(jnp.int32, (fibres, fibres), 0)
    col = lax.broadcasted_iota(jnp.int32, (fibres, fibres), 1)
    return (row < col).astype(F32).astype(BF16)


def write_send_table(fib_count, pack, per, rel, me, slots_ref, table_ref):
    fibres = table_ref.shape[1] // pack
    lanes = pack * per
    owner, _ = owners(slots_ref, fib_count, fibres)
    source = lax.broadcasted_iota(jnp.int32, owner.shape, 0)
    my_owner = jnp.sum(jnp.where(source == me, owner, 0.0), axis=0, keepdims=True).astype(jnp.int32)
    to_owner = (source == my_owner).astype(F32)
    counted = jnp.dot(to_owner.astype(BF16), earlier_fibres(fibres), preferred_element_type=F32)
    rank = jnp.sum(to_owner * counted, axis=0, keepdims=True).astype(jnp.int32)
    target = my_owner
    if rel:
        target = jnp.where(my_owner >= me, my_owner - me, my_owner - me + fib_count)
    base = target * lanes + rank
    place_of = jnp.concatenate([base + h * per for h in range(pack)], 1)
    row = lax.broadcasted_iota(jnp.int32, table_ref.shape, 0)
    table_ref[...] = (row == place_of).astype(F32).astype(BF16)


def write_recv_table(fib_count, pack, per, rel, me, slots_ref, table_ref):
    fibres = table_ref.shape[0] // pack
    lanes = pack * per
    total_lanes = fib_count * lanes
    owner, column = owners(slots_ref, fib_count, fibres)
    source = lax.broadcasted_iota(jnp.int32, owner.shape, 0)
    mine = (owner == me.astype(F32)).astype(F32)
    rank_in = jnp.dot(mine.astype(BF16), earlier_fibres(fibres), preferred_element_type=F32).astype(jnp.int32)
    order = source
    if rel:
        order = jnp.where(me >= source, me - source, me - source + fib_count)
    arrival = jnp.where(mine > 0.0, order * lanes + rank_in, -total_lanes)
    tall = lax.broadcasted_iota(jnp.int32, (total_lanes, fibres), 0)
    landing = jnp.zeros((ROWS, total_lanes), F32)
    for s in range(fib_count):
        hit = tall == arrival[s : s + 1, :]
        for h in range(1, pack):
            hit = hit | (tall == arrival[s : s + 1, :] + h * per)
        values = jnp.broadcast_to(column[s : s + 1, :], (ROWS, fibres)).astype(BF16)
        landing = landing + lax.dot_general(
            values, hit.astype(F32).astype(BF16), NT, preferred_element_type=F32
        )
    lane = lax.broadcasted_iota(jnp.int32, (1, total_lanes), 1)
    landing = landing[0:1, :].astype(jnp.int32)
    for h in range(1, pack):
        inside = (lane % lanes >= h * per) & (lane % lanes < (h + 1) * per)
        landing = jnp.where(inside, landing + h * fibres, landing)
    row = lax.broadcasted_iota(jnp.int32, table_ref.shape, 0)
    table_ref[...] = (row == landing).astype(F32).astype(BF16)


def stream_coupling(coupling_ref, expos):
    coupling = coupling_ref[...]
    blocks = coupling.shape[1] // LANES
    return jnp.concatenate(
        [jnp.broadcast_to(coupling[:, h * LANES : (h + 1) * LANES], (expos, LANES)) for h in range(blocks)], 0
    )


def weight_tile(coupling, usable, words, ivars, within, scale_row):
    links = scale_row * coupling
    weights = []
    weight_sum = band_sum = None
    for e, ivar in enumerate(ivars):
        weight = jnp.where(tile_words(words[e], within), ivar * usable[e], 0.0)
        band = weight * inverse_of(ivar + links)
        weights.append(weight)
        weight_sum = weight if e == 0 else weight_sum + weight
        band_sum = band if e == 0 else band_sum + band
    return weights, weight_sum, band_sum * coupling


def write_weights(place_ref, wav_count, which, coupling_v, counts_v, good_v, ivar_of, words_of, sums_ref, weight_ref, beside):
    expos, half, _ = weight_ref.shape
    coupling = coupling_v[...]
    usable = usable_rows(place_ref, counts_v, good_v)
    start = place_ref[1] * (2 * half) + which * half
    tiles = half // ROWS
    tiles_in_group = GROUP // ROWS
    for tile in range(tiles):
        beside(tile, tiles)
        group, within = divmod(tile, tiles_in_group)
        scale_row = 4.0
        if tile in (0, tiles - 1):
            row = start + ROWS * tile + lax.broadcasted_iota(jnp.int32, (ROWS, 1), 0)
            scale_row = jnp.where((row == 0) | (row == wav_count * 2 * half - 1), 2.0, 4.0)
        at = slice(ROWS * tile, ROWS * (tile + 1))
        weights, weight_sum, band_sum = weight_tile(
            coupling,
            usable,
            [words_of(e, group) for e in range(expos)],
            [ivar_of(e, tile) for e in range(expos)],
            within,
            scale_row,
        )
        for e in range(expos):
            weight_ref[e, at, :] = weights[e]
        sums_ref[0, at, :] = weight_sum
        sums_ref[1, at, :] = band_sum


def sent_kernel(
    moves, wav_count, place_ref, slots_ref, coupling_ref, counts_ref, good_ref, bits_ref, ivar_ref,
    sums_ref, weight_ref, table_ref, slots_v, coupling_v, counts_v, good_v, bits_v, ivar_v, sems,
):
    expos, width, _ = ivar_ref.shape
    half = width // 2
    which = 1 - place_ref[2]
    words = GROUP // BITS

    def part(source, target, first):
        at = pl.ds(pl.multiple_of(first, ROWS), GROUP)
        return source.at[:, at, :], target.at[:, at, :]

    waits = in_flight(
        [
            (slots_ref, slots_v),
            (coupling_ref, coupling_v),
            (counts_ref, counts_v),
            (good_ref, good_v),
            (bits_ref, bits_v),
        ]
        + [part(ivar_ref, ivar_v, which * half + g) for g in range(0, half, GROUP)]
        + [part(ivar_ref, ivar_v, (1 - which) * half + g) for g in range(0, half, GROUP)],
        sems,
    )
    waits[0].wait()
    write_send_table(*moves, place_ref[0], slots_v, table_ref)
    for wait in waits[1:5]:
        wait.wait()

    def arrive(tile, tiles):
        if ROWS * tile % GROUP == 0:
            waits[5 + ROWS * tile // GROUP].wait()

    write_weights(
        place_ref, wav_count, which, coupling_v, counts_v, good_v,
        lambda e, tile: ivar_v[e, pl.ds(pl.multiple_of(which * half + ROWS * tile, ROWS), ROWS), :],
        lambda e, group: bits_v[e, pl.ds(pl.multiple_of(which * (half // BITS) + words * group, words), words), :],
        sums_ref, weight_ref, arrive,
    )
    for wait in waits[5 + half // GROUP :]:
        wait.wait()


def sent_weights(moves, wav_count, place, slots, coupling, counts, good, bits, ivar):
    expos, width, fibres = ivar.shape
    half = width // 2
    fib_count, pack, per, _ = moves
    inputs = (slots, coupling, counts, good, bits, ivar)
    return pl.pallas_call(
        functools.partial(sent_kernel, moves, wav_count),
        in_specs=[in_smem] + [in_hbm] * 6,
        out_specs=[in_vmem] * 9,
        out_shape=[
            shaped((2, half, fibres)),
            shaped((expos, half, fibres)),
            shaped((fib_count * pack * per, pack * fibres), BF16),
        ]
        + [shaped(x.shape, x.dtype) for x in inputs],
        scratch_shapes=[pltpu.SemaphoreType.DMA((5 + width // GROUP,))],
        compiler_params=params(),
        cost_estimate=cost(20 * ivar.size, 6 * ivar.size),
        name="sent_weights",
    )(place, *held_in_hbm(*inputs))


def lay_out(source_ref, target_ref, pieces, pitch):
    expos, _, fibres = source_ref.shape
    for h in range(fibres // LANES):
        for e in range(expos):
            for first, length, at in pieces:
                target_ref[pl.ds((h * expos + e) * pitch + at, length), :] = source_ref[
                    e, pl.ds(first, length), pl.ds(h * LANES, LANES)
                ]


def kept_kernel(
    wav_count, place_ref, coupling_ref, counts_ref, good_ref, pixels_ref, ivar_ref, bits_ref,
    sums_ref, weight_ref, up_ref, down_ref, ivar_s, pixel_s,
):
    expos, width, fibres = ivar_ref.shape
    half = width // 2
    streams = expos * fibres // LANES
    count = -(-HALO // ROWS) * ROWS
    pitch = odd(2 * count)
    which = place_ref[2]
    words = GROUP // BITS
    edges = [(0, count, 0), (width - count, count, count)]
    lay_out(ivar_ref, ivar_s, edges, pitch)
    lay_out(pixels_ref, pixel_s, edges, pitch)
    coupling = stream_coupling(coupling_ref, expos)
    back = 1.0 / coupling
    zero = jnp.zeros((streams, LANES), F32)
    states = [(zero, zero + 1.0, zero), (zero, zero + 1.0, zero)]

    def eliminate(tile, tiles):
        for i in range(HALO * tile // tiles, HALO * (tile + 1) // tiles):
            for side, row in enumerate((2 * count - HALO + i, HALO - 1 - i)):
                at = pl.ds(row, streams, stride=pitch)
                states[side] = advance(states[side], ivar_s[at, :], pixel_s[at, :], back)
                if i % 24 == 23:
                    states[side] = rescaled(states[side])

    write_weights(
        place_ref, wav_count, which, coupling_ref, counts_ref, good_ref,
        lambda e, tile: ivar_ref[e, pl.ds(pl.multiple_of(which * half + ROWS * tile, ROWS), ROWS), :],
        lambda e, group: bits_ref[e, pl.ds(pl.multiple_of(which * (half // BITS) + words * group, words), words), :],
        sums_ref, weight_ref, eliminate,
    )
    for (n, d, b), out_ref in zip(states, (up_ref, down_ref)):
        scale = 1.0 / (d + n)
        out_ref[0] = coupling * (n * scale)
        out_ref[1] = b * scale


def kept_weights(wav_count, place, coupling, counts, good, pixels, ivar, bits):
    expos, width, fibres = ivar.shape
    half = width // 2
    streams = expos * fibres // LANES
    count = -(-HALO // ROWS) * ROWS
    edge = shaped((2, streams, LANES))
    edge_scratch = pltpu.VMEM((streams * odd(2 * count), LANES), F32)
    return pl.pallas_call(
        functools.partial(kept_kernel, wav_count),
        in_specs=[in_smem] + [in_vmem] * 6,
        out_specs=[in_vmem] * 4,
        out_shape=[shaped((2, half, fibres)), shaped((expos, half, fibres)), edge, edge],
        scratch_shapes=[edge_scratch, edge_scratch],
        compiler_params=params(),
        cost_estimate=cost(20 * ivar.size, 6 * ivar.size),
        name="kept_weights",
    )(place, coupling, counts, good, pixels, ivar, bits)


def layout_kernel(arrived_ref, pixels_ref, ivar_ref, pixel_out, ivar_out):
    width = ivar_ref.shape[1]
    lay_out(ivar_ref, ivar_out, [(0, width, 0)], odd(width))
    lay_out(pixels_ref, pixel_out, [(0, width, 0)], odd(width))


def stream_layout(arrived, pixels, ivar):
    expos, width, fibres = ivar.shape
    streams = expos * fibres // LANES
    laid = shaped((streams * odd(width), LANES))
    return pl.pallas_call(
        layout_kernel,
        in_specs=[in_vmem] * 3,
        out_specs=[in_vmem] * 2,
        out_shape=[laid, laid],
        compiler_params=params(),
        cost_estimate=cost(0, 16 * ivar.size),
        name="stream_layout",
    )(arrived, pixels, ivar)


def recv_kernel(moves, place_ref, slots_ref, table_ref):
    write_recv_table(*moves, place_ref[0], slots_ref, table_ref)


def recv_moves(moves, place, slots, fibres):
    fib_count, pack, per, _ = moves
    return pl.pallas_call(
        functools.partial(recv_kernel, moves),
        in_specs=[in_smem, in_vmem],
        out_specs=in_vmem,
        out_shape=shaped((pack * fibres, fib_count * pack * per), BF16),
        compiler_params=params(),
        cost_estimate=cost(1e6, 1e6),
        name="recv_moves",
    )(place, slots)


def solve_kernel(
    wav_count, place_ref, coupling_ref, left_ref, right_ref, pixel_ref, ivar_ref, weight_ref,
    theirs_ref, solved_s, lead_s, rest_s,
):
    streams = left_ref.shape[1]
    expos, half, fibres = weight_ref.shape
    width = 2 * half
    pitch = odd(width)
    middle = half
    coupling = stream_coupling(coupling_ref, expos)
    back = 1.0 / coupling

    def row_at(i):
        return pl.ds(i, streams, stride=pitch)

    def begin(edge_ref, outermost):
        n = jnp.where(place_ref[1] == outermost, 0.0, edge_ref[0]) * back
        return (n, 1.0 - n, jnp.where(place_ref[1] == outermost, 0.0, edge_ref[1]))

    def keep(side, i, state):
        n, d, b = state
        inverse = inverse_of(d + n)
        lead_s[side, i] = d * inverse
        rest_s[side, i] = b * inverse

    unrolled = divisor_of(middle, 24)

    def eliminate(it, states):
        states = list(states)
        for k in range(unrolled):
            i = it * unrolled + k
            for side, row in enumerate((i, width - 1 - i)):
                keep(side, i, states[side])
                states[side] = advance(states[side], ivar_ref[row_at(row), :], pixel_ref[row_at(row), :], back)
        return tuple(rescaled(state) for state in states)

    states = lax.fori_loop(0, middle // unrolled, eliminate, (begin(left_ref, 0), begin(right_ref, wav_count - 1)))
    for side in range(2):
        keep(side, middle, states[side])
    lead, rest = lead_s[0, middle], rest_s[0, middle]
    lead_r, rest_r = lead_s[1, middle], rest_s[1, middle]
    left = (rest + lead * rest_r) / (1.0 - lead * lead_r)
    right = rest_r + lead_r * left
    several = divisor_of(middle, 48)

    def after_both(near, far):
        return far[0] * near[0], far[1] + far[0] * near[1]

    def step(factors, value):
        return factors[1] + factors[0] * value

    def substitute(it, values):
        values = list(values)
        for k in range(0, several, 4):
            for side in range(2):
                rows = [middle - 1 - (it * several + k + m) for m in range(4)]
                one, two, three, four = [(lead_s[side, i], rest_s[side, i]) for i in rows]
                first_two = after_both(one, two)
                all_four = after_both(first_two, after_both(three, four))
                value = values[side]
                third = step(first_two, value)
                solved = [value, step(one, value), third, step(three, third)]
                values[side] = step(all_four, value)
                for i, x in zip(rows, solved):
                    solved_s[row_at(i if side == 0 else width - 1 - i), :] = x
        return tuple(values)

    lax.fori_loop(0, middle // several, substitute, (left, right))

    add_up(theirs_ref, weight_ref, solved_s, coupling_ref, 1 - place_ref[2])


def add_up(out_ref, weight_ref, solved_ref, coupling_ref, which):
    expos, half, fibres = weight_ref.shape
    pitch = odd(2 * half)
    start = which * half
    back = 1.0 / coupling_ref[...]
    unrolled = divisor_of(half // ROWS, 5)

    def body(g, carry):
        for k in range(unrolled):
            row = pl.multiple_of((g * unrolled + k) * ROWS, ROWS)
            for h in range(fibres // LANES):
                total = None
                for e in range(expos):
                    at = pl.ds((h * expos + e) * pitch + start + row, ROWS)
                    term = weight_ref[e, pl.ds(row, ROWS), pl.ds(h * LANES, LANES)] * solved_ref[at, :]
                    total = term if e == 0 else total + term
                out_ref[0, pl.ds(row, ROWS), pl.ds(h * LANES, LANES)] = total * back[:, h * LANES : (h + 1) * LANES]
        return carry

    lax.fori_loop(0, half // ROWS // unrolled, body, 0)


def flux_sums(wav_count, place, coupling, left, right, pixels, ivar, weight):
    expos, half, fibres = weight.shape
    streams = left.shape[1]
    factor_scratch = pltpu.VMEM((2, half + 1, streams, LANES), F32)
    return pl.pallas_call(
        functools.partial(solve_kernel, wav_count),
        in_specs=[in_smem] + [in_vmem] * 6,
        out_specs=[in_vmem, in_vmem],
        out_shape=[shaped((1, half, fibres)), shaped(pixels.shape)],
        scratch_shapes=[factor_scratch, factor_scratch],
        compiler_params=params(),
        cost_estimate=cost(0, 0),
        name="flux_sums",
    )(place, coupling, left, right, pixels, ivar, weight)


def kept_flux_kernel(place_ref, coupling_ref, solved_ref, weight_ref, out_ref):
    add_up(out_ref, weight_ref, solved_ref, coupling_ref, place_ref[2])


def kept_flux(place, coupling, solved, weight):
    expos, half, fibres = weight.shape
    return pl.pallas_call(
        kept_flux_kernel,
        in_specs=[in_smem] + [in_vmem] * 3,
        out_specs=in_vmem,
        out_shape=shaped((1, half, fibres)),
        compiler_params=params(),
        cost_estimate=cost(2 * weight.size, 8 * weight.size),
        name="kept_flux",
    )(place, coupling, solved, weight)


def split_dot(x, table, dims):
    top = x.astype(BF16)
    low = (x - top.astype(F32)).astype(BF16)
    both = lax.dot_general(jnp.concatenate([top, low], 0), table, dims, preferred_element_type=F32)
    return both[: x.shape[0]] + both[x.shape[0] :]


def sort_kernel(pack, scaled, theirs_ref, mine_ref, table_ref, *refs):
    values, rows, _ = mine_ref.shape
    part = rows // pack
    totals = [mine_ref[v] + theirs_ref[v] for v in range(values)]
    if scaled:
        scale_ref, _, *out_refs = refs
        totals = [t * scale_ref[...] for t in totals]
    else:
        *out_refs, scale_ref = refs
        scale = 1.0 / jnp.maximum(totals[0], 1.0)
        scale_ref[...] = scale
        totals[1] = totals[1] * scale
    x = jnp.concatenate(
        [jnp.concatenate([t[h * part : (h + 1) * part] for h in range(pack)], 1) for t in totals], 0
    )
    moved = split_dot(x, table_ref[...], NT)
    lanes = moved.shape[1] // len(out_refs)
    for d, out_ref in enumerate(out_refs):
        for v in range(values):
            out_ref[v] = moved[v * part : (v + 1) * part, d * lanes : (d + 1) * lanes]


def sort_fibres(theirs, mine, table, pack, pieces, scale=None, ahead=None):
    values, rows, fibres = mine.shape
    lanes = table.shape[0] // pieces
    scaled = scale is not None
    outs = [shaped((values, rows // pack, lanes))] * pieces + ([] if scaled else [shaped((rows, fibres))])
    args = (theirs, mine, table) + ((scale, ahead) if scaled else ())
    return pl.pallas_call(
        functools.partial(sort_kernel, pack, scaled),
        in_specs=[in_vmem] * len(args),
        out_specs=[in_vmem] * len(outs),
        out_shape=outs,
        compiler_params=params(),
        cost_estimate=cost(0, 0),
        name="sort_flux" if scaled else "sort_weights",
    )(*args)


def exchange(pieces, fib_count):
    if len(pieces) == 1:
        return [lax.all_to_all(pieces[0], "fib", split_axis=2, concat_axis=2, tiled=True)]
    arrived = [pieces[0]]
    for d in range(1, fib_count):
        arrived.append(lax.ppermute(pieces[d], "fib", [(i, (i + d) % fib_count) for i in range(fib_count)]))
    return arrived


def landed(refs, table):
    values, part, _ = refs[0].shape
    x = jnp.concatenate(
        [jnp.concatenate([ref[v] for ref in refs], 1) if len(refs) > 1 else refs[0][v] for v in range(values)], 0
    )
    moved = split_dot(x, table, NT)
    return [moved[v * part : (v + 1) * part] for v in range(values)]


def weights_end_kernel(pack, total, place_ref, table_ref, *refs):
    *piece_refs, ivar_ref, res_ref = refs
    weight, band = landed(piece_refs, table_ref[...])
    rows, fibres = ivar_ref.shape
    part = rows // pack
    start = (place_ref[1] * 2 + place_ref[2]) * rows
    for h in range(pack):
        at = slice(h * part, (h + 1) * part)
        cut = slice(h * fibres, (h + 1) * fibres)
        row = start + h * part + lax.broadcasted_iota(jnp.int32, (part, 1), 0)
        w, b = weight[:, cut], band[:, cut]
        before = jnp.where(row == 0, 0.0, b)
        after = jnp.where(row == total - 1, 0.0, b)
        ivar_ref[at, :] = w
        res_ref[0, at, :] = before
        res_ref[1, at, :] = jnp.minimum(w, 1.0) - before - after
        res_ref[2, at, :] = after


def end_weights(place, table, pieces, pack, fibres, total):
    rows = pieces[0].shape[1] * pack
    return pl.pallas_call(
        functools.partial(weights_end_kernel, pack, total),
        in_specs=[in_smem] + [in_vmem] * (1 + len(pieces)),
        out_specs=[in_vmem] * 2,
        out_shape=[shaped((rows, fibres)), shaped((3, rows, fibres))],
        compiler_params=params(),
        cost_estimate=cost(4 * rows * table.size, 6 * rows * fibres * 4),
        name="end_weights",
    )(place, table, *pieces)


def flux_end_kernel(pack, table_ref, *refs):
    *piece_refs, flux_ref = refs
    (flux,) = landed(piece_refs, table_ref[...])
    rows, fibres = flux_ref.shape
    part = rows // pack
    for h in range(pack):
        flux_ref[h * part : (h + 1) * part, :] = flux[:, h * fibres : (h + 1) * fibres]


def end_flux(table, pieces, pack, fibres):
    rows = pieces[0].shape[1] * pack
    return pl.pallas_call(
        functools.partial(flux_end_kernel, pack),
        in_specs=[in_vmem] * (1 + len(pieces)),
        out_specs=in_vmem,
        out_shape=shaped((rows, fibres)),
        compiler_params=params(),
        cost_estimate=cost(2 * rows * table.size, 2 * rows * fibres * 4),
        name="end_flux",
    )(table, *pieces)


def after(value, done):
    return lax.optimization_barrier((value, done))[0]


def per_device(pixels, pixel_ivar, clip_bits, coupling, counts, good_flags, owner_slot):
    expos, width, fibres = pixels.shape
    fib_count, wav_count = lax.axis_size("fib"), lax.axis_size("wav")
    total = width * wav_count
    per = fibres // fib_count
    rows = width // 2
    pack = max(1, LANES // per)
    while pack > 1 and rows % (pack * ROWS):
        pack //= 2
    rel = pack * per == LANES
    pieces = fib_count if rel else 1
    place = jnp.stack([lax.axis_index(axis) for axis in ("fib", "wav", "exp")]).astype(jnp.int32)
    coupling, counts, slots = coupling[None], counts[None], owner_slot[None]
    swap = [(0, 1), (1, 0)]
    moves = (fib_count, pack, per, rel)

    theirs, weight_t, send_table, slots, coupling, counts, good, bits, ivar = sent_weights(
        moves, wav_count, place, slots, coupling, counts, good_flags, clip_bits, pixel_ivar
    )
    arriving = lax.ppermute(theirs, "exp", swap)
    mine, weight_m, up, down = kept_weights(
        wav_count, place, coupling, counts, good, pixels, ivar, bits
    )
    upward = [(i, (i + 1) % wav_count) for i in range(wav_count)]
    left = lax.ppermute(up, "wav", upward)
    right = lax.ppermute(down, "wav", [(j, i) for i, j in upward])
    *sorted_pieces, scale = sort_fibres(arriving, mine, send_table, pack, pieces)
    weight_pieces = exchange(sorted_pieces, fib_count)

    pixel_s, ivar_s = stream_layout(left[0] + right[0], pixels, ivar)
    theirs, solved = flux_sums(wav_count, place, coupling, left, right, pixel_s, ivar_s, weight_t)
    early = [piece for d, piece in enumerate(weight_pieces) if d not in (0, fib_count // 2)] or weight_pieces
    ahead = sum(piece[0, :ROWS, :] for piece in early)
    arriving = lax.ppermute(theirs, "exp", swap)
    mine = kept_flux(after(place, theirs), coupling, solved, weight_m)
    sorted_pieces = sort_fibres(arriving, mine, send_table, pack, pieces, scale, ahead)
    flux_pieces = exchange(sorted_pieces, fib_count)
    recv_table = recv_moves(moves, after(place, sorted_pieces[0]), slots, fibres)

    ivar, res = end_weights(place, recv_table, weight_pieces, pack, fibres, total)
    flux = end_flux(recv_table, flux_pieces, pack, fibres)
    return (flux, ivar, res)


def solution(mesh):
    return jax.shard_map(
        per_device,
        mesh=mesh,
        in_specs=(
            P("exp", "wav", "fib"),
            P("exp", "wav", "fib"),
            P("exp", "wav", "fib"),
            P("fib"),
            P("fib"),
            P("exp", "fib"),
            P(),
        ),
        out_specs=(
            P(("wav", "exp"), "fib"),
            P(("wav", "exp"), "fib"),
            P(None, ("wav", "exp"), "fib"),
        ),
        check_vma=False,
    )
```

```python
import functools

import jax
import jax.numpy as jnp
from jax import lax
from jax.experimental import pallas as pl
from jax.experimental.pallas import tpu as pltpu
from jax.sharding import PartitionSpec as P

HALO = 50
BITS = 15
LANES = 128
ROWS = 8
GROUP = 120
VMEM_BYTES = 32 * 1024 * 1024
F32 = jnp.float32
BF16 = jnp.bfloat16
NT = (((1,), (1,)), ((), ()))

in_vmem = pl.BlockSpec(memory_space=pltpu.VMEM)
in_smem = pl.BlockSpec(memory_space=pltpu.SMEM)
in_hbm = pl.BlockSpec(memory_space=pltpu.HBM)


def params():
    return pltpu.CompilerParams(vmem_limit_bytes=VMEM_BYTES)


def cost(flops, moved):
    return pl.CostEstimate(flops=int(flops), bytes_accessed=int(moved), transcendentals=0)


def held_in_hbm(*arrays):
    return [pltpu.with_memory_space_constraint(array, pltpu.HBM) for array in arrays]


def shaped(shape, dtype=F32):
    return jax.ShapeDtypeStruct(shape, dtype)


def usable_rows(place_ref, counts_ref, good_ref):
    count = good_ref.shape[0]
    return [
        good_ref[e : e + 1, :].astype(F32)
        * jnp.where(place_ref[2] * count + e < counts_ref[...], 1.0, 0.0)
        for e in range(count)
    ]


def tile_bits(tile):
    first, last = (ROWS * tile) // BITS, (ROWS * tile + ROWS - 1) // BITS
    split = BITS * last - ROWS * tile
    row = lax.broadcasted_iota(jnp.int32, (ROWS, 1), 0)
    word = jnp.where(row >= split, last, first)
    return first, last, split, jnp.left_shift(1, ROWS * tile + row - BITS * word)


def tile_words(words, tile):
    first, last, split, mask = tile_bits(tile)
    picked = words[first : first + 1, :]
    if last != first:
        row = lax.broadcasted_iota(jnp.int32, (ROWS, 1), 0)
        picked = jnp.where(row >= split, words[last : last + 1, :], picked)
    return (picked & mask) != 0


def in_flight(pairs, sems, at=0):
    copies = [pltpu.make_async_copy(source, target, sems.at[at + i]) for i, (source, target) in enumerate(pairs)]
    for copy in copies:
        copy.start()
    return copies


def inverse_of(x):
    guess = pl.reciprocal(x, approx=True)
    return guess * (2.0 - x * guess)


def advance(state, ivar, pixel, back_coupling):
    n, d, b = state
    ratio = ivar * back_coupling
    next_d = d + n
    return (n * (1.0 + ratio) + ratio * d, next_d, b + (ivar * pixel) * next_d)


def rescaled(state):
    scale = inverse_of(state[1])
    return tuple(part * scale for part in state)


def odd(rows):
    return rows + 1 - rows % 2


def divisor_of(size, most):
    return max(k for k in range(1, most + 1) if size % k == 0)


def owners(slots_ref, fib_count, fibres):
    rows = [slots_ref[:, s * fibres : (s + 1) * fibres].astype(F32) for s in range(fib_count)]
    sources = -(-fib_count // ROWS) * ROWS
    if sources > fib_count:
        rows.append(jnp.full((sources - fib_count, fibres), -1.0, F32))
    slots = jnp.concatenate(rows, 0)
    owner = jnp.floor((slots + 0.5) * (1.0 / fibres))
    return owner, slots - owner * fibres


def earlier_fibres(fibres):
    row = lax.broadcasted_iota(jnp.int32, (fibres, fibres), 0)
    col = lax.broadcasted_iota(jnp.int32, (fibres, fibres), 1)
    return (row < col).astype(F32).astype(BF16)


def write_send_table(fib_count, pack, per, rel, me, slots_ref, table_ref):
    fibres = table_ref.shape[1] // pack
    lanes = pack * per
    owner, _ = owners(slots_ref, fib_count, fibres)
    source = lax.broadcasted_iota(jnp.int32, owner.shape, 0)
    my_owner = jnp.sum(jnp.where(source == me, owner, 0.0), axis=0, keepdims=True).astype(jnp.int32)
    to_owner = (source == my_owner).astype(F32)
    counted = jnp.dot(to_owner.astype(BF16), earlier_fibres(fibres), preferred_element_type=F32)
    rank = jnp.sum(to_owner * counted, axis=0, keepdims=True).astype(jnp.int32)
    target = my_owner ^ me if rel else my_owner
    base = target * lanes + rank
    place_of = jnp.concatenate([base + h * per for h in range(pack)], 1)
    row = lax.broadcasted_iota(jnp.int32, table_ref.shape, 0)
    table_ref[...] = (row == place_of).astype(F32).astype(BF16)


def write_recv_table(fib_count, pack, per, rel, me, slots_ref, table_ref):
    fibres = table_ref.shape[0] // pack
    lanes = pack * per
    total_lanes = fib_count * lanes
    owner, column = owners(slots_ref, fib_count, fibres)
    source = lax.broadcasted_iota(jnp.int32, owner.shape, 0)
    mine = (owner == me.astype(F32)).astype(F32)
    rank_in = jnp.dot(mine.astype(BF16), earlier_fibres(fibres), preferred_element_type=F32).astype(jnp.int32)
    order = source ^ me if rel else source
    arrival = jnp.where(mine > 0.0, order * lanes + rank_in, -total_lanes)
    tall = lax.broadcasted_iota(jnp.int32, (total_lanes, fibres), 0)
    landing = jnp.zeros((ROWS, total_lanes), F32)
    for s in range(fib_count):
        hit = tall == arrival[s : s + 1, :]
        for h in range(1, pack):
            hit = hit | (tall == arrival[s : s + 1, :] + h * per)
        values = jnp.broadcast_to(column[s : s + 1, :], (ROWS, fibres)).astype(BF16)
        landing = landing + lax.dot_general(
            values, hit.astype(F32).astype(BF16), NT, preferred_element_type=F32
        )
    lane = lax.broadcasted_iota(jnp.int32, (1, total_lanes), 1)
    landing = landing[0:1, :].astype(jnp.int32)
    for h in range(1, pack):
        inside = (lane % lanes >= h * per) & (lane % lanes < (h + 1) * per)
        landing = jnp.where(inside, landing + h * fibres, landing)
    row = lax.broadcasted_iota(jnp.int32, table_ref.shape, 0)
    table_ref[...] = (row == landing).astype(F32).astype(BF16)


def stream_coupling(coupling_ref, expos):
    coupling = coupling_ref[...]
    blocks = coupling.shape[1] // LANES
    return jnp.concatenate(
        [jnp.broadcast_to(coupling[:, h * LANES : (h + 1) * LANES], (expos, LANES)) for h in range(blocks)], 0
    )


def weight_tile(coupling, usable, words, ivars, within, scale_row):
    links = scale_row * coupling
    weights = []
    weight_sum = band_sum = None
    for e, ivar in enumerate(ivars):
        weight = jnp.where(tile_words(words[e], within), ivar * usable[e], 0.0)
        band = weight * inverse_of(ivar + links)
        weights.append(weight)
        weight_sum = weight if e == 0 else weight_sum + weight
        band_sum = band if e == 0 else band_sum + band
    return weights, weight_sum, band_sum * coupling


def write_weights(place_ref, wav_count, which, coupling_v, counts_v, good_v, ivar_of, words_of, sums_ref, weight_ref, beside):
    expos, half, _ = weight_ref.shape
    coupling = coupling_v[...]
    usable = usable_rows(place_ref, counts_v, good_v)
    start = place_ref[1] * (2 * half) + which * half
    tiles = half // ROWS
    tiles_in_group = GROUP // ROWS
    for tile in range(tiles):
        beside(tile, tiles)
        group, within = divmod(tile, tiles_in_group)
        scale_row = 4.0
        if tile in (0, tiles - 1):
            row = start + ROWS * tile + lax.broadcasted_iota(jnp.int32, (ROWS, 1), 0)
            scale_row = jnp.where((row == 0) | (row == wav_count * 2 * half - 1), 2.0, 4.0)
        at = slice(ROWS * tile, ROWS * (tile + 1))
        weights, weight_sum, band_sum = weight_tile(
            coupling,
            usable,
            [words_of(e, group) for e in range(expos)],
            [ivar_of(e, tile) for e in range(expos)],
            within,
            scale_row,
        )
        for e in range(expos):
            weight_ref[e, at, :] = weights[e]
        sums_ref[0, at, :] = weight_sum
        sums_ref[1, at, :] = band_sum


def sent_kernel(
    moves, wav_count, place_ref, slots_ref, coupling_ref, counts_ref, good_ref, bits_ref, ivar_ref,
    sums_ref, weight_ref, table_ref, slots_v, coupling_v, counts_v, good_v, bits_v, ivar_v, sems,
):
    expos, width, _ = ivar_ref.shape
    half = width // 2
    which = 1 - place_ref[2]
    words = GROUP // BITS

    def part(source, target, first):
        at = pl.ds(pl.multiple_of(first, ROWS), GROUP)
        return source.at[:, at, :], target.at[:, at, :]

    waits = in_flight(
        [
            (slots_ref, slots_v),
            (coupling_ref, coupling_v),
            (counts_ref, counts_v),
            (good_ref, good_v),
            (bits_ref, bits_v),
        ]
        + [part(ivar_ref, ivar_v, which * half + g) for g in range(0, half, GROUP)]
        + [part(ivar_ref, ivar_v, (1 - which) * half + g) for g in range(0, half, GROUP)],
        sems,
    )
    waits[0].wait()
    write_send_table(*moves, place_ref[0], slots_v, table_ref)
    for wait in waits[1:5]:
        wait.wait()

    def arrive(tile, tiles):
        if ROWS * tile % GROUP == 0:
            waits[5 + ROWS * tile // GROUP].wait()

    write_weights(
        place_ref, wav_count, which, coupling_v, counts_v, good_v,
        lambda e, tile: ivar_v[e, pl.ds(pl.multiple_of(which * half + ROWS * tile, ROWS), ROWS), :],
        lambda e, group: bits_v[e, pl.ds(pl.multiple_of(which * (half // BITS) + words * group, words), words), :],
        sums_ref, weight_ref, arrive,
    )
    for wait in waits[5 + half // GROUP :]:
        wait.wait()


def sent_weights(moves, wav_count, place, slots, coupling, counts, good, bits, ivar):
    expos, width, fibres = ivar.shape
    half = width // 2
    fib_count, pack, per, _ = moves
    inputs = (slots, coupling, counts, good, bits, ivar)
    return pl.pallas_call(
        functools.partial(sent_kernel, moves, wav_count),
        in_specs=[in_smem] + [in_hbm] * 6,
        out_specs=[in_vmem] * 9,
        out_shape=[
            shaped((2, half, fibres)),
            shaped((expos, half, fibres)),
            shaped((fib_count * pack * per, pack * fibres), BF16),
        ]
        + [shaped(x.shape, x.dtype) for x in inputs],
        scratch_shapes=[pltpu.SemaphoreType.DMA((5 + width // GROUP,))],
        compiler_params=params(),
        cost_estimate=cost(20 * ivar.size, 6 * ivar.size),
        name="sent_weights",
    )(place, *held_in_hbm(*inputs))


def lay_out(source_ref, target_ref, pieces, pitch):
    expos, _, fibres = source_ref.shape
    for h in range(fibres // LANES):
        for e in range(expos):
            for first, length, at in pieces:
                target_ref[pl.ds((h * expos + e) * pitch + at, length), :] = source_ref[
                    e, pl.ds(first, length), pl.ds(h * LANES, LANES)
                ]


def kept_kernel(
    wav_count, place_ref, coupling_ref, counts_ref, good_ref, pixels_ref, ivar_ref, bits_ref,
    sums_ref, weight_ref, up_ref, down_ref, ivar_s, pixel_s,
):
    expos, width, fibres = ivar_ref.shape
    half = width // 2
    streams = expos * fibres // LANES
    count = -(-HALO // ROWS) * ROWS
    pitch = odd(2 * count)
    which = place_ref[2]
    words = GROUP // BITS
    edges = [(0, count, 0), (width - count, count, count)]
    lay_out(ivar_ref, ivar_s, edges, pitch)
    lay_out(pixels_ref, pixel_s, edges, pitch)
    coupling = stream_coupling(coupling_ref, expos)
    back = 1.0 / coupling
    zero = jnp.zeros((streams, LANES), F32)
    states = [(zero, zero + 1.0, zero), (zero, zero + 1.0, zero)]

    def eliminate(tile, tiles):
        for i in range(HALO * tile // tiles, HALO * (tile + 1) // tiles):
            for side, row in enumerate((2 * count - HALO + i, HALO - 1 - i)):
                at = pl.ds(row, streams, stride=pitch)
                states[side] = advance(states[side], ivar_s[at, :], pixel_s[at, :], back)
                if i % 24 == 23:
                    states[side] = rescaled(states[side])

    write_weights(
        place_ref, wav_count, which, coupling_ref, counts_ref, good_ref,
        lambda e, tile: ivar_ref[e, pl.ds(pl.multiple_of(which * half + ROWS * tile, ROWS), ROWS), :],
        lambda e, group: bits_ref[e, pl.ds(pl.multiple_of(which * (half // BITS) + words * group, words), words), :],
        sums_ref, weight_ref, eliminate,
    )
    for (n, d, b), out_ref in zip(states, (up_ref, down_ref)):
        scale = 1.0 / (d + n)
        out_ref[0] = coupling * (n * scale)
        out_ref[1] = b * scale


def kept_weights(wav_count, place, coupling, counts, good, pixels, ivar, bits):
    expos, width, fibres = ivar.shape
    half = width // 2
    streams = expos * fibres // LANES
    count = -(-HALO // ROWS) * ROWS
    edge = shaped((2, streams, LANES))
    edge_scratch = pltpu.VMEM((streams * odd(2 * count), LANES), F32)
    return pl.pallas_call(
        functools.partial(kept_kernel, wav_count),
        in_specs=[in_smem] + [in_vmem] * 6,
        out_specs=[in_vmem] * 4,
        out_shape=[shaped((2, half, fibres)), shaped((expos, half, fibres)), edge, edge],
        scratch_shapes=[edge_scratch, edge_scratch],
        compiler_params=params(),
        cost_estimate=cost(20 * ivar.size, 6 * ivar.size),
        name="kept_weights",
    )(place, coupling, counts, good, pixels, ivar, bits)


def layout_kernel(arrived_ref, pixels_ref, ivar_ref, pixel_out, ivar_out):
    width = ivar_ref.shape[1]
    lay_out(ivar_ref, ivar_out, [(0, width, 0)], odd(width))
    lay_out(pixels_ref, pixel_out, [(0, width, 0)], odd(width))


def stream_layout(arrived, pixels, ivar):
    expos, width, fibres = ivar.shape
    streams = expos * fibres // LANES
    laid = shaped((streams * odd(width), LANES))
    return pl.pallas_call(
        layout_kernel,
        in_specs=[in_vmem] * 3,
        out_specs=[in_vmem] * 2,
        out_shape=[laid, laid],
        compiler_params=params(),
        cost_estimate=cost(0, 16 * ivar.size),
        name="stream_layout",
    )(arrived, pixels, ivar)


def solve_kernel(
    wav_count, place_ref, coupling_ref, left_ref, right_ref, pixel_ref, ivar_ref, weight_ref,
    theirs_ref, solved_s, lead_s, rest_s,
):
    streams = left_ref.shape[1]
    expos, half, fibres = weight_ref.shape
    width = 2 * half
    pitch = odd(width)
    middle = half
    coupling = stream_coupling(coupling_ref, expos)
    back = 1.0 / coupling

    def row_at(i):
        return pl.ds(i, streams, stride=pitch)

    def begin(edge_ref, outermost):
        n = jnp.where(place_ref[1] == outermost, 0.0, edge_ref[0]) * back
        return (n, 1.0 - n, jnp.where(place_ref[1] == outermost, 0.0, edge_ref[1]))

    def keep(side, i, state):
        n, d, b = state
        inverse = inverse_of(d + n)
        lead_s[side, i] = d * inverse
        rest_s[side, i] = b * inverse

    unrolled = divisor_of(middle, 24)

    def eliminate(it, states):
        states = list(states)
        for k in range(unrolled):
            i = it * unrolled + k
            for side, row in enumerate((i, width - 1 - i)):
                keep(side, i, states[side])
                states[side] = advance(states[side], ivar_ref[row_at(row), :], pixel_ref[row_at(row), :], back)
        return tuple(rescaled(state) for state in states)

    states = lax.fori_loop(0, middle // unrolled, eliminate, (begin(left_ref, 0), begin(right_ref, wav_count - 1)))
    for side in range(2):
        keep(side, middle, states[side])
    lead, rest = lead_s[0, middle], rest_s[0, middle]
    lead_r, rest_r = lead_s[1, middle], rest_s[1, middle]
    left = (rest + lead * rest_r) / (1.0 - lead * lead_r)
    right = rest_r + lead_r * left
    several = divisor_of(middle, 48)

    def after_both(near, far):
        return far[0] * near[0], far[1] + far[0] * near[1]

    def step(factors, value):
        return factors[1] + factors[0] * value

    def substitute(it, values):
        values = list(values)
        for k in range(0, several, 4):
            for side in range(2):
                rows = [middle - 1 - (it * several + k + m) for m in range(4)]
                one, two, three, four = [(lead_s[side, i], rest_s[side, i]) for i in rows]
                first_two = after_both(one, two)
                all_four = after_both(first_two, after_both(three, four))
                value = values[side]
                third = step(first_two, value)
                solved = [value, step(one, value), third, step(three, third)]
                values[side] = step(all_four, value)
                for i, x in zip(rows, solved):
                    solved_s[row_at(i if side == 0 else width - 1 - i), :] = x
        return tuple(values)

    lax.fori_loop(0, middle // several, substitute, (left, right))

    add_up(theirs_ref, weight_ref, solved_s, coupling_ref, 1 - place_ref[2])


def add_up(out_ref, weight_ref, solved_ref, coupling_ref, which):
    expos, half, fibres = weight_ref.shape
    pitch = odd(2 * half)
    start = which * half
    back = 1.0 / coupling_ref[...]
    unrolled = divisor_of(half // ROWS, 5)

    def body(g, carry):
        for k in range(unrolled):
            row = pl.multiple_of((g * unrolled + k) * ROWS, ROWS)
            for h in range(fibres // LANES):
                total = None
                for e in range(expos):
                    at = pl.ds((h * expos + e) * pitch + start + row, ROWS)
                    term = weight_ref[e, pl.ds(row, ROWS), pl.ds(h * LANES, LANES)] * solved_ref[at, :]
                    total = term if e == 0 else total + term
                out_ref[0, pl.ds(row, ROWS), pl.ds(h * LANES, LANES)] = total * back[:, h * LANES : (h + 1) * LANES]
        return carry

    lax.fori_loop(0, half // ROWS // unrolled, body, 0)


def flux_sums(wav_count, place, coupling, left, right, pixels, ivar, weight):
    expos, half, fibres = weight.shape
    streams = left.shape[1]
    factor_scratch = pltpu.VMEM((2, half + 1, streams, LANES), F32)
    return pl.pallas_call(
        functools.partial(solve_kernel, wav_count),
        in_specs=[in_smem] + [in_vmem] * 6,
        out_specs=[in_vmem, in_vmem],
        out_shape=[shaped((1, half, fibres)), shaped(pixels.shape)],
        scratch_shapes=[factor_scratch, factor_scratch],
        compiler_params=params(),
        cost_estimate=cost(0, 0),
        name="flux_sums",
    )(place, coupling, left, right, pixels, ivar, weight)


def kept_flux_kernel(place_ref, coupling_ref, solved_ref, weight_ref, out_ref):
    add_up(out_ref, weight_ref, solved_ref, coupling_ref, place_ref[2])


def kept_flux(place, coupling, solved, weight):
    expos, half, fibres = weight.shape
    return pl.pallas_call(
        kept_flux_kernel,
        in_specs=[in_smem] + [in_vmem] * 3,
        out_specs=in_vmem,
        out_shape=shaped((1, half, fibres)),
        compiler_params=params(),
        cost_estimate=cost(2 * weight.size, 8 * weight.size),
        name="kept_flux",
    )(place, coupling, solved, weight)


def split_dot(x, table, dims):
    top = x.astype(BF16)
    low = (x - top.astype(F32)).astype(BF16)
    both = lax.dot_general(jnp.concatenate([top, low], 0), table, dims, preferred_element_type=F32)
    return both[: x.shape[0]] + both[x.shape[0] :]


def sort_kernel(pack, scaled, theirs_ref, mine_ref, table_ref, *refs):
    values, rows, _ = mine_ref.shape
    part = rows // pack
    totals = [mine_ref[v] + theirs_ref[v] for v in range(values)]
    if scaled:
        scale_ref, _, *out_refs = refs
        totals = [t * scale_ref[...] for t in totals]
    else:
        *out_refs, scale_ref = refs
        scale = 1.0 / jnp.maximum(totals[0], 1.0)
        scale_ref[...] = scale
        totals[1] = totals[1] * scale
    x = jnp.concatenate(
        [jnp.concatenate([t[h * part : (h + 1) * part] for h in range(pack)], 1) for t in totals], 0
    )
    moved = split_dot(x, table_ref[...], NT)
    lanes = moved.shape[1] // len(out_refs)
    for d, out_ref in enumerate(out_refs):
        for v in range(values):
            out_ref[v] = moved[v * part : (v + 1) * part, d * lanes : (d + 1) * lanes]


def sort_fibres(theirs, mine, table, pack, pieces, scale=None, ahead=None):
    values, rows, fibres = mine.shape
    lanes = table.shape[0] // pieces
    scaled = scale is not None
    outs = [shaped((values, rows // pack, lanes))] * pieces + ([] if scaled else [shaped((rows, fibres))])
    args = (theirs, mine, table) + ((scale, ahead) if scaled else ())
    return pl.pallas_call(
        functools.partial(sort_kernel, pack, scaled),
        in_specs=[in_vmem] * len(args),
        out_specs=[in_vmem] * len(outs),
        out_shape=outs,
        compiler_params=params(),
        cost_estimate=cost(0, 0),
        name="sort_flux" if scaled else "sort_weights",
    )(*args)


def exchange(pieces, fib_count):
    if len(pieces) == 1:
        return [lax.all_to_all(pieces[0], "fib", split_axis=2, concat_axis=2, tiled=True)]
    swapped = [lax.ppermute(pieces[d], "fib", [(i, i ^ d) for i in range(fib_count)]) for d in range(1, fib_count)]
    return [pieces[0]] + swapped


def landed(refs, table):
    values, part, _ = refs[0].shape
    x = jnp.concatenate(
        [jnp.concatenate([ref[v] for ref in refs], 1) if len(refs) > 1 else refs[0][v] for v in range(values)], 0
    )
    moved = split_dot(x, table, NT)
    return [moved[v * part : (v + 1) * part] for v in range(values)]


def columns_of(table, which, pieces):
    lanes = table.shape[1] // pieces
    return jnp.concatenate([table[:, d * lanes : (d + 1) * lanes] for d in which], 1)


def early_kernel(moves, which, pieces, place_ref, slots_ref, *refs):
    *piece_refs, table_ref, sums_ref = refs
    write_recv_table(*moves, place_ref[0], slots_ref, table_ref)
    for v, moved in enumerate(landed(piece_refs, columns_of(table_ref[...], which, pieces))):
        sums_ref[v] = moved


def place_early(moves, which, place, slots, weight_pieces, fibres):
    fib_count, pack, per, _ = moves
    early = [weight_pieces[d] for d in which]
    values, part, _ = early[0].shape
    return pl.pallas_call(
        functools.partial(early_kernel, moves, which, len(weight_pieces)),
        in_specs=[in_smem] + [in_vmem] * (1 + len(early)),
        out_specs=[in_vmem] * 2,
        out_shape=[
            shaped((pack * fibres, fib_count * pack * per), BF16),
            shaped((values, part, pack * fibres)),
        ],
        compiler_params=params(),
        cost_estimate=cost(0, 0),
        name="place_early",
    )(place, slots, *early)


def last_kernel(pack, total, late, pieces, place_ref, table_ref, sums_ref, *refs):
    late_refs, refs = refs[: len(late)], refs[len(late) :]
    flux_refs, (flux_v, ivar_v, res_v) = refs[:pieces], refs[pieces:]
    table = table_ref[...]
    sums = [sums_ref[v] for v in range(2)]
    if late:
        sums = [x + y for x, y in zip(sums, landed(late_refs, columns_of(table, late, pieces)))]
    rows, fibres = ivar_v.shape
    part = rows // pack
    start = (place_ref[1] * 2 + place_ref[2]) * rows
    for h in range(pack):
        at = slice(h * part, (h + 1) * part)
        cut = slice(h * fibres, (h + 1) * fibres)
        row = start + h * part + lax.broadcasted_iota(jnp.int32, (part, 1), 0)
        weight, band = sums[0][:, cut], sums[1][:, cut]
        before = jnp.where(row == 0, 0.0, band)
        after = jnp.where(row == total - 1, 0.0, band)
        ivar_v[at, :] = weight
        res_v[0, at, :] = before
        res_v[1, at, :] = jnp.minimum(weight, 1.0) - before - after
        res_v[2, at, :] = after
    (flux,) = landed(flux_refs, table)
    for h in range(pack):
        flux_v[h * part : (h + 1) * part, :] = flux[:, h * fibres : (h + 1) * fibres]


def place_last(place, table, sums, late, weight_pieces, flux_pieces, pack, fibres, total):
    rows = flux_pieces[0].shape[1] * pack
    late_pieces = [weight_pieces[d] for d in late]
    args = (table, sums, *late_pieces, *flux_pieces)
    outs = [shaped((rows, fibres)), shaped((rows, fibres)), shaped((3, rows, fibres))]
    return pl.pallas_call(
        functools.partial(last_kernel, pack, total, late, len(flux_pieces)),
        in_specs=[in_smem] + [in_vmem] * len(args),
        out_specs=[in_vmem] * 3,
        out_shape=outs,
        compiler_params=params(),
        cost_estimate=cost(0, 0),
        name="place_last",
    )(place, *args)


def after(value, done):
    return lax.optimization_barrier((value, done))[0]


def per_device(pixels, pixel_ivar, clip_bits, coupling, counts, good_flags, owner_slot):
    expos, width, fibres = pixels.shape
    fib_count, wav_count = lax.axis_size("fib"), lax.axis_size("wav")
    total = width * wav_count
    per = fibres // fib_count
    rows = width // 2
    pack = max(1, LANES // per)
    while pack > 1 and rows % (pack * ROWS):
        pack //= 2
    rel = pack * per == LANES and fib_count & (fib_count - 1) == 0
    pieces = fib_count if rel else 1
    place = jnp.stack([lax.axis_index(axis) for axis in ("fib", "wav", "exp")]).astype(jnp.int32)
    coupling, counts, slots = coupling[None], counts[None], owner_slot[None]
    swap = [(0, 1), (1, 0)]
    moves = (fib_count, pack, per, rel)

    theirs, weight_t, send_table, slots, coupling, counts, good, bits, ivar = sent_weights(
        moves, wav_count, place, slots, coupling, counts, good_flags, clip_bits, pixel_ivar
    )
    arriving = lax.ppermute(theirs, "exp", swap)
    mine, weight_m, up, down = kept_weights(
        wav_count, place, coupling, counts, good, pixels, ivar, bits
    )
    upward = [(i, (i + 1) % wav_count) for i in range(wav_count)]
    left = lax.ppermute(up, "wav", upward)
    right = lax.ppermute(down, "wav", [(j, i) for i, j in upward])
    *sorted_pieces, scale = sort_fibres(arriving, mine, send_table, pack, pieces)
    weight_pieces = exchange(sorted_pieces, fib_count)

    pixel_s, ivar_s = stream_layout(left[0] + right[0], pixels, ivar)
    theirs, solved = flux_sums(wav_count, place, coupling, left, right, pixel_s, ivar_s, weight_t)
    late = [fib_count // 2] if rel else []
    early = [d for d in range(len(weight_pieces)) if d not in late]
    ahead = sum(weight_pieces[d][0, :ROWS, :] for d in early[1:] or early)
    arriving = lax.ppermute(theirs, "exp", swap)
    mine = kept_flux(after(place, theirs), coupling, solved, weight_m)
    sorted_pieces = sort_fibres(arriving, mine, send_table, pack, pieces, scale, ahead)
    flux_pieces = exchange(sorted_pieces, fib_count)
    recv_table, placed = place_early(moves, early, after(place, sorted_pieces[0]), slots, weight_pieces, fibres)
    return place_last(place, recv_table, placed, late, weight_pieces, flux_pieces, pack, fibres, total)


def solution(mesh):
    return jax.shard_map(
        per_device,
        mesh=mesh,
        in_specs=(
            P("exp", "wav", "fib"),
            P("exp", "wav", "fib"),
            P("exp", "wav", "fib"),
            P("fib"),
            P("fib"),
            P("exp", "fib"),
            P(),
        ),
        out_specs=(
            P(("wav", "exp"), "fib"),
            P(("wav", "exp"), "fib"),
            P(None, ("wav", "exp"), "fib"),
        ),
        check_vma=False,
    )
```

```python
import functools

import jax
import jax.numpy as jnp
from jax import lax
from jax.experimental import pallas as pl
from jax.experimental.pallas import tpu as pltpu
from jax.sharding import PartitionSpec as P

HALO = 50
BITS = 15
LANES = 128
ROWS = 8
GROUP = 120
VMEM_BYTES = 32 * 1024 * 1024
F32 = jnp.float32
BF16 = jnp.bfloat16
NT = (((1,), (1,)), ((), ()))

in_vmem = pl.BlockSpec(memory_space=pltpu.VMEM)
in_smem = pl.BlockSpec(memory_space=pltpu.SMEM)
in_hbm = pl.BlockSpec(memory_space=pltpu.HBM)


def params():
    return pltpu.CompilerParams(vmem_limit_bytes=VMEM_BYTES)


def cost(flops, moved):
    return pl.CostEstimate(flops=int(flops), bytes_accessed=int(moved), transcendentals=0)


def held_in_hbm(*arrays):
    return [pltpu.with_memory_space_constraint(array, pltpu.HBM) for array in arrays]


def shaped(shape, dtype=F32):
    return jax.ShapeDtypeStruct(shape, dtype)


def usable_rows(place_ref, counts_ref, good_ref):
    count = good_ref.shape[0]
    return [
        good_ref[e : e + 1, :].astype(F32)
        * jnp.where(place_ref[2] * count + e < counts_ref[...], 1.0, 0.0)
        for e in range(count)
    ]


def tile_bits(tile):
    first, last = (ROWS * tile) // BITS, (ROWS * tile + ROWS - 1) // BITS
    split = BITS * last - ROWS * tile
    row = lax.broadcasted_iota(jnp.int32, (ROWS, 1), 0)
    word = jnp.where(row >= split, last, first)
    return first, last, split, jnp.left_shift(1, ROWS * tile + row - BITS * word)


def tile_words(words, tile):
    first, last, split, mask = tile_bits(tile)
    picked = words[first : first + 1, :]
    if last != first:
        row = lax.broadcasted_iota(jnp.int32, (ROWS, 1), 0)
        picked = jnp.where(row >= split, words[last : last + 1, :], picked)
    return (picked & mask) != 0


def in_flight(pairs, sems, at=0):
    copies = [pltpu.make_async_copy(source, target, sems.at[at + i]) for i, (source, target) in enumerate(pairs)]
    for copy in copies:
        copy.start()
    return copies


def inverse_of(x):
    guess = pl.reciprocal(x, approx=True)
    return guess * (2.0 - x * guess)


def advance(state, ivar, pixel, back_coupling):
    n, d, b = state
    ratio = ivar * back_coupling
    next_d = d + n
    return (n * (1.0 + ratio) + ratio * d, next_d, b + (ivar * pixel) * next_d)


def rescaled(state):
    scale = inverse_of(state[1])
    return tuple(part * scale for part in state)


def odd(rows):
    return rows + 1 - rows % 2


def divisor_of(size, most):
    return max(k for k in range(1, most + 1) if size % k == 0)


def owners(slots_ref, fib_count, fibres):
    rows = [slots_ref[:, s * fibres : (s + 1) * fibres].astype(F32) for s in range(fib_count)]
    sources = -(-fib_count // ROWS) * ROWS
    if sources > fib_count:
        rows.append(jnp.full((sources - fib_count, fibres), -1.0, F32))
    slots = jnp.concatenate(rows, 0)
    owner = jnp.floor((slots + 0.5) * (1.0 / fibres))
    return owner, slots - owner * fibres


def earlier_fibres(fibres):
    row = lax.broadcasted_iota(jnp.int32, (fibres, fibres), 0)
    col = lax.broadcasted_iota(jnp.int32, (fibres, fibres), 1)
    return (row < col).astype(F32).astype(BF16)


def write_send_table(fib_count, pack, per, rel, me, slots_ref, table_ref):
    fibres = table_ref.shape[1] // pack
    lanes = pack * per
    owner, _ = owners(slots_ref, fib_count, fibres)
    source = lax.broadcasted_iota(jnp.int32, owner.shape, 0)
    my_owner = jnp.sum(jnp.where(source == me, owner, 0.0), axis=0, keepdims=True).astype(jnp.int32)
    to_owner = (source == my_owner).astype(F32)
    counted = jnp.dot(to_owner.astype(BF16), earlier_fibres(fibres), preferred_element_type=F32)
    rank = jnp.sum(to_owner * counted, axis=0, keepdims=True).astype(jnp.int32)
    target = my_owner
    if rel:
        target = jnp.where(my_owner >= me, my_owner - me, my_owner - me + fib_count)
    base = target * lanes + rank
    place_of = jnp.concatenate([base + h * per for h in range(pack)], 1)
    row = lax.broadcasted_iota(jnp.int32, table_ref.shape, 0)
    table_ref[...] = (row == place_of).astype(F32).astype(BF16)


def write_recv_table(fib_count, pack, per, rel, me, slots_ref, table_ref):
    fibres = table_ref.shape[0] // pack
    lanes = pack * per
    total_lanes = fib_count * lanes
    owner, column = owners(slots_ref, fib_count, fibres)
    source = lax.broadcasted_iota(jnp.int32, owner.shape, 0)
    mine = (owner == me.astype(F32)).astype(F32)
    rank_in = jnp.dot(mine.astype(BF16), earlier_fibres(fibres), preferred_element_type=F32).astype(jnp.int32)
    order = source
    if rel:
        order = jnp.where(me >= source, me - source, me - source + fib_count)
    arrival = jnp.where(mine > 0.0, order * lanes + rank_in, -total_lanes)
    tall = lax.broadcasted_iota(jnp.int32, (total_lanes, fibres), 0)
    landing = jnp.zeros((ROWS, total_lanes), F32)
    for s in range(fib_count):
        hit = tall == arrival[s : s + 1, :]
        for h in range(1, pack):
            hit = hit | (tall == arrival[s : s + 1, :] + h * per)
        values = jnp.broadcast_to(column[s : s + 1, :], (ROWS, fibres)).astype(BF16)
        landing = landing + lax.dot_general(
            values, hit.astype(F32).astype(BF16), NT, preferred_element_type=F32
        )
    lane = lax.broadcasted_iota(jnp.int32, (1, total_lanes), 1)
    landing = landing[0:1, :].astype(jnp.int32)
    for h in range(1, pack):
        inside = (lane % lanes >= h * per) & (lane % lanes < (h + 1) * per)
        landing = jnp.where(inside, landing + h * fibres, landing)
    row = lax.broadcasted_iota(jnp.int32, table_ref.shape, 0)
    table_ref[...] = (row == landing).astype(F32).astype(BF16)


def stream_coupling(coupling_ref, expos):
    coupling = coupling_ref[...]
    blocks = coupling.shape[1] // LANES
    return jnp.concatenate(
        [jnp.broadcast_to(coupling[:, h * LANES : (h + 1) * LANES], (expos, LANES)) for h in range(blocks)], 0
    )


def weight_tile(coupling, usable, words, ivars, within, scale_row):
    links = scale_row * coupling
    weights = []
    weight_sum = band_sum = None
    for e, ivar in enumerate(ivars):
        weight = jnp.where(tile_words(words[e], within), ivar * usable[e], 0.0)
        band = weight * inverse_of(ivar + links)
        weights.append(weight)
        weight_sum = weight if e == 0 else weight_sum + weight
        band_sum = band if e == 0 else band_sum + band
    return weights, weight_sum, band_sum * coupling


def write_weights(place_ref, wav_count, which, coupling_v, counts_v, good_v, ivar_of, words_of, sums_ref, weight_ref, beside):
    expos, half, _ = weight_ref.shape
    coupling = coupling_v[...]
    usable = usable_rows(place_ref, counts_v, good_v)
    start = place_ref[1] * (2 * half) + which * half
    tiles = half // ROWS
    tiles_in_group = GROUP // ROWS
    for tile in range(tiles):
        beside(tile, tiles)
        group, within = divmod(tile, tiles_in_group)
        scale_row = 4.0
        if tile in (0, tiles - 1):
            row = start + ROWS * tile + lax.broadcasted_iota(jnp.int32, (ROWS, 1), 0)
            scale_row = jnp.where((row == 0) | (row == wav_count * 2 * half - 1), 2.0, 4.0)
        at = slice(ROWS * tile, ROWS * (tile + 1))
        weights, weight_sum, band_sum = weight_tile(
            coupling,
            usable,
            [words_of(e, group) for e in range(expos)],
            [ivar_of(e, tile) for e in range(expos)],
            within,
            scale_row,
        )
        for e in range(expos):
            weight_ref[e, at, :] = weights[e]
        sums_ref[0, at, :] = weight_sum
        sums_ref[1, at, :] = band_sum


def sent_kernel(
    moves, wav_count, place_ref, slots_ref, coupling_ref, counts_ref, good_ref, bits_ref, ivar_ref,
    sums_ref, weight_ref, table_ref, slots_v, coupling_v, counts_v, good_v, bits_v, ivar_v, sems,
):
    expos, width, _ = ivar_ref.shape
    half = width // 2
    which = 1 - place_ref[2]
    words = GROUP // BITS

    def part(source, target, first):
        at = pl.ds(pl.multiple_of(first, ROWS), GROUP)
        return source.at[:, at, :], target.at[:, at, :]

    waits = in_flight(
        [
            (slots_ref, slots_v),
            (coupling_ref, coupling_v),
            (counts_ref, counts_v),
            (good_ref, good_v),
            (bits_ref, bits_v),
        ]
        + [part(ivar_ref, ivar_v, which * half + g) for g in range(0, half, GROUP)]
        + [part(ivar_ref, ivar_v, (1 - which) * half + g) for g in range(0, half, GROUP)],
        sems,
    )
    waits[0].wait()
    write_send_table(*moves, place_ref[0], slots_v, table_ref)
    for wait in waits[1:5]:
        wait.wait()

    def arrive(tile, tiles):
        if ROWS * tile % GROUP == 0:
            waits[5 + ROWS * tile // GROUP].wait()

    write_weights(
        place_ref, wav_count, which, coupling_v, counts_v, good_v,
        lambda e, tile: ivar_v[e, pl.ds(pl.multiple_of(which * half + ROWS * tile, ROWS), ROWS), :],
        lambda e, group: bits_v[e, pl.ds(pl.multiple_of(which * (half // BITS) + words * group, words), words), :],
        sums_ref, weight_ref, arrive,
    )
    for wait in waits[5 + half // GROUP :]:
        wait.wait()


def sent_weights(moves, wav_count, place, slots, coupling, counts, good, bits, ivar):
    expos, width, fibres = ivar.shape
    half = width // 2
    fib_count, pack, per, _ = moves
    inputs = (slots, coupling, counts, good, bits, ivar)
    return pl.pallas_call(
        functools.partial(sent_kernel, moves, wav_count),
        in_specs=[in_smem] + [in_hbm] * 6,
        out_specs=[in_vmem] * 9,
        out_shape=[
            shaped((2, half, fibres)),
            shaped((expos, half, fibres)),
            shaped((fib_count * pack * per, pack * fibres), BF16),
        ]
        + [shaped(x.shape, x.dtype) for x in inputs],
        scratch_shapes=[pltpu.SemaphoreType.DMA((5 + width // GROUP,))],
        compiler_params=params(),
        cost_estimate=cost(20 * ivar.size, 6 * ivar.size),
        name="sent_weights",
    )(place, *held_in_hbm(*inputs))


def lay_out(source_ref, target_ref, pieces, pitch):
    expos, _, fibres = source_ref.shape
    for h in range(fibres // LANES):
        for e in range(expos):
            for first, length, at in pieces:
                target_ref[pl.ds((h * expos + e) * pitch + at, length), :] = source_ref[
                    e, pl.ds(first, length), pl.ds(h * LANES, LANES)
                ]


def kept_kernel(
    wav_count, place_ref, coupling_ref, counts_ref, good_ref, pixels_ref, ivar_ref, bits_ref,
    sums_ref, weight_ref, edges_ref, ivar_s, pixel_s,
):
    expos, width, fibres = ivar_ref.shape
    half = width // 2
    streams = expos * fibres // LANES
    count = -(-HALO // ROWS) * ROWS
    pitch = odd(2 * count)
    which = place_ref[2]
    words = GROUP // BITS
    edges = [(0, count, 0), (width - count, count, count)]
    lay_out(ivar_ref, ivar_s, edges, pitch)
    lay_out(pixels_ref, pixel_s, edges, pitch)
    coupling = stream_coupling(coupling_ref, expos)
    back = 1.0 / coupling
    zero = jnp.zeros((streams, LANES), F32)
    states = [(zero, zero + 1.0, zero), (zero, zero + 1.0, zero)]

    def eliminate(tile, tiles):
        for i in range(HALO * tile // tiles, HALO * (tile + 1) // tiles):
            for side, row in enumerate((2 * count - HALO + i, HALO - 1 - i)):
                at = pl.ds(row, streams, stride=pitch)
                states[side] = advance(states[side], ivar_s[at, :], pixel_s[at, :], back)
                if i % 24 == 23:
                    states[side] = rescaled(states[side])

    write_weights(
        place_ref, wav_count, which, coupling_ref, counts_ref, good_ref,
        lambda e, tile: ivar_ref[e, pl.ds(pl.multiple_of(which * half + ROWS * tile, ROWS), ROWS), :],
        lambda e, group: bits_ref[e, pl.ds(pl.multiple_of(which * (half // BITS) + words * group, words), words), :],
        sums_ref, weight_ref, eliminate,
    )
    ends = []
    for n, d, b in states:
        scale = 1.0 / (d + n)
        ends.append((coupling * (n * scale), b * scale))
    for other in range(wav_count):
        for value in range(2):
            edges_ref[other, value] = jnp.where(place_ref[1] < other, ends[0][value], ends[1][value])


def kept_weights(wav_count, place, coupling, counts, good, pixels, ivar, bits):
    expos, width, fibres = ivar.shape
    half = width // 2
    streams = expos * fibres // LANES
    count = -(-HALO // ROWS) * ROWS
    edge_scratch = pltpu.VMEM((streams * odd(2 * count), LANES), F32)
    return pl.pallas_call(
        functools.partial(kept_kernel, wav_count),
        in_specs=[in_smem] + [in_vmem] * 6,
        out_specs=[in_vmem] * 3,
        out_shape=[
            shaped((2, half, fibres)),
            shaped((expos, half, fibres)),
            shaped((wav_count, 2, streams, LANES)),
        ],
        scratch_shapes=[edge_scratch, edge_scratch],
        compiler_params=params(),
        cost_estimate=cost(20 * ivar.size, 6 * ivar.size),
        name="kept_weights",
    )(place, coupling, counts, good, pixels, ivar, bits)


def layout_kernel(arrived_ref, pixels_ref, ivar_ref, pixel_out, ivar_out):
    width = ivar_ref.shape[1]
    lay_out(ivar_ref, ivar_out, [(0, width, 0)], odd(width))
    lay_out(pixels_ref, pixel_out, [(0, width, 0)], odd(width))


def stream_layout(arrived, pixels, ivar):
    expos, width, fibres = ivar.shape
    streams = expos * fibres // LANES
    laid = shaped((streams * odd(width), LANES))
    return pl.pallas_call(
        layout_kernel,
        in_specs=[in_vmem] * 3,
        out_specs=[in_vmem] * 2,
        out_shape=[laid, laid],
        compiler_params=params(),
        cost_estimate=cost(0, 16 * ivar.size),
        name="stream_layout",
    )(arrived, pixels, ivar)


def solve_kernel(
    wav_count, place_ref, coupling_ref, edges_ref, pixel_ref, ivar_ref, weight_ref,
    theirs_ref, solved_s, lead_s, rest_s,
):
    streams = edges_ref.shape[2]
    expos, half, fibres = weight_ref.shape
    width = 2 * half
    pitch = odd(width)
    middle = half
    coupling = stream_coupling(coupling_ref, expos)
    back = 1.0 / coupling

    def row_at(i):
        return pl.ds(i, streams, stride=pitch)

    def begin(neighbour):
        there = (neighbour >= 0) & (neighbour < wav_count)
        at = jnp.clip(neighbour, 0, wav_count - 1)
        n = jnp.where(there, edges_ref[at, 0], 0.0) * back
        return (n, 1.0 - n, jnp.where(there, edges_ref[at, 1], 0.0))

    def keep(side, i, state):
        n, d, b = state
        inverse = inverse_of(d + n)
        lead_s[side, i] = d * inverse
        rest_s[side, i] = b * inverse

    unrolled = divisor_of(middle, 24)

    def eliminate(it, states):
        states = list(states)
        for k in range(unrolled):
            i = it * unrolled + k
            for side, row in enumerate((i, width - 1 - i)):
                keep(side, i, states[side])
                states[side] = advance(states[side], ivar_ref[row_at(row), :], pixel_ref[row_at(row), :], back)
        return tuple(rescaled(state) for state in states)

    states = lax.fori_loop(0, middle // unrolled, eliminate, (begin(place_ref[1] - 1), begin(place_ref[1] + 1)))
    for side in range(2):
        keep(side, middle, states[side])
    lead, rest = lead_s[0, middle], rest_s[0, middle]
    lead_r, rest_r = lead_s[1, middle], rest_s[1, middle]
    left = (rest + lead * rest_r) / (1.0 - lead * lead_r)
    right = rest_r + lead_r * left
    several = divisor_of(middle, 48)

    def after_both(near, far):
        return far[0] * near[0], far[1] + far[0] * near[1]

    def step(factors, value):
        return factors[1] + factors[0] * value

    def substitute(it, values):
        values = list(values)
        for k in range(0, several, 4):
            for side in range(2):
                rows = [middle - 1 - (it * several + k + m) for m in range(4)]
                one, two, three, four = [(lead_s[side, i], rest_s[side, i]) for i in rows]
                first_two = after_both(one, two)
                all_four = after_both(first_two, after_both(three, four))
                value = values[side]
                third = step(first_two, value)
                solved = [value, step(one, value), third, step(three, third)]
                values[side] = step(all_four, value)
                for i, x in zip(rows, solved):
                    solved_s[row_at(i if side == 0 else width - 1 - i), :] = x
        return tuple(values)

    lax.fori_loop(0, middle // several, substitute, (left, right))

    add_up(theirs_ref, weight_ref, solved_s, coupling_ref, 1 - place_ref[2])


def add_up(out_ref, weight_ref, solved_ref, coupling_ref, which):
    expos, half, fibres = weight_ref.shape
    pitch = odd(2 * half)
    start = which * half
    back = 1.0 / coupling_ref[...]
    unrolled = divisor_of(half // ROWS, 5)

    def body(g, carry):
        for k in range(unrolled):
            row = pl.multiple_of((g * unrolled + k) * ROWS, ROWS)
            for h in range(fibres // LANES):
                total = None
                for e in range(expos):
                    at = pl.ds((h * expos + e) * pitch + start + row, ROWS)
                    term = weight_ref[e, pl.ds(row, ROWS), pl.ds(h * LANES, LANES)] * solved_ref[at, :]
                    total = term if e == 0 else total + term
                out_ref[0, pl.ds(row, ROWS), pl.ds(h * LANES, LANES)] = total * back[:, h * LANES : (h + 1) * LANES]
        return carry

    lax.fori_loop(0, half // ROWS // unrolled, body, 0)


def flux_sums(wav_count, place, coupling, edges, pixels, ivar, weight):
    expos, half, fibres = weight.shape
    streams = edges.shape[2]
    factor_scratch = pltpu.VMEM((2, half + 1, streams, LANES), F32)
    return pl.pallas_call(
        functools.partial(solve_kernel, wav_count),
        in_specs=[in_smem] + [in_vmem] * 5,
        out_specs=[in_vmem, in_vmem],
        out_shape=[shaped((1, half, fibres)), shaped(pixels.shape)],
        scratch_shapes=[factor_scratch, factor_scratch],
        compiler_params=params(),
        cost_estimate=cost(0, 0),
        name="flux_sums",
    )(place, coupling, edges, pixels, ivar, weight)


def kept_flux_kernel(place_ref, coupling_ref, solved_ref, weight_ref, out_ref):
    add_up(out_ref, weight_ref, solved_ref, coupling_ref, place_ref[2])


def kept_flux(place, coupling, solved, weight):
    expos, half, fibres = weight.shape
    return pl.pallas_call(
        kept_flux_kernel,
        in_specs=[in_smem] + [in_vmem] * 3,
        out_specs=in_vmem,
        out_shape=shaped((1, half, fibres)),
        compiler_params=params(),
        cost_estimate=cost(2 * weight.size, 8 * weight.size),
        name="kept_flux",
    )(place, coupling, solved, weight)


def split_dot(x, table, dims):
    top = x.astype(BF16)
    low = (x - top.astype(F32)).astype(BF16)
    both = lax.dot_general(jnp.concatenate([top, low], 0), table, dims, preferred_element_type=F32)
    return both[: x.shape[0]] + both[x.shape[0] :]


def sort_kernel(pack, scaled, theirs_ref, mine_ref, table_ref, *refs):
    values, rows, _ = mine_ref.shape
    part = rows // pack
    totals = [mine_ref[v] + theirs_ref[v] for v in range(values)]
    if scaled:
        scale_ref, _, *out_refs = refs
        totals = [t * scale_ref[...] for t in totals]
    else:
        *out_refs, scale_ref = refs
        scale = 1.0 / jnp.maximum(totals[0], 1.0)
        scale_ref[...] = scale
        totals[1] = totals[1] * scale
    x = jnp.concatenate(
        [jnp.concatenate([t[h * part : (h + 1) * part] for h in range(pack)], 1) for t in totals], 0
    )
    moved = split_dot(x, table_ref[...], NT)
    lanes = moved.shape[1] // len(out_refs)
    for d, out_ref in enumerate(out_refs):
        for v in range(values):
            out_ref[v] = moved[v * part : (v + 1) * part, d * lanes : (d + 1) * lanes]


def sort_fibres(theirs, mine, table, pack, pieces, scale=None, ahead=None):
    values, rows, fibres = mine.shape
    lanes = table.shape[0] // pieces
    scaled = scale is not None
    outs = [shaped((values, rows // pack, lanes))] * pieces + ([] if scaled else [shaped((rows, fibres))])
    args = (theirs, mine, table) + ((scale, ahead) if scaled else ())
    return pl.pallas_call(
        functools.partial(sort_kernel, pack, scaled),
        in_specs=[in_vmem] * len(args),
        out_specs=[in_vmem] * len(outs),
        out_shape=outs,
        compiler_params=params(),
        cost_estimate=cost(0, 0),
        name="sort_flux" if scaled else "sort_weights",
    )(*args)


def exchange(pieces, fib_count):
    if len(pieces) == 1:
        return [lax.all_to_all(pieces[0], "fib", split_axis=2, concat_axis=2, tiled=True)]
    arrived = [pieces[0]]
    for d in range(1, fib_count):
        arrived.append(lax.ppermute(pieces[d], "fib", [(i, (i + d) % fib_count) for i in range(fib_count)]))
    return arrived


def landed(refs, table):
    values, part, _ = refs[0].shape
    x = jnp.concatenate(
        [jnp.concatenate([ref[v] for ref in refs], 1) if len(refs) > 1 else refs[0][v] for v in range(values)], 0
    )
    moved = split_dot(x, table, NT)
    return [moved[v * part : (v + 1) * part] for v in range(values)]


def columns_of(table, which, pieces):
    lanes = table.shape[1] // pieces
    return jnp.concatenate([table[:, d * lanes : (d + 1) * lanes] for d in which], 1)


def early_kernel(moves, which, pieces, place_ref, slots_ref, *refs):
    *piece_refs, table_ref, sums_ref = refs
    write_recv_table(*moves, place_ref[0], slots_ref, table_ref)
    for v, moved in enumerate(landed(piece_refs, columns_of(table_ref[...], which, pieces))):
        sums_ref[v] = moved


def place_early(moves, which, place, slots, weight_pieces, fibres):
    fib_count, pack, per, _ = moves
    early = [weight_pieces[d] for d in which]
    values, part, _ = early[0].shape
    return pl.pallas_call(
        functools.partial(early_kernel, moves, which, len(weight_pieces)),
        in_specs=[in_smem] + [in_vmem] * (1 + len(early)),
        out_specs=[in_vmem] * 2,
        out_shape=[
            shaped((pack * fibres, fib_count * pack * per), BF16),
            shaped((values, part, pack * fibres)),
        ],
        compiler_params=params(),
        cost_estimate=cost(0, 0),
        name="place_early",
    )(place, slots, *early)


def weights_end_kernel(pack, total, late, pieces, place_ref, table_ref, sums_ref, *refs):
    *late_refs, ivar_ref, res_ref = refs
    weight, band = sums_ref[0], sums_ref[1]
    if late:
        more_weight, more_band = landed(late_refs, columns_of(table_ref[...], late, pieces))
        weight, band = weight + more_weight, band + more_band
    rows, fibres = ivar_ref.shape
    part = rows // pack
    start = (place_ref[1] * 2 + place_ref[2]) * rows
    for h in range(pack):
        at = slice(h * part, (h + 1) * part)
        cut = slice(h * fibres, (h + 1) * fibres)
        row = start + h * part + lax.broadcasted_iota(jnp.int32, (part, 1), 0)
        w, b = weight[:, cut], band[:, cut]
        before = jnp.where(row == 0, 0.0, b)
        after = jnp.where(row == total - 1, 0.0, b)
        ivar_ref[at, :] = w
        res_ref[0, at, :] = before
        res_ref[1, at, :] = jnp.minimum(w, 1.0) - before - after
        res_ref[2, at, :] = after


def end_weights(place, table, sums, late, weight_pieces, pack, fibres, total):
    rows = sums.shape[1] * pack
    late_pieces = [weight_pieces[d] for d in late]
    return pl.pallas_call(
        functools.partial(weights_end_kernel, pack, total, late, len(weight_pieces)),
        in_specs=[in_smem] + [in_vmem] * (2 + len(late)),
        out_specs=[in_vmem] * 2,
        out_shape=[shaped((rows, fibres)), shaped((3, rows, fibres))],
        compiler_params=params(),
        cost_estimate=cost(0, 0),
        name="end_weights",
    )(place, table, sums, *late_pieces)


def flux_end_kernel(pack, table_ref, *refs):
    *piece_refs, flux_ref = refs
    (flux,) = landed(piece_refs, table_ref[...])
    rows, fibres = flux_ref.shape
    part = rows // pack
    for h in range(pack):
        flux_ref[h * part : (h + 1) * part, :] = flux[:, h * fibres : (h + 1) * fibres]


def end_flux(table, pieces, pack, fibres):
    rows = pieces[0].shape[1] * pack
    return pl.pallas_call(
        functools.partial(flux_end_kernel, pack),
        in_specs=[in_vmem] * (1 + len(pieces)),
        out_specs=in_vmem,
        out_shape=shaped((rows, fibres)),
        compiler_params=params(),
        cost_estimate=cost(2 * rows * table.size, 2 * rows * fibres * 4),
        name="end_flux",
    )(table, *pieces)


def after(value, done):
    return lax.optimization_barrier((value, done))[0]


def per_device(pixels, pixel_ivar, clip_bits, coupling, counts, good_flags, owner_slot):
    expos, width, fibres = pixels.shape
    fib_count, wav_count = lax.axis_size("fib"), lax.axis_size("wav")
    total = width * wav_count
    per = fibres // fib_count
    rows = width // 2
    pack = max(1, LANES // per)
    while pack > 1 and rows % (pack * ROWS):
        pack //= 2
    rel = pack * per == LANES
    pieces = fib_count if rel else 1
    place = jnp.stack([lax.axis_index(axis) for axis in ("fib", "wav", "exp")]).astype(jnp.int32)
    coupling, counts, slots = coupling[None], counts[None], owner_slot[None]
    swap = [(0, 1), (1, 0)]
    moves = (fib_count, pack, per, rel)

    theirs, weight_t, send_table, slots, coupling, counts, good, bits, ivar = sent_weights(
        moves, wav_count, place, slots, coupling, counts, good_flags, clip_bits, pixel_ivar
    )
    arriving = lax.ppermute(theirs, "exp", swap)
    mine, weight_m, edges = kept_weights(
        wav_count, place, coupling, counts, good, pixels, ivar, bits
    )
    edges = lax.all_to_all(edges, "wav", split_axis=0, concat_axis=0, tiled=True)
    *sorted_pieces, scale = sort_fibres(arriving, mine, send_table, pack, pieces)
    weight_pieces = exchange(sorted_pieces, fib_count)

    pixel_s, ivar_s = stream_layout(edges[0, 0] + edges[-1, 0], pixels, ivar)
    theirs, solved = flux_sums(wav_count, place, coupling, edges, pixel_s, ivar_s, weight_t)
    late = [fib_count // 2] if rel else []
    early = [d for d in range(len(weight_pieces)) if d not in late]
    ahead = sum(weight_pieces[d][0, :ROWS, :] for d in early[1:] or early)
    arriving = lax.ppermute(theirs, "exp", swap)
    mine = kept_flux(after(place, theirs), coupling, solved, weight_m)
    sorted_pieces = sort_fibres(arriving, mine, send_table, pack, pieces, scale, ahead)
    flux_pieces = exchange(sorted_pieces, fib_count)
    recv_table, placed = place_early(moves, early, after(place, sorted_pieces[0]), slots, weight_pieces, fibres)
    ivar, res = end_weights(place, recv_table, placed, late, weight_pieces, pack, fibres, total)
    flux = end_flux(recv_table, flux_pieces, pack, fibres)
    return (flux, ivar, res)


def solution(mesh):
    return jax.shard_map(
        per_device,
        mesh=mesh,
        in_specs=(
            P("exp", "wav", "fib"),
            P("exp", "wav", "fib"),
            P("exp", "wav", "fib"),
            P("fib"),
            P("fib"),
            P("exp", "fib"),
            P(),
        ),
        out_specs=(
            P(("wav", "exp"), "fib"),
            P(("wav", "exp"), "fib"),
            P(None, ("wav", "exp"), "fib"),
        ),
        check_vma=False,
    )
```

```python
import functools

import jax
import jax.numpy as jnp
from jax import lax
from jax.experimental import pallas as pl
from jax.experimental.pallas import tpu as pltpu
from jax.sharding import PartitionSpec as P

HALO = 50
BITS = 15
LANES = 128
ROWS = 8
GROUP = 120
VMEM_BYTES = 32 * 1024 * 1024
F32 = jnp.float32
BF16 = jnp.bfloat16
NT = (((1,), (1,)), ((), ()))

in_vmem = pl.BlockSpec(memory_space=pltpu.VMEM)
in_smem = pl.BlockSpec(memory_space=pltpu.SMEM)
in_hbm = pl.BlockSpec(memory_space=pltpu.HBM)


def params():
    return pltpu.CompilerParams(vmem_limit_bytes=VMEM_BYTES)


def cost(flops, moved):
    return pl.CostEstimate(flops=int(flops), bytes_accessed=int(moved), transcendentals=0)


def held_in_hbm(*arrays):
    return [pltpu.with_memory_space_constraint(array, pltpu.HBM) for array in arrays]


def shaped(shape, dtype=F32):
    return jax.ShapeDtypeStruct(shape, dtype)


def usable_rows(place_ref, counts_ref, good_ref):
    count = good_ref.shape[0]
    return [
        good_ref[e : e + 1, :].astype(F32)
        * jnp.where(place_ref[2] * count + e < counts_ref[...], 1.0, 0.0)
        for e in range(count)
    ]


def tile_bits(tile):
    first, last = (ROWS * tile) // BITS, (ROWS * tile + ROWS - 1) // BITS
    split = BITS * last - ROWS * tile
    row = lax.broadcasted_iota(jnp.int32, (ROWS, 1), 0)
    word = jnp.where(row >= split, last, first)
    return first, last, split, jnp.left_shift(1, ROWS * tile + row - BITS * word)


def tile_words(words, tile):
    first, last, split, mask = tile_bits(tile)
    picked = words[first : first + 1, :]
    if last != first:
        row = lax.broadcasted_iota(jnp.int32, (ROWS, 1), 0)
        picked = jnp.where(row >= split, words[last : last + 1, :], picked)
    return (picked & mask) != 0


def in_flight(pairs, sems, at=0):
    copies = [pltpu.make_async_copy(source, target, sems.at[at + i]) for i, (source, target) in enumerate(pairs)]
    for copy in copies:
        copy.start()
    return copies


def inverse_of(x):
    guess = pl.reciprocal(x, approx=True)
    return guess * (2.0 - x * guess)


def advance(state, ivar, pixel, back_coupling):
    n, d, b = state
    ratio = ivar * back_coupling
    next_d = d + n
    return (n * (1.0 + ratio) + ratio * d, next_d, b + (ivar * pixel) * next_d)


def rescaled(state):
    scale = inverse_of(state[1])
    return tuple(part * scale for part in state)


def odd(rows):
    return rows + 1 - rows % 2


def divisor_of(size, most):
    return max(k for k in range(1, most + 1) if size % k == 0)


def owners(slots_ref, fib_count, fibres):
    rows = [slots_ref[:, s * fibres : (s + 1) * fibres].astype(F32) for s in range(fib_count)]
    sources = -(-fib_count // ROWS) * ROWS
    if sources > fib_count:
        rows.append(jnp.full((sources - fib_count, fibres), -1.0, F32))
    slots = jnp.concatenate(rows, 0)
    owner = jnp.floor((slots + 0.5) * (1.0 / fibres))
    return owner, slots - owner * fibres


def earlier_fibres(fibres):
    row = lax.broadcasted_iota(jnp.int32, (fibres, fibres), 0)
    col = lax.broadcasted_iota(jnp.int32, (fibres, fibres), 1)
    return (row < col).astype(F32).astype(BF16)


def write_send_table(fib_count, pack, per, rel, me, slots_ref, table_ref):
    fibres = table_ref.shape[1] // pack
    lanes = pack * per
    owner, _ = owners(slots_ref, fib_count, fibres)
    source = lax.broadcasted_iota(jnp.int32, owner.shape, 0)
    my_owner = jnp.sum(jnp.where(source == me, owner, 0.0), axis=0, keepdims=True).astype(jnp.int32)
    to_owner = (source == my_owner).astype(F32)
    counted = jnp.dot(to_owner.astype(BF16), earlier_fibres(fibres), preferred_element_type=F32)
    rank = jnp.sum(to_owner * counted, axis=0, keepdims=True).astype(jnp.int32)
    target = my_owner
    if rel:
        target = jnp.where(my_owner >= me, my_owner - me, my_owner - me + fib_count)
    base = target * lanes + rank
    place_of = jnp.concatenate([base + h * per for h in range(pack)], 1)
    row = lax.broadcasted_iota(jnp.int32, table_ref.shape, 0)
    table_ref[...] = (row == place_of).astype(F32).astype(BF16)


def write_recv_table(fib_count, pack, per, rel, me, slots_ref, table_ref):
    fibres = table_ref.shape[0] // pack
    lanes = pack * per
    total_lanes = fib_count * lanes
    owner, column = owners(slots_ref, fib_count, fibres)
    source = lax.broadcasted_iota(jnp.int32, owner.shape, 0)
    mine = (owner == me.astype(F32)).astype(F32)
    rank_in = jnp.dot(mine.astype(BF16), earlier_fibres(fibres), preferred_element_type=F32).astype(jnp.int32)
    order = source
    if rel:
        order = jnp.where(me >= source, me - source, me - source + fib_count)
    arrival = jnp.where(mine > 0.0, order * lanes + rank_in, -total_lanes)
    tall = lax.broadcasted_iota(jnp.int32, (total_lanes, fibres), 0)
    landing = jnp.zeros((ROWS, total_lanes), F32)
    for s in range(fib_count):
        hit = tall == arrival[s : s + 1, :]
        for h in range(1, pack):
            hit = hit | (tall == arrival[s : s + 1, :] + h * per)
        values = jnp.broadcast_to(column[s : s + 1, :], (ROWS, fibres)).astype(BF16)
        landing = landing + lax.dot_general(
            values, hit.astype(F32).astype(BF16), NT, preferred_element_type=F32
        )
    lane = lax.broadcasted_iota(jnp.int32, (1, total_lanes), 1)
    landing = landing[0:1, :].astype(jnp.int32)
    for h in range(1, pack):
        inside = (lane % lanes >= h * per) & (lane % lanes < (h + 1) * per)
        landing = jnp.where(inside, landing + h * fibres, landing)
    row = lax.broadcasted_iota(jnp.int32, table_ref.shape, 0)
    table_ref[...] = (row == landing).astype(F32).astype(BF16)


def stream_coupling(coupling_ref, expos):
    coupling = coupling_ref[...]
    blocks = coupling.shape[1] // LANES
    return jnp.concatenate(
        [jnp.broadcast_to(coupling[:, h * LANES : (h + 1) * LANES], (expos, LANES)) for h in range(blocks)], 0
    )


def weight_tile(coupling, usable, words, ivars, within, scale_row):
    links = scale_row * coupling
    weights = []
    weight_sum = band_sum = None
    for e, ivar in enumerate(ivars):
        weight = jnp.where(tile_words(words[e], within), ivar * usable[e], 0.0)
        band = weight * inverse_of(ivar + links)
        weights.append(weight)
        weight_sum = weight if e == 0 else weight_sum + weight
        band_sum = band if e == 0 else band_sum + band
    return weights, weight_sum, band_sum * coupling


def write_weights(place_ref, wav_count, which, coupling_v, counts_v, good_v, ivar_of, words_of, sums_ref, weight_ref, beside):
    expos, half, _ = weight_ref.shape
    coupling = coupling_v[...]
    usable = usable_rows(place_ref, counts_v, good_v)
    start = place_ref[1] * (2 * half) + which * half
    tiles = half // ROWS
    tiles_in_group = GROUP // ROWS
    for tile in range(tiles):
        beside(tile, tiles)
        group, within = divmod(tile, tiles_in_group)
        scale_row = 4.0
        if tile in (0, tiles - 1):
            row = start + ROWS * tile + lax.broadcasted_iota(jnp.int32, (ROWS, 1), 0)
            scale_row = jnp.where((row == 0) | (row == wav_count * 2 * half - 1), 2.0, 4.0)
        at = slice(ROWS * tile, ROWS * (tile + 1))
        weights, weight_sum, band_sum = weight_tile(
            coupling,
            usable,
            [words_of(e, group) for e in range(expos)],
            [ivar_of(e, tile) for e in range(expos)],
            within,
            scale_row,
        )
        for e in range(expos):
            weight_ref[e, at, :] = weights[e]
        sums_ref[0, at, :] = weight_sum
        sums_ref[1, at, :] = band_sum


def sent_kernel(
    moves, wav_count, place_ref, slots_ref, coupling_ref, counts_ref, good_ref, bits_ref, ivar_ref,
    sums_ref, weight_ref, table_ref, slots_v, coupling_v, counts_v, good_v, bits_v, ivar_v, sems,
):
    expos, width, _ = ivar_ref.shape
    half = width // 2
    which = 1 - place_ref[2]
    words = GROUP // BITS

    def part(source, target, first):
        at = pl.ds(pl.multiple_of(first, ROWS), GROUP)
        return source.at[:, at, :], target.at[:, at, :]

    waits = in_flight(
        [
            (slots_ref, slots_v),
            (coupling_ref, coupling_v),
            (counts_ref, counts_v),
            (good_ref, good_v),
            (bits_ref, bits_v),
        ]
        + [part(ivar_ref, ivar_v, which * half + g) for g in range(0, half, GROUP)]
        + [part(ivar_ref, ivar_v, (1 - which) * half + g) for g in range(0, half, GROUP)],
        sems,
    )
    waits[0].wait()
    write_send_table(*moves, place_ref[0], slots_v, table_ref)
    for wait in waits[1:5]:
        wait.wait()

    def arrive(tile, tiles):
        if ROWS * tile % GROUP == 0:
            waits[5 + ROWS * tile // GROUP].wait()

    write_weights(
        place_ref, wav_count, which, coupling_v, counts_v, good_v,
        lambda e, tile: ivar_v[e, pl.ds(pl.multiple_of(which * half + ROWS * tile, ROWS), ROWS), :],
        lambda e, group: bits_v[e, pl.ds(pl.multiple_of(which * (half // BITS) + words * group, words), words), :],
        sums_ref, weight_ref, arrive,
    )
    for wait in waits[5 + half // GROUP :]:
        wait.wait()


def sent_weights(moves, wav_count, place, slots, coupling, counts, good, bits, ivar):
    expos, width, fibres = ivar.shape
    half = width // 2
    fib_count, pack, per, _ = moves
    inputs = (slots, coupling, counts, good, bits, ivar)
    return pl.pallas_call(
        functools.partial(sent_kernel, moves, wav_count),
        in_specs=[in_smem] + [in_hbm] * 6,
        out_specs=[in_vmem] * 9,
        out_shape=[
            shaped((2, half, fibres)),
            shaped((expos, half, fibres)),
            shaped((fib_count * pack * per, pack * fibres), BF16),
        ]
        + [shaped(x.shape, x.dtype) for x in inputs],
        scratch_shapes=[pltpu.SemaphoreType.DMA((5 + width // GROUP,))],
        compiler_params=params(),
        cost_estimate=cost(20 * ivar.size, 6 * ivar.size),
        name="sent_weights",
    )(place, *held_in_hbm(*inputs))


def lay_out(source_ref, target_ref, pieces, pitch):
    expos, _, fibres = source_ref.shape
    for h in range(fibres // LANES):
        for e in range(expos):
            for first, length, at in pieces:
                target_ref[pl.ds((h * expos + e) * pitch + at, length), :] = source_ref[
                    e, pl.ds(first, length), pl.ds(h * LANES, LANES)
                ]


def kept_kernel(
    wav_count, place_ref, coupling_ref, counts_ref, good_ref, pixels_ref, ivar_ref, bits_ref,
    sums_ref, weight_ref, up_ref, down_ref, ivar_s, pixel_s,
):
    expos, width, fibres = ivar_ref.shape
    half = width // 2
    streams = expos * fibres // LANES
    count = -(-HALO // ROWS) * ROWS
    pitch = odd(2 * count)
    which = place_ref[2]
    words = GROUP // BITS
    edges = [(0, count, 0), (width - count, count, count)]
    lay_out(ivar_ref, ivar_s, edges, pitch)
    lay_out(pixels_ref, pixel_s, edges, pitch)
    coupling = stream_coupling(coupling_ref, expos)
    back = 1.0 / coupling
    zero = jnp.zeros((streams, LANES), F32)
    states = [(zero, zero + 1.0, zero), (zero, zero + 1.0, zero)]

    def eliminate(tile, tiles):
        for i in range(HALO * tile // tiles, HALO * (tile + 1) // tiles):
            for side, row in enumerate((2 * count - HALO + i, HALO - 1 - i)):
                at = pl.ds(row, streams, stride=pitch)
                states[side] = advance(states[side], ivar_s[at, :], pixel_s[at, :], back)
                if i % 24 == 23:
                    states[side] = rescaled(states[side])

    write_weights(
        place_ref, wav_count, which, coupling_ref, counts_ref, good_ref,
        lambda e, tile: ivar_ref[e, pl.ds(pl.multiple_of(which * half + ROWS * tile, ROWS), ROWS), :],
        lambda e, group: bits_ref[e, pl.ds(pl.multiple_of(which * (half // BITS) + words * group, words), words), :],
        sums_ref, weight_ref, eliminate,
    )
    for (n, d, b), out_ref in zip(states, (up_ref, down_ref)):
        scale = 1.0 / (d + n)
        out_ref[0] = coupling * (n * scale)
        out_ref[1] = b * scale


def kept_weights(wav_count, place, coupling, counts, good, pixels, ivar, bits):
    expos, width, fibres = ivar.shape
    half = width // 2
    streams = expos * fibres // LANES
    count = -(-HALO // ROWS) * ROWS
    edge = shaped((2, streams, LANES))
    edge_scratch = pltpu.VMEM((streams * odd(2 * count), LANES), F32)
    return pl.pallas_call(
        functools.partial(kept_kernel, wav_count),
        in_specs=[in_smem] + [in_vmem] * 6,
        out_specs=[in_vmem] * 4,
        out_shape=[shaped((2, half, fibres)), shaped((expos, half, fibres)), edge, edge],
        scratch_shapes=[edge_scratch, edge_scratch],
        compiler_params=params(),
        cost_estimate=cost(20 * ivar.size, 6 * ivar.size),
        name="kept_weights",
    )(place, coupling, counts, good, pixels, ivar, bits)


def layout_kernel(arrived_ref, pixels_ref, ivar_ref, pixel_out, ivar_out):
    width = ivar_ref.shape[1]
    lay_out(ivar_ref, ivar_out, [(0, width, 0)], odd(width))
    lay_out(pixels_ref, pixel_out, [(0, width, 0)], odd(width))


def stream_layout(arrived, pixels, ivar):
    expos, width, fibres = ivar.shape
    streams = expos * fibres // LANES
    laid = shaped((streams * odd(width), LANES))
    return pl.pallas_call(
        layout_kernel,
        in_specs=[in_vmem] * 3,
        out_specs=[in_vmem] * 2,
        out_shape=[laid, laid],
        compiler_params=params(),
        cost_estimate=cost(0, 16 * ivar.size),
        name="stream_layout",
    )(arrived, pixels, ivar)


def solve_kernel(
    wav_count, place_ref, coupling_ref, left_ref, right_ref, pixel_ref, ivar_ref, weight_ref,
    theirs_ref, solved_s, lead_s, rest_s,
):
    streams = left_ref.shape[1]
    expos, half, fibres = weight_ref.shape
    width = 2 * half
    pitch = odd(width)
    middle = half
    coupling = stream_coupling(coupling_ref, expos)
    back = 1.0 / coupling

    def row_at(i):
        return pl.ds(i, streams, stride=pitch)

    def begin(edge_ref, outermost):
        n = jnp.where(place_ref[1] == outermost, 0.0, edge_ref[0]) * back
        return (n, 1.0 - n, jnp.where(place_ref[1] == outermost, 0.0, edge_ref[1]))

    def keep(side, i, state):
        n, d, b = state
        inverse = inverse_of(d + n)
        lead_s[side, i] = d * inverse
        rest_s[side, i] = b * inverse

    unrolled = divisor_of(middle, 24)

    def eliminate(it, states):
        states = list(states)
        for k in range(unrolled):
            i = it * unrolled + k
            for side, row in enumerate((i, width - 1 - i)):
                keep(side, i, states[side])
                states[side] = advance(states[side], ivar_ref[row_at(row), :], pixel_ref[row_at(row), :], back)
        return tuple(rescaled(state) for state in states)

    states = lax.fori_loop(0, middle // unrolled, eliminate, (begin(left_ref, 0), begin(right_ref, wav_count - 1)))
    for side in range(2):
        keep(side, middle, states[side])
    lead, rest = lead_s[0, middle], rest_s[0, middle]
    lead_r, rest_r = lead_s[1, middle], rest_s[1, middle]
    left = (rest + lead * rest_r) / (1.0 - lead * lead_r)
    right = rest_r + lead_r * left
    several = divisor_of(middle, 48)

    def after_both(near, far):
        return far[0] * near[0], far[1] + far[0] * near[1]

    def step(factors, value):
        return factors[1] + factors[0] * value

    def substitute(it, values):
        values = list(values)
        for k in range(0, several, 4):
            for side in range(2):
                rows = [middle - 1 - (it * several + k + m) for m in range(4)]
                one, two, three, four = [(lead_s[side, i], rest_s[side, i]) for i in rows]
                first_two = after_both(one, two)
                all_four = after_both(first_two, after_both(three, four))
                value = values[side]
                third = step(first_two, value)
                solved = [value, step(one, value), third, step(three, third)]
                values[side] = step(all_four, value)
                for i, x in zip(rows, solved):
                    solved_s[row_at(i if side == 0 else width - 1 - i), :] = x
        return tuple(values)

    lax.fori_loop(0, middle // several, substitute, (left, right))

    add_up(theirs_ref, weight_ref, solved_s, coupling_ref, 1 - place_ref[2])


def add_up(out_ref, weight_ref, solved_ref, coupling_ref, which):
    expos, half, fibres = weight_ref.shape
    pitch = odd(2 * half)
    start = which * half
    back = 1.0 / coupling_ref[...]
    unrolled = divisor_of(half // ROWS, 5)

    def body(g, carry):
        for k in range(unrolled):
            row = pl.multiple_of((g * unrolled + k) * ROWS, ROWS)
            for h in range(fibres // LANES):
                total = None
                for e in range(expos):
                    at = pl.ds((h * expos + e) * pitch + start + row, ROWS)
                    term = weight_ref[e, pl.ds(row, ROWS), pl.ds(h * LANES, LANES)] * solved_ref[at, :]
                    total = term if e == 0 else total + term
                out_ref[0, pl.ds(row, ROWS), pl.ds(h * LANES, LANES)] = total * back[:, h * LANES : (h + 1) * LANES]
        return carry

    lax.fori_loop(0, half // ROWS // unrolled, body, 0)


def flux_sums(wav_count, place, coupling, left, right, pixels, ivar, weight):
    expos, half, fibres = weight.shape
    streams = left.shape[1]
    factor_scratch = pltpu.VMEM((2, half + 1, streams, LANES), F32)
    return pl.pallas_call(
        functools.partial(solve_kernel, wav_count),
        in_specs=[in_smem] + [in_vmem] * 6,
        out_specs=[in_vmem, in_vmem],
        out_shape=[shaped((1, half, fibres)), shaped(pixels.shape)],
        scratch_shapes=[factor_scratch, factor_scratch],
        compiler_params=params(),
        cost_estimate=cost(0, 0),
        name="flux_sums",
    )(place, coupling, left, right, pixels, ivar, weight)


def kept_flux_kernel(place_ref, coupling_ref, solved_ref, weight_ref, out_ref):
    add_up(out_ref, weight_ref, solved_ref, coupling_ref, place_ref[2])


def kept_flux(place, coupling, solved, weight):
    expos, half, fibres = weight.shape
    return pl.pallas_call(
        kept_flux_kernel,
        in_specs=[in_smem] + [in_vmem] * 3,
        out_specs=in_vmem,
        out_shape=shaped((1, half, fibres)),
        compiler_params=params(),
        cost_estimate=cost(2 * weight.size, 8 * weight.size),
        name="kept_flux",
    )(place, coupling, solved, weight)


def split_dot(x, table, dims):
    top = x.astype(BF16)
    low = (x - top.astype(F32)).astype(BF16)
    both = lax.dot_general(jnp.concatenate([top, low], 0), table, dims, preferred_element_type=F32)
    return both[: x.shape[0]] + both[x.shape[0] :]


def sort_kernel(pack, scaled, theirs_ref, mine_ref, table_ref, *refs):
    values, rows, _ = mine_ref.shape
    part = rows // pack
    totals = [mine_ref[v] + theirs_ref[v] for v in range(values)]
    if scaled:
        scale_ref, _, *out_refs = refs
        totals = [t * scale_ref[...] for t in totals]
    else:
        *out_refs, scale_ref = refs
        scale = 1.0 / jnp.maximum(totals[0], 1.0)
        scale_ref[...] = scale
        totals[1] = totals[1] * scale
    x = jnp.concatenate(
        [jnp.concatenate([t[h * part : (h + 1) * part] for h in range(pack)], 1) for t in totals], 0
    )
    moved = split_dot(x, table_ref[...], NT)
    lanes = moved.shape[1] // len(out_refs)
    for d, out_ref in enumerate(out_refs):
        for v in range(values):
            out_ref[v] = moved[v * part : (v + 1) * part, d * lanes : (d + 1) * lanes]


def sort_fibres(theirs, mine, table, pack, pieces, scale=None, ahead=None):
    values, rows, fibres = mine.shape
    lanes = table.shape[0] // pieces
    scaled = scale is not None
    outs = [shaped((values, rows // pack, lanes))] * pieces + ([] if scaled else [shaped((rows, fibres))])
    args = (theirs, mine, table) + ((scale, ahead) if scaled else ())
    return pl.pallas_call(
        functools.partial(sort_kernel, pack, scaled),
        in_specs=[in_vmem] * len(args),
        out_specs=[in_vmem] * len(outs),
        out_shape=outs,
        compiler_params=params(),
        cost_estimate=cost(0, 0),
        name="sort_flux" if scaled else "sort_weights",
    )(*args)


def exchange(pieces, fib_count):
    if len(pieces) == 1:
        return [lax.all_to_all(pieces[0], "fib", split_axis=2, concat_axis=2, tiled=True)]
    arrived = [pieces[0]]
    for d in range(1, fib_count):
        arrived.append(lax.ppermute(pieces[d], "fib", [(i, (i + d) % fib_count) for i in range(fib_count)]))
    return arrived


def landed(refs, table):
    values, part, _ = refs[0].shape
    x = jnp.concatenate(
        [jnp.concatenate([ref[v] for ref in refs], 1) if len(refs) > 1 else refs[0][v] for v in range(values)], 0
    )
    moved = split_dot(x, table, NT)
    return [moved[v * part : (v + 1) * part] for v in range(values)]


def columns_of(table, which, pieces):
    lanes = table.shape[1] // pieces
    return jnp.concatenate([table[:, d * lanes : (d + 1) * lanes] for d in which], 1)


def early_kernel(moves, which, pieces, place_ref, slots_ref, *refs):
    *piece_refs, table_ref, sums_ref = refs
    write_recv_table(*moves, place_ref[0], slots_ref, table_ref)
    for v, moved in enumerate(landed(piece_refs, columns_of(table_ref[...], which, pieces))):
        sums_ref[v] = moved


def place_early(moves, which, place, slots, weight_pieces, fibres):
    fib_count, pack, per, _ = moves
    early = [weight_pieces[d] for d in which]
    values, part, _ = early[0].shape
    return pl.pallas_call(
        functools.partial(early_kernel, moves, which, len(weight_pieces)),
        in_specs=[in_smem] + [in_vmem] * (1 + len(early)),
        out_specs=[in_vmem] * 2,
        out_shape=[
            shaped((pack * fibres, fib_count * pack * per), BF16),
            shaped((values, part, pack * fibres)),
        ],
        compiler_params=params(),
        cost_estimate=cost(0, 0),
        name="place_early",
    )(place, slots, *early)


def weights_end_kernel(pack, total, late, pieces, place_ref, table_ref, sums_ref, *refs):
    *late_refs, ivar_ref, res_ref = refs
    weight, band = sums_ref[0], sums_ref[1]
    if late:
        more_weight, more_band = landed(late_refs, columns_of(table_ref[...], late, pieces))
        weight, band = weight + more_weight, band + more_band
    rows, fibres = ivar_ref.shape
    part = rows // pack
    start = (place_ref[1] * 2 + place_ref[2]) * rows
    for h in range(pack):
        at = slice(h * part, (h + 1) * part)
        cut = slice(h * fibres, (h + 1) * fibres)
        row = start + h * part + lax.broadcasted_iota(jnp.int32, (part, 1), 0)
        w, b = weight[:, cut], band[:, cut]
        before = jnp.where(row == 0, 0.0, b)
        after = jnp.where(row == total - 1, 0.0, b)
        ivar_ref[at, :] = w
        res_ref[0, at, :] = before
        res_ref[1, at, :] = jnp.minimum(w, 1.0) - before - after
        res_ref[2, at, :] = after


def end_weights(place, table, sums, late, weight_pieces, pack, fibres, total):
    rows = sums.shape[1] * pack
    late_pieces = [weight_pieces[d] for d in late]
    return pl.pallas_call(
        functools.partial(weights_end_kernel, pack, total, late, len(weight_pieces)),
        in_specs=[in_smem] + [in_vmem] * (2 + len(late)),
        out_specs=[in_vmem] * 2,
        out_shape=[shaped((rows, fibres)), shaped((3, rows, fibres))],
        compiler_params=params(),
        cost_estimate=cost(0, 0),
        name="end_weights",
    )(place, table, sums, *late_pieces)


def flux_end_kernel(pack, table_ref, *refs):
    *piece_refs, flux_ref = refs
    (flux,) = landed(piece_refs, table_ref[...])
    rows, fibres = flux_ref.shape
    part = rows // pack
    for h in range(pack):
        flux_ref[h * part : (h + 1) * part, :] = flux[:, h * fibres : (h + 1) * fibres]


def end_flux(table, pieces, pack, fibres):
    rows = pieces[0].shape[1] * pack
    return pl.pallas_call(
        functools.partial(flux_end_kernel, pack),
        in_specs=[in_vmem] * (1 + len(pieces)),
        out_specs=in_vmem,
        out_shape=shaped((rows, fibres)),
        compiler_params=params(),
        cost_estimate=cost(2 * rows * table.size, 2 * rows * fibres * 4),
        name="end_flux",
    )(table, *pieces)


def after(value, done):
    return lax.optimization_barrier((value, done))[0]


def per_device(pixels, pixel_ivar, clip_bits, coupling, counts, good_flags, owner_slot):
    expos, width, fibres = pixels.shape
    fib_count, wav_count = lax.axis_size("fib"), lax.axis_size("wav")
    total = width * wav_count
    per = fibres // fib_count
    rows = width // 2
    pack = max(1, LANES // per)
    while pack > 1 and rows % (pack * ROWS):
        pack //= 2
    rel = pack * per == LANES
    pieces = fib_count if rel else 1
    place = jnp.stack([lax.axis_index(axis) for axis in ("fib", "wav", "exp")]).astype(jnp.int32)
    coupling, counts, slots = coupling[None], counts[None], owner_slot[None]
    swap = [(0, 1), (1, 0)]
    moves = (fib_count, pack, per, rel)

    theirs, weight_t, send_table, slots, coupling, counts, good, bits, ivar = sent_weights(
        moves, wav_count, place, slots, coupling, counts, good_flags, clip_bits, pixel_ivar
    )
    arriving = lax.ppermute(theirs, "exp", swap)
    mine, weight_m, up, down = kept_weights(
        wav_count, place, coupling, counts, good, pixels, ivar, bits
    )
    upward = [(i, (i + 1) % wav_count) for i in range(wav_count)]
    left = lax.ppermute(up, "wav", upward)
    right = lax.ppermute(down, "wav", [(j, i) for i, j in upward])
    *sorted_pieces, scale = sort_fibres(arriving, mine, send_table, pack, pieces)
    weight_pieces = exchange(sorted_pieces, fib_count)

    pixel_s, ivar_s = stream_layout(left[0] + right[0], pixels, ivar)
    theirs, solved = flux_sums(wav_count, place, coupling, left, right, pixel_s, ivar_s, weight_t)
    late = [fib_count // 2] if rel else []
    early = [d for d in range(len(weight_pieces)) if d not in late]
    ahead = sum(weight_pieces[d][0, :ROWS, :] for d in early[1:] or early)
    arriving = lax.ppermute(theirs, "exp", swap)
    mine = kept_flux(after(place, theirs), coupling, solved, weight_m)
    sorted_pieces = sort_fibres(arriving, mine, send_table, pack, pieces, scale, ahead)
    flux_pieces = exchange(sorted_pieces, fib_count)
    recv_table, placed = place_early(moves, early, after(place, sorted_pieces[0]), slots, weight_pieces, fibres)
    ivar, res = end_weights(place, recv_table, placed, late, weight_pieces, pack, fibres, total)
    flux = end_flux(recv_table, flux_pieces, pack, fibres)
    return (flux, ivar, res)


def solution(mesh):
    return jax.shard_map(
        per_device,
        mesh=mesh,
        in_specs=(
            P("exp", "wav", "fib"),
            P("exp", "wav", "fib"),
            P("exp", "wav", "fib"),
            P("fib"),
            P("fib"),
            P("exp", "fib"),
            P(),
        ),
        out_specs=(
            P(("wav", "exp"), "fib"),
            P(("wav", "exp"), "fib"),
            P(None, ("wav", "exp"), "fib"),
        ),
        check_vma=False,
    )
```

```python
import functools

import jax
import jax.numpy as jnp
from jax import lax
from jax.experimental import pallas as pl
from jax.experimental.pallas import tpu as pltpu
from jax.sharding import PartitionSpec as P

HALO = 50
BITS = 15
LANES = 128
ROWS = 8
GROUP = 120
VMEM_BYTES = 32 * 1024 * 1024
F32 = jnp.float32
BF16 = jnp.bfloat16
NT = (((1,), (1,)), ((), ()))

in_vmem = pl.BlockSpec(memory_space=pltpu.VMEM)
in_smem = pl.BlockSpec(memory_space=pltpu.SMEM)
in_hbm = pl.BlockSpec(memory_space=pltpu.HBM)


def params():
    return pltpu.CompilerParams(vmem_limit_bytes=VMEM_BYTES)


def cost(flops, moved):
    return pl.CostEstimate(flops=int(flops), bytes_accessed=int(moved), transcendentals=0)


def held_in_hbm(*arrays):
    return [pltpu.with_memory_space_constraint(array, pltpu.HBM) for array in arrays]


def shaped(shape, dtype=F32):
    return jax.ShapeDtypeStruct(shape, dtype)


def usable_rows(place_ref, counts_ref, good_ref):
    count = good_ref.shape[0]
    return [
        good_ref[e : e + 1, :].astype(F32)
        * jnp.where(place_ref[2] * count + e < counts_ref[...], 1.0, 0.0)
        for e in range(count)
    ]


def tile_bits(tile):
    first, last = (ROWS * tile) // BITS, (ROWS * tile + ROWS - 1) // BITS
    split = BITS * last - ROWS * tile
    row = lax.broadcasted_iota(jnp.int32, (ROWS, 1), 0)
    word = jnp.where(row >= split, last, first)
    return first, last, split, jnp.left_shift(1, ROWS * tile + row - BITS * word)


def tile_words(words, tile):
    first, last, split, mask = tile_bits(tile)
    picked = words[first : first + 1, :]
    if last != first:
        row = lax.broadcasted_iota(jnp.int32, (ROWS, 1), 0)
        picked = jnp.where(row >= split, words[last : last + 1, :], picked)
    return (picked & mask) != 0


def in_flight(pairs, sems, at=0):
    copies = [pltpu.make_async_copy(source, target, sems.at[at + i]) for i, (source, target) in enumerate(pairs)]
    for copy in copies:
        copy.start()
    return copies


def inverse_of(x):
    guess = pl.reciprocal(x, approx=True)
    return guess * (2.0 - x * guess)


def advance(state, ivar, pixel, back_coupling):
    n, d, b = state
    ratio = ivar * back_coupling
    next_d = d + n
    return (n * (1.0 + ratio) + ratio * d, next_d, b + (ivar * pixel) * next_d)


def rescaled(state):
    scale = inverse_of(state[1])
    return tuple(part * scale for part in state)


def odd(rows):
    return rows + 1 - rows % 2


def divisor_of(size, most):
    return max(k for k in range(1, most + 1) if size % k == 0)


def owners(slots_ref, fib_count, fibres):
    rows = [slots_ref[:, s * fibres : (s + 1) * fibres].astype(F32) for s in range(fib_count)]
    sources = -(-fib_count // ROWS) * ROWS
    if sources > fib_count:
        rows.append(jnp.full((sources - fib_count, fibres), -1.0, F32))
    slots = jnp.concatenate(rows, 0)
    owner = jnp.floor((slots + 0.5) * (1.0 / fibres))
    return owner, slots - owner * fibres


def earlier_fibres(fibres):
    row = lax.broadcasted_iota(jnp.int32, (fibres, fibres), 0)
    col = lax.broadcasted_iota(jnp.int32, (fibres, fibres), 1)
    return (row < col).astype(F32).astype(BF16)


def write_send_table(fib_count, pack, per, rel, me, slots_ref, table_ref):
    fibres = table_ref.shape[1] // pack
    lanes = pack * per
    owner, _ = owners(slots_ref, fib_count, fibres)
    source = lax.broadcasted_iota(jnp.int32, owner.shape, 0)
    my_owner = jnp.sum(jnp.where(source == me, owner, 0.0), axis=0, keepdims=True).astype(jnp.int32)
    to_owner = (source == my_owner).astype(F32)
    counted = jnp.dot(to_owner.astype(BF16), earlier_fibres(fibres), preferred_element_type=F32)
    rank = jnp.sum(to_owner * counted, axis=0, keepdims=True).astype(jnp.int32)
    target = my_owner
    if rel:
        target = jnp.where(my_owner >= me, my_owner - me, my_owner - me + fib_count)
    base = target * lanes + rank
    place_of = jnp.concatenate([base + h * per for h in range(pack)], 1)
    row = lax.broadcasted_iota(jnp.int32, table_ref.shape, 0)
    table_ref[...] = (row == place_of).astype(F32).astype(BF16)


def write_recv_table(fib_count, pack, per, rel, me, slots_ref, table_ref):
    fibres = table_ref.shape[0] // pack
    lanes = pack * per
    total_lanes = fib_count * lanes
    owner, column = owners(slots_ref, fib_count, fibres)
    source = lax.broadcasted_iota(jnp.int32, owner.shape, 0)
    mine = (owner == me.astype(F32)).astype(F32)
    rank_in = jnp.dot(mine.astype(BF16), earlier_fibres(fibres), preferred_element_type=F32).astype(jnp.int32)
    order = source
    if rel:
        order = jnp.where(me >= source, me - source, me - source + fib_count)
    arrival = jnp.where(mine > 0.0, order * lanes + rank_in, -total_lanes)
    tall = lax.broadcasted_iota(jnp.int32, (total_lanes, fibres), 0)
    landing = jnp.zeros((ROWS, total_lanes), F32)
    for s in range(fib_count):
        hit = tall == arrival[s : s + 1, :]
        for h in range(1, pack):
            hit = hit | (tall == arrival[s : s + 1, :] + h * per)
        values = jnp.broadcast_to(column[s : s + 1, :], (ROWS, fibres)).astype(BF16)
        landing = landing + lax.dot_general(
            values, hit.astype(F32).astype(BF16), NT, preferred_element_type=F32
        )
    lane = lax.broadcasted_iota(jnp.int32, (1, total_lanes), 1)
    landing = landing[0:1, :].astype(jnp.int32)
    for h in range(1, pack):
        inside = (lane % lanes >= h * per) & (lane % lanes < (h + 1) * per)
        landing = jnp.where(inside, landing + h * fibres, landing)
    row = lax.broadcasted_iota(jnp.int32, table_ref.shape, 0)
    table_ref[...] = (row == landing).astype(F32).astype(BF16)


def stream_coupling(coupling_ref, expos):
    coupling = coupling_ref[...]
    blocks = coupling.shape[1] // LANES
    return jnp.concatenate(
        [jnp.broadcast_to(coupling[:, h * LANES : (h + 1) * LANES], (expos, LANES)) for h in range(blocks)], 0
    )


def weight_tile(coupling, usable, words, ivars, within, scale_row):
    links = scale_row * coupling
    weights = []
    weight_sum = band_sum = None
    for e, ivar in enumerate(ivars):
        weight = jnp.where(tile_words(words[e], within), ivar * usable[e], 0.0)
        band = weight * inverse_of(ivar + links)
        weights.append(weight)
        weight_sum = weight if e == 0 else weight_sum + weight
        band_sum = band if e == 0 else band_sum + band
    return weights, weight_sum, band_sum * coupling


def write_weights(place_ref, wav_count, which, coupling_v, counts_v, good_v, ivar_of, words_of, sums_ref, weight_ref, beside):
    expos, half, _ = weight_ref.shape
    coupling = coupling_v[...]
    usable = usable_rows(place_ref, counts_v, good_v)
    start = place_ref[1] * (2 * half) + which * half
    tiles = half // ROWS
    tiles_in_group = GROUP // ROWS
    for tile in range(tiles):
        beside(tile, tiles)
        group, within = divmod(tile, tiles_in_group)
        scale_row = 4.0
        if tile in (0, tiles - 1):
            row = start + ROWS * tile + lax.broadcasted_iota(jnp.int32, (ROWS, 1), 0)
            scale_row = jnp.where((row == 0) | (row == wav_count * 2 * half - 1), 2.0, 4.0)
        at = slice(ROWS * tile, ROWS * (tile + 1))
        weights, weight_sum, band_sum = weight_tile(
            coupling,
            usable,
            [words_of(e, group) for e in range(expos)],
            [ivar_of(e, tile) for e in range(expos)],
            within,
            scale_row,
        )
        for e in range(expos):
            weight_ref[e, at, :] = weights[e]
        sums_ref[0, at, :] = weight_sum
        sums_ref[1, at, :] = band_sum


def sent_kernel(
    moves, wav_count, place_ref, slots_ref, coupling_ref, counts_ref, good_ref, bits_ref, ivar_ref,
    sums_ref, weight_ref, table_ref, slots_v, coupling_v, counts_v, good_v, bits_v, ivar_v, sems,
):
    expos, width, _ = ivar_ref.shape
    half = width // 2
    which = 1 - place_ref[2]
    words = GROUP // BITS

    def part(source, target, first):
        at = pl.ds(pl.multiple_of(first, ROWS), GROUP)
        return source.at[:, at, :], target.at[:, at, :]

    waits = in_flight(
        [
            (slots_ref, slots_v),
            (coupling_ref, coupling_v),
            (counts_ref, counts_v),
            (good_ref, good_v),
            (bits_ref, bits_v),
        ]
        + [part(ivar_ref, ivar_v, which * half + g) for g in range(0, half, GROUP)]
        + [part(ivar_ref, ivar_v, (1 - which) * half + g) for g in range(0, half, GROUP)],
        sems,
    )
    waits[0].wait()
    write_send_table(*moves, place_ref[0], slots_v, table_ref)
    for wait in waits[1:5]:
        wait.wait()

    def arrive(tile, tiles):
        if ROWS * tile % GROUP == 0:
            waits[5 + ROWS * tile // GROUP].wait()

    write_weights(
        place_ref, wav_count, which, coupling_v, counts_v, good_v,
        lambda e, tile: ivar_v[e, pl.ds(pl.multiple_of(which * half + ROWS * tile, ROWS), ROWS), :],
        lambda e, group: bits_v[e, pl.ds(pl.multiple_of(which * (half // BITS) + words * group, words), words), :],
        sums_ref, weight_ref, arrive,
    )
    for wait in waits[5 + half // GROUP :]:
        wait.wait()


def sent_weights(moves, wav_count, place, slots, coupling, counts, good, bits, ivar):
    expos, width, fibres = ivar.shape
    half = width // 2
    fib_count, pack, per, _ = moves
    inputs = (slots, coupling, counts, good, bits, ivar)
    return pl.pallas_call(
        functools.partial(sent_kernel, moves, wav_count),
        in_specs=[in_smem] + [in_hbm] * 6,
        out_specs=[in_vmem] * 9,
        out_shape=[
            shaped((2, half, fibres)),
            shaped((expos, half, fibres)),
            shaped((fib_count * pack * per, pack * fibres), BF16),
        ]
        + [shaped(x.shape, x.dtype) for x in inputs],
        scratch_shapes=[pltpu.SemaphoreType.DMA((5 + width // GROUP,))],
        compiler_params=params(),
        cost_estimate=cost(20 * ivar.size, 6 * ivar.size),
        name="sent_weights",
    )(place, *held_in_hbm(*inputs))


def lay_out(source_ref, target_ref, pieces, pitch):
    expos, _, fibres = source_ref.shape
    for h in range(fibres // LANES):
        for e in range(expos):
            for first, length, at in pieces:
                target_ref[pl.ds((h * expos + e) * pitch + at, length), :] = source_ref[
                    e, pl.ds(first, length), pl.ds(h * LANES, LANES)
                ]


def kept_kernel(
    wav_count, place_ref, coupling_ref, counts_ref, good_ref, pixels_ref, ivar_ref, bits_ref,
    sums_ref, weight_ref, up_ref, down_ref, ivar_s, pixel_s,
):
    expos, width, fibres = ivar_ref.shape
    half = width // 2
    streams = expos * fibres // LANES
    count = -(-HALO // ROWS) * ROWS
    pitch = odd(2 * count)
    which = place_ref[2]
    words = GROUP // BITS
    edges = [(0, count, 0), (width - count, count, count)]
    lay_out(ivar_ref, ivar_s, edges, pitch)
    lay_out(pixels_ref, pixel_s, edges, pitch)
    coupling = stream_coupling(coupling_ref, expos)
    back = 1.0 / coupling
    zero = jnp.zeros((streams, LANES), F32)
    states = [(zero, zero + 1.0, zero), (zero, zero + 1.0, zero)]

    def eliminate(tile, tiles):
        for i in range(HALO * tile // tiles, HALO * (tile + 1) // tiles):
            for side, row in enumerate((2 * count - HALO + i, HALO - 1 - i)):
                at = pl.ds(row, streams, stride=pitch)
                states[side] = advance(states[side], ivar_s[at, :], pixel_s[at, :], back)
                if i % 24 == 23:
                    states[side] = rescaled(states[side])

    write_weights(
        place_ref, wav_count, which, coupling_ref, counts_ref, good_ref,
        lambda e, tile: ivar_ref[e, pl.ds(pl.multiple_of(which * half + ROWS * tile, ROWS), ROWS), :],
        lambda e, group: bits_ref[e, pl.ds(pl.multiple_of(which * (half // BITS) + words * group, words), words), :],
        sums_ref, weight_ref, eliminate,
    )
    for (n, d, b), out_ref in zip(states, (up_ref, down_ref)):
        scale = 1.0 / (d + n)
        out_ref[0] = coupling * (n * scale)
        out_ref[1] = b * scale


def kept_weights(wav_count, place, coupling, counts, good, pixels, ivar, bits):
    expos, width, fibres = ivar.shape
    half = width // 2
    streams = expos * fibres // LANES
    count = -(-HALO // ROWS) * ROWS
    edge = shaped((2, streams, LANES))
    edge_scratch = pltpu.VMEM((streams * odd(2 * count), LANES), F32)
    return pl.pallas_call(
        functools.partial(kept_kernel, wav_count),
        in_specs=[in_smem] + [in_vmem] * 6,
        out_specs=[in_vmem] * 4,
        out_shape=[shaped((2, half, fibres)), shaped((expos, half, fibres)), edge, edge],
        scratch_shapes=[edge_scratch, edge_scratch],
        compiler_params=params(),
        cost_estimate=cost(20 * ivar.size, 6 * ivar.size),
        name="kept_weights",
    )(place, coupling, counts, good, pixels, ivar, bits)


def layout_kernel(arrived_ref, pixels_ref, ivar_ref, pixel_out, ivar_out):
    width = ivar_ref.shape[1]
    lay_out(ivar_ref, ivar_out, [(0, width, 0)], odd(width))
    lay_out(pixels_ref, pixel_out, [(0, width, 0)], odd(width))


def stream_layout(arrived, pixels, ivar):
    expos, width, fibres = ivar.shape
    streams = expos * fibres // LANES
    laid = shaped((streams * odd(width), LANES))
    return pl.pallas_call(
        layout_kernel,
        in_specs=[in_vmem] * 3,
        out_specs=[in_vmem] * 2,
        out_shape=[laid, laid],
        compiler_params=params(),
        cost_estimate=cost(0, 16 * ivar.size),
        name="stream_layout",
    )(arrived, pixels, ivar)


def solve_kernel(
    wav_count, place_ref, coupling_ref, left_ref, right_ref, pixel_ref, ivar_ref, weight_ref,
    theirs_ref, solved_s, lead_s, rest_s,
):
    streams = left_ref.shape[1]
    expos, half, fibres = weight_ref.shape
    width = 2 * half
    pitch = odd(width)
    middle = half
    coupling = stream_coupling(coupling_ref, expos)
    back = 1.0 / coupling

    def row_at(i):
        return pl.ds(i, streams, stride=pitch)

    def begin(edge_ref, outermost):
        n = jnp.where(place_ref[1] == outermost, 0.0, edge_ref[0]) * back
        return (n, 1.0 - n, jnp.where(place_ref[1] == outermost, 0.0, edge_ref[1]))

    def keep(side, i, state):
        n, d, b = state
        inverse = inverse_of(d + n)
        lead_s[side, i] = d * inverse
        rest_s[side, i] = b * inverse

    unrolled = divisor_of(middle, 24)

    def eliminate(it, states):
        states = list(states)
        for k in range(unrolled):
            i = it * unrolled + k
            for side, row in enumerate((i, width - 1 - i)):
                keep(side, i, states[side])
                states[side] = advance(states[side], ivar_ref[row_at(row), :], pixel_ref[row_at(row), :], back)
        return tuple(rescaled(state) for state in states)

    states = lax.fori_loop(0, middle // unrolled, eliminate, (begin(left_ref, 0), begin(right_ref, wav_count - 1)))
    for side in range(2):
        keep(side, middle, states[side])
    lead, rest = lead_s[0, middle], rest_s[0, middle]
    lead_r, rest_r = lead_s[1, middle], rest_s[1, middle]
    left = (rest + lead * rest_r) / (1.0 - lead * lead_r)
    right = rest_r + lead_r * left
    several = divisor_of(middle, 48)

    def after_both(near, far):
        return far[0] * near[0], far[1] + far[0] * near[1]

    def step(factors, value):
        return factors[1] + factors[0] * value

    def substitute(it, values):
        values = list(values)
        for k in range(0, several, 4):
            for side in range(2):
                rows = [middle - 1 - (it * several + k + m) for m in range(4)]
                one, two, three, four = [(lead_s[side, i], rest_s[side, i]) for i in rows]
                first_two = after_both(one, two)
                all_four = after_both(first_two, after_both(three, four))
                value = values[side]
                third = step(first_two, value)
                solved = [value, step(one, value), third, step(three, third)]
                values[side] = step(all_four, value)
                for i, x in zip(rows, solved):
                    solved_s[row_at(i if side == 0 else width - 1 - i), :] = x
        return tuple(values)

    lax.fori_loop(0, middle // several, substitute, (left, right))

    add_up(theirs_ref, weight_ref, solved_s, coupling_ref, 1 - place_ref[2])


def add_up(out_ref, weight_ref, solved_ref, coupling_ref, which):
    expos, half, fibres = weight_ref.shape
    pitch = odd(2 * half)
    start = which * half
    back = 1.0 / coupling_ref[...]
    unrolled = divisor_of(half // ROWS, 5)

    def body(g, carry):
        for k in range(unrolled):
            row = pl.multiple_of((g * unrolled + k) * ROWS, ROWS)
            for h in range(fibres // LANES):
                total = None
                for e in range(expos):
                    at = pl.ds((h * expos + e) * pitch + start + row, ROWS)
                    term = weight_ref[e, pl.ds(row, ROWS), pl.ds(h * LANES, LANES)] * solved_ref[at, :]
                    total = term if e == 0 else total + term
                out_ref[0, pl.ds(row, ROWS), pl.ds(h * LANES, LANES)] = total * back[:, h * LANES : (h + 1) * LANES]
        return carry

    lax.fori_loop(0, half // ROWS // unrolled, body, 0)


def flux_sums(wav_count, place, coupling, left, right, pixels, ivar, weight):
    expos, half, fibres = weight.shape
    streams = left.shape[1]
    factor_scratch = pltpu.VMEM((2, half + 1, streams, LANES), F32)
    return pl.pallas_call(
        functools.partial(solve_kernel, wav_count),
        in_specs=[in_smem] + [in_vmem] * 6,
        out_specs=[in_vmem, in_vmem],
        out_shape=[shaped((1, half, fibres)), shaped(pixels.shape)],
        scratch_shapes=[factor_scratch, factor_scratch],
        compiler_params=params(),
        cost_estimate=cost(0, 0),
        name="flux_sums",
    )(place, coupling, left, right, pixels, ivar, weight)


def kept_flux_kernel(place_ref, coupling_ref, solved_ref, weight_ref, out_ref):
    add_up(out_ref, weight_ref, solved_ref, coupling_ref, place_ref[2])


def kept_flux(place, coupling, solved, weight):
    expos, half, fibres = weight.shape
    return pl.pallas_call(
        kept_flux_kernel,
        in_specs=[in_smem] + [in_vmem] * 3,
        out_specs=in_vmem,
        out_shape=shaped((1, half, fibres)),
        compiler_params=params(),
        cost_estimate=cost(2 * weight.size, 8 * weight.size),
        name="kept_flux",
    )(place, coupling, solved, weight)


def split_dot(x, table, dims):
    top = x.astype(BF16)
    low = (x - top.astype(F32)).astype(BF16)
    both = lax.dot_general(jnp.concatenate([top, low], 0), table, dims, preferred_element_type=F32)
    return both[: x.shape[0]] + both[x.shape[0] :]


def sort_kernel(pack, scaled, theirs_ref, mine_ref, table_ref, *refs):
    values, rows, _ = mine_ref.shape
    part = rows // pack
    totals = [mine_ref[v] + theirs_ref[v] for v in range(values)]
    if scaled:
        scale_ref, _, *out_refs = refs
        totals = [t * scale_ref[...] for t in totals]
    else:
        *out_refs, scale_ref = refs
        scale = 1.0 / jnp.maximum(totals[0], 1.0)
        scale_ref[...] = scale
        totals[1] = totals[1] * scale
    x = jnp.concatenate(
        [jnp.concatenate([t[h * part : (h + 1) * part] for h in range(pack)], 1) for t in totals], 0
    )
    moved = split_dot(x, table_ref[...], NT)
    lanes = moved.shape[1] // len(out_refs)
    for d, out_ref in enumerate(out_refs):
        for v in range(values):
            out_ref[v] = moved[v * part : (v + 1) * part, d * lanes : (d + 1) * lanes]


def sort_fibres(theirs, mine, table, pack, pieces, scale=None, ahead=None):
    values, rows, fibres = mine.shape
    lanes = table.shape[0] // pieces
    scaled = scale is not None
    outs = [shaped((values, rows // pack, lanes))] * pieces + ([] if scaled else [shaped((rows, fibres))])
    args = (theirs, mine, table) + ((scale, ahead) if scaled else ())
    return pl.pallas_call(
        functools.partial(sort_kernel, pack, scaled),
        in_specs=[in_vmem] * len(args),
        out_specs=[in_vmem] * len(outs),
        out_shape=outs,
        compiler_params=params(),
        cost_estimate=cost(0, 0),
        name="sort_flux" if scaled else "sort_weights",
    )(*args)


def exchange(pieces, fib_count):
    if len(pieces) == 1:
        return [lax.all_to_all(pieces[0], "fib", split_axis=2, concat_axis=2, tiled=True)]
    arrived = [pieces[0]]
    for d in range(1, fib_count):
        arrived.append(lax.ppermute(pieces[d], "fib", [(i, (i + d) % fib_count) for i in range(fib_count)]))
    return arrived


def landed(refs, table):
    values, part, _ = refs[0].shape
    x = jnp.concatenate(
        [jnp.concatenate([ref[v] for ref in refs], 1) if len(refs) > 1 else refs[0][v] for v in range(values)], 0
    )
    moved = split_dot(x, table, NT)
    return [moved[v * part : (v + 1) * part] for v in range(values)]


def columns_of(table, which, pieces):
    lanes = table.shape[1] // pieces
    return jnp.concatenate([table[:, d * lanes : (d + 1) * lanes] for d in which], 1)


def early_kernel(moves, which, pieces, place_ref, slots_ref, *refs):
    *piece_refs, table_ref, sums_ref = refs
    write_recv_table(*moves, place_ref[0], slots_ref, table_ref)
    for v, moved in enumerate(landed(piece_refs, columns_of(table_ref[...], which, pieces))):
        sums_ref[v] = moved


def place_early(moves, which, place, slots, weight_pieces, fibres):
    fib_count, pack, per, _ = moves
    early = [weight_pieces[d] for d in which]
    values, part, _ = early[0].shape
    return pl.pallas_call(
        functools.partial(early_kernel, moves, which, len(weight_pieces)),
        in_specs=[in_smem] + [in_vmem] * (1 + len(early)),
        out_specs=[in_vmem] * 2,
        out_shape=[
            shaped((pack * fibres, fib_count * pack * per), BF16),
            shaped((values, part, pack * fibres)),
        ],
        compiler_params=params(),
        cost_estimate=cost(0, 0),
        name="place_early",
    )(place, slots, *early)


def weights_end_kernel(pack, total, late, pieces, place_ref, table_ref, sums_ref, *refs):
    *late_refs, ivar_ref, res_ref = refs
    weight, band = sums_ref[0], sums_ref[1]
    if late:
        more_weight, more_band = landed(late_refs, columns_of(table_ref[...], late, pieces))
        weight, band = weight + more_weight, band + more_band
    rows, fibres = ivar_ref.shape
    part = rows // pack
    start = (place_ref[1] * 2 + place_ref[2]) * rows
    for h in range(pack):
        at = slice(h * part, (h + 1) * part)
        cut = slice(h * fibres, (h + 1) * fibres)
        row = start + h * part + lax.broadcasted_iota(jnp.int32, (part, 1), 0)
        w, b = weight[:, cut], band[:, cut]
        before = jnp.where(row == 0, 0.0, b)
        after = jnp.where(row == total - 1, 0.0, b)
        ivar_ref[at, :] = w
        res_ref[0, at, :] = before
        res_ref[1, at, :] = jnp.minimum(w, 1.0) - before - after
        res_ref[2, at, :] = after


def end_weights(place, table, sums, late, weight_pieces, pack, fibres, total):
    rows = sums.shape[1] * pack
    late_pieces = [weight_pieces[d] for d in late]
    return pl.pallas_call(
        functools.partial(weights_end_kernel, pack, total, late, len(weight_pieces)),
        in_specs=[in_smem] + [in_vmem] * (2 + len(late)),
        out_specs=[in_vmem] * 2,
        out_shape=[shaped((rows, fibres)), shaped((3, rows, fibres))],
        compiler_params=params(),
        cost_estimate=cost(0, 0),
        name="end_weights",
    )(place, table, sums, *late_pieces)


def flux_end_kernel(pack, table_ref, *refs):
    *piece_refs, flux_ref = refs
    (flux,) = landed(piece_refs, table_ref[...])
    rows, fibres = flux_ref.shape
    part = rows // pack
    for h in range(pack):
        flux_ref[h * part : (h + 1) * part, :] = flux[:, h * fibres : (h + 1) * fibres]


def end_flux(table, pieces, pack, fibres):
    rows = pieces[0].shape[1] * pack
    return pl.pallas_call(
        functools.partial(flux_end_kernel, pack),
        in_specs=[in_vmem] * (1 + len(pieces)),
        out_specs=in_vmem,
        out_shape=shaped((rows, fibres)),
        compiler_params=params(),
        cost_estimate=cost(2 * rows * table.size, 2 * rows * fibres * 4),
        name="end_flux",
    )(table, *pieces)


def after(value, done):
    return lax.optimization_barrier((value, done))[0]


def per_device(pixels, pixel_ivar, clip_bits, coupling, counts, good_flags, owner_slot):
    expos, width, fibres = pixels.shape
    fib_count, wav_count = lax.axis_size("fib"), lax.axis_size("wav")
    total = width * wav_count
    per = fibres // fib_count
    rows = width // 2
    pack = max(1, LANES // per)
    while pack > 1 and rows % (pack * ROWS):
        pack //= 2
    rel = pack * per == LANES
    pieces = fib_count if rel else 1
    place = jnp.stack([lax.axis_index(axis) for axis in ("fib", "wav", "exp")]).astype(jnp.int32)
    coupling, counts, slots = coupling[None], counts[None], owner_slot[None]
    swap = [(0, 1), (1, 0)]
    moves = (fib_count, pack, per, rel)

    theirs, weight_t, send_table, slots, coupling, counts, good, bits, ivar = sent_weights(
        moves, wav_count, place, slots, coupling, counts, good_flags, clip_bits, pixel_ivar
    )
    arriving = lax.ppermute(theirs, "exp", swap)
    mine, weight_m, up, down = kept_weights(
        wav_count, place, coupling, counts, good, pixels, ivar, bits
    )
    upward = [(i, (i + 1) % wav_count) for i in range(wav_count)]
    left = lax.ppermute(up, "wav", upward)
    right = lax.ppermute(down, "wav", [(j, i) for i, j in upward])
    *sorted_pieces, scale = sort_fibres(arriving, mine, send_table, pack, pieces)
    weight_pieces = exchange(sorted_pieces, fib_count)

    pixel_s, ivar_s = stream_layout(left[0] + right[0], pixels, ivar)
    theirs, solved = flux_sums(wav_count, place, coupling, left, right, pixel_s, ivar_s, weight_t)
    early = [0, fib_count // 2] if rel else [0]
    late = [d for d in range(pieces) if d not in early]
    ahead = weight_pieces[early[-1]][0, :ROWS, :] * 0.5
    arriving = lax.ppermute(theirs, "exp", swap)
    mine = kept_flux(after(place, theirs), coupling, solved, weight_m)
    sorted_pieces = sort_fibres(arriving, mine, send_table, pack, pieces, scale, ahead)
    flux_pieces = exchange(sorted_pieces, fib_count)
    recv_table, placed = place_early(moves, early, after(place, sorted_pieces[0]), slots, weight_pieces, fibres)
    ivar, res = end_weights(place, recv_table, placed, late, weight_pieces, pack, fibres, total)
    flux = end_flux(recv_table, flux_pieces, pack, fibres)
    return (flux, ivar, res)


def solution(mesh):
    return jax.shard_map(
        per_device,
        mesh=mesh,
        in_specs=(
            P("exp", "wav", "fib"),
            P("exp", "wav", "fib"),
            P("exp", "wav", "fib"),
            P("fib"),
            P("fib"),
            P("exp", "fib"),
            P(),
        ),
        out_specs=(
            P(("wav", "exp"), "fib"),
            P(("wav", "exp"), "fib"),
            P(None, ("wav", "exp"), "fib"),
        ),
        check_vma=False,
    )
```

```python
import functools

import jax
import jax.numpy as jnp
from jax import lax
from jax.experimental import pallas as pl
from jax.experimental.pallas import tpu as pltpu
from jax.sharding import PartitionSpec as P

HALO = 50
BITS = 15
LANES = 128
ROWS = 8
GROUP = 120
VMEM_BYTES = 32 * 1024 * 1024
F32 = jnp.float32
BF16 = jnp.bfloat16
NT = (((1,), (1,)), ((), ()))

in_vmem = pl.BlockSpec(memory_space=pltpu.VMEM)
in_smem = pl.BlockSpec(memory_space=pltpu.SMEM)
in_hbm = pl.BlockSpec(memory_space=pltpu.HBM)


def params():
    return pltpu.CompilerParams(vmem_limit_bytes=VMEM_BYTES)


def cost(flops, moved):
    return pl.CostEstimate(flops=int(flops), bytes_accessed=int(moved), transcendentals=0)


def held_in_hbm(*arrays):
    return [pltpu.with_memory_space_constraint(array, pltpu.HBM) for array in arrays]


def shaped(shape, dtype=F32):
    return jax.ShapeDtypeStruct(shape, dtype)


def usable_rows(place_ref, counts_ref, good_ref):
    count = good_ref.shape[0]
    return [
        good_ref[e : e + 1, :].astype(F32)
        * jnp.where(place_ref[2] * count + e < counts_ref[...], 1.0, 0.0)
        for e in range(count)
    ]


def tile_bits(tile):
    first, last = (ROWS * tile) // BITS, (ROWS * tile + ROWS - 1) // BITS
    split = BITS * last - ROWS * tile
    row = lax.broadcasted_iota(jnp.int32, (ROWS, 1), 0)
    word = jnp.where(row >= split, last, first)
    return first, last, split, jnp.left_shift(1, ROWS * tile + row - BITS * word)


def tile_words(words, tile):
    first, last, split, mask = tile_bits(tile)
    picked = words[first : first + 1, :]
    if last != first:
        row = lax.broadcasted_iota(jnp.int32, (ROWS, 1), 0)
        picked = jnp.where(row >= split, words[last : last + 1, :], picked)
    return (picked & mask) != 0


def in_flight(pairs, sems, at=0):
    copies = [pltpu.make_async_copy(source, target, sems.at[at + i]) for i, (source, target) in enumerate(pairs)]
    for copy in copies:
        copy.start()
    return copies


def inverse_of(x):
    guess = pl.reciprocal(x, approx=True)
    return guess * (2.0 - x * guess)


def advance(state, ivar, pixel, back_coupling):
    n, d, b = state
    ratio = ivar * back_coupling
    next_d = d + n
    return (n * (1.0 + ratio) + ratio * d, next_d, b + (ivar * pixel) * next_d)


def rescaled(state):
    scale = inverse_of(state[1])
    return tuple(part * scale for part in state)


def odd(rows):
    return rows + 1 - rows % 2


def divisor_of(size, most):
    return max(k for k in range(1, most + 1) if size % k == 0)


def owners(slots_ref, fib_count, fibres):
    rows = [slots_ref[:, s * fibres : (s + 1) * fibres].astype(F32) for s in range(fib_count)]
    sources = -(-fib_count // ROWS) * ROWS
    if sources > fib_count:
        rows.append(jnp.full((sources - fib_count, fibres), -1.0, F32))
    slots = jnp.concatenate(rows, 0)
    owner = jnp.floor((slots + 0.5) * (1.0 / fibres))
    return owner, slots - owner * fibres


def earlier_fibres(fibres):
    row = lax.broadcasted_iota(jnp.int32, (fibres, fibres), 0)
    col = lax.broadcasted_iota(jnp.int32, (fibres, fibres), 1)
    return (row < col).astype(F32).astype(BF16)


def write_send_table(fib_count, pack, per, rel, me, slots_ref, table_ref):
    fibres = table_ref.shape[1] // pack
    lanes = pack * per
    owner, _ = owners(slots_ref, fib_count, fibres)
    source = lax.broadcasted_iota(jnp.int32, owner.shape, 0)
    my_owner = jnp.sum(jnp.where(source == me, owner, 0.0), axis=0, keepdims=True).astype(jnp.int32)
    to_owner = (source == my_owner).astype(F32)
    counted = jnp.dot(to_owner.astype(BF16), earlier_fibres(fibres), preferred_element_type=F32)
    rank = jnp.sum(to_owner * counted, axis=0, keepdims=True).astype(jnp.int32)
    target = my_owner
    if rel:
        target = jnp.where(my_owner >= me, my_owner - me, my_owner - me + fib_count)
    base = target * lanes + rank
    place_of = jnp.concatenate([base + h * per for h in range(pack)], 1)
    row = lax.broadcasted_iota(jnp.int32, table_ref.shape, 0)
    table_ref[...] = (row == place_of).astype(F32).astype(BF16)


def write_recv_table(fib_count, pack, per, rel, me, slots_ref, table_ref):
    fibres = table_ref.shape[0] // pack
    lanes = pack * per
    total_lanes = fib_count * lanes
    owner, column = owners(slots_ref, fib_count, fibres)
    source = lax.broadcasted_iota(jnp.int32, owner.shape, 0)
    mine = (owner == me.astype(F32)).astype(F32)
    rank_in = jnp.dot(mine.astype(BF16), earlier_fibres(fibres), preferred_element_type=F32).astype(jnp.int32)
    order = source
    if rel:
        order = jnp.where(me >= source, me - source, me - source + fib_count)
    arrival = jnp.where(mine > 0.0, order * lanes + rank_in, -total_lanes)
    tall = lax.broadcasted_iota(jnp.int32, (total_lanes, fibres), 0)
    landing = jnp.zeros((ROWS, total_lanes), F32)
    for s in range(fib_count):
        hit = tall == arrival[s : s + 1, :]
        for h in range(1, pack):
            hit = hit | (tall == arrival[s : s + 1, :] + h * per)
        values = jnp.broadcast_to(column[s : s + 1, :], (ROWS, fibres)).astype(BF16)
        landing = landing + lax.dot_general(
            values, hit.astype(F32).astype(BF16), NT, preferred_element_type=F32
        )
    lane = lax.broadcasted_iota(jnp.int32, (1, total_lanes), 1)
    landing = landing[0:1, :].astype(jnp.int32)
    for h in range(1, pack):
        inside = (lane % lanes >= h * per) & (lane % lanes < (h + 1) * per)
        landing = jnp.where(inside, landing + h * fibres, landing)
    row = lax.broadcasted_iota(jnp.int32, table_ref.shape, 0)
    table_ref[...] = (row == landing).astype(F32).astype(BF16)


def stream_coupling(coupling_ref, expos):
    coupling = coupling_ref[...]
    blocks = coupling.shape[1] // LANES
    return jnp.concatenate(
        [jnp.broadcast_to(coupling[:, h * LANES : (h + 1) * LANES], (expos, LANES)) for h in range(blocks)], 0
    )


def weight_tile(coupling, usable, words, ivars, within, scale_row):
    links = scale_row * coupling
    weights = []
    weight_sum = band_sum = None
    for e, ivar in enumerate(ivars):
        weight = jnp.where(tile_words(words[e], within), ivar * usable[e], 0.0)
        band = weight * inverse_of(ivar + links)
        weights.append(weight)
        weight_sum = weight if e == 0 else weight_sum + weight
        band_sum = band if e == 0 else band_sum + band
    return weights, weight_sum, band_sum * coupling


def write_weights(place_ref, wav_count, which, coupling_v, counts_v, good_v, ivar_of, words_of, sums_ref, weight_ref, beside):
    expos, half, _ = weight_ref.shape
    coupling = coupling_v[...]
    usable = usable_rows(place_ref, counts_v, good_v)
    start = place_ref[1] * (2 * half) + which * half
    tiles = half // ROWS
    tiles_in_group = GROUP // ROWS
    for tile in range(tiles):
        beside(tile, tiles)
        group, within = divmod(tile, tiles_in_group)
        scale_row = 4.0
        if tile in (0, tiles - 1):
            row = start + ROWS * tile + lax.broadcasted_iota(jnp.int32, (ROWS, 1), 0)
            scale_row = jnp.where((row == 0) | (row == wav_count * 2 * half - 1), 2.0, 4.0)
        at = slice(ROWS * tile, ROWS * (tile + 1))
        weights, weight_sum, band_sum = weight_tile(
            coupling,
            usable,
            [words_of(e, group) for e in range(expos)],
            [ivar_of(e, tile) for e in range(expos)],
            within,
            scale_row,
        )
        for e in range(expos):
            weight_ref[e, at, :] = weights[e]
        sums_ref[0, at, :] = weight_sum
        sums_ref[1, at, :] = band_sum


def sent_kernel(
    moves, wav_count, place_ref, slots_ref, coupling_ref, counts_ref, good_ref, bits_ref, ivar_ref,
    sums_ref, weight_ref, table_ref, slots_v, coupling_v, counts_v, good_v, bits_v, ivar_v, sems,
):
    expos, width, _ = ivar_ref.shape
    half = width // 2
    which = 1 - place_ref[2]
    words = GROUP // BITS

    def part(source, target, first):
        at = pl.ds(pl.multiple_of(first, ROWS), GROUP)
        return source.at[:, at, :], target.at[:, at, :]

    waits = in_flight(
        [
            (slots_ref, slots_v),
            (coupling_ref, coupling_v),
            (counts_ref, counts_v),
            (good_ref, good_v),
            (bits_ref, bits_v),
        ]
        + [part(ivar_ref, ivar_v, which * half + g) for g in range(0, half, GROUP)]
        + [part(ivar_ref, ivar_v, (1 - which) * half + g) for g in range(0, half, GROUP)],
        sems,
    )
    waits[0].wait()
    write_send_table(*moves, place_ref[0], slots_v, table_ref)
    for wait in waits[1:5]:
        wait.wait()

    def arrive(tile, tiles):
        if ROWS * tile % GROUP == 0:
            waits[5 + ROWS * tile // GROUP].wait()

    write_weights(
        place_ref, wav_count, which, coupling_v, counts_v, good_v,
        lambda e, tile: ivar_v[e, pl.ds(pl.multiple_of(which * half + ROWS * tile, ROWS), ROWS), :],
        lambda e, group: bits_v[e, pl.ds(pl.multiple_of(which * (half // BITS) + words * group, words), words), :],
        sums_ref, weight_ref, arrive,
    )
    for wait in waits[5 + half // GROUP :]:
        wait.wait()


def sent_weights(moves, wav_count, place, slots, coupling, counts, good, bits, ivar):
    expos, width, fibres = ivar.shape
    half = width // 2
    fib_count, pack, per, _ = moves
    inputs = (slots, coupling, counts, good, bits, ivar)
    return pl.pallas_call(
        functools.partial(sent_kernel, moves, wav_count),
        in_specs=[in_smem] + [in_hbm] * 6,
        out_specs=[in_vmem] * 9,
        out_shape=[
            shaped((2, half, fibres)),
            shaped((expos, half, fibres)),
            shaped((fib_count * pack * per, pack * fibres), BF16),
        ]
        + [shaped(x.shape, x.dtype) for x in inputs],
        scratch_shapes=[pltpu.SemaphoreType.DMA((5 + width // GROUP,))],
        compiler_params=params(),
        cost_estimate=cost(20 * ivar.size, 6 * ivar.size),
        name="sent_weights",
    )(place, *held_in_hbm(*inputs))


def lay_out(source_ref, target_ref, pieces, pitch):
    expos, _, fibres = source_ref.shape
    for h in range(fibres // LANES):
        for e in range(expos):
            for first, length, at in pieces:
                target_ref[pl.ds((h * expos + e) * pitch + at, length), :] = source_ref[
                    e, pl.ds(first, length), pl.ds(h * LANES, LANES)
                ]


def kept_kernel(
    wav_count, place_ref, coupling_ref, counts_ref, good_ref, pixels_ref, ivar_ref, bits_ref,
    sums_ref, weight_ref, up_ref, down_ref, ivar_s, pixel_s,
):
    expos, width, fibres = ivar_ref.shape
    half = width // 2
    streams = expos * fibres // LANES
    count = -(-HALO // ROWS) * ROWS
    pitch = odd(2 * count)
    which = place_ref[2]
    words = GROUP // BITS
    edges = [(0, count, 0), (width - count, count, count)]
    lay_out(ivar_ref, ivar_s, edges, pitch)
    lay_out(pixels_ref, pixel_s, edges, pitch)
    coupling = stream_coupling(coupling_ref, expos)
    back = 1.0 / coupling
    zero = jnp.zeros((streams, LANES), F32)
    states = [(zero, zero + 1.0, zero), (zero, zero + 1.0, zero)]

    def eliminate(tile, tiles):
        for i in range(HALO * tile // tiles, HALO * (tile + 1) // tiles):
            for side, row in enumerate((2 * count - HALO + i, HALO - 1 - i)):
                at = pl.ds(row, streams, stride=pitch)
                states[side] = advance(states[side], ivar_s[at, :], pixel_s[at, :], back)
                if i % 24 == 23:
                    states[side] = rescaled(states[side])

    write_weights(
        place_ref, wav_count, which, coupling_ref, counts_ref, good_ref,
        lambda e, tile: ivar_ref[e, pl.ds(pl.multiple_of(which * half + ROWS * tile, ROWS), ROWS), :],
        lambda e, group: bits_ref[e, pl.ds(pl.multiple_of(which * (half // BITS) + words * group, words), words), :],
        sums_ref, weight_ref, eliminate,
    )
    for (n, d, b), out_ref in zip(states, (up_ref, down_ref)):
        scale = 1.0 / (d + n)
        out_ref[0] = coupling * (n * scale)
        out_ref[1] = b * scale


def kept_weights(wav_count, place, coupling, counts, good, pixels, ivar, bits):
    expos, width, fibres = ivar.shape
    half = width // 2
    streams = expos * fibres // LANES
    count = -(-HALO // ROWS) * ROWS
    edge = shaped((2, streams, LANES))
    edge_scratch = pltpu.VMEM((streams * odd(2 * count), LANES), F32)
    return pl.pallas_call(
        functools.partial(kept_kernel, wav_count),
        in_specs=[in_smem] + [in_vmem] * 6,
        out_specs=[in_vmem] * 4,
        out_shape=[shaped((2, half, fibres)), shaped((expos, half, fibres)), edge, edge],
        scratch_shapes=[edge_scratch, edge_scratch],
        compiler_params=params(),
        cost_estimate=cost(20 * ivar.size, 6 * ivar.size),
        name="kept_weights",
    )(place, coupling, counts, good, pixels, ivar, bits)


def layout_kernel(arrived_ref, pixels_ref, ivar_ref, pixel_out, ivar_out):
    width = ivar_ref.shape[1]
    lay_out(ivar_ref, ivar_out, [(0, width, 0)], odd(width))
    lay_out(pixels_ref, pixel_out, [(0, width, 0)], odd(width))


def stream_layout(arrived, pixels, ivar):
    expos, width, fibres = ivar.shape
    streams = expos * fibres // LANES
    laid = shaped((streams * odd(width), LANES))
    return pl.pallas_call(
        layout_kernel,
        in_specs=[in_vmem] * 3,
        out_specs=[in_vmem] * 2,
        out_shape=[laid, laid],
        compiler_params=params(),
        cost_estimate=cost(0, 16 * ivar.size),
        name="stream_layout",
    )(arrived, pixels, ivar)


def solve_kernel(
    wav_count, place_ref, coupling_ref, left_ref, right_ref, pixel_ref, ivar_ref, weight_ref,
    theirs_ref, solved_s, lead_s, rest_s,
):
    streams = left_ref.shape[1]
    expos, half, fibres = weight_ref.shape
    width = 2 * half
    pitch = odd(width)
    middle = half
    coupling = stream_coupling(coupling_ref, expos)
    back = 1.0 / coupling

    def row_at(i):
        return pl.ds(i, streams, stride=pitch)

    def begin(edge_ref, outermost):
        n = jnp.where(place_ref[1] == outermost, 0.0, edge_ref[0]) * back
        return (n, 1.0 - n, jnp.where(place_ref[1] == outermost, 0.0, edge_ref[1]))

    def keep(side, i, state):
        n, d, b = state
        inverse = inverse_of(d + n)
        lead_s[side, i] = d * inverse
        rest_s[side, i] = b * inverse

    unrolled = divisor_of(middle, 24)

    def eliminate(it, states):
        states = list(states)
        for k in range(unrolled):
            i = it * unrolled + k
            for side, row in enumerate((i, width - 1 - i)):
                keep(side, i, states[side])
                states[side] = advance(states[side], ivar_ref[row_at(row), :], pixel_ref[row_at(row), :], back)
        return tuple(rescaled(state) for state in states)

    states = lax.fori_loop(0, middle // unrolled, eliminate, (begin(left_ref, 0), begin(right_ref, wav_count - 1)))
    for side in range(2):
        keep(side, middle, states[side])
    lead, rest = lead_s[0, middle], rest_s[0, middle]
    lead_r, rest_r = lead_s[1, middle], rest_s[1, middle]
    left = (rest + lead * rest_r) / (1.0 - lead * lead_r)
    right = rest_r + lead_r * left
    several = divisor_of(middle, 48)

    def after_both(near, far):
        return far[0] * near[0], far[1] + far[0] * near[1]

    def step(factors, value):
        return factors[1] + factors[0] * value

    def substitute(it, values):
        values = list(values)
        for k in range(0, several, 4):
            for side in range(2):
                rows = [middle - 1 - (it * several + k + m) for m in range(4)]
                one, two, three, four = [(lead_s[side, i], rest_s[side, i]) for i in rows]
                first_two = after_both(one, two)
                all_four = after_both(first_two, after_both(three, four))
                value = values[side]
                third = step(first_two, value)
                solved = [value, step(one, value), third, step(three, third)]
                values[side] = step(all_four, value)
                for i, x in zip(rows, solved):
                    solved_s[row_at(i if side == 0 else width - 1 - i), :] = x
        return tuple(values)

    lax.fori_loop(0, middle // several, substitute, (left, right))

    add_up(theirs_ref, weight_ref, solved_s, coupling_ref, 1 - place_ref[2])


def add_up(out_ref, weight_ref, solved_ref, coupling_ref, which):
    expos, half, fibres = weight_ref.shape
    pitch = odd(2 * half)
    start = which * half
    back = 1.0 / coupling_ref[...]
    unrolled = divisor_of(half // ROWS, 5)

    def body(g, carry):
        for k in range(unrolled):
            row = pl.multiple_of((g * unrolled + k) * ROWS, ROWS)
            for h in range(fibres // LANES):
                total = None
                for e in range(expos):
                    at = pl.ds((h * expos + e) * pitch + start + row, ROWS)
                    term = weight_ref[e, pl.ds(row, ROWS), pl.ds(h * LANES, LANES)] * solved_ref[at, :]
                    total = term if e == 0 else total + term
                out_ref[0, pl.ds(row, ROWS), pl.ds(h * LANES, LANES)] = total * back[:, h * LANES : (h + 1) * LANES]
        return carry

    lax.fori_loop(0, half // ROWS // unrolled, body, 0)


def flux_sums(wav_count, place, coupling, left, right, pixels, ivar, weight):
    expos, half, fibres = weight.shape
    streams = left.shape[1]
    factor_scratch = pltpu.VMEM((2, half + 1, streams, LANES), F32)
    return pl.pallas_call(
        functools.partial(solve_kernel, wav_count),
        in_specs=[in_smem] + [in_vmem] * 6,
        out_specs=[in_vmem, in_vmem],
        out_shape=[shaped((1, half, fibres)), shaped(pixels.shape)],
        scratch_shapes=[factor_scratch, factor_scratch],
        compiler_params=params(),
        cost_estimate=cost(0, 0),
        name="flux_sums",
    )(place, coupling, left, right, pixels, ivar, weight)


def kept_flux_kernel(place_ref, coupling_ref, solved_ref, weight_ref, out_ref):
    add_up(out_ref, weight_ref, solved_ref, coupling_ref, place_ref[2])


def kept_flux(place, coupling, solved, weight):
    expos, half, fibres = weight.shape
    return pl.pallas_call(
        kept_flux_kernel,
        in_specs=[in_smem] + [in_vmem] * 3,
        out_specs=in_vmem,
        out_shape=shaped((1, half, fibres)),
        compiler_params=params(),
        cost_estimate=cost(2 * weight.size, 8 * weight.size),
        name="kept_flux",
    )(place, coupling, solved, weight)


def split_dot(x, table, dims):
    top = x.astype(BF16)
    low = (x - top.astype(F32)).astype(BF16)
    both = lax.dot_general(jnp.concatenate([top, low], 0), table, dims, preferred_element_type=F32)
    return both[: x.shape[0]] + both[x.shape[0] :]


def sort_kernel(pack, scaled, theirs_ref, mine_ref, table_ref, *refs):
    values, rows, _ = mine_ref.shape
    part = rows // pack
    totals = [mine_ref[v] + theirs_ref[v] for v in range(values)]
    if scaled:
        scale_ref, _, *out_refs = refs
        totals = [t * scale_ref[...] for t in totals]
    else:
        *out_refs, scale_ref = refs
        scale = 1.0 / jnp.maximum(totals[0], 1.0)
        scale_ref[...] = scale
        totals[1] = totals[1] * scale
    x = jnp.concatenate(
        [jnp.concatenate([t[h * part : (h + 1) * part] for h in range(pack)], 1) for t in totals], 0
    )
    moved = split_dot(x, table_ref[...], NT)
    lanes = moved.shape[1] // len(out_refs)
    for d, out_ref in enumerate(out_refs):
        for v in range(values):
            out_ref[v] = moved[v * part : (v + 1) * part, d * lanes : (d + 1) * lanes]


def sort_fibres(theirs, mine, table, pack, pieces, scale=None, ahead=None):
    values, rows, fibres = mine.shape
    lanes = table.shape[0] // pieces
    scaled = scale is not None
    outs = [shaped((values, rows // pack, lanes))] * pieces + ([] if scaled else [shaped((rows, fibres))])
    args = (theirs, mine, table) + ((scale, ahead) if scaled else ())
    return pl.pallas_call(
        functools.partial(sort_kernel, pack, scaled),
        in_specs=[in_vmem] * len(args),
        out_specs=[in_vmem] * len(outs),
        out_shape=outs,
        compiler_params=params(),
        cost_estimate=cost(0, 0),
        name="sort_flux" if scaled else "sort_weights",
    )(*args)


def exchange(pieces, fib_count):
    if len(pieces) == 1:
        return [lax.all_to_all(pieces[0], "fib", split_axis=2, concat_axis=2, tiled=True)]
    arrived = [pieces[0]]
    for d in range(1, fib_count):
        arrived.append(lax.ppermute(pieces[d], "fib", [(i, (i + d) % fib_count) for i in range(fib_count)]))
    return arrived


def landed(refs, table):
    values, part, _ = refs[0].shape
    x = jnp.concatenate(
        [jnp.concatenate([ref[v] for ref in refs], 1) if len(refs) > 1 else refs[0][v] for v in range(values)], 0
    )
    moved = split_dot(x, table, NT)
    return [moved[v * part : (v + 1) * part] for v in range(values)]


def columns_of(table, which, pieces):
    lanes = table.shape[1] // pieces
    return jnp.concatenate([table[:, d * lanes : (d + 1) * lanes] for d in which], 1)


def early_kernel(moves, which, pieces, place_ref, slots_ref, *refs):
    *piece_refs, table_ref, sums_ref = refs
    write_recv_table(*moves, place_ref[0], slots_ref, table_ref)
    for v, moved in enumerate(landed(piece_refs, columns_of(table_ref[...], which, pieces))):
        sums_ref[v] = moved


def place_early(moves, which, place, slots, weight_pieces, fibres):
    fib_count, pack, per, _ = moves
    early = [weight_pieces[d] for d in which]
    values, part, _ = early[0].shape
    return pl.pallas_call(
        functools.partial(early_kernel, moves, which, len(weight_pieces)),
        in_specs=[in_smem] + [in_vmem] * (1 + len(early)),
        out_specs=[in_vmem] * 2,
        out_shape=[
            shaped((pack * fibres, fib_count * pack * per), BF16),
            shaped((values, part, pack * fibres)),
        ],
        compiler_params=params(),
        cost_estimate=cost(0, 0),
        name="place_early",
    )(place, slots, *early)


def weights_end_kernel(pack, total, late, pieces, place_ref, table_ref, sums_ref, *refs):
    *late_refs, ivar_ref, res_ref = refs
    weight, band = sums_ref[0], sums_ref[1]
    if late:
        more_weight, more_band = landed(late_refs, columns_of(table_ref[...], late, pieces))
        weight, band = weight + more_weight, band + more_band
    rows, fibres = ivar_ref.shape
    part = rows // pack
    start = (place_ref[1] * 2 + place_ref[2]) * rows
    for h in range(pack):
        at = slice(h * part, (h + 1) * part)
        cut = slice(h * fibres, (h + 1) * fibres)
        row = start + h * part + lax.broadcasted_iota(jnp.int32, (part, 1), 0)
        w, b = weight[:, cut], band[:, cut]
        before = jnp.where(row == 0, 0.0, b)
        after = jnp.where(row == total - 1, 0.0, b)
        ivar_ref[at, :] = w
        res_ref[0, at, :] = before
        res_ref[1, at, :] = jnp.minimum(w, 1.0) - before - after
        res_ref[2, at, :] = after


def end_weights(place, table, sums, late, weight_pieces, pack, fibres, total):
    rows = sums.shape[1] * pack
    late_pieces = [weight_pieces[d] for d in late]
    return pl.pallas_call(
        functools.partial(weights_end_kernel, pack, total, late, len(weight_pieces)),
        in_specs=[in_smem] + [in_vmem] * (2 + len(late)),
        out_specs=[in_vmem] * 2,
        out_shape=[shaped((rows, fibres)), shaped((3, rows, fibres))],
        compiler_params=params(),
        cost_estimate=cost(0, 0),
        name="end_weights",
    )(place, table, sums, *late_pieces)


def flux_end_kernel(pack, order, table_ref, *refs):
    *piece_refs, flux_ref = refs
    (flux,) = landed([piece_refs[order.index(d)] for d in range(len(order))], table_ref[...])
    rows, fibres = flux_ref.shape
    part = rows // pack
    for h in range(pack):
        flux_ref[h * part : (h + 1) * part, :] = flux[:, h * fibres : (h + 1) * fibres]


def end_flux(table, pieces, pack, fibres):
    rows = pieces[0].shape[1] * pack
    order = sorted(range(len(pieces)), key=lambda d: (d > 0, abs(2 * d - len(pieces))))
    return pl.pallas_call(
        functools.partial(flux_end_kernel, pack, order),
        in_specs=[in_vmem] * (1 + len(pieces)),
        out_specs=in_vmem,
        out_shape=shaped((rows, fibres)),
        compiler_params=params(),
        cost_estimate=cost(2 * rows * table.size, 2 * rows * fibres * 4),
        name="end_flux",
    )(table, *(pieces[d] for d in order))


def after(value, done):
    return lax.optimization_barrier((value, done))[0]


def per_device(pixels, pixel_ivar, clip_bits, coupling, counts, good_flags, owner_slot):
    expos, width, fibres = pixels.shape
    fib_count, wav_count = lax.axis_size("fib"), lax.axis_size("wav")
    total = width * wav_count
    per = fibres // fib_count
    rows = width // 2
    pack = max(1, LANES // per)
    while pack > 1 and rows % (pack * ROWS):
        pack //= 2
    rel = pack * per == LANES
    pieces = fib_count if rel else 1
    place = jnp.stack([lax.axis_index(axis) for axis in ("fib", "wav", "exp")]).astype(jnp.int32)
    coupling, counts, slots = coupling[None], counts[None], owner_slot[None]
    swap = [(0, 1), (1, 0)]
    moves = (fib_count, pack, per, rel)

    theirs, weight_t, send_table, slots, coupling, counts, good, bits, ivar = sent_weights(
        moves, wav_count, place, slots, coupling, counts, good_flags, clip_bits, pixel_ivar
    )
    arriving = lax.ppermute(theirs, "exp", swap)
    mine, weight_m, up, down = kept_weights(
        wav_count, place, coupling, counts, good, pixels, ivar, bits
    )
    upward = [(i, (i + 1) % wav_count) for i in range(wav_count)]
    left = lax.ppermute(up, "wav", upward)
    right = lax.ppermute(down, "wav", [(j, i) for i, j in upward])
    *sorted_pieces, scale = sort_fibres(arriving, mine, send_table, pack, pieces)
    weight_pieces = exchange(sorted_pieces, fib_count)

    pixel_s, ivar_s = stream_layout(left[0] + right[0], pixels, ivar)
    theirs, solved = flux_sums(wav_count, place, coupling, left, right, pixel_s, ivar_s, weight_t)
    early = [0, fib_count // 2] if rel else [0]
    late = [d for d in range(pieces) if d not in early]
    ahead = weight_pieces[early[-1]][0, :ROWS, :] * 0.5
    arriving = lax.ppermute(theirs, "exp", swap)
    mine = kept_flux(after(place, theirs), coupling, solved, weight_m)
    sorted_pieces = sort_fibres(arriving, mine, send_table, pack, pieces, scale, ahead)
    flux_pieces = exchange(sorted_pieces, fib_count)
    recv_table, placed = place_early(moves, early, after(place, sorted_pieces[0]), slots, weight_pieces, fibres)
    ivar, res = end_weights(place, recv_table, placed, late, weight_pieces, pack, fibres, total)
    flux = end_flux(recv_table, flux_pieces, pack, fibres)
    return (flux, ivar, res)


def solution(mesh):
    return jax.shard_map(
        per_device,
        mesh=mesh,
        in_specs=(
            P("exp", "wav", "fib"),
            P("exp", "wav", "fib"),
            P("exp", "wav", "fib"),
            P("fib"),
            P("fib"),
            P("exp", "fib"),
            P(),
        ),
        out_specs=(
            P(("wav", "exp"), "fib"),
            P(("wav", "exp"), "fib"),
            P(None, ("wav", "exp"), "fib"),
        ),
        check_vma=False,
    )
```

```python
import functools

import jax
import jax.numpy as jnp
from jax import lax
from jax.experimental import pallas as pl
from jax.experimental.pallas import tpu as pltpu
from jax.sharding import PartitionSpec as P

HALO = 50
BITS = 15
LANES = 128
ROWS = 8
GROUP = 120
VMEM_BYTES = 32 * 1024 * 1024
F32 = jnp.float32
BF16 = jnp.bfloat16
NT = (((1,), (1,)), ((), ()))

in_vmem = pl.BlockSpec(memory_space=pltpu.VMEM)
in_smem = pl.BlockSpec(memory_space=pltpu.SMEM)
in_hbm = pl.BlockSpec(memory_space=pltpu.HBM)


def params():
    return pltpu.CompilerParams(vmem_limit_bytes=VMEM_BYTES)


def cost(flops, moved):
    return pl.CostEstimate(flops=int(flops), bytes_accessed=int(moved), transcendentals=0)


def held_in_hbm(*arrays):
    return [pltpu.with_memory_space_constraint(array, pltpu.HBM) for array in arrays]


def shaped(shape, dtype=F32):
    return jax.ShapeDtypeStruct(shape, dtype)


def usable_rows(place_ref, counts_ref, good_ref):
    count = good_ref.shape[0]
    return [
        good_ref[e : e + 1, :].astype(F32)
        * jnp.where(place_ref[2] * count + e < counts_ref[...], 1.0, 0.0)
        for e in range(count)
    ]


def tile_bits(tile):
    first, last = (ROWS * tile) // BITS, (ROWS * tile + ROWS - 1) // BITS
    split = BITS * last - ROWS * tile
    row = lax.broadcasted_iota(jnp.int32, (ROWS, 1), 0)
    word = jnp.where(row >= split, last, first)
    return first, last, split, jnp.left_shift(1, ROWS * tile + row - BITS * word)


def tile_words(words, tile):
    first, last, split, mask = tile_bits(tile)
    picked = words[first : first + 1, :]
    if last != first:
        row = lax.broadcasted_iota(jnp.int32, (ROWS, 1), 0)
        picked = jnp.where(row >= split, words[last : last + 1, :], picked)
    return (picked & mask) != 0


def in_flight(pairs, sems, at=0):
    copies = [pltpu.make_async_copy(source, target, sems.at[at + i]) for i, (source, target) in enumerate(pairs)]
    for copy in copies:
        copy.start()
    return copies


def inverse_of(x):
    guess = pl.reciprocal(x, approx=True)
    return guess * (2.0 - x * guess)


def advance(state, ivar, pixel, back_coupling):
    n, d, b = state
    ratio = ivar * back_coupling
    next_d = d + n
    return (n * (1.0 + ratio) + ratio * d, next_d, b + (ivar * pixel) * next_d)


def rescaled(state):
    scale = inverse_of(state[1])
    return tuple(part * scale for part in state)


def odd(rows):
    return rows + 1 - rows % 2


def divisor_of(size, most):
    return max(k for k in range(1, most + 1) if size % k == 0)


def owners(slots_ref, fib_count, fibres):
    rows = [slots_ref[:, s * fibres : (s + 1) * fibres].astype(F32) for s in range(fib_count)]
    sources = -(-fib_count // ROWS) * ROWS
    if sources > fib_count:
        rows.append(jnp.full((sources - fib_count, fibres), -1.0, F32))
    slots = jnp.concatenate(rows, 0)
    owner = jnp.floor((slots + 0.5) * (1.0 / fibres))
    return owner, slots - owner * fibres


def earlier_fibres(fibres):
    row = lax.broadcasted_iota(jnp.int32, (fibres, fibres), 0)
    col = lax.broadcasted_iota(jnp.int32, (fibres, fibres), 1)
    return (row < col).astype(F32).astype(BF16)


def write_send_table(fib_count, pack, per, rel, me, slots_ref, table_ref):
    fibres = table_ref.shape[1] // pack
    lanes = pack * per
    owner, _ = owners(slots_ref, fib_count, fibres)
    source = lax.broadcasted_iota(jnp.int32, owner.shape, 0)
    my_owner = jnp.sum(jnp.where(source == me, owner, 0.0), axis=0, keepdims=True).astype(jnp.int32)
    to_owner = (source == my_owner).astype(F32)
    counted = jnp.dot(to_owner.astype(BF16), earlier_fibres(fibres), preferred_element_type=F32)
    rank = jnp.sum(to_owner * counted, axis=0, keepdims=True).astype(jnp.int32)
    target = my_owner ^ me if rel else my_owner
    base = target * lanes + rank
    place_of = jnp.concatenate([base + h * per for h in range(pack)], 1)
    row = lax.broadcasted_iota(jnp.int32, table_ref.shape, 0)
    table_ref[...] = (row == place_of).astype(F32).astype(BF16)


def write_recv_table(fib_count, pack, per, rel, me, slots_ref, table_ref):
    fibres = table_ref.shape[0] // pack
    lanes = pack * per
    total_lanes = fib_count * lanes
    owner, column = owners(slots_ref, fib_count, fibres)
    source = lax.broadcasted_iota(jnp.int32, owner.shape, 0)
    mine = (owner == me.astype(F32)).astype(F32)
    rank_in = jnp.dot(mine.astype(BF16), earlier_fibres(fibres), preferred_element_type=F32).astype(jnp.int32)
    order = source ^ me if rel else source
    arrival = jnp.where(mine > 0.0, order * lanes + rank_in, -total_lanes)
    tall = lax.broadcasted_iota(jnp.int32, (total_lanes, fibres), 0)
    landing = jnp.zeros((ROWS, total_lanes), F32)
    for s in range(fib_count):
        hit = tall == arrival[s : s + 1, :]
        for h in range(1, pack):
            hit = hit | (tall == arrival[s : s + 1, :] + h * per)
        values = jnp.broadcast_to(column[s : s + 1, :], (ROWS, fibres)).astype(BF16)
        landing = landing + lax.dot_general(
            values, hit.astype(F32).astype(BF16), NT, preferred_element_type=F32
        )
    lane = lax.broadcasted_iota(jnp.int32, (1, total_lanes), 1)
    landing = landing[0:1, :].astype(jnp.int32)
    for h in range(1, pack):
        inside = (lane % lanes >= h * per) & (lane % lanes < (h + 1) * per)
        landing = jnp.where(inside, landing + h * fibres, landing)
    row = lax.broadcasted_iota(jnp.int32, table_ref.shape, 0)
    table_ref[...] = (row == landing).astype(F32).astype(BF16)


def stream_coupling(coupling_ref, expos):
    coupling = coupling_ref[...]
    blocks = coupling.shape[1] // LANES
    return jnp.concatenate(
        [jnp.broadcast_to(coupling[:, h * LANES : (h + 1) * LANES], (expos, LANES)) for h in range(blocks)], 0
    )


def weight_tile(coupling, usable, words, ivars, within, scale_row):
    links = scale_row * coupling
    weights = []
    weight_sum = band_sum = None
    for e, ivar in enumerate(ivars):
        weight = jnp.where(tile_words(words[e], within), ivar * usable[e], 0.0)
        band = weight * inverse_of(ivar + links)
        weights.append(weight)
        weight_sum = weight if e == 0 else weight_sum + weight
        band_sum = band if e == 0 else band_sum + band
    return weights, weight_sum, band_sum * coupling


def write_weights(place_ref, wav_count, which, coupling_v, counts_v, good_v, ivar_of, words_of, sums_ref, weight_ref, beside):
    expos, half, _ = weight_ref.shape
    coupling = coupling_v[...]
    usable = usable_rows(place_ref, counts_v, good_v)
    start = place_ref[1] * (2 * half) + which * half
    tiles = half // ROWS
    tiles_in_group = GROUP // ROWS
    for tile in range(tiles):
        beside(tile, tiles)
        group, within = divmod(tile, tiles_in_group)
        scale_row = 4.0
        if tile in (0, tiles - 1):
            row = start + ROWS * tile + lax.broadcasted_iota(jnp.int32, (ROWS, 1), 0)
            scale_row = jnp.where((row == 0) | (row == wav_count * 2 * half - 1), 2.0, 4.0)
        at = slice(ROWS * tile, ROWS * (tile + 1))
        weights, weight_sum, band_sum = weight_tile(
            coupling,
            usable,
            [words_of(e, group) for e in range(expos)],
            [ivar_of(e, tile) for e in range(expos)],
            within,
            scale_row,
        )
        for e in range(expos):
            weight_ref[e, at, :] = weights[e]
        sums_ref[0, at, :] = weight_sum
        sums_ref[1, at, :] = band_sum


def sent_kernel(
    moves, wav_count, place_ref, slots_ref, coupling_ref, counts_ref, good_ref, bits_ref, ivar_ref,
    sums_ref, weight_ref, table_ref, slots_v, coupling_v, counts_v, good_v, bits_v, ivar_v, sems,
):
    expos, width, _ = ivar_ref.shape
    half = width // 2
    which = 1 - place_ref[2]
    words = GROUP // BITS

    def part(source, target, first):
        at = pl.ds(pl.multiple_of(first, ROWS), GROUP)
        return source.at[:, at, :], target.at[:, at, :]

    waits = in_flight(
        [
            (slots_ref, slots_v),
            (coupling_ref, coupling_v),
            (counts_ref, counts_v),
            (good_ref, good_v),
            (bits_ref, bits_v),
        ]
        + [part(ivar_ref, ivar_v, which * half + g) for g in range(0, half, GROUP)]
        + [part(ivar_ref, ivar_v, (1 - which) * half + g) for g in range(0, half, GROUP)],
        sems,
    )
    waits[0].wait()
    write_send_table(*moves, place_ref[0], slots_v, table_ref)
    for wait in waits[1:5]:
        wait.wait()

    def arrive(tile, tiles):
        if ROWS * tile % GROUP == 0:
            waits[5 + ROWS * tile // GROUP].wait()

    write_weights(
        place_ref, wav_count, which, coupling_v, counts_v, good_v,
        lambda e, tile: ivar_v[e, pl.ds(pl.multiple_of(which * half + ROWS * tile, ROWS), ROWS), :],
        lambda e, group: bits_v[e, pl.ds(pl.multiple_of(which * (half // BITS) + words * group, words), words), :],
        sums_ref, weight_ref, arrive,
    )
    for wait in waits[5 + half // GROUP :]:
        wait.wait()


def sent_weights(moves, wav_count, place, slots, coupling, counts, good, bits, ivar):
    expos, width, fibres = ivar.shape
    half = width // 2
    fib_count, pack, per, _ = moves
    inputs = (slots, coupling, counts, good, bits, ivar)
    return pl.pallas_call(
        functools.partial(sent_kernel, moves, wav_count),
        in_specs=[in_smem] + [in_hbm] * 6,
        out_specs=[in_vmem] * 9,
        out_shape=[
            shaped((2, half, fibres)),
            shaped((expos, half, fibres)),
            shaped((fib_count * pack * per, pack * fibres), BF16),
        ]
        + [shaped(x.shape, x.dtype) for x in inputs],
        scratch_shapes=[pltpu.SemaphoreType.DMA((5 + width // GROUP,))],
        compiler_params=params(),
        cost_estimate=cost(20 * ivar.size, 6 * ivar.size),
        name="sent_weights",
    )(place, *held_in_hbm(*inputs))


def lay_out(source_ref, target_ref, pieces, pitch):
    expos, _, fibres = source_ref.shape
    for h in range(fibres // LANES):
        for e in range(expos):
            for first, length, at in pieces:
                target_ref[pl.ds((h * expos + e) * pitch + at, length), :] = source_ref[
                    e, pl.ds(first, length), pl.ds(h * LANES, LANES)
                ]


def kept_kernel(
    wav_count, place_ref, coupling_ref, counts_ref, good_ref, pixels_ref, ivar_ref, bits_ref,
    sums_ref, weight_ref, up_ref, down_ref, ivar_s, pixel_s,
):
    expos, width, fibres = ivar_ref.shape
    half = width // 2
    streams = expos * fibres // LANES
    count = -(-HALO // ROWS) * ROWS
    pitch = odd(2 * count)
    which = place_ref[2]
    words = GROUP // BITS
    edges = [(0, count, 0), (width - count, count, count)]
    lay_out(ivar_ref, ivar_s, edges, pitch)
    lay_out(pixels_ref, pixel_s, edges, pitch)
    coupling = stream_coupling(coupling_ref, expos)
    back = 1.0 / coupling
    zero = jnp.zeros((streams, LANES), F32)
    states = [(zero, zero + 1.0, zero), (zero, zero + 1.0, zero)]

    def eliminate(tile, tiles):
        for i in range(HALO * tile // tiles, HALO * (tile + 1) // tiles):
            for side, row in enumerate((2 * count - HALO + i, HALO - 1 - i)):
                at = pl.ds(row, streams, stride=pitch)
                states[side] = advance(states[side], ivar_s[at, :], pixel_s[at, :], back)
                if i % 24 == 23:
                    states[side] = rescaled(states[side])

    write_weights(
        place_ref, wav_count, which, coupling_ref, counts_ref, good_ref,
        lambda e, tile: ivar_ref[e, pl.ds(pl.multiple_of(which * half + ROWS * tile, ROWS), ROWS), :],
        lambda e, group: bits_ref[e, pl.ds(pl.multiple_of(which * (half // BITS) + words * group, words), words), :],
        sums_ref, weight_ref, eliminate,
    )
    for (n, d, b), out_ref in zip(states, (up_ref, down_ref)):
        scale = 1.0 / (d + n)
        out_ref[0] = coupling * (n * scale)
        out_ref[1] = b * scale


def kept_weights(wav_count, place, coupling, counts, good, pixels, ivar, bits):
    expos, width, fibres = ivar.shape
    half = width // 2
    streams = expos * fibres // LANES
    count = -(-HALO // ROWS) * ROWS
    edge = shaped((2, streams, LANES))
    edge_scratch = pltpu.VMEM((streams * odd(2 * count), LANES), F32)
    return pl.pallas_call(
        functools.partial(kept_kernel, wav_count),
        in_specs=[in_smem] + [in_vmem] * 6,
        out_specs=[in_vmem] * 4,
        out_shape=[shaped((2, half, fibres)), shaped((expos, half, fibres)), edge, edge],
        scratch_shapes=[edge_scratch, edge_scratch],
        compiler_params=params(),
        cost_estimate=cost(20 * ivar.size, 6 * ivar.size),
        name="kept_weights",
    )(place, coupling, counts, good, pixels, ivar, bits)


def layout_kernel(arrived_ref, pixels_ref, ivar_ref, pixel_out, ivar_out):
    width = ivar_ref.shape[1]
    lay_out(ivar_ref, ivar_out, [(0, width, 0)], odd(width))
    lay_out(pixels_ref, pixel_out, [(0, width, 0)], odd(width))


def stream_layout(arrived, pixels, ivar):
    expos, width, fibres = ivar.shape
    streams = expos * fibres // LANES
    laid = shaped((streams * odd(width), LANES))
    return pl.pallas_call(
        layout_kernel,
        in_specs=[in_vmem] * 3,
        out_specs=[in_vmem] * 2,
        out_shape=[laid, laid],
        compiler_params=params(),
        cost_estimate=cost(0, 16 * ivar.size),
        name="stream_layout",
    )(arrived, pixels, ivar)


def solve_kernel(
    wav_count, place_ref, coupling_ref, left_ref, right_ref, pixel_ref, ivar_ref, weight_ref,
    theirs_ref, solved_s, lead_s, rest_s,
):
    streams = left_ref.shape[1]
    expos, half, fibres = weight_ref.shape
    width = 2 * half
    pitch = odd(width)
    middle = half
    coupling = stream_coupling(coupling_ref, expos)
    back = 1.0 / coupling

    def row_at(i):
        return pl.ds(i, streams, stride=pitch)

    def begin(edge_ref, outermost):
        n = jnp.where(place_ref[1] == outermost, 0.0, edge_ref[0]) * back
        return (n, 1.0 - n, jnp.where(place_ref[1] == outermost, 0.0, edge_ref[1]))

    def keep(side, i, state):
        n, d, b = state
        inverse = inverse_of(d + n)
        lead_s[side, i] = d * inverse
        rest_s[side, i] = b * inverse

    unrolled = divisor_of(middle, 24)

    def eliminate(it, states):
        states = list(states)
        for k in range(unrolled):
            i = it * unrolled + k
            for side, row in enumerate((i, width - 1 - i)):
                keep(side, i, states[side])
                states[side] = advance(states[side], ivar_ref[row_at(row), :], pixel_ref[row_at(row), :], back)
        return tuple(rescaled(state) for state in states)

    states = lax.fori_loop(0, middle // unrolled, eliminate, (begin(left_ref, 0), begin(right_ref, wav_count - 1)))
    for side in range(2):
        keep(side, middle, states[side])
    lead, rest = lead_s[0, middle], rest_s[0, middle]
    lead_r, rest_r = lead_s[1, middle], rest_s[1, middle]
    left = (rest + lead * rest_r) / (1.0 - lead * lead_r)
    right = rest_r + lead_r * left
    several = divisor_of(middle, 48)

    def after_both(near, far):
        return far[0] * near[0], far[1] + far[0] * near[1]

    def step(factors, value):
        return factors[1] + factors[0] * value

    def substitute(it, values):
        values = list(values)
        for k in range(0, several, 4):
            for side in range(2):
                rows = [middle - 1 - (it * several + k + m) for m in range(4)]
                one, two, three, four = [(lead_s[side, i], rest_s[side, i]) for i in rows]
                first_two = after_both(one, two)
                all_four = after_both(first_two, after_both(three, four))
                value = values[side]
                third = step(first_two, value)
                solved = [value, step(one, value), third, step(three, third)]
                values[side] = step(all_four, value)
                for i, x in zip(rows, solved):
                    solved_s[row_at(i if side == 0 else width - 1 - i), :] = x
        return tuple(values)

    lax.fori_loop(0, middle // several, substitute, (left, right))

    add_up(theirs_ref, weight_ref, solved_s, coupling_ref, 1 - place_ref[2])


def add_up(out_ref, weight_ref, solved_ref, coupling_ref, which):
    expos, half, fibres = weight_ref.shape
    pitch = odd(2 * half)
    start = which * half
    back = 1.0 / coupling_ref[...]
    unrolled = divisor_of(half // ROWS, 5)

    def body(g, carry):
        for k in range(unrolled):
            row = pl.multiple_of((g * unrolled + k) * ROWS, ROWS)
            for h in range(fibres // LANES):
                total = None
                for e in range(expos):
                    at = pl.ds((h * expos + e) * pitch + start + row, ROWS)
                    term = weight_ref[e, pl.ds(row, ROWS), pl.ds(h * LANES, LANES)] * solved_ref[at, :]
                    total = term if e == 0 else total + term
                out_ref[0, pl.ds(row, ROWS), pl.ds(h * LANES, LANES)] = total * back[:, h * LANES : (h + 1) * LANES]
        return carry

    lax.fori_loop(0, half // ROWS // unrolled, body, 0)


def flux_sums(wav_count, place, coupling, left, right, pixels, ivar, weight):
    expos, half, fibres = weight.shape
    streams = left.shape[1]
    factor_scratch = pltpu.VMEM((2, half + 1, streams, LANES), F32)
    return pl.pallas_call(
        functools.partial(solve_kernel, wav_count),
        in_specs=[in_smem] + [in_vmem] * 6,
        out_specs=[in_vmem, in_vmem],
        out_shape=[shaped((1, half, fibres)), shaped(pixels.shape)],
        scratch_shapes=[factor_scratch, factor_scratch],
        compiler_params=params(),
        cost_estimate=cost(0, 0),
        name="flux_sums",
    )(place, coupling, left, right, pixels, ivar, weight)


def kept_flux_kernel(place_ref, coupling_ref, solved_ref, weight_ref, out_ref):
    add_up(out_ref, weight_ref, solved_ref, coupling_ref, place_ref[2])


def kept_flux(place, coupling, solved, weight):
    expos, half, fibres = weight.shape
    return pl.pallas_call(
        kept_flux_kernel,
        in_specs=[in_smem] + [in_vmem] * 3,
        out_specs=in_vmem,
        out_shape=shaped((1, half, fibres)),
        compiler_params=params(),
        cost_estimate=cost(2 * weight.size, 8 * weight.size),
        name="kept_flux",
    )(place, coupling, solved, weight)


def split_dot(x, table, dims):
    top = x.astype(BF16)
    low = (x - top.astype(F32)).astype(BF16)
    both = lax.dot_general(jnp.concatenate([top, low], 0), table, dims, preferred_element_type=F32)
    return both[: x.shape[0]] + both[x.shape[0] :]


def sort_kernel(pack, scaled, theirs_ref, mine_ref, table_ref, *refs):
    values, rows, _ = mine_ref.shape
    part = rows // pack
    totals = [mine_ref[v] + theirs_ref[v] for v in range(values)]
    if scaled:
        scale_ref, _, *out_refs = refs
        totals = [t * scale_ref[...] for t in totals]
    else:
        *out_refs, scale_ref = refs
        scale = 1.0 / jnp.maximum(totals[0], 1.0)
        scale_ref[...] = scale
        totals[1] = totals[1] * scale
    x = jnp.concatenate(
        [jnp.concatenate([t[h * part : (h + 1) * part] for h in range(pack)], 1) for t in totals], 0
    )
    moved = split_dot(x, table_ref[...], NT)
    lanes = moved.shape[1] // len(out_refs)
    for d, out_ref in enumerate(out_refs):
        for v in range(values):
            out_ref[v] = moved[v * part : (v + 1) * part, d * lanes : (d + 1) * lanes]


def sort_fibres(theirs, mine, table, pack, pieces, scale=None, ahead=None):
    values, rows, fibres = mine.shape
    lanes = table.shape[0] // pieces
    scaled = scale is not None
    outs = [shaped((values, rows // pack, lanes))] * pieces + ([] if scaled else [shaped((rows, fibres))])
    args = (theirs, mine, table) + ((scale, ahead) if scaled else ())
    return pl.pallas_call(
        functools.partial(sort_kernel, pack, scaled),
        in_specs=[in_vmem] * len(args),
        out_specs=[in_vmem] * len(outs),
        out_shape=outs,
        compiler_params=params(),
        cost_estimate=cost(0, 0),
        name="sort_flux" if scaled else "sort_weights",
    )(*args)


def exchange(pieces, fib_count):
    if len(pieces) == 1:
        return [lax.all_to_all(pieces[0], "fib", split_axis=2, concat_axis=2, tiled=True)]
    swapped = [lax.ppermute(pieces[d], "fib", [(i, i ^ d) for i in range(fib_count)]) for d in range(1, fib_count)]
    return [pieces[0]] + swapped


def landed(refs, table):
    values, part, _ = refs[0].shape
    x = jnp.concatenate(
        [jnp.concatenate([ref[v] for ref in refs], 1) if len(refs) > 1 else refs[0][v] for v in range(values)], 0
    )
    moved = split_dot(x, table, NT)
    return [moved[v * part : (v + 1) * part] for v in range(values)]


def columns_of(table, which, pieces):
    lanes = table.shape[1] // pieces
    return jnp.concatenate([table[:, d * lanes : (d + 1) * lanes] for d in which], 1)


def early_kernel(moves, which, pieces, place_ref, slots_ref, *refs):
    *piece_refs, table_ref, sums_ref = refs
    write_recv_table(*moves, place_ref[0], slots_ref, table_ref)
    for v, moved in enumerate(landed(piece_refs, columns_of(table_ref[...], which, pieces))):
        sums_ref[v] = moved


def place_early(moves, which, place, slots, weight_pieces, fibres):
    fib_count, pack, per, _ = moves
    early = [weight_pieces[d] for d in which]
    values, part, _ = early[0].shape
    return pl.pallas_call(
        functools.partial(early_kernel, moves, which, len(weight_pieces)),
        in_specs=[in_smem] + [in_vmem] * (1 + len(early)),
        out_specs=[in_vmem] * 2,
        out_shape=[
            shaped((pack * fibres, fib_count * pack * per), BF16),
            shaped((values, part, pack * fibres)),
        ],
        compiler_params=params(),
        cost_estimate=cost(0, 0),
        name="place_early",
    )(place, slots, *early)


def weights_end_kernel(pack, total, late, pieces, place_ref, table_ref, sums_ref, *refs):
    *late_refs, ivar_ref, res_ref = refs
    weight, band = sums_ref[0], sums_ref[1]
    if late:
        more_weight, more_band = landed(late_refs, columns_of(table_ref[...], late, pieces))
        weight, band = weight + more_weight, band + more_band
    rows, fibres = ivar_ref.shape
    part = rows // pack
    start = (place_ref[1] * 2 + place_ref[2]) * rows
    for h in range(pack):
        at = slice(h * part, (h + 1) * part)
        cut = slice(h * fibres, (h + 1) * fibres)
        row = start + h * part + lax.broadcasted_iota(jnp.int32, (part, 1), 0)
        w, b = weight[:, cut], band[:, cut]
        before = jnp.where(row == 0, 0.0, b)
        after = jnp.where(row == total - 1, 0.0, b)
        ivar_ref[at, :] = w
        res_ref[0, at, :] = before
        res_ref[1, at, :] = jnp.minimum(w, 1.0) - before - after
        res_ref[2, at, :] = after


def end_weights(place, table, sums, late, weight_pieces, pack, fibres, total):
    rows = sums.shape[1] * pack
    late_pieces = [weight_pieces[d] for d in late]
    return pl.pallas_call(
        functools.partial(weights_end_kernel, pack, total, late, len(weight_pieces)),
        in_specs=[in_smem] + [in_vmem] * (2 + len(late)),
        out_specs=[in_vmem] * 2,
        out_shape=[shaped((rows, fibres)), shaped((3, rows, fibres))],
        compiler_params=params(),
        cost_estimate=cost(0, 0),
        name="end_weights",
    )(place, table, sums, *late_pieces)


def flux_end_kernel(pack, order, table_ref, *refs):
    *piece_refs, flux_ref = refs
    (flux,) = landed([piece_refs[order.index(d)] for d in range(len(order))], table_ref[...])
    rows, fibres = flux_ref.shape
    part = rows // pack
    for h in range(pack):
        flux_ref[h * part : (h + 1) * part, :] = flux[:, h * fibres : (h + 1) * fibres]


def end_flux(table, pieces, pack, fibres):
    rows = pieces[0].shape[1] * pack
    order = sorted(range(len(pieces)), key=lambda d: (d > 0, abs(2 * d - len(pieces))))
    return pl.pallas_call(
        functools.partial(flux_end_kernel, pack, order),
        in_specs=[in_vmem] * (1 + len(pieces)),
        out_specs=in_vmem,
        out_shape=shaped((rows, fibres)),
        compiler_params=params(),
        cost_estimate=cost(2 * rows * table.size, 2 * rows * fibres * 4),
        name="end_flux",
    )(table, *(pieces[d] for d in order))


def after(value, done):
    return lax.optimization_barrier((value, done))[0]


def per_device(pixels, pixel_ivar, clip_bits, coupling, counts, good_flags, owner_slot):
    expos, width, fibres = pixels.shape
    fib_count, wav_count = lax.axis_size("fib"), lax.axis_size("wav")
    total = width * wav_count
    per = fibres // fib_count
    rows = width // 2
    pack = max(1, LANES // per)
    while pack > 1 and rows % (pack * ROWS):
        pack //= 2
    rel = pack * per == LANES and fib_count & (fib_count - 1) == 0
    pieces = fib_count if rel else 1
    place = jnp.stack([lax.axis_index(axis) for axis in ("fib", "wav", "exp")]).astype(jnp.int32)
    coupling, counts, slots = coupling[None], counts[None], owner_slot[None]
    swap = [(0, 1), (1, 0)]
    moves = (fib_count, pack, per, rel)

    theirs, weight_t, send_table, slots, coupling, counts, good, bits, ivar = sent_weights(
        moves, wav_count, place, slots, coupling, counts, good_flags, clip_bits, pixel_ivar
    )
    arriving = lax.ppermute(theirs, "exp", swap)
    mine, weight_m, up, down = kept_weights(
        wav_count, place, coupling, counts, good, pixels, ivar, bits
    )
    upward = [(i, (i + 1) % wav_count) for i in range(wav_count)]
    left = lax.ppermute(up, "wav", upward)
    right = lax.ppermute(down, "wav", [(j, i) for i, j in upward])
    *sorted_pieces, scale = sort_fibres(arriving, mine, send_table, pack, pieces)
    weight_pieces = exchange(sorted_pieces, fib_count)

    pixel_s, ivar_s = stream_layout(left[0] + right[0], pixels, ivar)
    theirs, solved = flux_sums(wav_count, place, coupling, left, right, pixel_s, ivar_s, weight_t)
    early = [0, fib_count // 2] if rel else [0]
    late = [d for d in range(pieces) if d not in early]
    ahead = weight_pieces[early[-1]][0, :ROWS, :] * 0.5
    arriving = lax.ppermute(theirs, "exp", swap)
    mine = kept_flux(after(place, theirs), coupling, solved, weight_m)
    sorted_pieces = sort_fibres(arriving, mine, send_table, pack, pieces, scale, ahead)
    flux_pieces = exchange(sorted_pieces, fib_count)
    recv_table, placed = place_early(moves, early, after(place, sorted_pieces[0]), slots, weight_pieces, fibres)
    ivar, res = end_weights(place, recv_table, placed, late, weight_pieces, pack, fibres, total)
    flux = end_flux(recv_table, flux_pieces, pack, fibres)
    return (flux, ivar, res)


def solution(mesh):
    return jax.shard_map(
        per_device,
        mesh=mesh,
        in_specs=(
            P("exp", "wav", "fib"),
            P("exp", "wav", "fib"),
            P("exp", "wav", "fib"),
            P("fib"),
            P("fib"),
            P("exp", "fib"),
            P(),
        ),
        out_specs=(
            P(("wav", "exp"), "fib"),
            P(("wav", "exp"), "fib"),
            P(None, ("wav", "exp"), "fib"),
        ),
        check_vma=False,
    )
```

```python
import functools

import jax
import jax.numpy as jnp
from jax import lax
from jax.experimental import pallas as pl
from jax.experimental.pallas import tpu as pltpu
from jax.sharding import PartitionSpec as P

HALO = 50
BITS = 15
LANES = 128
ROWS = 8
GROUP = 120
VMEM_BYTES = 32 * 1024 * 1024
F32 = jnp.float32
BF16 = jnp.bfloat16
NT = (((1,), (1,)), ((), ()))

in_vmem = pl.BlockSpec(memory_space=pltpu.VMEM)
in_smem = pl.BlockSpec(memory_space=pltpu.SMEM)
in_hbm = pl.BlockSpec(memory_space=pltpu.HBM)


def params():
    return pltpu.CompilerParams(vmem_limit_bytes=VMEM_BYTES)


def cost(flops, moved):
    return pl.CostEstimate(flops=int(flops), bytes_accessed=int(moved), transcendentals=0)


def held_in_hbm(*arrays):
    return [pltpu.with_memory_space_constraint(array, pltpu.HBM) for array in arrays]


def shaped(shape, dtype=F32):
    return jax.ShapeDtypeStruct(shape, dtype)


def usable_rows(place_ref, counts_ref, good_ref):
    count = good_ref.shape[0]
    return [
        good_ref[e : e + 1, :].astype(F32)
        * jnp.where(place_ref[2] * count + e < counts_ref[...], 1.0, 0.0)
        for e in range(count)
    ]


def tile_bits(tile):
    first, last = (ROWS * tile) // BITS, (ROWS * tile + ROWS - 1) // BITS
    split = BITS * last - ROWS * tile
    row = lax.broadcasted_iota(jnp.int32, (ROWS, 1), 0)
    word = jnp.where(row >= split, last, first)
    return first, last, split, jnp.left_shift(1, ROWS * tile + row - BITS * word)


def tile_words(words, tile):
    first, last, split, mask = tile_bits(tile)
    picked = words[first : first + 1, :]
    if last != first:
        row = lax.broadcasted_iota(jnp.int32, (ROWS, 1), 0)
        picked = jnp.where(row >= split, words[last : last + 1, :], picked)
    return (picked & mask) != 0


def in_flight(pairs, sems, at=0):
    copies = [pltpu.make_async_copy(source, target, sems.at[at + i]) for i, (source, target) in enumerate(pairs)]
    for copy in copies:
        copy.start()
    return copies


def inverse_of(x):
    guess = pl.reciprocal(x, approx=True)
    return guess * (2.0 - x * guess)


def advance(state, ivar, pixel, back_coupling):
    n, d, b = state
    ratio = ivar * back_coupling
    next_d = d + n
    return (n * (1.0 + ratio) + ratio * d, next_d, b + (ivar * pixel) * next_d)


def rescaled(state):
    scale = inverse_of(state[1])
    return tuple(part * scale for part in state)


def odd(rows):
    return rows + 1 - rows % 2


def divisor_of(size, most):
    return max(k for k in range(1, most + 1) if size % k == 0)


def owners(slots_ref, fib_count, fibres):
    rows = [slots_ref[:, s * fibres : (s + 1) * fibres].astype(F32) for s in range(fib_count)]
    sources = -(-fib_count // ROWS) * ROWS
    if sources > fib_count:
        rows.append(jnp.full((sources - fib_count, fibres), -1.0, F32))
    slots = jnp.concatenate(rows, 0)
    owner = jnp.floor((slots + 0.5) * (1.0 / fibres))
    return owner, slots - owner * fibres


def earlier_fibres(fibres):
    row = lax.broadcasted_iota(jnp.int32, (fibres, fibres), 0)
    col = lax.broadcasted_iota(jnp.int32, (fibres, fibres), 1)
    return (row < col).astype(F32).astype(BF16)


def write_send_table(fib_count, pack, per, rel, me, slots_ref, table_ref):
    fibres = table_ref.shape[1] // pack
    lanes = pack * per
    owner, _ = owners(slots_ref, fib_count, fibres)
    source = lax.broadcasted_iota(jnp.int32, owner.shape, 0)
    my_owner = jnp.sum(jnp.where(source == me, owner, 0.0), axis=0, keepdims=True).astype(jnp.int32)
    to_owner = (source == my_owner).astype(F32)
    counted = jnp.dot(to_owner.astype(BF16), earlier_fibres(fibres), preferred_element_type=F32)
    rank = jnp.sum(to_owner * counted, axis=0, keepdims=True).astype(jnp.int32)
    target = my_owner ^ me if rel else my_owner
    base = target * lanes + rank
    place_of = jnp.concatenate([base + h * per for h in range(pack)], 1)
    row = lax.broadcasted_iota(jnp.int32, table_ref.shape, 0)
    table_ref[...] = (row == place_of).astype(F32).astype(BF16)


def write_recv_table(fib_count, pack, per, rel, me, slots_ref, table_ref):
    fibres = table_ref.shape[0] // pack
    lanes = pack * per
    total_lanes = fib_count * lanes
    owner, column = owners(slots_ref, fib_count, fibres)
    source = lax.broadcasted_iota(jnp.int32, owner.shape, 0)
    mine = (owner == me.astype(F32)).astype(F32)
    rank_in = jnp.dot(mine.astype(BF16), earlier_fibres(fibres), preferred_element_type=F32).astype(jnp.int32)
    order = source ^ me if rel else source
    arrival = jnp.where(mine > 0.0, order * lanes + rank_in, -total_lanes)
    tall = lax.broadcasted_iota(jnp.int32, (total_lanes, fibres), 0)
    landing = jnp.zeros((ROWS, total_lanes), F32)
    for s in range(fib_count):
        hit = tall == arrival[s : s + 1, :]
        for h in range(1, pack):
            hit = hit | (tall == arrival[s : s + 1, :] + h * per)
        values = jnp.broadcast_to(column[s : s + 1, :], (ROWS, fibres)).astype(BF16)
        landing = landing + lax.dot_general(
            values, hit.astype(F32).astype(BF16), NT, preferred_element_type=F32
        )
    lane = lax.broadcasted_iota(jnp.int32, (1, total_lanes), 1)
    landing = landing[0:1, :].astype(jnp.int32)
    for h in range(1, pack):
        inside = (lane % lanes >= h * per) & (lane % lanes < (h + 1) * per)
        landing = jnp.where(inside, landing + h * fibres, landing)
    row = lax.broadcasted_iota(jnp.int32, table_ref.shape, 0)
    table_ref[...] = (row == landing).astype(F32).astype(BF16)


def stream_coupling(coupling_ref, expos):
    coupling = coupling_ref[...]
    blocks = coupling.shape[1] // LANES
    return jnp.concatenate(
        [jnp.broadcast_to(coupling[:, h * LANES : (h + 1) * LANES], (expos, LANES)) for h in range(blocks)], 0
    )


def weight_tile(coupling, usable, words, ivars, within, scale_row):
    links = scale_row * coupling
    weights = []
    weight_sum = band_sum = None
    for e, ivar in enumerate(ivars):
        weight = jnp.where(tile_words(words[e], within), ivar * usable[e], 0.0)
        band = weight * inverse_of(ivar + links)
        weights.append(weight)
        weight_sum = weight if e == 0 else weight_sum + weight
        band_sum = band if e == 0 else band_sum + band
    return weights, weight_sum, band_sum * coupling


def write_weights(place_ref, wav_count, which, coupling_v, counts_v, good_v, ivar_of, words_of, sums_ref, weight_ref, beside):
    expos, half, _ = weight_ref.shape
    coupling = coupling_v[...]
    usable = usable_rows(place_ref, counts_v, good_v)
    start = place_ref[1] * (2 * half) + which * half
    tiles = half // ROWS
    tiles_in_group = GROUP // ROWS
    for tile in range(tiles):
        beside(tile, tiles)
        group, within = divmod(tile, tiles_in_group)
        scale_row = 4.0
        if tile in (0, tiles - 1):
            row = start + ROWS * tile + lax.broadcasted_iota(jnp.int32, (ROWS, 1), 0)
            scale_row = jnp.where((row == 0) | (row == wav_count * 2 * half - 1), 2.0, 4.0)
        at = slice(ROWS * tile, ROWS * (tile + 1))
        weights, weight_sum, band_sum = weight_tile(
            coupling,
            usable,
            [words_of(e, group) for e in range(expos)],
            [ivar_of(e, tile) for e in range(expos)],
            within,
            scale_row,
        )
        for e in range(expos):
            weight_ref[e, at, :] = weights[e]
        sums_ref[0, at, :] = weight_sum
        sums_ref[1, at, :] = band_sum


def sent_kernel(
    moves, wav_count, place_ref, slots_ref, coupling_ref, counts_ref, good_ref, bits_ref, ivar_ref,
    sums_ref, weight_ref, table_ref, slots_v, coupling_v, counts_v, good_v, bits_v, ivar_v, sems,
):
    expos, width, _ = ivar_ref.shape
    half = width // 2
    which = 1 - place_ref[2]
    words = GROUP // BITS

    def part(source, target, first):
        at = pl.ds(pl.multiple_of(first, ROWS), GROUP)
        return source.at[:, at, :], target.at[:, at, :]

    waits = in_flight(
        [
            (slots_ref, slots_v),
            (coupling_ref, coupling_v),
            (counts_ref, counts_v),
            (good_ref, good_v),
            (bits_ref, bits_v),
        ]
        + [part(ivar_ref, ivar_v, which * half + g) for g in range(0, half, GROUP)]
        + [part(ivar_ref, ivar_v, (1 - which) * half + g) for g in range(0, half, GROUP)],
        sems,
    )
    waits[0].wait()
    write_send_table(*moves, place_ref[0], slots_v, table_ref)
    for wait in waits[1:5]:
        wait.wait()

    def arrive(tile, tiles):
        if ROWS * tile % GROUP == 0:
            waits[5 + ROWS * tile // GROUP].wait()

    write_weights(
        place_ref, wav_count, which, coupling_v, counts_v, good_v,
        lambda e, tile: ivar_v[e, pl.ds(pl.multiple_of(which * half + ROWS * tile, ROWS), ROWS), :],
        lambda e, group: bits_v[e, pl.ds(pl.multiple_of(which * (half // BITS) + words * group, words), words), :],
        sums_ref, weight_ref, arrive,
    )
    for wait in waits[5 + half // GROUP :]:
        wait.wait()


def sent_weights(moves, wav_count, place, slots, coupling, counts, good, bits, ivar):
    expos, width, fibres = ivar.shape
    half = width // 2
    fib_count, pack, per, _ = moves
    inputs = (slots, coupling, counts, good, bits, ivar)
    return pl.pallas_call(
        functools.partial(sent_kernel, moves, wav_count),
        in_specs=[in_smem] + [in_hbm] * 6,
        out_specs=[in_vmem] * 9,
        out_shape=[
            shaped((2, half, fibres)),
            shaped((expos, half, fibres)),
            shaped((fib_count * pack * per, pack * fibres), BF16),
        ]
        + [shaped(x.shape, x.dtype) for x in inputs],
        scratch_shapes=[pltpu.SemaphoreType.DMA((5 + width // GROUP,))],
        compiler_params=params(),
        cost_estimate=cost(20 * ivar.size, 6 * ivar.size),
        name="sent_weights",
    )(place, *held_in_hbm(*inputs))


def lay_out(source_ref, target_ref, pieces, pitch):
    expos, _, fibres = source_ref.shape
    for h in range(fibres // LANES):
        for e in range(expos):
            for first, length, at in pieces:
                target_ref[pl.ds((h * expos + e) * pitch + at, length), :] = source_ref[
                    e, pl.ds(first, length), pl.ds(h * LANES, LANES)
                ]


def kept_kernel(
    wav_count, place_ref, coupling_ref, counts_ref, good_ref, pixels_ref, ivar_ref, bits_ref,
    sums_ref, weight_ref, up_ref, down_ref, ivar_s, pixel_s,
):
    expos, width, fibres = ivar_ref.shape
    half = width // 2
    streams = expos * fibres // LANES
    count = -(-HALO // ROWS) * ROWS
    pitch = odd(2 * count)
    which = place_ref[2]
    words = GROUP // BITS
    edges = [(0, count, 0), (width - count, count, count)]
    lay_out(ivar_ref, ivar_s, edges, pitch)
    lay_out(pixels_ref, pixel_s, edges, pitch)
    coupling = stream_coupling(coupling_ref, expos)
    back = 1.0 / coupling
    zero = jnp.zeros((streams, LANES), F32)
    states = [(zero, zero + 1.0, zero), (zero, zero + 1.0, zero)]

    def eliminate(tile, tiles):
        for i in range(HALO * tile // tiles, HALO * (tile + 1) // tiles):
            for side, row in enumerate((2 * count - HALO + i, HALO - 1 - i)):
                at = pl.ds(row, streams, stride=pitch)
                states[side] = advance(states[side], ivar_s[at, :], pixel_s[at, :], back)
                if i % 24 == 23:
                    states[side] = rescaled(states[side])

    write_weights(
        place_ref, wav_count, which, coupling_ref, counts_ref, good_ref,
        lambda e, tile: ivar_ref[e, pl.ds(pl.multiple_of(which * half + ROWS * tile, ROWS), ROWS), :],
        lambda e, group: bits_ref[e, pl.ds(pl.multiple_of(which * (half // BITS) + words * group, words), words), :],
        sums_ref, weight_ref, eliminate,
    )
    for (n, d, b), out_ref in zip(states, (up_ref, down_ref)):
        scale = 1.0 / (d + n)
        out_ref[0] = coupling * (n * scale)
        out_ref[1] = b * scale


def kept_weights(wav_count, place, coupling, counts, good, pixels, ivar, bits):
    expos, width, fibres = ivar.shape
    half = width // 2
    streams = expos * fibres // LANES
    count = -(-HALO // ROWS) * ROWS
    edge = shaped((2, streams, LANES))
    edge_scratch = pltpu.VMEM((streams * odd(2 * count), LANES), F32)
    return pl.pallas_call(
        functools.partial(kept_kernel, wav_count),
        in_specs=[in_smem] + [in_vmem] * 6,
        out_specs=[in_vmem] * 4,
        out_shape=[shaped((2, half, fibres)), shaped((expos, half, fibres)), edge, edge],
        scratch_shapes=[edge_scratch, edge_scratch],
        compiler_params=params(),
        cost_estimate=cost(20 * ivar.size, 6 * ivar.size),
        name="kept_weights",
    )(place, coupling, counts, good, pixels, ivar, bits)


def layout_kernel(arrived_ref, pixels_ref, ivar_ref, pixel_out, ivar_out):
    width = ivar_ref.shape[1]
    lay_out(ivar_ref, ivar_out, [(0, width, 0)], odd(width))
    lay_out(pixels_ref, pixel_out, [(0, width, 0)], odd(width))


def stream_layout(arrived, pixels, ivar):
    expos, width, fibres = ivar.shape
    streams = expos * fibres // LANES
    laid = shaped((streams * odd(width), LANES))
    return pl.pallas_call(
        layout_kernel,
        in_specs=[in_vmem] * 3,
        out_specs=[in_vmem] * 2,
        out_shape=[laid, laid],
        compiler_params=params(),
        cost_estimate=cost(0, 16 * ivar.size),
        name="stream_layout",
    )(arrived, pixels, ivar)


def solve_kernel(
    wav_count, place_ref, coupling_ref, left_ref, right_ref, pixel_ref, ivar_ref, weight_ref,
    theirs_ref, solved_s, lead_s, rest_s,
):
    streams = left_ref.shape[1]
    expos, half, fibres = weight_ref.shape
    width = 2 * half
    pitch = odd(width)
    middle = half
    coupling = stream_coupling(coupling_ref, expos)
    back = 1.0 / coupling

    def row_at(i):
        return pl.ds(i, streams, stride=pitch)

    def begin(edge_ref, outermost):
        n = jnp.where(place_ref[1] == outermost, 0.0, edge_ref[0]) * back
        return (n, 1.0 - n, jnp.where(place_ref[1] == outermost, 0.0, edge_ref[1]))

    def keep(side, i, state):
        n, d, b = state
        inverse = inverse_of(d + n)
        lead_s[side, i] = d * inverse
        rest_s[side, i] = b * inverse

    unrolled = divisor_of(middle, 24)

    def eliminate(it, states):
        states = list(states)
        for k in range(unrolled):
            i = it * unrolled + k
            for side, row in enumerate((i, width - 1 - i)):
                keep(side, i, states[side])
                states[side] = advance(states[side], ivar_ref[row_at(row), :], pixel_ref[row_at(row), :], back)
        return tuple(rescaled(state) for state in states)

    states = lax.fori_loop(0, middle // unrolled, eliminate, (begin(left_ref, 0), begin(right_ref, wav_count - 1)))
    for side in range(2):
        keep(side, middle, states[side])
    lead, rest = lead_s[0, middle], rest_s[0, middle]
    lead_r, rest_r = lead_s[1, middle], rest_s[1, middle]
    left = (rest + lead * rest_r) / (1.0 - lead * lead_r)
    right = rest_r + lead_r * left
    several = divisor_of(middle, 48)

    def after_both(near, far):
        return far[0] * near[0], far[1] + far[0] * near[1]

    def step(factors, value):
        return factors[1] + factors[0] * value

    def substitute(it, values):
        values = list(values)
        for k in range(0, several, 4):
            for side in range(2):
                rows = [middle - 1 - (it * several + k + m) for m in range(4)]
                one, two, three, four = [(lead_s[side, i], rest_s[side, i]) for i in rows]
                first_two = after_both(one, two)
                all_four = after_both(first_two, after_both(three, four))
                value = values[side]
                third = step(first_two, value)
                solved = [value, step(one, value), third, step(three, third)]
                values[side] = step(all_four, value)
                for i, x in zip(rows, solved):
                    solved_s[row_at(i if side == 0 else width - 1 - i), :] = x
        return tuple(values)

    lax.fori_loop(0, middle // several, substitute, (left, right))

    add_up(theirs_ref, weight_ref, solved_s, coupling_ref, 1 - place_ref[2])


def add_up(out_ref, weight_ref, solved_ref, coupling_ref, which):
    expos, half, fibres = weight_ref.shape
    pitch = odd(2 * half)
    start = which * half
    back = 1.0 / coupling_ref[...]
    unrolled = divisor_of(half // ROWS, 5)

    def body(g, carry):
        for k in range(unrolled):
            row = pl.multiple_of((g * unrolled + k) * ROWS, ROWS)
            for h in range(fibres // LANES):
                total = None
                for e in range(expos):
                    at = pl.ds((h * expos + e) * pitch + start + row, ROWS)
                    term = weight_ref[e, pl.ds(row, ROWS), pl.ds(h * LANES, LANES)] * solved_ref[at, :]
                    total = term if e == 0 else total + term
                out_ref[0, pl.ds(row, ROWS), pl.ds(h * LANES, LANES)] = total * back[:, h * LANES : (h + 1) * LANES]
        return carry

    lax.fori_loop(0, half // ROWS // unrolled, body, 0)


def flux_sums(wav_count, place, coupling, left, right, pixels, ivar, weight):
    expos, half, fibres = weight.shape
    streams = left.shape[1]
    factor_scratch = pltpu.VMEM((2, half + 1, streams, LANES), F32)
    return pl.pallas_call(
        functools.partial(solve_kernel, wav_count),
        in_specs=[in_smem] + [in_vmem] * 6,
        out_specs=[in_vmem, in_vmem],
        out_shape=[shaped((1, half, fibres)), shaped(pixels.shape)],
        scratch_shapes=[factor_scratch, factor_scratch],
        compiler_params=params(),
        cost_estimate=cost(0, 0),
        name="flux_sums",
    )(place, coupling, left, right, pixels, ivar, weight)


def kept_flux_kernel(place_ref, coupling_ref, solved_ref, weight_ref, out_ref):
    add_up(out_ref, weight_ref, solved_ref, coupling_ref, place_ref[2])


def kept_flux(place, coupling, solved, weight):
    expos, half, fibres = weight.shape
    return pl.pallas_call(
        kept_flux_kernel,
        in_specs=[in_smem] + [in_vmem] * 3,
        out_specs=in_vmem,
        out_shape=shaped((1, half, fibres)),
        compiler_params=params(),
        cost_estimate=cost(2 * weight.size, 8 * weight.size),
        name="kept_flux",
    )(place, coupling, solved, weight)


def split_dot(x, table, dims):
    top = x.astype(BF16)
    low = (x - top.astype(F32)).astype(BF16)
    both = lax.dot_general(jnp.concatenate([top, low], 0), table, dims, preferred_element_type=F32)
    return both[: x.shape[0]] + both[x.shape[0] :]


def sort_kernel(pack, scaled, theirs_ref, mine_ref, table_ref, *refs):
    values, rows, _ = mine_ref.shape
    part = rows // pack
    totals = [mine_ref[v] + theirs_ref[v] for v in range(values)]
    if scaled:
        scale_ref, _, *out_refs = refs
        totals = [t * scale_ref[...] for t in totals]
    else:
        *out_refs, scale_ref = refs
        scale = 1.0 / jnp.maximum(totals[0], 1.0)
        scale_ref[...] = scale
        totals[1] = totals[1] * scale
    x = jnp.concatenate(
        [jnp.concatenate([t[h * part : (h + 1) * part] for h in range(pack)], 1) for t in totals], 0
    )
    moved = split_dot(x, table_ref[...], NT)
    lanes = moved.shape[1] // len(out_refs)
    for d, out_ref in enumerate(out_refs):
        for v in range(values):
            out_ref[v] = moved[v * part : (v + 1) * part, d * lanes : (d + 1) * lanes]


def sort_fibres(theirs, mine, table, pack, pieces, scale=None, ahead=None):
    values, rows, fibres = mine.shape
    lanes = table.shape[0] // pieces
    scaled = scale is not None
    outs = [shaped((values, rows // pack, lanes))] * pieces + ([] if scaled else [shaped((rows, fibres))])
    args = (theirs, mine, table) + ((scale, ahead) if scaled else ())
    return pl.pallas_call(
        functools.partial(sort_kernel, pack, scaled),
        in_specs=[in_vmem] * len(args),
        out_specs=[in_vmem] * len(outs),
        out_shape=outs,
        compiler_params=params(),
        cost_estimate=cost(0, 0),
        name="sort_flux" if scaled else "sort_weights",
    )(*args)


def exchange(pieces, fib_count):
    if len(pieces) == 1:
        return [lax.all_to_all(pieces[0], "fib", split_axis=2, concat_axis=2, tiled=True)]
    swapped = [lax.ppermute(pieces[d], "fib", [(i, i ^ d) for i in range(fib_count)]) for d in range(1, fib_count)]
    return [pieces[0]] + swapped


def landed(refs, table):
    values, part, _ = refs[0].shape
    x = jnp.concatenate(
        [jnp.concatenate([ref[v] for ref in refs], 1) if len(refs) > 1 else refs[0][v] for v in range(values)], 0
    )
    moved = split_dot(x, table, NT)
    return [moved[v * part : (v + 1) * part] for v in range(values)]


def columns_of(table, which, pieces):
    lanes = table.shape[1] // pieces
    return jnp.concatenate([table[:, d * lanes : (d + 1) * lanes] for d in which], 1)


def early_kernel(moves, which, pieces, place_ref, slots_ref, *refs):
    *piece_refs, table_ref, sums_ref = refs
    write_recv_table(*moves, place_ref[0], slots_ref, table_ref)
    for v, moved in enumerate(landed(piece_refs, columns_of(table_ref[...], which, pieces))):
        sums_ref[v] = moved


def place_early(moves, which, place, slots, weight_pieces, fibres):
    fib_count, pack, per, _ = moves
    early = [weight_pieces[d] for d in which]
    values, part, _ = early[0].shape
    return pl.pallas_call(
        functools.partial(early_kernel, moves, which, len(weight_pieces)),
        in_specs=[in_smem] + [in_vmem] * (1 + len(early)),
        out_specs=[in_vmem] * 2,
        out_shape=[
            shaped((pack * fibres, fib_count * pack * per), BF16),
            shaped((values, part, pack * fibres)),
        ],
        compiler_params=params(),
        cost_estimate=cost(0, 0),
        name="place_early",
    )(place, slots, *early)


def weights_end_kernel(pack, total, late, pieces, place_ref, table_ref, sums_ref, *refs):
    *late_refs, ivar_ref, res_ref = refs
    weight, band = sums_ref[0], sums_ref[1]
    if late:
        more_weight, more_band = landed(late_refs, columns_of(table_ref[...], late, pieces))
        weight, band = weight + more_weight, band + more_band
    rows, fibres = ivar_ref.shape
    part = rows // pack
    start = (place_ref[1] * 2 + place_ref[2]) * rows
    for h in range(pack):
        at = slice(h * part, (h + 1) * part)
        cut = slice(h * fibres, (h + 1) * fibres)
        row = start + h * part + lax.broadcasted_iota(jnp.int32, (part, 1), 0)
        w, b = weight[:, cut], band[:, cut]
        before = jnp.where(row == 0, 0.0, b)
        after = jnp.where(row == total - 1, 0.0, b)
        ivar_ref[at, :] = w
        res_ref[0, at, :] = before
        res_ref[1, at, :] = jnp.minimum(w, 1.0) - before - after
        res_ref[2, at, :] = after


def end_weights(place, table, sums, late, weight_pieces, pack, fibres, total):
    rows = sums.shape[1] * pack
    late_pieces = [weight_pieces[d] for d in late]
    return pl.pallas_call(
        functools.partial(weights_end_kernel, pack, total, late, len(weight_pieces)),
        in_specs=[in_smem] + [in_vmem] * (2 + len(late)),
        out_specs=[in_vmem] * 2,
        out_shape=[shaped((rows, fibres)), shaped((3, rows, fibres))],
        compiler_params=params(),
        cost_estimate=cost(0, 0),
        name="end_weights",
    )(place, table, sums, *late_pieces)


def flux_end_kernel(pack, order, table_ref, *refs):
    *piece_refs, flux_ref = refs
    (flux,) = landed([piece_refs[order.index(d)] for d in range(len(order))], table_ref[...])
    rows, fibres = flux_ref.shape
    part = rows // pack
    for h in range(pack):
        flux_ref[h * part : (h + 1) * part, :] = flux[:, h * fibres : (h + 1) * fibres]


def end_flux(table, pieces, pack, fibres):
    rows = pieces[0].shape[1] * pack
    order = [0] + sorted(range(1, len(pieces)), key=lambda d: (d < len(pieces) // 2, d))
    return pl.pallas_call(
        functools.partial(flux_end_kernel, pack, order),
        in_specs=[in_vmem] * (1 + len(pieces)),
        out_specs=in_vmem,
        out_shape=shaped((rows, fibres)),
        compiler_params=params(),
        cost_estimate=cost(2 * rows * table.size, 2 * rows * fibres * 4),
        name="end_flux",
    )(table, *(pieces[d] for d in order))


def after(value, done):
    return lax.optimization_barrier((value, done))[0]


def per_device(pixels, pixel_ivar, clip_bits, coupling, counts, good_flags, owner_slot):
    expos, width, fibres = pixels.shape
    fib_count, wav_count = lax.axis_size("fib"), lax.axis_size("wav")
    total = width * wav_count
    per = fibres // fib_count
    rows = width // 2
    pack = max(1, LANES // per)
    while pack > 1 and rows % (pack * ROWS):
        pack //= 2
    rel = pack * per == LANES and fib_count & (fib_count - 1) == 0
    pieces = fib_count if rel else 1
    place = jnp.stack([lax.axis_index(axis) for axis in ("fib", "wav", "exp")]).astype(jnp.int32)
    coupling, counts, slots = coupling[None], counts[None], owner_slot[None]
    swap = [(0, 1), (1, 0)]
    moves = (fib_count, pack, per, rel)

    theirs, weight_t, send_table, slots, coupling, counts, good, bits, ivar = sent_weights(
        moves, wav_count, place, slots, coupling, counts, good_flags, clip_bits, pixel_ivar
    )
    arriving = lax.ppermute(theirs, "exp", swap)
    mine, weight_m, up, down = kept_weights(
        wav_count, place, coupling, counts, good, pixels, ivar, bits
    )
    upward = [(i, (i + 1) % wav_count) for i in range(wav_count)]
    left = lax.ppermute(up, "wav", upward)
    right = lax.ppermute(down, "wav", [(j, i) for i, j in upward])
    *sorted_pieces, scale = sort_fibres(arriving, mine, send_table, pack, pieces)
    weight_pieces = exchange(sorted_pieces, fib_count)

    pixel_s, ivar_s = stream_layout(left[0] + right[0], pixels, ivar)
    theirs, solved = flux_sums(wav_count, place, coupling, left, right, pixel_s, ivar_s, weight_t)
    early = [0, fib_count // 2] if rel else [0]
    late = [d for d in reversed(range(pieces)) if d not in early]
    ahead = weight_pieces[early[-1]][0, :ROWS, :] * 0.5
    arriving = lax.ppermute(theirs, "exp", swap)
    mine = kept_flux(after(place, theirs), coupling, solved, weight_m)
    sorted_pieces = sort_fibres(arriving, mine, send_table, pack, pieces, scale, ahead)
    flux_pieces = exchange(sorted_pieces, fib_count)
    recv_table, placed = place_early(moves, early, after(place, sorted_pieces[0]), slots, weight_pieces, fibres)
    ivar, res = end_weights(place, recv_table, placed, late, weight_pieces, pack, fibres, total)
    flux = end_flux(recv_table, flux_pieces, pack, fibres)
    return (flux, ivar, res)


def solution(mesh):
    return jax.shard_map(
        per_device,
        mesh=mesh,
        in_specs=(
            P("exp", "wav", "fib"),
            P("exp", "wav", "fib"),
            P("exp", "wav", "fib"),
            P("fib"),
            P("fib"),
            P("exp", "fib"),
            P(),
        ),
        out_specs=(
            P(("wav", "exp"), "fib"),
            P(("wav", "exp"), "fib"),
            P(None, ("wav", "exp"), "fib"),
        ),
        check_vma=False,
    )
```

```python
import functools

import jax
import jax.numpy as jnp
from jax import lax
from jax.experimental import pallas as pl
from jax.experimental.pallas import tpu as pltpu
from jax.sharding import PartitionSpec as P

HALO = 50
BITS = 15
LANES = 128
ROWS = 8
GROUP = 120
VMEM_BYTES = 32 * 1024 * 1024
F32 = jnp.float32
BF16 = jnp.bfloat16
NT = (((1,), (1,)), ((), ()))

in_vmem = pl.BlockSpec(memory_space=pltpu.VMEM)
in_smem = pl.BlockSpec(memory_space=pltpu.SMEM)
in_hbm = pl.BlockSpec(memory_space=pltpu.HBM)


def params():
    return pltpu.CompilerParams(vmem_limit_bytes=VMEM_BYTES)


def cost(flops, moved):
    return pl.CostEstimate(flops=int(flops), bytes_accessed=int(moved), transcendentals=0)


def held_in_hbm(*arrays):
    return [pltpu.with_memory_space_constraint(array, pltpu.HBM) for array in arrays]


def shaped(shape, dtype=F32):
    return jax.ShapeDtypeStruct(shape, dtype)


def usable_rows(place_ref, counts_ref, good_ref):
    count = good_ref.shape[0]
    return [
        good_ref[e : e + 1, :].astype(F32)
        * jnp.where(place_ref[2] * count + e < counts_ref[...], 1.0, 0.0)
        for e in range(count)
    ]


def tile_bits(tile):
    first, last = (ROWS * tile) // BITS, (ROWS * tile + ROWS - 1) // BITS
    split = BITS * last - ROWS * tile
    row = lax.broadcasted_iota(jnp.int32, (ROWS, 1), 0)
    word = jnp.where(row >= split, last, first)
    return first, last, split, jnp.left_shift(1, ROWS * tile + row - BITS * word)


def tile_words(words, tile):
    first, last, split, mask = tile_bits(tile)
    picked = words[first : first + 1, :]
    if last != first:
        row = lax.broadcasted_iota(jnp.int32, (ROWS, 1), 0)
        picked = jnp.where(row >= split, words[last : last + 1, :], picked)
    return (picked & mask) != 0


def in_flight(pairs, sems, at=0):
    copies = [pltpu.make_async_copy(source, target, sems.at[at + i]) for i, (source, target) in enumerate(pairs)]
    for copy in copies:
        copy.start()
    return copies


def inverse_of(x):
    guess = pl.reciprocal(x, approx=True)
    return guess * (2.0 - x * guess)


def advance(state, ivar, pixel, back_coupling):
    n, d, b = state
    ratio = ivar * back_coupling
    next_d = d + n
    return (n * (1.0 + ratio) + ratio * d, next_d, b + (ivar * pixel) * next_d)


def rescaled(state):
    scale = inverse_of(state[1])
    return tuple(part * scale for part in state)


def odd(rows):
    return rows + 1 - rows % 2


def divisor_of(size, most):
    return max(k for k in range(1, most + 1) if size % k == 0)


def owners(slots_ref, fib_count, fibres):
    rows = [slots_ref[:, s * fibres : (s + 1) * fibres].astype(F32) for s in range(fib_count)]
    sources = -(-fib_count // ROWS) * ROWS
    if sources > fib_count:
        rows.append(jnp.full((sources - fib_count, fibres), -1.0, F32))
    slots = jnp.concatenate(rows, 0)
    owner = jnp.floor((slots + 0.5) * (1.0 / fibres))
    return owner, slots - owner * fibres


def earlier_fibres(fibres):
    row = lax.broadcasted_iota(jnp.int32, (fibres, fibres), 0)
    col = lax.broadcasted_iota(jnp.int32, (fibres, fibres), 1)
    return (row < col).astype(F32).astype(BF16)


def write_send_table(fib_count, per, rel, me, slots_ref, table_ref):
    fibres = table_ref.shape[1]
    owner, _ = owners(slots_ref, fib_count, fibres)
    source = lax.broadcasted_iota(jnp.int32, owner.shape, 0)
    my_owner = jnp.sum(jnp.where(source == me, owner, 0.0), axis=0, keepdims=True).astype(jnp.int32)
    to_owner = (source == my_owner).astype(F32)
    counted = jnp.dot(to_owner.astype(BF16), earlier_fibres(fibres), preferred_element_type=F32)
    rank = jnp.sum(to_owner * counted, axis=0, keepdims=True).astype(jnp.int32)
    target = my_owner ^ me if rel else my_owner
    row = lax.broadcasted_iota(jnp.int32, table_ref.shape, 0)
    table_ref[...] = (row == target * per + rank).astype(F32).astype(BF16)


def write_recv_table(fib_count, per, rel, me, slots_ref, table_ref):
    fibres = table_ref.shape[0]
    total_lanes = fib_count * per
    owner, column = owners(slots_ref, fib_count, fibres)
    source = lax.broadcasted_iota(jnp.int32, owner.shape, 0)
    mine = (owner == me.astype(F32)).astype(F32)
    rank_in = jnp.dot(mine.astype(BF16), earlier_fibres(fibres), preferred_element_type=F32).astype(jnp.int32)
    order = source ^ me if rel else source
    arrival = jnp.where(mine > 0.0, order * per + rank_in, -1)
    tall = lax.broadcasted_iota(jnp.int32, (total_lanes, fibres), 0)
    landing = jnp.zeros((ROWS, total_lanes), F32)
    for s in range(fib_count):
        hit = tall == arrival[s : s + 1, :]
        values = jnp.broadcast_to(column[s : s + 1, :], (ROWS, fibres)).astype(BF16)
        landing = landing + lax.dot_general(
            values, hit.astype(F32).astype(BF16), NT, preferred_element_type=F32
        )
    row = lax.broadcasted_iota(jnp.int32, table_ref.shape, 0)
    table_ref[...] = (row == landing[0:1, :].astype(jnp.int32)).astype(F32).astype(BF16)


def stream_coupling(coupling_ref, expos):
    coupling = coupling_ref[...]
    blocks = coupling.shape[1] // LANES
    return jnp.concatenate(
        [jnp.broadcast_to(coupling[:, h * LANES : (h + 1) * LANES], (expos, LANES)) for h in range(blocks)], 0
    )


def weight_tile(coupling, usable, words, ivars, within, scale_row):
    links = scale_row * coupling
    weights = []
    weight_sum = band_sum = None
    for e, ivar in enumerate(ivars):
        weight = jnp.where(tile_words(words[e], within), ivar * usable[e], 0.0)
        band = weight * inverse_of(ivar + links)
        weights.append(weight)
        weight_sum = weight if e == 0 else weight_sum + weight
        band_sum = band if e == 0 else band_sum + band
    return weights, weight_sum, band_sum * coupling


def write_weights(place_ref, wav_count, which, coupling_v, counts_v, good_v, ivar_of, words_of, sums_ref, weight_ref, beside):
    expos, half, _ = weight_ref.shape
    coupling = coupling_v[...]
    usable = usable_rows(place_ref, counts_v, good_v)
    start = place_ref[1] * (2 * half) + which * half
    tiles = half // ROWS
    tiles_in_group = GROUP // ROWS
    for tile in range(tiles):
        beside(tile, tiles)
        group, within = divmod(tile, tiles_in_group)
        scale_row = 4.0
        if tile in (0, tiles - 1):
            row = start + ROWS * tile + lax.broadcasted_iota(jnp.int32, (ROWS, 1), 0)
            scale_row = jnp.where((row == 0) | (row == wav_count * 2 * half - 1), 2.0, 4.0)
        at = slice(ROWS * tile, ROWS * (tile + 1))
        weights, weight_sum, band_sum = weight_tile(
            coupling,
            usable,
            [words_of(e, group) for e in range(expos)],
            [ivar_of(e, tile) for e in range(expos)],
            within,
            scale_row,
        )
        for e in range(expos):
            weight_ref[e, at, :] = weights[e]
        sums_ref[0, at, :] = weight_sum
        sums_ref[1, at, :] = band_sum


def sent_kernel(
    moves, wav_count, place_ref, slots_ref, coupling_ref, counts_ref, good_ref, bits_ref, ivar_ref,
    sums_ref, weight_ref, table_ref, slots_v, coupling_v, counts_v, good_v, bits_v, ivar_v, sems,
):
    expos, width, _ = ivar_ref.shape
    half = width // 2
    which = 1 - place_ref[2]
    words = GROUP // BITS

    def part(source, target, first):
        at = pl.ds(pl.multiple_of(first, ROWS), GROUP)
        return source.at[:, at, :], target.at[:, at, :]

    waits = in_flight(
        [
            (slots_ref, slots_v),
            (coupling_ref, coupling_v),
            (counts_ref, counts_v),
            (good_ref, good_v),
            (bits_ref, bits_v),
        ]
        + [part(ivar_ref, ivar_v, which * half + g) for g in range(0, half, GROUP)]
        + [part(ivar_ref, ivar_v, (1 - which) * half + g) for g in range(0, half, GROUP)],
        sems,
    )
    waits[0].wait()
    write_send_table(*moves, place_ref[0], slots_v, table_ref)
    for wait in waits[1:5]:
        wait.wait()

    def arrive(tile, tiles):
        if ROWS * tile % GROUP == 0:
            waits[5 + ROWS * tile // GROUP].wait()

    write_weights(
        place_ref, wav_count, which, coupling_v, counts_v, good_v,
        lambda e, tile: ivar_v[e, pl.ds(pl.multiple_of(which * half + ROWS * tile, ROWS), ROWS), :],
        lambda e, group: bits_v[e, pl.ds(pl.multiple_of(which * (half // BITS) + words * group, words), words), :],
        sums_ref, weight_ref, arrive,
    )
    for wait in waits[5 + half // GROUP :]:
        wait.wait()


def sent_weights(moves, wav_count, place, slots, coupling, counts, good, bits, ivar):
    expos, width, fibres = ivar.shape
    half = width // 2
    fib_count, per, _ = moves
    inputs = (slots, coupling, counts, good, bits, ivar)
    return pl.pallas_call(
        functools.partial(sent_kernel, moves, wav_count),
        in_specs=[in_smem] + [in_hbm] * 6,
        out_specs=[in_vmem] * 9,
        out_shape=[
            shaped((2, half, fibres)),
            shaped((expos, half, fibres)),
            shaped((fib_count * per, fibres), BF16),
        ]
        + [shaped(x.shape, x.dtype) for x in inputs],
        scratch_shapes=[pltpu.SemaphoreType.DMA((5 + width // GROUP,))],
        compiler_params=params(),
        cost_estimate=cost(20 * ivar.size, 6 * ivar.size),
        name="sent_weights",
    )(place, *held_in_hbm(*inputs))


def lay_out(source_ref, target_ref, pieces, pitch):
    expos, _, fibres = source_ref.shape
    for h in range(fibres // LANES):
        for e in range(expos):
            for first, length, at in pieces:
                target_ref[pl.ds((h * expos + e) * pitch + at, length), :] = source_ref[
                    e, pl.ds(first, length), pl.ds(h * LANES, LANES)
                ]


def kept_kernel(
    wav_count, place_ref, coupling_ref, counts_ref, good_ref, pixels_ref, ivar_ref, bits_ref,
    sums_ref, weight_ref, up_ref, down_ref, ivar_s, pixel_s,
):
    expos, width, fibres = ivar_ref.shape
    half = width // 2
    streams = expos * fibres // LANES
    count = -(-HALO // ROWS) * ROWS
    pitch = odd(2 * count)
    which = place_ref[2]
    words = GROUP // BITS
    edges = [(0, count, 0), (width - count, count, count)]
    lay_out(ivar_ref, ivar_s, edges, pitch)
    lay_out(pixels_ref, pixel_s, edges, pitch)
    coupling = stream_coupling(coupling_ref, expos)
    back = 1.0 / coupling
    zero = jnp.zeros((streams, LANES), F32)
    states = [(zero, zero + 1.0, zero), (zero, zero + 1.0, zero)]

    def eliminate(tile, tiles):
        for i in range(HALO * tile // tiles, HALO * (tile + 1) // tiles):
            for side, row in enumerate((2 * count - HALO + i, HALO - 1 - i)):
                at = pl.ds(row, streams, stride=pitch)
                states[side] = advance(states[side], ivar_s[at, :], pixel_s[at, :], back)
                if i % 24 == 23:
                    states[side] = rescaled(states[side])

    write_weights(
        place_ref, wav_count, which, coupling_ref, counts_ref, good_ref,
        lambda e, tile: ivar_ref[e, pl.ds(pl.multiple_of(which * half + ROWS * tile, ROWS), ROWS), :],
        lambda e, group: bits_ref[e, pl.ds(pl.multiple_of(which * (half // BITS) + words * group, words), words), :],
        sums_ref, weight_ref, eliminate,
    )
    for (n, d, b), out_ref in zip(states, (up_ref, down_ref)):
        scale = 1.0 / (d + n)
        out_ref[0] = coupling * (n * scale)
        out_ref[1] = b * scale


def kept_weights(wav_count, place, coupling, counts, good, pixels, ivar, bits):
    expos, width, fibres = ivar.shape
    half = width // 2
    streams = expos * fibres // LANES
    count = -(-HALO // ROWS) * ROWS
    edge = shaped((2, streams, LANES))
    edge_scratch = pltpu.VMEM((streams * odd(2 * count), LANES), F32)
    return pl.pallas_call(
        functools.partial(kept_kernel, wav_count),
        in_specs=[in_smem] + [in_vmem] * 6,
        out_specs=[in_vmem] * 4,
        out_shape=[shaped((2, half, fibres)), shaped((expos, half, fibres)), edge, edge],
        scratch_shapes=[edge_scratch, edge_scratch],
        compiler_params=params(),
        cost_estimate=cost(20 * ivar.size, 6 * ivar.size),
        name="kept_weights",
    )(place, coupling, counts, good, pixels, ivar, bits)


def layout_kernel(arrived_ref, pixels_ref, ivar_ref, pixel_out, ivar_out):
    width = ivar_ref.shape[1]
    lay_out(ivar_ref, ivar_out, [(0, width, 0)], odd(width))
    lay_out(pixels_ref, pixel_out, [(0, width, 0)], odd(width))


def stream_layout(arrived, pixels, ivar):
    expos, width, fibres = ivar.shape
    streams = expos * fibres // LANES
    laid = shaped((streams * odd(width), LANES))
    return pl.pallas_call(
        layout_kernel,
        in_specs=[in_vmem] * 3,
        out_specs=[in_vmem] * 2,
        out_shape=[laid, laid],
        compiler_params=params(),
        cost_estimate=cost(0, 16 * ivar.size),
        name="stream_layout",
    )(arrived, pixels, ivar)


def solve_kernel(
    wav_count, place_ref, coupling_ref, left_ref, right_ref, pixel_ref, ivar_ref, weight_ref,
    theirs_ref, solved_s, lead_s, rest_s,
):
    streams = left_ref.shape[1]
    expos, half, fibres = weight_ref.shape
    width = 2 * half
    pitch = odd(width)
    middle = half
    coupling = stream_coupling(coupling_ref, expos)
    back = 1.0 / coupling

    def row_at(i):
        return pl.ds(i, streams, stride=pitch)

    def begin(edge_ref, outermost):
        n = jnp.where(place_ref[1] == outermost, 0.0, edge_ref[0]) * back
        return (n, 1.0 - n, jnp.where(place_ref[1] == outermost, 0.0, edge_ref[1]))

    def keep(side, i, state):
        n, d, b = state
        inverse = inverse_of(d + n)
        lead_s[side, i] = d * inverse
        rest_s[side, i] = b * inverse

    unrolled = divisor_of(middle, 24)

    def eliminate(it, states):
        states = list(states)
        for k in range(unrolled):
            i = it * unrolled + k
            for side, row in enumerate((i, width - 1 - i)):
                keep(side, i, states[side])
                states[side] = advance(states[side], ivar_ref[row_at(row), :], pixel_ref[row_at(row), :], back)
        return tuple(rescaled(state) for state in states)

    states = lax.fori_loop(0, middle // unrolled, eliminate, (begin(left_ref, 0), begin(right_ref, wav_count - 1)))
    for side in range(2):
        keep(side, middle, states[side])
    lead, rest = lead_s[0, middle], rest_s[0, middle]
    lead_r, rest_r = lead_s[1, middle], rest_s[1, middle]
    left = (rest + lead * rest_r) / (1.0 - lead * lead_r)
    right = rest_r + lead_r * left
    several = divisor_of(middle, 48)

    def after_both(near, far):
        return far[0] * near[0], far[1] + far[0] * near[1]

    def step(factors, value):
        return factors[1] + factors[0] * value

    def substitute(it, values):
        values = list(values)
        for k in range(0, several, 4):
            for side in range(2):
                rows = [middle - 1 - (it * several + k + m) for m in range(4)]
                one, two, three, four = [(lead_s[side, i], rest_s[side, i]) for i in rows]
                first_two = after_both(one, two)
                all_four = after_both(first_two, after_both(three, four))
                value = values[side]
                third = step(first_two, value)
                solved = [value, step(one, value), third, step(three, third)]
                values[side] = step(all_four, value)
                for i, x in zip(rows, solved):
                    solved_s[row_at(i if side == 0 else width - 1 - i), :] = x
        return tuple(values)

    lax.fori_loop(0, middle // several, substitute, (left, right))

    add_up(theirs_ref, weight_ref, solved_s, coupling_ref, 1 - place_ref[2])


def add_up(out_ref, weight_ref, solved_ref, coupling_ref, which):
    expos, half, fibres = weight_ref.shape
    pitch = odd(2 * half)
    start = which * half
    back = 1.0 / coupling_ref[...]
    unrolled = divisor_of(half // ROWS, 5)

    def body(g, carry):
        for k in range(unrolled):
            row = pl.multiple_of((g * unrolled + k) * ROWS, ROWS)
            for h in range(fibres // LANES):
                total = None
                for e in range(expos):
                    at = pl.ds((h * expos + e) * pitch + start + row, ROWS)
                    term = weight_ref[e, pl.ds(row, ROWS), pl.ds(h * LANES, LANES)] * solved_ref[at, :]
                    total = term if e == 0 else total + term
                out_ref[0, pl.ds(row, ROWS), pl.ds(h * LANES, LANES)] = total * back[:, h * LANES : (h + 1) * LANES]
        return carry

    lax.fori_loop(0, half // ROWS // unrolled, body, 0)


def flux_sums(wav_count, place, coupling, left, right, pixels, ivar, weight):
    expos, half, fibres = weight.shape
    streams = left.shape[1]
    factor_scratch = pltpu.VMEM((2, half + 1, streams, LANES), F32)
    return pl.pallas_call(
        functools.partial(solve_kernel, wav_count),
        in_specs=[in_smem] + [in_vmem] * 6,
        out_specs=[in_vmem, in_vmem],
        out_shape=[shaped((1, half, fibres)), shaped(pixels.shape)],
        scratch_shapes=[factor_scratch, factor_scratch],
        compiler_params=params(),
        cost_estimate=cost(0, 0),
        name="flux_sums",
    )(place, coupling, left, right, pixels, ivar, weight)


def kept_flux_kernel(place_ref, coupling_ref, solved_ref, weight_ref, out_ref):
    add_up(out_ref, weight_ref, solved_ref, coupling_ref, place_ref[2])


def kept_flux(place, coupling, solved, weight):
    expos, half, fibres = weight.shape
    return pl.pallas_call(
        kept_flux_kernel,
        in_specs=[in_smem] + [in_vmem] * 3,
        out_specs=in_vmem,
        out_shape=shaped((1, half, fibres)),
        compiler_params=params(),
        cost_estimate=cost(2 * weight.size, 8 * weight.size),
        name="kept_flux",
    )(place, coupling, solved, weight)


def split_dot(x, table, dims):
    top = x.astype(BF16)
    low = (x - top.astype(F32)).astype(BF16)
    both = lax.dot_general(jnp.concatenate([top, low], 0), table, dims, preferred_element_type=F32)
    return both[: x.shape[0]] + both[x.shape[0] :]


def sort_kernel(pack, scaled, theirs_ref, mine_ref, table_ref, *refs):
    values, rows, _ = mine_ref.shape
    part = rows // pack
    totals = [mine_ref[v] + theirs_ref[v] for v in range(values)]
    if scaled:
        scale_ref, _, *out_refs = refs
        totals = [t * scale_ref[...] for t in totals]
    else:
        *out_refs, scale_ref = refs
        scale = 1.0 / jnp.maximum(totals[0], 1.0)
        scale_ref[...] = scale
        totals[1] = totals[1] * scale
    moved = split_dot(jnp.concatenate(totals, 0), table_ref[...], NT)
    lanes = out_refs[0].shape[2]
    for v in range(values):
        halves = [moved[v * rows + h * part : v * rows + (h + 1) * part] for h in range(pack)]
        for d, out_ref in enumerate(out_refs):
            out_ref[v] = side_by_side(halves, d, lanes)


def side_by_side(halves, d, lanes):
    if len(halves) == 1:
        return halves[0][:, d * lanes : (d + 1) * lanes]
    at = slice(d // 2 * lanes, (d // 2 + 1) * lanes)
    first, second = halves[0][:, at], halves[1][:, at]
    if d % 2:
        first = pltpu.roll(first, lanes // 2, 1)
    else:
        second = pltpu.roll(second, lanes // 2, 1)
    lane = lax.broadcasted_iota(jnp.int32, first.shape, 1)
    return jnp.where(lane < lanes // 2, first, second)


def sort_fibres(theirs, mine, table, pack, pieces, scale=None, ahead=None):
    values, rows, fibres = mine.shape
    lanes = table.shape[0] * pack // pieces
    scaled = scale is not None
    outs = [shaped((values, rows // pack, lanes))] * pieces + ([] if scaled else [shaped((rows, fibres))])
    args = (theirs, mine, table) + ((scale, ahead) if scaled else ())
    return pl.pallas_call(
        functools.partial(sort_kernel, pack, scaled),
        in_specs=[in_vmem] * len(args),
        out_specs=[in_vmem] * len(outs),
        out_shape=outs,
        compiler_params=params(),
        cost_estimate=cost(0, 0),
        name="sort_flux" if scaled else "sort_weights",
    )(*args)


def exchange(pieces, fib_count):
    if len(pieces) == 1:
        return [lax.all_to_all(pieces[0], "fib", split_axis=2, concat_axis=2, tiled=True)]
    swapped = [lax.ppermute(pieces[d], "fib", [(i, i ^ d) for i in range(fib_count)]) for d in range(1, fib_count)]
    return [pieces[0]] + swapped


def landed(pieces, table, pack):
    values, part, lanes = pieces[0].shape
    parts = []
    for v in range(values):
        blocks = [piece[v] for piece in pieces]
        if pack == 1:
            parts.append(jnp.concatenate(blocks, 1) if len(blocks) > 1 else blocks[0])
        else:
            for h in range(2):
                pairs = range(0, len(blocks), 2)
                parts.append(jnp.concatenate([side_by_side(blocks[d : d + 2], h, lanes) for d in pairs], 1))
    moved = split_dot(jnp.concatenate(parts, 0), table, NT)
    rows = part * pack
    return [moved[v * rows : (v + 1) * rows] for v in range(values)]


def recv_kernel(moves, place_ref, slots_ref, table_ref):
    write_recv_table(*moves, place_ref[0], slots_ref, table_ref)


def recv_moves(moves, place, slots, fibres):
    fib_count, per, _ = moves
    return pl.pallas_call(
        functools.partial(recv_kernel, moves),
        in_specs=[in_smem, in_vmem],
        out_specs=in_vmem,
        out_shape=shaped((fibres, fib_count * per), BF16),
        compiler_params=params(),
        cost_estimate=cost(1e6, 1e6),
        name="recv_moves",
    )(place, slots)


def weights_end_kernel(pack, total, place_ref, table_ref, *refs):
    *piece_refs, ivar_ref, res_ref = refs
    weight, band = landed(piece_refs, table_ref[...], pack)
    rows = weight.shape[0]
    start = (place_ref[1] * 2 + place_ref[2]) * rows
    row = start + lax.broadcasted_iota(jnp.int32, (rows, 1), 0)
    before = jnp.where(row == 0, 0.0, band)
    after = jnp.where(row == total - 1, 0.0, band)
    ivar_ref[...] = weight
    res_ref[0] = before
    res_ref[1] = jnp.minimum(weight, 1.0) - before - after
    res_ref[2] = after


def end_weights(place, table, pieces, pack, fibres, total):
    rows = pieces[0].shape[1] * pack
    return pl.pallas_call(
        functools.partial(weights_end_kernel, pack, total),
        in_specs=[in_smem] + [in_vmem] * (1 + len(pieces)),
        out_specs=[in_vmem] * 2,
        out_shape=[shaped((rows, fibres)), shaped((3, rows, fibres))],
        compiler_params=params(),
        cost_estimate=cost(0, 0),
        name="end_weights",
    )(place, table, *pieces)


def flux_end_kernel(pack, order, table_ref, *refs):
    *piece_refs, flux_ref = refs
    (flux_ref[...],) = landed([piece_refs[order.index(d)] for d in range(len(order))], table_ref[...], pack)


def end_flux(table, pieces, pack, fibres):
    rows = pieces[0].shape[1] * pack
    order = sorted(range(len(pieces)), key=lambda d: (d > 0, abs(2 * d - len(pieces))))
    return pl.pallas_call(
        functools.partial(flux_end_kernel, pack, order),
        in_specs=[in_vmem] * (1 + len(pieces)),
        out_specs=in_vmem,
        out_shape=shaped((rows, fibres)),
        compiler_params=params(),
        cost_estimate=cost(2 * rows * table.size, 2 * rows * fibres * 4),
        name="end_flux",
    )(table, *(pieces[d] for d in order))


def after(value, done):
    return lax.optimization_barrier((value, done))[0]


def per_device(pixels, pixel_ivar, clip_bits, coupling, counts, good_flags, owner_slot):
    expos, width, fibres = pixels.shape
    fib_count, wav_count = lax.axis_size("fib"), lax.axis_size("wav")
    total = width * wav_count
    per = fibres // fib_count
    rows = width // 2
    pack = 2 if 2 * per == LANES and rows % (2 * ROWS) == 0 else 1
    rel = pack * per == LANES and fib_count & (fib_count - 1) == 0
    if not rel:
        pack = 1
    pieces = fib_count if rel else 1
    place = jnp.stack([lax.axis_index(axis) for axis in ("fib", "wav", "exp")]).astype(jnp.int32)
    coupling, counts, slots = coupling[None], counts[None], owner_slot[None]
    swap = [(0, 1), (1, 0)]
    moves = (fib_count, per, rel)

    theirs, weight_t, send_table, slots, coupling, counts, good, bits, ivar = sent_weights(
        moves, wav_count, place, slots, coupling, counts, good_flags, clip_bits, pixel_ivar
    )
    arriving = lax.ppermute(theirs, "exp", swap)
    mine, weight_m, up, down = kept_weights(
        wav_count, place, coupling, counts, good, pixels, ivar, bits
    )
    upward = [(i, (i + 1) % wav_count) for i in range(wav_count)]
    left = lax.ppermute(up, "wav", upward)
    right = lax.ppermute(down, "wav", [(j, i) for i, j in upward])
    *sorted_pieces, scale = sort_fibres(arriving, mine, send_table, pack, pieces)
    weight_pieces = exchange(sorted_pieces, fib_count)

    pixel_s, ivar_s = stream_layout(left[0] + right[0], pixels, ivar)
    theirs, solved = flux_sums(wav_count, place, coupling, left, right, pixel_s, ivar_s, weight_t)
    ahead = weight_pieces[fib_count // 2 if rel else 0][0, :ROWS, :LANES] * 0.5
    arriving = lax.ppermute(theirs, "exp", swap)
    mine = kept_flux(after(place, theirs), coupling, solved, weight_m)
    sorted_pieces = sort_fibres(arriving, mine, send_table, pack, pieces, scale, ahead)
    flux_pieces = exchange(sorted_pieces, fib_count)
    recv_table = recv_moves(moves, after(place, sorted_pieces[0]), slots, fibres)
    ivar, res = end_weights(place, recv_table, weight_pieces, pack, fibres, total)
    flux = end_flux(recv_table, flux_pieces, pack, fibres)
    return (flux, ivar, res)


def solution(mesh):
    return jax.shard_map(
        per_device,
        mesh=mesh,
        in_specs=(
            P("exp", "wav", "fib"),
            P("exp", "wav", "fib"),
            P("exp", "wav", "fib"),
            P("fib"),
            P("fib"),
            P("exp", "fib"),
            P(),
        ),
        out_specs=(
            P(("wav", "exp"), "fib"),
            P(("wav", "exp"), "fib"),
            P(None, ("wav", "exp"), "fib"),
        ),
        check_vma=False,
    )
```

```python
import functools

import jax
import jax.numpy as jnp
from jax import lax
from jax.experimental import pallas as pl
from jax.experimental.pallas import tpu as pltpu
from jax.sharding import PartitionSpec as P

HALO = 50
BITS = 15
LANES = 128
ROWS = 8
GROUP = 120
VMEM_BYTES = 32 * 1024 * 1024
F32 = jnp.float32
BF16 = jnp.bfloat16
NT = (((1,), (1,)), ((), ()))

in_vmem = pl.BlockSpec(memory_space=pltpu.VMEM)
in_smem = pl.BlockSpec(memory_space=pltpu.SMEM)
in_hbm = pl.BlockSpec(memory_space=pltpu.HBM)


def params():
    return pltpu.CompilerParams(vmem_limit_bytes=VMEM_BYTES)


def cost(flops, moved):
    return pl.CostEstimate(flops=int(flops), bytes_accessed=int(moved), transcendentals=0)


def held_in_hbm(*arrays):
    return [pltpu.with_memory_space_constraint(array, pltpu.HBM) for array in arrays]


def shaped(shape, dtype=F32):
    return jax.ShapeDtypeStruct(shape, dtype)


def usable_rows(place_ref, counts_ref, good_ref):
    count = good_ref.shape[0]
    return [
        good_ref[e : e + 1, :].astype(F32)
        * jnp.where(place_ref[2] * count + e < counts_ref[...], 1.0, 0.0)
        for e in range(count)
    ]


def tile_bits(tile):
    first, last = (ROWS * tile) // BITS, (ROWS * tile + ROWS - 1) // BITS
    split = BITS * last - ROWS * tile
    row = lax.broadcasted_iota(jnp.int32, (ROWS, 1), 0)
    word = jnp.where(row >= split, last, first)
    return first, last, split, jnp.left_shift(1, ROWS * tile + row - BITS * word)


def tile_words(words, tile):
    first, last, split, mask = tile_bits(tile)
    picked = words[first : first + 1, :]
    if last != first:
        row = lax.broadcasted_iota(jnp.int32, (ROWS, 1), 0)
        picked = jnp.where(row >= split, words[last : last + 1, :], picked)
    return (picked & mask) != 0


def in_flight(pairs, sems, at=0):
    copies = [pltpu.make_async_copy(source, target, sems.at[at + i]) for i, (source, target) in enumerate(pairs)]
    for copy in copies:
        copy.start()
    return copies


def inverse_of(x):
    guess = pl.reciprocal(x, approx=True)
    return guess * (2.0 - x * guess)


def advance(state, ivar, pixel, back_coupling):
    n, d, b = state
    ratio = ivar * back_coupling
    next_d = d + n
    return (n * (1.0 + ratio) + ratio * d, next_d, b + (ivar * pixel) * next_d)


def rescaled(state):
    scale = inverse_of(state[1])
    return tuple(part * scale for part in state)


def odd(rows):
    return rows + 1 - rows % 2


def divisor_of(size, most):
    return max(k for k in range(1, most + 1) if size % k == 0)


def owners(slots_ref, fib_count, fibres):
    rows = [slots_ref[:, s * fibres : (s + 1) * fibres].astype(F32) for s in range(fib_count)]
    sources = -(-fib_count // ROWS) * ROWS
    if sources > fib_count:
        rows.append(jnp.full((sources - fib_count, fibres), -1.0, F32))
    slots = jnp.concatenate(rows, 0)
    owner = jnp.floor((slots + 0.5) * (1.0 / fibres))
    return owner, slots - owner * fibres


def earlier_fibres(fibres):
    row = lax.broadcasted_iota(jnp.int32, (fibres, fibres), 0)
    col = lax.broadcasted_iota(jnp.int32, (fibres, fibres), 1)
    return (row < col).astype(F32).astype(BF16)


def write_send_table(fib_count, per, rel, me, slots_ref, table_ref):
    fibres = table_ref.shape[1]
    owner, _ = owners(slots_ref, fib_count, fibres)
    source = lax.broadcasted_iota(jnp.int32, owner.shape, 0)
    my_owner = jnp.sum(jnp.where(source == me, owner, 0.0), axis=0, keepdims=True).astype(jnp.int32)
    to_owner = (source == my_owner).astype(F32)
    counted = jnp.dot(to_owner.astype(BF16), earlier_fibres(fibres), preferred_element_type=F32)
    rank = jnp.sum(to_owner * counted, axis=0, keepdims=True).astype(jnp.int32)
    target = my_owner ^ me if rel else my_owner
    row = lax.broadcasted_iota(jnp.int32, table_ref.shape, 0)
    table_ref[...] = (row == target * per + rank).astype(F32).astype(BF16)


def write_recv_table(fib_count, per, rel, me, slots_ref, table_ref):
    fibres = table_ref.shape[0]
    total_lanes = fib_count * per
    owner, column = owners(slots_ref, fib_count, fibres)
    source = lax.broadcasted_iota(jnp.int32, owner.shape, 0)
    mine = (owner == me.astype(F32)).astype(F32)
    rank_in = jnp.dot(mine.astype(BF16), earlier_fibres(fibres), preferred_element_type=F32).astype(jnp.int32)
    order = source ^ me if rel else source
    arrival = jnp.where(mine > 0.0, order * per + rank_in, -1)
    tall = lax.broadcasted_iota(jnp.int32, (total_lanes, fibres), 0)
    landing = jnp.zeros((ROWS, total_lanes), F32)
    for s in range(fib_count):
        hit = tall == arrival[s : s + 1, :]
        values = jnp.broadcast_to(column[s : s + 1, :], (ROWS, fibres)).astype(BF16)
        landing = landing + lax.dot_general(
            values, hit.astype(F32).astype(BF16), NT, preferred_element_type=F32
        )
    row = lax.broadcasted_iota(jnp.int32, table_ref.shape, 0)
    table_ref[...] = (row == landing[0:1, :].astype(jnp.int32)).astype(F32).astype(BF16)


def stream_coupling(coupling_ref, expos):
    coupling = coupling_ref[...]
    blocks = coupling.shape[1] // LANES
    return jnp.concatenate(
        [jnp.broadcast_to(coupling[:, h * LANES : (h + 1) * LANES], (expos, LANES)) for h in range(blocks)], 0
    )


def weight_tile(coupling, usable, words, ivars, within, scale_row):
    links = scale_row * coupling
    weights = []
    weight_sum = band_sum = None
    for e, ivar in enumerate(ivars):
        weight = jnp.where(tile_words(words[e], within), ivar * usable[e], 0.0)
        band = weight * inverse_of(ivar + links)
        weights.append(weight)
        weight_sum = weight if e == 0 else weight_sum + weight
        band_sum = band if e == 0 else band_sum + band
    return weights, weight_sum, band_sum * coupling


def write_weights(place_ref, wav_count, which, coupling_v, counts_v, good_v, ivar_of, words_of, sums_ref, weight_ref, beside):
    expos, half, _ = weight_ref.shape
    coupling = coupling_v[...]
    usable = usable_rows(place_ref, counts_v, good_v)
    start = place_ref[1] * (2 * half) + which * half
    tiles = half // ROWS
    tiles_in_group = GROUP // ROWS
    for tile in range(tiles):
        beside(tile, tiles)
        group, within = divmod(tile, tiles_in_group)
        scale_row = 4.0
        if tile in (0, tiles - 1):
            row = start + ROWS * tile + lax.broadcasted_iota(jnp.int32, (ROWS, 1), 0)
            scale_row = jnp.where((row == 0) | (row == wav_count * 2 * half - 1), 2.0, 4.0)
        at = slice(ROWS * tile, ROWS * (tile + 1))
        weights, weight_sum, band_sum = weight_tile(
            coupling,
            usable,
            [words_of(e, group) for e in range(expos)],
            [ivar_of(e, tile) for e in range(expos)],
            within,
            scale_row,
        )
        for e in range(expos):
            weight_ref[e, at, :] = weights[e]
        sums_ref[0, at, :] = weight_sum
        sums_ref[1, at, :] = band_sum


def edge_copies(source_ref, target_ref):
    expos, width, fibres = source_ref.shape
    count = -(-HALO // ROWS) * ROWS
    pitch = odd(2 * count)
    return [
        (
            source_ref.at[e, pl.ds(first, count), pl.ds(h * LANES, LANES)],
            target_ref.at[pl.ds((h * expos + e) * pitch + at, count), :],
        )
        for h in range(fibres // LANES)
        for e in range(expos)
        for first, at in ((0, 0), (width - count, count))
    ]


def sent_kernel(
    moves, wav_count, place_ref, slots_ref, coupling_ref, counts_ref, good_ref, bits_ref, ivar_ref, pixels_ref,
    sums_ref, weight_ref, table_ref, slots_v, coupling_v, counts_v, good_v, bits_v, ivar_v, edges_v, sems,
):
    expos, width, _ = ivar_ref.shape
    half = width // 2
    which = 1 - place_ref[2]
    words = GROUP // BITS

    def part(source, target, first):
        at = pl.ds(pl.multiple_of(first, ROWS), GROUP)
        return source.at[:, at, :], target.at[:, at, :]

    waits = in_flight(
        [
            (slots_ref, slots_v),
            (coupling_ref, coupling_v),
            (counts_ref, counts_v),
            (good_ref, good_v),
            (bits_ref, bits_v),
        ]
        + [part(ivar_ref, ivar_v, which * half + g) for g in range(0, half, GROUP)]
        + [part(ivar_ref, ivar_v, (1 - which) * half + g) for g in range(0, half, GROUP)]
        + edge_copies(pixels_ref, edges_v),
        sems,
    )
    waits[0].wait()
    write_send_table(*moves, place_ref[0], slots_v, table_ref)
    for wait in waits[1:5]:
        wait.wait()

    def arrive(tile, tiles):
        if ROWS * tile % GROUP == 0:
            waits[5 + ROWS * tile // GROUP].wait()

    write_weights(
        place_ref, wav_count, which, coupling_v, counts_v, good_v,
        lambda e, tile: ivar_v[e, pl.ds(pl.multiple_of(which * half + ROWS * tile, ROWS), ROWS), :],
        lambda e, group: bits_v[e, pl.ds(pl.multiple_of(which * (half // BITS) + words * group, words), words), :],
        sums_ref, weight_ref, arrive,
    )
    for wait in waits[5 + half // GROUP :]:
        wait.wait()


def sent_weights(moves, wav_count, place, slots, coupling, counts, good, bits, ivar, pixels):
    expos, width, fibres = ivar.shape
    half = width // 2
    fib_count, per, _ = moves
    inputs = (slots, coupling, counts, good, bits, ivar)
    streams = expos * fibres // LANES
    count = -(-HALO // ROWS) * ROWS
    return pl.pallas_call(
        functools.partial(sent_kernel, moves, wav_count),
        in_specs=[in_smem] + [in_hbm] * 7,
        out_specs=[in_vmem] * 10,
        out_shape=[
            shaped((2, half, fibres)),
            shaped((expos, half, fibres)),
            shaped((fib_count * per, fibres), BF16),
        ]
        + [shaped(x.shape, x.dtype) for x in inputs]
        + [shaped((streams * odd(2 * count), LANES))],
        scratch_shapes=[pltpu.SemaphoreType.DMA((5 + width // GROUP + 2 * streams,))],
        compiler_params=params(),
        cost_estimate=cost(20 * ivar.size, 6 * ivar.size),
        name="sent_weights",
    )(place, *held_in_hbm(*inputs, pixels))


def lay_out(source_ref, target_ref, pieces, pitch):
    expos, _, fibres = source_ref.shape
    for h in range(fibres // LANES):
        for e in range(expos):
            for first, length, at in pieces:
                target_ref[pl.ds((h * expos + e) * pitch + at, length), :] = source_ref[
                    e, pl.ds(first, length), pl.ds(h * LANES, LANES)
                ]


def kept_kernel(
    wav_count, place_ref, coupling_ref, counts_ref, good_ref, pixel_s, ivar_ref, bits_ref,
    sums_ref, weight_ref, up_ref, down_ref, ivar_s,
):
    expos, width, fibres = ivar_ref.shape
    half = width // 2
    streams = expos * fibres // LANES
    count = -(-HALO // ROWS) * ROWS
    pitch = odd(2 * count)
    which = place_ref[2]
    words = GROUP // BITS
    edges = [(0, count, 0), (width - count, count, count)]
    lay_out(ivar_ref, ivar_s, edges, pitch)
    coupling = stream_coupling(coupling_ref, expos)
    back = 1.0 / coupling
    zero = jnp.zeros((streams, LANES), F32)
    states = [(zero, zero + 1.0, zero), (zero, zero + 1.0, zero)]

    def eliminate(tile, tiles):
        for i in range(HALO * tile // tiles, HALO * (tile + 1) // tiles):
            for side, row in enumerate((2 * count - HALO + i, HALO - 1 - i)):
                at = pl.ds(row, streams, stride=pitch)
                states[side] = advance(states[side], ivar_s[at, :], pixel_s[at, :], back)
                if i % 24 == 23:
                    states[side] = rescaled(states[side])

    write_weights(
        place_ref, wav_count, which, coupling_ref, counts_ref, good_ref,
        lambda e, tile: ivar_ref[e, pl.ds(pl.multiple_of(which * half + ROWS * tile, ROWS), ROWS), :],
        lambda e, group: bits_ref[e, pl.ds(pl.multiple_of(which * (half // BITS) + words * group, words), words), :],
        sums_ref, weight_ref, eliminate,
    )
    for (n, d, b), out_ref in zip(states, (up_ref, down_ref)):
        scale = 1.0 / (d + n)
        out_ref[0] = coupling * (n * scale)
        out_ref[1] = b * scale


def kept_weights(wav_count, place, coupling, counts, good, pixels, ivar, bits):
    expos, width, fibres = ivar.shape
    half = width // 2
    streams = expos * fibres // LANES
    count = -(-HALO // ROWS) * ROWS
    edge = shaped((2, streams, LANES))
    edge_scratch = pltpu.VMEM((streams * odd(2 * count), LANES), F32)
    return pl.pallas_call(
        functools.partial(kept_kernel, wav_count),
        in_specs=[in_smem] + [in_vmem] * 6,
        out_specs=[in_vmem] * 4,
        out_shape=[shaped((2, half, fibres)), shaped((expos, half, fibres)), edge, edge],
        scratch_shapes=[edge_scratch],
        compiler_params=params(),
        cost_estimate=cost(20 * ivar.size, 6 * ivar.size),
        name="kept_weights",
    )(place, coupling, counts, good, pixels, ivar, bits)


def layout_kernel(arrived_ref, pixels_ref, ivar_ref, pixel_out, ivar_out):
    width = ivar_ref.shape[1]
    lay_out(ivar_ref, ivar_out, [(0, width, 0)], odd(width))
    lay_out(pixels_ref, pixel_out, [(0, width, 0)], odd(width))


def stream_layout(arrived, pixels, ivar):
    expos, width, fibres = ivar.shape
    streams = expos * fibres // LANES
    laid = shaped((streams * odd(width), LANES))
    return pl.pallas_call(
        layout_kernel,
        in_specs=[in_vmem] * 3,
        out_specs=[in_vmem] * 2,
        out_shape=[laid, laid],
        compiler_params=params(),
        cost_estimate=cost(0, 16 * ivar.size),
        name="stream_layout",
    )(arrived, pixels, ivar)


def solve_kernel(
    wav_count, place_ref, coupling_ref, left_ref, right_ref, pixel_ref, ivar_ref, weight_ref,
    theirs_ref, solved_s, lead_s, rest_s,
):
    streams = left_ref.shape[1]
    expos, half, fibres = weight_ref.shape
    width = 2 * half
    pitch = odd(width)
    middle = half
    coupling = stream_coupling(coupling_ref, expos)
    back = 1.0 / coupling

    def row_at(i):
        return pl.ds(i, streams, stride=pitch)

    def begin(edge_ref, outermost):
        n = jnp.where(place_ref[1] == outermost, 0.0, edge_ref[0]) * back
        return (n, 1.0 - n, jnp.where(place_ref[1] == outermost, 0.0, edge_ref[1]))

    def keep(side, i, state):
        n, d, b = state
        inverse = inverse_of(d + n)
        lead_s[side, i] = d * inverse
        rest_s[side, i] = b * inverse

    unrolled = divisor_of(middle, 24)

    def eliminate(it, states):
        states = list(states)
        for k in range(unrolled):
            i = it * unrolled + k
            for side, row in enumerate((i, width - 1 - i)):
                keep(side, i, states[side])
                states[side] = advance(states[side], ivar_ref[row_at(row), :], pixel_ref[row_at(row), :], back)
        return tuple(rescaled(state) for state in states)

    states = lax.fori_loop(0, middle // unrolled, eliminate, (begin(left_ref, 0), begin(right_ref, wav_count - 1)))
    for side in range(2):
        keep(side, middle, states[side])
    lead, rest = lead_s[0, middle], rest_s[0, middle]
    lead_r, rest_r = lead_s[1, middle], rest_s[1, middle]
    left = (rest + lead * rest_r) / (1.0 - lead * lead_r)
    right = rest_r + lead_r * left
    several = divisor_of(middle, 48)

    def after_both(near, far):
        return far[0] * near[0], far[1] + far[0] * near[1]

    def step(factors, value):
        return factors[1] + factors[0] * value

    def substitute(it, values):
        values = list(values)
        for k in range(0, several, 4):
            for side in range(2):
                rows = [middle - 1 - (it * several + k + m) for m in range(4)]
                one, two, three, four = [(lead_s[side, i], rest_s[side, i]) for i in rows]
                first_two = after_both(one, two)
                all_four = after_both(first_two, after_both(three, four))
                value = values[side]
                third = step(first_two, value)
                solved = [value, step(one, value), third, step(three, third)]
                values[side] = step(all_four, value)
                for i, x in zip(rows, solved):
                    solved_s[row_at(i if side == 0 else width - 1 - i), :] = x
        return tuple(values)

    lax.fori_loop(0, middle // several, substitute, (left, right))

    add_up(theirs_ref, weight_ref, solved_s, coupling_ref, 1 - place_ref[2])


def add_up(out_ref, weight_ref, solved_ref, coupling_ref, which):
    expos, half, fibres = weight_ref.shape
    pitch = odd(2 * half)
    start = which * half
    back = 1.0 / coupling_ref[...]
    unrolled = divisor_of(half // ROWS, 5)

    def body(g, carry):
        for k in range(unrolled):
            row = pl.multiple_of((g * unrolled + k) * ROWS, ROWS)
            for h in range(fibres // LANES):
                total = None
                for e in range(expos):
                    at = pl.ds((h * expos + e) * pitch + start + row, ROWS)
                    term = weight_ref[e, pl.ds(row, ROWS), pl.ds(h * LANES, LANES)] * solved_ref[at, :]
                    total = term if e == 0 else total + term
                out_ref[0, pl.ds(row, ROWS), pl.ds(h * LANES, LANES)] = total * back[:, h * LANES : (h + 1) * LANES]
        return carry

    lax.fori_loop(0, half // ROWS // unrolled, body, 0)


def flux_sums(wav_count, place, coupling, left, right, pixels, ivar, weight):
    expos, half, fibres = weight.shape
    streams = left.shape[1]
    factor_scratch = pltpu.VMEM((2, half + 1, streams, LANES), F32)
    return pl.pallas_call(
        functools.partial(solve_kernel, wav_count),
        in_specs=[in_smem] + [in_vmem] * 6,
        out_specs=[in_vmem, in_vmem],
        out_shape=[shaped((1, half, fibres)), shaped(pixels.shape)],
        scratch_shapes=[factor_scratch, factor_scratch],
        compiler_params=params(),
        cost_estimate=cost(0, 0),
        name="flux_sums",
    )(place, coupling, left, right, pixels, ivar, weight)


def kept_flux_kernel(place_ref, coupling_ref, solved_ref, weight_ref, out_ref):
    add_up(out_ref, weight_ref, solved_ref, coupling_ref, place_ref[2])


def kept_flux(place, coupling, solved, weight):
    expos, half, fibres = weight.shape
    return pl.pallas_call(
        kept_flux_kernel,
        in_specs=[in_smem] + [in_vmem] * 3,
        out_specs=in_vmem,
        out_shape=shaped((1, half, fibres)),
        compiler_params=params(),
        cost_estimate=cost(2 * weight.size, 8 * weight.size),
        name="kept_flux",
    )(place, coupling, solved, weight)


def split_dot(x, table, dims):
    top = x.astype(BF16)
    low = (x - top.astype(F32)).astype(BF16)
    both = lax.dot_general(jnp.concatenate([top, low], 0), table, dims, preferred_element_type=F32)
    return both[: x.shape[0]] + both[x.shape[0] :]


def sort_kernel(pack, scaled, theirs_ref, mine_ref, table_ref, *refs):
    values, rows, _ = mine_ref.shape
    part = rows // pack
    totals = [mine_ref[v] + theirs_ref[v] for v in range(values)]
    if scaled:
        scale_ref, _, *out_refs = refs
        totals = [t * scale_ref[...] for t in totals]
    else:
        *out_refs, scale_ref = refs
        scale = 1.0 / jnp.maximum(totals[0], 1.0)
        scale_ref[...] = scale
        totals[1] = totals[1] * scale
    moved = split_dot(jnp.concatenate(totals, 0), table_ref[...], NT)
    lanes = out_refs[0].shape[2]
    for v in range(values):
        halves = [moved[v * rows + h * part : v * rows + (h + 1) * part] for h in range(pack)]
        for d, out_ref in enumerate(out_refs):
            out_ref[v] = side_by_side(halves, d, lanes)


def side_by_side(halves, d, lanes):
    if len(halves) == 1:
        return halves[0][:, d * lanes : (d + 1) * lanes]
    at = slice(d // 2 * lanes, (d // 2 + 1) * lanes)
    first, second = halves[0][:, at], halves[1][:, at]
    if d % 2:
        first = pltpu.roll(first, lanes // 2, 1)
    else:
        second = pltpu.roll(second, lanes // 2, 1)
    lane = lax.broadcasted_iota(jnp.int32, first.shape, 1)
    return jnp.where(lane < lanes // 2, first, second)


def sort_fibres(theirs, mine, table, pack, pieces, scale=None, ahead=None):
    values, rows, fibres = mine.shape
    lanes = table.shape[0] * pack // pieces
    scaled = scale is not None
    outs = [shaped((values, rows // pack, lanes))] * pieces + ([] if scaled else [shaped((rows, fibres))])
    args = (theirs, mine, table) + ((scale, ahead) if scaled else ())
    return pl.pallas_call(
        functools.partial(sort_kernel, pack, scaled),
        in_specs=[in_vmem] * len(args),
        out_specs=[in_vmem] * len(outs),
        out_shape=outs,
        compiler_params=params(),
        cost_estimate=cost(0, 0),
        name="sort_flux" if scaled else "sort_weights",
    )(*args)


def exchange(pieces, fib_count):
    if len(pieces) == 1:
        return [lax.all_to_all(pieces[0], "fib", split_axis=2, concat_axis=2, tiled=True)]
    swapped = [lax.ppermute(pieces[d], "fib", [(i, i ^ d) for i in range(fib_count)]) for d in range(1, fib_count)]
    return [pieces[0]] + swapped


def landed(pieces, table, pack):
    values, part, lanes = pieces[0].shape
    parts = []
    for v in range(values):
        blocks = [piece[v] for piece in pieces]
        if pack == 1:
            parts.append(jnp.concatenate(blocks, 1) if len(blocks) > 1 else blocks[0])
        else:
            for h in range(2):
                pairs = range(0, len(blocks), 2)
                parts.append(jnp.concatenate([side_by_side(blocks[d : d + 2], h, lanes) for d in pairs], 1))
    moved = split_dot(jnp.concatenate(parts, 0), table, NT)
    rows = part * pack
    return [moved[v * rows : (v + 1) * rows] for v in range(values)]


def recv_kernel(moves, place_ref, slots_ref, table_ref):
    write_recv_table(*moves, place_ref[0], slots_ref, table_ref)


def recv_moves(moves, place, slots, fibres):
    fib_count, per, _ = moves
    return pl.pallas_call(
        functools.partial(recv_kernel, moves),
        in_specs=[in_smem, in_vmem],
        out_specs=in_vmem,
        out_shape=shaped((fibres, fib_count * per), BF16),
        compiler_params=params(),
        cost_estimate=cost(1e6, 1e6),
        name="recv_moves",
    )(place, slots)


def weights_end_kernel(pack, total, place_ref, table_ref, *refs):
    *piece_refs, ivar_ref, res_ref = refs
    weight, band = landed(piece_refs, table_ref[...], pack)
    rows = weight.shape[0]
    start = (place_ref[1] * 2 + place_ref[2]) * rows
    row = start + lax.broadcasted_iota(jnp.int32, (rows, 1), 0)
    before = jnp.where(row == 0, 0.0, band)
    after = jnp.where(row == total - 1, 0.0, band)
    ivar_ref[...] = weight
    res_ref[0] = before
    res_ref[1] = jnp.minimum(weight, 1.0) - before - after
    res_ref[2] = after


def end_weights(place, table, pieces, pack, fibres, total):
    rows = pieces[0].shape[1] * pack
    return pl.pallas_call(
        functools.partial(weights_end_kernel, pack, total),
        in_specs=[in_smem] + [in_vmem] * (1 + len(pieces)),
        out_specs=[in_vmem] * 2,
        out_shape=[shaped((rows, fibres)), shaped((3, rows, fibres))],
        compiler_params=params(),
        cost_estimate=cost(0, 0),
        name="end_weights",
    )(place, table, *pieces)


def flux_end_kernel(pack, order, table_ref, *refs):
    *piece_refs, flux_ref = refs
    (flux_ref[...],) = landed([piece_refs[order.index(d)] for d in range(len(order))], table_ref[...], pack)


def end_flux(table, pieces, pack, fibres):
    rows = pieces[0].shape[1] * pack
    order = sorted(range(len(pieces)), key=lambda d: (d > 0, abs(2 * d - len(pieces))))
    return pl.pallas_call(
        functools.partial(flux_end_kernel, pack, order),
        in_specs=[in_vmem] * (1 + len(pieces)),
        out_specs=in_vmem,
        out_shape=shaped((rows, fibres)),
        compiler_params=params(),
        cost_estimate=cost(2 * rows * table.size, 2 * rows * fibres * 4),
        name="end_flux",
    )(table, *(pieces[d] for d in order))


def after(value, done):
    return lax.optimization_barrier((value, done))[0]


def per_device(pixels, pixel_ivar, clip_bits, coupling, counts, good_flags, owner_slot):
    expos, width, fibres = pixels.shape
    fib_count, wav_count = lax.axis_size("fib"), lax.axis_size("wav")
    total = width * wav_count
    per = fibres // fib_count
    rows = width // 2
    pack = 2 if 2 * per == LANES and rows % (2 * ROWS) == 0 else 1
    rel = pack * per == LANES and fib_count & (fib_count - 1) == 0
    if not rel:
        pack = 1
    pieces = fib_count if rel else 1
    place = jnp.stack([lax.axis_index(axis) for axis in ("fib", "wav", "exp")]).astype(jnp.int32)
    coupling, counts, slots = coupling[None], counts[None], owner_slot[None]
    swap = [(0, 1), (1, 0)]
    moves = (fib_count, per, rel)

    theirs, weight_t, send_table, slots, coupling, counts, good, bits, ivar, pixel_edges = sent_weights(
        moves, wav_count, place, slots, coupling, counts, good_flags, clip_bits, pixel_ivar, pixels
    )
    arriving = lax.ppermute(theirs, "exp", swap)
    mine, weight_m, up, down = kept_weights(
        wav_count, place, coupling, counts, good, pixel_edges, ivar, bits
    )
    upward = [(i, (i + 1) % wav_count) for i in range(wav_count)]
    left = lax.ppermute(up, "wav", upward)
    right = lax.ppermute(down, "wav", [(j, i) for i, j in upward])
    *sorted_pieces, scale = sort_fibres(arriving, mine, send_table, pack, pieces)
    weight_pieces = exchange(sorted_pieces, fib_count)

    pixel_s, ivar_s = stream_layout(left[0] + right[0], after(pixels, theirs), ivar)
    theirs, solved = flux_sums(wav_count, place, coupling, left, right, pixel_s, ivar_s, weight_t)
    ahead = weight_pieces[fib_count // 2 if rel else 0][0, :ROWS, :LANES] * 0.5
    arriving = lax.ppermute(theirs, "exp", swap)
    mine = kept_flux(after(place, theirs), coupling, solved, weight_m)
    sorted_pieces = sort_fibres(arriving, mine, send_table, pack, pieces, scale, ahead)
    flux_pieces = exchange(sorted_pieces, fib_count)
    recv_table = recv_moves(moves, after(place, sorted_pieces[0]), slots, fibres)
    ivar, res = end_weights(place, recv_table, weight_pieces, pack, fibres, total)
    flux = end_flux(recv_table, flux_pieces, pack, fibres)
    return (flux, ivar, res)


def solution(mesh):
    return jax.shard_map(
        per_device,
        mesh=mesh,
        in_specs=(
            P("exp", "wav", "fib"),
            P("exp", "wav", "fib"),
            P("exp", "wav", "fib"),
            P("fib"),
            P("fib"),
            P("exp", "fib"),
            P(),
        ),
        out_specs=(
            P(("wav", "exp"), "fib"),
            P(("wav", "exp"), "fib"),
            P(None, ("wav", "exp"), "fib"),
        ),
        check_vma=False,
    )
```

```python
import functools

import jax
import jax.numpy as jnp
from jax import lax
from jax.experimental import pallas as pl
from jax.experimental.pallas import tpu as pltpu
from jax.sharding import PartitionSpec as P

HALO = 50
BITS = 15
LANES = 128
ROWS = 8
GROUP = 120
VMEM_BYTES = 32 * 1024 * 1024
F32 = jnp.float32
BF16 = jnp.bfloat16
NT = (((1,), (1,)), ((), ()))

in_vmem = pl.BlockSpec(memory_space=pltpu.VMEM)
in_smem = pl.BlockSpec(memory_space=pltpu.SMEM)
in_hbm = pl.BlockSpec(memory_space=pltpu.HBM)


def params():
    return pltpu.CompilerParams(vmem_limit_bytes=VMEM_BYTES)


def cost(flops, moved):
    return pl.CostEstimate(flops=int(flops), bytes_accessed=int(moved), transcendentals=0)


def held_in_hbm(*arrays):
    return [pltpu.with_memory_space_constraint(array, pltpu.HBM) for array in arrays]


def shaped(shape, dtype=F32):
    return jax.ShapeDtypeStruct(shape, dtype)


def usable_rows(place_ref, counts_ref, good_ref):
    count = good_ref.shape[0]
    return [
        good_ref[e : e + 1, :].astype(F32)
        * jnp.where(place_ref[2] * count + e < counts_ref[...], 1.0, 0.0)
        for e in range(count)
    ]


def tile_bits(tile):
    first, last = (ROWS * tile) // BITS, (ROWS * tile + ROWS - 1) // BITS
    split = BITS * last - ROWS * tile
    row = lax.broadcasted_iota(jnp.int32, (ROWS, 1), 0)
    word = jnp.where(row >= split, last, first)
    return first, last, split, jnp.left_shift(1, ROWS * tile + row - BITS * word)


def tile_words(words, tile):
    first, last, split, mask = tile_bits(tile)
    picked = words[first : first + 1, :]
    if last != first:
        row = lax.broadcasted_iota(jnp.int32, (ROWS, 1), 0)
        picked = jnp.where(row >= split, words[last : last + 1, :], picked)
    return (picked & mask) != 0


def in_flight(pairs, sems, at=0):
    copies = [pltpu.make_async_copy(source, target, sems.at[at + i]) for i, (source, target) in enumerate(pairs)]
    for copy in copies:
        copy.start()
    return copies


def inverse_of(x):
    guess = pl.reciprocal(x, approx=True)
    return guess * (2.0 - x * guess)


def advance(state, ivar, pixel, back_coupling):
    n, d, b = state
    ratio = ivar * back_coupling
    next_d = d + n
    return (n * (1.0 + ratio) + ratio * d, next_d, b + (ivar * pixel) * next_d)


def rescaled(state):
    scale = inverse_of(state[1])
    return tuple(part * scale for part in state)


def odd(rows):
    return rows + 1 - rows % 2


def divisor_of(size, most):
    return max(k for k in range(1, most + 1) if size % k == 0)


def owners(slots_ref, fib_count, fibres):
    rows = [slots_ref[:, s * fibres : (s + 1) * fibres].astype(F32) for s in range(fib_count)]
    sources = -(-fib_count // ROWS) * ROWS
    if sources > fib_count:
        rows.append(jnp.full((sources - fib_count, fibres), -1.0, F32))
    slots = jnp.concatenate(rows, 0)
    owner = jnp.floor((slots + 0.5) * (1.0 / fibres))
    return owner, slots - owner * fibres


def earlier_fibres(fibres):
    row = lax.broadcasted_iota(jnp.int32, (fibres, fibres), 0)
    col = lax.broadcasted_iota(jnp.int32, (fibres, fibres), 1)
    return (row < col).astype(F32).astype(BF16)


def write_send_table(fib_count, pack, per, rel, me, slots_ref, table_ref):
    fibres = table_ref.shape[1] // pack
    lanes = pack * per
    owner, _ = owners(slots_ref, fib_count, fibres)
    source = lax.broadcasted_iota(jnp.int32, owner.shape, 0)
    my_owner = jnp.sum(jnp.where(source == me, owner, 0.0), axis=0, keepdims=True).astype(jnp.int32)
    to_owner = (source == my_owner).astype(F32)
    counted = jnp.dot(to_owner.astype(BF16), earlier_fibres(fibres), preferred_element_type=F32)
    rank = jnp.sum(to_owner * counted, axis=0, keepdims=True).astype(jnp.int32)
    target = my_owner ^ me if rel else my_owner
    base = target * lanes + rank
    place_of = jnp.concatenate([base + h * per for h in range(pack)], 1)
    row = lax.broadcasted_iota(jnp.int32, table_ref.shape, 0)
    table_ref[...] = (row == place_of).astype(F32).astype(BF16)


def write_recv_table(fib_count, pack, per, rel, me, slots_ref, table_ref):
    fibres = table_ref.shape[0] // pack
    lanes = pack * per
    total_lanes = fib_count * lanes
    owner, column = owners(slots_ref, fib_count, fibres)
    source = lax.broadcasted_iota(jnp.int32, owner.shape, 0)
    mine = (owner == me.astype(F32)).astype(F32)
    rank_in = jnp.dot(mine.astype(BF16), earlier_fibres(fibres), preferred_element_type=F32).astype(jnp.int32)
    order = source ^ me if rel else source
    arrival = jnp.where(mine > 0.0, order * lanes + rank_in, -total_lanes)
    tall = lax.broadcasted_iota(jnp.int32, (total_lanes, fibres), 0)
    landing = jnp.zeros((ROWS, total_lanes), F32)
    for s in range(fib_count):
        hit = tall == arrival[s : s + 1, :]
        for h in range(1, pack):
            hit = hit | (tall == arrival[s : s + 1, :] + h * per)
        values = jnp.broadcast_to(column[s : s + 1, :], (ROWS, fibres)).astype(BF16)
        landing = landing + lax.dot_general(
            values, hit.astype(F32).astype(BF16), NT, preferred_element_type=F32
        )
    lane = lax.broadcasted_iota(jnp.int32, (1, total_lanes), 1)
    landing = landing[0:1, :].astype(jnp.int32)
    for h in range(1, pack):
        inside = (lane % lanes >= h * per) & (lane % lanes < (h + 1) * per)
        landing = jnp.where(inside, landing + h * fibres, landing)
    row = lax.broadcasted_iota(jnp.int32, table_ref.shape, 0)
    table_ref[...] = (row == landing).astype(F32).astype(BF16)


def stream_coupling(coupling_ref, expos):
    coupling = coupling_ref[...]
    blocks = coupling.shape[1] // LANES
    return jnp.concatenate(
        [jnp.broadcast_to(coupling[:, h * LANES : (h + 1) * LANES], (expos, LANES)) for h in range(blocks)], 0
    )


def weight_tile(coupling, usable, words, ivars, within, scale_row):
    links = scale_row * coupling
    weights = []
    weight_sum = band_sum = None
    for e, ivar in enumerate(ivars):
        weight = jnp.where(tile_words(words[e], within), ivar * usable[e], 0.0)
        band = weight * inverse_of(ivar + links)
        weights.append(weight)
        weight_sum = weight if e == 0 else weight_sum + weight
        band_sum = band if e == 0 else band_sum + band
    return weights, weight_sum, band_sum * coupling


def write_weights(place_ref, wav_count, which, coupling_v, counts_v, good_v, ivar_of, words_of, sums_ref, weight_ref, beside):
    expos, half, _ = weight_ref.shape
    coupling = coupling_v[...]
    usable = usable_rows(place_ref, counts_v, good_v)
    start = place_ref[1] * (2 * half) + which * half
    tiles = half // ROWS
    tiles_in_group = GROUP // ROWS
    for tile in range(tiles):
        beside(tile, tiles)
        group, within = divmod(tile, tiles_in_group)
        scale_row = 4.0
        if tile in (0, tiles - 1):
            row = start + ROWS * tile + lax.broadcasted_iota(jnp.int32, (ROWS, 1), 0)
            scale_row = jnp.where((row == 0) | (row == wav_count * 2 * half - 1), 2.0, 4.0)
        at = slice(ROWS * tile, ROWS * (tile + 1))
        weights, weight_sum, band_sum = weight_tile(
            coupling,
            usable,
            [words_of(e, group) for e in range(expos)],
            [ivar_of(e, tile) for e in range(expos)],
            within,
            scale_row,
        )
        for e in range(expos):
            weight_ref[e, at, :] = weights[e]
        sums_ref[0, at, :] = weight_sum
        sums_ref[1, at, :] = band_sum


def sent_kernel(
    moves, wav_count, place_ref, slots_ref, coupling_ref, counts_ref, good_ref, bits_ref, ivar_ref,
    sums_ref, weight_ref, table_ref, slots_v, coupling_v, counts_v, good_v, bits_v, ivar_v, sems,
):
    expos, width, _ = ivar_ref.shape
    half = width // 2
    which = 1 - place_ref[2]
    words = GROUP // BITS

    def part(source, target, first):
        at = pl.ds(pl.multiple_of(first, ROWS), GROUP)
        return source.at[:, at, :], target.at[:, at, :]

    waits = in_flight(
        [
            (slots_ref, slots_v),
            (coupling_ref, coupling_v),
            (counts_ref, counts_v),
            (good_ref, good_v),
            (bits_ref, bits_v),
        ]
        + [part(ivar_ref, ivar_v, which * half + g) for g in range(0, half, GROUP)]
        + [part(ivar_ref, ivar_v, (1 - which) * half + g) for g in range(0, half, GROUP)],
        sems,
    )
    waits[0].wait()
    write_send_table(*moves, place_ref[0], slots_v, table_ref)
    for wait in waits[1:5]:
        wait.wait()

    def arrive(tile, tiles):
        if ROWS * tile % GROUP == 0:
            waits[5 + ROWS * tile // GROUP].wait()

    write_weights(
        place_ref, wav_count, which, coupling_v, counts_v, good_v,
        lambda e, tile: ivar_v[e, pl.ds(pl.multiple_of(which * half + ROWS * tile, ROWS), ROWS), :],
        lambda e, group: bits_v[e, pl.ds(pl.multiple_of(which * (half // BITS) + words * group, words), words), :],
        sums_ref, weight_ref, arrive,
    )
    for wait in waits[5 + half // GROUP :]:
        wait.wait()


def sent_weights(moves, wav_count, place, slots, coupling, counts, good, bits, ivar):
    expos, width, fibres = ivar.shape
    half = width // 2
    fib_count, pack, per, _ = moves
    inputs = (slots, coupling, counts, good, bits, ivar)
    return pl.pallas_call(
        functools.partial(sent_kernel, moves, wav_count),
        in_specs=[in_smem] + [in_hbm] * 6,
        out_specs=[in_vmem] * 9,
        out_shape=[
            shaped((2, half, fibres)),
            shaped((expos, half, fibres)),
            shaped((fib_count * pack * per, pack * fibres), BF16),
        ]
        + [shaped(x.shape, x.dtype) for x in inputs],
        scratch_shapes=[pltpu.SemaphoreType.DMA((5 + width // GROUP,))],
        compiler_params=params(),
        cost_estimate=cost(20 * ivar.size, 6 * ivar.size),
        name="sent_weights",
    )(place, *held_in_hbm(*inputs))


def lay_out(source_ref, target_ref, pieces, pitch):
    expos, _, fibres = source_ref.shape
    for h in range(fibres // LANES):
        for e in range(expos):
            for first, length, at in pieces:
                target_ref[pl.ds((h * expos + e) * pitch + at, length), :] = source_ref[
                    e, pl.ds(first, length), pl.ds(h * LANES, LANES)
                ]


def kept_kernel(
    wav_count, place_ref, coupling_ref, counts_ref, good_ref, pixels_ref, ivar_ref, bits_ref,
    sums_ref, weight_ref, up_ref, down_ref, ivar_s, pixel_s,
):
    expos, width, fibres = ivar_ref.shape
    half = width // 2
    streams = expos * fibres // LANES
    count = -(-HALO // ROWS) * ROWS
    pitch = odd(2 * count)
    which = place_ref[2]
    words = GROUP // BITS
    edges = [(0, count, 0), (width - count, count, count)]
    lay_out(ivar_ref, ivar_s, edges, pitch)
    lay_out(pixels_ref, pixel_s, edges, pitch)
    coupling = stream_coupling(coupling_ref, expos)
    back = 1.0 / coupling
    zero = jnp.zeros((streams, LANES), F32)
    states = [(zero, zero + 1.0, zero), (zero, zero + 1.0, zero)]

    def eliminate(tile, tiles):
        for i in range(HALO * tile // tiles, HALO * (tile + 1) // tiles):
            for side, row in enumerate((2 * count - HALO + i, HALO - 1 - i)):
                at = pl.ds(row, streams, stride=pitch)
                states[side] = advance(states[side], ivar_s[at, :], pixel_s[at, :], back)
                if i % 24 == 23:
                    states[side] = rescaled(states[side])

    write_weights(
        place_ref, wav_count, which, coupling_ref, counts_ref, good_ref,
        lambda e, tile: ivar_ref[e, pl.ds(pl.multiple_of(which * half + ROWS * tile, ROWS), ROWS), :],
        lambda e, group: bits_ref[e, pl.ds(pl.multiple_of(which * (half // BITS) + words * group, words), words), :],
        sums_ref, weight_ref, eliminate,
    )
    for (n, d, b), out_ref in zip(states, (up_ref, down_ref)):
        scale = 1.0 / (d + n)
        out_ref[0] = coupling * (n * scale)
        out_ref[1] = b * scale


def kept_weights(wav_count, place, coupling, counts, good, pixels, ivar, bits):
    expos, width, fibres = ivar.shape
    half = width // 2
    streams = expos * fibres // LANES
    count = -(-HALO // ROWS) * ROWS
    edge = shaped((2, streams, LANES))
    edge_scratch = pltpu.VMEM((streams * odd(2 * count), LANES), F32)
    return pl.pallas_call(
        functools.partial(kept_kernel, wav_count),
        in_specs=[in_smem] + [in_vmem] * 6,
        out_specs=[in_vmem] * 4,
        out_shape=[shaped((2, half, fibres)), shaped((expos, half, fibres)), edge, edge],
        scratch_shapes=[edge_scratch, edge_scratch],
        compiler_params=params(),
        cost_estimate=cost(20 * ivar.size, 6 * ivar.size),
        name="kept_weights",
    )(place, coupling, counts, good, pixels, ivar, bits)


def layout_kernel(arrived_ref, pixels_ref, ivar_ref, pixel_out, ivar_out):
    width = ivar_ref.shape[1]
    lay_out(ivar_ref, ivar_out, [(0, width, 0)], odd(width))
    lay_out(pixels_ref, pixel_out, [(0, width, 0)], odd(width))


def stream_layout(arrived, pixels, ivar):
    expos, width, fibres = ivar.shape
    streams = expos * fibres // LANES
    laid = shaped((streams * odd(width), LANES))
    return pl.pallas_call(
        layout_kernel,
        in_specs=[in_vmem] * 3,
        out_specs=[in_vmem] * 2,
        out_shape=[laid, laid],
        compiler_params=params(),
        cost_estimate=cost(0, 16 * ivar.size),
        name="stream_layout",
    )(arrived, pixels, ivar)


def solve_kernel(
    wav_count, place_ref, coupling_ref, left_ref, right_ref, pixel_ref, ivar_ref, weight_ref,
    theirs_ref, solved_s, lead_s, rest_s,
):
    streams = left_ref.shape[1]
    expos, half, fibres = weight_ref.shape
    width = 2 * half
    pitch = odd(width)
    middle = half
    coupling = stream_coupling(coupling_ref, expos)
    back = 1.0 / coupling

    def row_at(i):
        return pl.ds(i, streams, stride=pitch)

    def begin(edge_ref, outermost):
        n = jnp.where(place_ref[1] == outermost, 0.0, edge_ref[0]) * back
        return (n, 1.0 - n, jnp.where(place_ref[1] == outermost, 0.0, edge_ref[1]))

    def keep(side, i, state):
        n, d, b = state
        inverse = inverse_of(d + n)
        lead_s[side, i] = d * inverse
        rest_s[side, i] = b * inverse

    unrolled = divisor_of(middle, 24)

    def eliminate(it, states):
        states = list(states)
        for k in range(unrolled):
            i = it * unrolled + k
            for side, row in enumerate((i, width - 1 - i)):
                keep(side, i, states[side])
                states[side] = advance(states[side], ivar_ref[row_at(row), :], pixel_ref[row_at(row), :], back)
        return tuple(rescaled(state) for state in states)

    states = lax.fori_loop(0, middle // unrolled, eliminate, (begin(left_ref, 0), begin(right_ref, wav_count - 1)))
    for side in range(2):
        keep(side, middle, states[side])
    lead, rest = lead_s[0, middle], rest_s[0, middle]
    lead_r, rest_r = lead_s[1, middle], rest_s[1, middle]
    left = (rest + lead * rest_r) / (1.0 - lead * lead_r)
    right = rest_r + lead_r * left
    several = divisor_of(middle, 48)

    def after_both(near, far):
        return far[0] * near[0], far[1] + far[0] * near[1]

    def step(factors, value):
        return factors[1] + factors[0] * value

    def substitute(it, values):
        values = list(values)
        for k in range(0, several, 4):
            for side in range(2):
                rows = [middle - 1 - (it * several + k + m) for m in range(4)]
                one, two, three, four = [(lead_s[side, i], rest_s[side, i]) for i in rows]
                first_two = after_both(one, two)
                all_four = after_both(first_two, after_both(three, four))
                value = values[side]
                third = step(first_two, value)
                solved = [value, step(one, value), third, step(three, third)]
                values[side] = step(all_four, value)
                for i, x in zip(rows, solved):
                    solved_s[row_at(i if side == 0 else width - 1 - i), :] = x
        return tuple(values)

    lax.fori_loop(0, middle // several, substitute, (left, right))

    add_up(theirs_ref, weight_ref, solved_s, coupling_ref, 1 - place_ref[2])


def add_up(out_ref, weight_ref, solved_ref, coupling_ref, which):
    expos, half, fibres = weight_ref.shape
    pitch = odd(2 * half)
    start = which * half
    back = 1.0 / coupling_ref[...]
    unrolled = divisor_of(half // ROWS, 5)

    def body(g, carry):
        for k in range(unrolled):
            row = pl.multiple_of((g * unrolled + k) * ROWS, ROWS)
            for h in range(fibres // LANES):
                total = None
                for e in range(expos):
                    at = pl.ds((h * expos + e) * pitch + start + row, ROWS)
                    term = weight_ref[e, pl.ds(row, ROWS), pl.ds(h * LANES, LANES)] * solved_ref[at, :]
                    total = term if e == 0 else total + term
                out_ref[0, pl.ds(row, ROWS), pl.ds(h * LANES, LANES)] = total * back[:, h * LANES : (h + 1) * LANES]
        return carry

    lax.fori_loop(0, half // ROWS // unrolled, body, 0)


def flux_sums(wav_count, place, coupling, left, right, pixels, ivar, weight):
    expos, half, fibres = weight.shape
    streams = left.shape[1]
    factor_scratch = pltpu.VMEM((2, half + 1, streams, LANES), F32)
    return pl.pallas_call(
        functools.partial(solve_kernel, wav_count),
        in_specs=[in_smem] + [in_vmem] * 6,
        out_specs=[in_vmem, in_vmem],
        out_shape=[shaped((1, half, fibres)), shaped(pixels.shape)],
        scratch_shapes=[factor_scratch, factor_scratch],
        compiler_params=params(),
        cost_estimate=cost(0, 0),
        name="flux_sums",
    )(place, coupling, left, right, pixels, ivar, weight)


def kept_flux_kernel(place_ref, coupling_ref, solved_ref, weight_ref, out_ref):
    add_up(out_ref, weight_ref, solved_ref, coupling_ref, place_ref[2])


def kept_flux(place, coupling, solved, weight):
    expos, half, fibres = weight.shape
    return pl.pallas_call(
        kept_flux_kernel,
        in_specs=[in_smem] + [in_vmem] * 3,
        out_specs=in_vmem,
        out_shape=shaped((1, half, fibres)),
        compiler_params=params(),
        cost_estimate=cost(2 * weight.size, 8 * weight.size),
        name="kept_flux",
    )(place, coupling, solved, weight)


def split_dot(x, table, dims):
    top = x.astype(BF16)
    low = (x - top.astype(F32)).astype(BF16)
    both = lax.dot_general(jnp.concatenate([top, low], 0), table, dims, preferred_element_type=F32)
    return both[: x.shape[0]] + both[x.shape[0] :]


def sort_kernel(pack, scaled, theirs_ref, mine_ref, table_ref, *refs):
    values, rows, _ = mine_ref.shape
    part = rows // pack
    totals = [mine_ref[v] + theirs_ref[v] for v in range(values)]
    if scaled:
        scale_ref, _, *out_refs = refs
        totals = [t * scale_ref[...] for t in totals]
    else:
        *out_refs, scale_ref = refs
        scale = 1.0 / jnp.maximum(totals[0], 1.0)
        scale_ref[...] = scale
        totals[1] = totals[1] * scale
    x = jnp.concatenate(
        [jnp.concatenate([t[h * part : (h + 1) * part] for h in range(pack)], 1) for t in totals], 0
    )
    moved = split_dot(x, table_ref[...], NT)
    lanes = moved.shape[1] // len(out_refs)
    for d, out_ref in enumerate(out_refs):
        for v in range(values):
            out_ref[v] = moved[v * part : (v + 1) * part, d * lanes : (d + 1) * lanes]


def sort_fibres(theirs, mine, table, pack, pieces, scale=None, ahead=None):
    values, rows, fibres = mine.shape
    lanes = table.shape[0] // pieces
    scaled = scale is not None
    outs = [shaped((values, rows // pack, lanes))] * pieces + ([] if scaled else [shaped((rows, fibres))])
    args = (theirs, mine, table) + ((scale, ahead) if scaled else ())
    return pl.pallas_call(
        functools.partial(sort_kernel, pack, scaled),
        in_specs=[in_vmem] * len(args),
        out_specs=[in_vmem] * len(outs),
        out_shape=outs,
        compiler_params=params(),
        cost_estimate=cost(0, 0),
        name="sort_flux" if scaled else "sort_weights",
    )(*args)


def exchange(pieces, fib_count):
    if len(pieces) == 1:
        return [lax.all_to_all(pieces[0], "fib", split_axis=2, concat_axis=2, tiled=True)]
    swapped = [lax.ppermute(pieces[d], "fib", [(i, i ^ d) for i in range(fib_count)]) for d in range(1, fib_count)]
    return [pieces[0]] + swapped


def landed(refs, table):
    values, part, _ = refs[0].shape
    x = jnp.concatenate(
        [jnp.concatenate([ref[v] for ref in refs], 1) if len(refs) > 1 else refs[0][v] for v in range(values)], 0
    )
    moved = split_dot(x, table, NT)
    return [moved[v * part : (v + 1) * part] for v in range(values)]


def columns_of(table, which, pieces):
    lanes = table.shape[1] // pieces
    return jnp.concatenate([table[:, d * lanes : (d + 1) * lanes] for d in which], 1)


def early_kernel(moves, which, pieces, place_ref, slots_ref, *refs):
    *piece_refs, table_ref, sums_ref = refs
    write_recv_table(*moves, place_ref[0], slots_ref, table_ref)
    for v, moved in enumerate(landed(piece_refs, columns_of(table_ref[...], which, pieces))):
        sums_ref[v] = moved


def place_early(moves, which, place, slots, weight_pieces, fibres):
    fib_count, pack, per, _ = moves
    early = [weight_pieces[d] for d in which]
    values, part, _ = early[0].shape
    return pl.pallas_call(
        functools.partial(early_kernel, moves, which, len(weight_pieces)),
        in_specs=[in_smem] + [in_vmem] * (1 + len(early)),
        out_specs=[in_vmem] * 2,
        out_shape=[
            shaped((pack * fibres, fib_count * pack * per), BF16),
            shaped((values, part, pack * fibres)),
        ],
        compiler_params=params(),
        cost_estimate=cost(0, 0),
        name="place_early",
    )(place, slots, *early)


def weights_end_kernel(pack, total, late, pieces, place_ref, table_ref, sums_ref, *refs):
    *late_refs, ivar_ref, res_ref = refs
    weight, band = sums_ref[0], sums_ref[1]
    if late:
        more_weight, more_band = landed(late_refs, columns_of(table_ref[...], late, pieces))
        weight, band = weight + more_weight, band + more_band
    rows, fibres = ivar_ref.shape
    part = rows // pack
    start = (place_ref[1] * 2 + place_ref[2]) * rows
    for h in range(pack):
        at = slice(h * part, (h + 1) * part)
        cut = slice(h * fibres, (h + 1) * fibres)
        row = start + h * part + lax.broadcasted_iota(jnp.int32, (part, 1), 0)
        w, b = weight[:, cut], band[:, cut]
        before = jnp.where(row == 0, 0.0, b)
        after = jnp.where(row == total - 1, 0.0, b)
        ivar_ref[at, :] = w
        res_ref[0, at, :] = before
        res_ref[1, at, :] = jnp.minimum(w, 1.0) - before - after
        res_ref[2, at, :] = after


def end_weights(place, table, sums, late, weight_pieces, pack, fibres, total):
    rows = sums.shape[1] * pack
    late_pieces = [weight_pieces[d] for d in late]
    return pl.pallas_call(
        functools.partial(weights_end_kernel, pack, total, late, len(weight_pieces)),
        in_specs=[in_smem] + [in_vmem] * (2 + len(late)),
        out_specs=[in_vmem] * 2,
        out_shape=[shaped((rows, fibres)), shaped((3, rows, fibres))],
        compiler_params=params(),
        cost_estimate=cost(0, 0),
        name="end_weights",
    )(place, table, sums, *late_pieces)


def flux_end_kernel(pack, order, table_ref, *refs):
    *piece_refs, flux_ref = refs
    (flux,) = landed([piece_refs[order.index(d)] for d in range(len(order))], table_ref[...])
    rows, fibres = flux_ref.shape
    part = rows // pack
    for h in range(pack):
        flux_ref[h * part : (h + 1) * part, :] = flux[:, h * fibres : (h + 1) * fibres]


def end_flux(table, pieces, pack, fibres):
    rows = pieces[0].shape[1] * pack
    order = sorted(range(len(pieces)), key=lambda d: (d > 0, abs(2 * d - len(pieces))))
    return pl.pallas_call(
        functools.partial(flux_end_kernel, pack, order),
        in_specs=[in_vmem] * (1 + len(pieces)),
        out_specs=in_vmem,
        out_shape=shaped((rows, fibres)),
        compiler_params=params(),
        cost_estimate=cost(2 * rows * table.size, 2 * rows * fibres * 4),
        name="end_flux",
    )(table, *(pieces[d] for d in order))


def after(value, done):
    return lax.optimization_barrier((value, done))[0]


def per_device(pixels, pixel_ivar, clip_bits, coupling, counts, good_flags, owner_slot):
    expos, width, fibres = pixels.shape
    fib_count, wav_count = lax.axis_size("fib"), lax.axis_size("wav")
    total = width * wav_count
    per = fibres // fib_count
    rows = width // 2
    pack = max(1, LANES // per)
    while pack > 1 and rows % (pack * ROWS):
        pack //= 2
    rel = pack * per == LANES and fib_count & (fib_count - 1) == 0
    pieces = fib_count if rel else 1
    place = jnp.stack([lax.axis_index(axis) for axis in ("fib", "wav", "exp")]).astype(jnp.int32)
    coupling, counts, slots = coupling[None], counts[None], owner_slot[None]
    swap = [(0, 1), (1, 0)]
    moves = (fib_count, pack, per, rel)

    theirs, weight_t, send_table, slots, coupling, counts, good, bits, ivar = sent_weights(
        moves, wav_count, place, slots, coupling, counts, good_flags, clip_bits, pixel_ivar
    )
    arriving = lax.ppermute(theirs, "exp", swap)
    mine, weight_m, up, down = kept_weights(
        wav_count, place, coupling, counts, good, pixels, ivar, bits
    )
    upward = [(i, (i + 1) % wav_count) for i in range(wav_count)]
    left = lax.ppermute(up, "wav", upward)
    right = lax.ppermute(down, "wav", [(j, i) for i, j in upward])
    *sorted_pieces, scale = sort_fibres(arriving, mine, send_table, pack, pieces)
    weight_pieces = exchange(sorted_pieces, fib_count)

    pixel_s, ivar_s = stream_layout(left[0] + right[0], pixels, ivar)
    theirs, solved = flux_sums(wav_count, place, coupling, left, right, pixel_s, ivar_s, weight_t)
    early = [0, fib_count // 2] if rel else [0]
    late = [d for d in reversed(range(pieces)) if d not in early]
    ahead = weight_pieces[early[-1]][0, :ROWS, :] * 0.5
    arriving = lax.ppermute(theirs, "exp", swap)
    mine = kept_flux(after(place, theirs), coupling, solved, weight_m)
    sorted_pieces = sort_fibres(arriving, mine, send_table, pack, pieces, scale, ahead)
    flux_pieces = exchange(sorted_pieces, fib_count)
    recv_table, placed = place_early(moves, early, after(place, sorted_pieces[0]), slots, weight_pieces, fibres)
    ivar, res = end_weights(place, recv_table, placed, late, weight_pieces, pack, fibres, total)
    flux = end_flux(recv_table, flux_pieces, pack, fibres)
    return (flux, ivar, res)


def solution(mesh):
    return jax.shard_map(
        per_device,
        mesh=mesh,
        in_specs=(
            P("exp", "wav", "fib"),
            P("exp", "wav", "fib"),
            P("exp", "wav", "fib"),
            P("fib"),
            P("fib"),
            P("exp", "fib"),
            P(),
        ),
        out_specs=(
            P(("wav", "exp"), "fib"),
            P(("wav", "exp"), "fib"),
            P(None, ("wav", "exp"), "fib"),
        ),
        check_vma=False,
    )
```

```python
import functools

import jax
import jax.numpy as jnp
from jax import lax
from jax.experimental import pallas as pl
from jax.experimental.pallas import tpu as pltpu
from jax.sharding import PartitionSpec as P

HALO = 50
BITS = 15
LANES = 128
ROWS = 8
GROUP = 120
VMEM_BYTES = 32 * 1024 * 1024
F32 = jnp.float32
BF16 = jnp.bfloat16
NT = (((1,), (1,)), ((), ()))

in_vmem = pl.BlockSpec(memory_space=pltpu.VMEM)
in_smem = pl.BlockSpec(memory_space=pltpu.SMEM)
in_hbm = pl.BlockSpec(memory_space=pltpu.HBM)


def params():
    return pltpu.CompilerParams(vmem_limit_bytes=VMEM_BYTES)


def cost(flops, moved):
    return pl.CostEstimate(flops=int(flops), bytes_accessed=int(moved), transcendentals=0)


def held_in_hbm(*arrays):
    return [pltpu.with_memory_space_constraint(array, pltpu.HBM) for array in arrays]


def shaped(shape, dtype=F32):
    return jax.ShapeDtypeStruct(shape, dtype)


def usable_rows(place_ref, counts_ref, good_ref):
    count = good_ref.shape[0]
    return [
        good_ref[e : e + 1, :].astype(F32)
        * jnp.where(place_ref[2] * count + e < counts_ref[...], 1.0, 0.0)
        for e in range(count)
    ]


def tile_bits(tile):
    first, last = (ROWS * tile) // BITS, (ROWS * tile + ROWS - 1) // BITS
    split = BITS * last - ROWS * tile
    row = lax.broadcasted_iota(jnp.int32, (ROWS, 1), 0)
    word = jnp.where(row >= split, last, first)
    return first, last, split, jnp.left_shift(1, ROWS * tile + row - BITS * word)


def tile_words(words, tile):
    first, last, split, mask = tile_bits(tile)
    picked = words[first : first + 1, :]
    if last != first:
        row = lax.broadcasted_iota(jnp.int32, (ROWS, 1), 0)
        picked = jnp.where(row >= split, words[last : last + 1, :], picked)
    return (picked & mask) != 0


def in_flight(pairs, sems, at=0):
    copies = [pltpu.make_async_copy(source, target, sems.at[at + i]) for i, (source, target) in enumerate(pairs)]
    for copy in copies:
        copy.start()
    return copies


def inverse_of(x):
    guess = pl.reciprocal(x, approx=True)
    return guess * (2.0 - x * guess)


def advance(state, ivar, pixel, back_coupling):
    n, d, b = state
    ratio = ivar * back_coupling
    next_d = d + n
    return (n * (1.0 + ratio) + ratio * d, next_d, b + (ivar * pixel) * next_d)


def rescaled(state):
    scale = inverse_of(state[1])
    return tuple(part * scale for part in state)


def odd(rows):
    return rows + 1 - rows % 2


def divisor_of(size, most):
    return max(k for k in range(1, most + 1) if size % k == 0)


def owners(slots_ref, fib_count, fibres):
    rows = [slots_ref[:, s * fibres : (s + 1) * fibres].astype(F32) for s in range(fib_count)]
    sources = -(-fib_count // ROWS) * ROWS
    if sources > fib_count:
        rows.append(jnp.full((sources - fib_count, fibres), -1.0, F32))
    slots = jnp.concatenate(rows, 0)
    owner = jnp.floor((slots + 0.5) * (1.0 / fibres))
    return owner, slots - owner * fibres


def earlier_fibres(fibres):
    row = lax.broadcasted_iota(jnp.int32, (fibres, fibres), 0)
    col = lax.broadcasted_iota(jnp.int32, (fibres, fibres), 1)
    return (row < col).astype(F32).astype(BF16)


def write_send_table(fib_count, pack, per, rel, me, slots_ref, table_ref):
    fibres = table_ref.shape[1] // pack
    lanes = pack * per
    owner, _ = owners(slots_ref, fib_count, fibres)
    source = lax.broadcasted_iota(jnp.int32, owner.shape, 0)
    my_owner = jnp.sum(jnp.where(source == me, owner, 0.0), axis=0, keepdims=True).astype(jnp.int32)
    to_owner = (source == my_owner).astype(F32)
    counted = jnp.dot(to_owner.astype(BF16), earlier_fibres(fibres), preferred_element_type=F32)
    rank = jnp.sum(to_owner * counted, axis=0, keepdims=True).astype(jnp.int32)
    target = my_owner ^ me if rel else my_owner
    base = target * lanes + rank
    place_of = jnp.concatenate([base + h * per for h in range(pack)], 1)
    row = lax.broadcasted_iota(jnp.int32, table_ref.shape, 0)
    table_ref[...] = (row == place_of).astype(F32).astype(BF16)


def write_recv_table(fib_count, pack, per, rel, me, slots_ref, table_ref):
    fibres = table_ref.shape[0] // pack
    lanes = pack * per
    total_lanes = fib_count * lanes
    owner, column = owners(slots_ref, fib_count, fibres)
    source = lax.broadcasted_iota(jnp.int32, owner.shape, 0)
    mine = (owner == me.astype(F32)).astype(F32)
    rank_in = jnp.dot(mine.astype(BF16), earlier_fibres(fibres), preferred_element_type=F32).astype(jnp.int32)
    order = source ^ me if rel else source
    arrival = jnp.where(mine > 0.0, order * lanes + rank_in, -total_lanes)
    tall = lax.broadcasted_iota(jnp.int32, (total_lanes, fibres), 0)
    landing = jnp.zeros((ROWS, total_lanes), F32)
    for s in range(fib_count):
        hit = tall == arrival[s : s + 1, :]
        for h in range(1, pack):
            hit = hit | (tall == arrival[s : s + 1, :] + h * per)
        values = jnp.broadcast_to(column[s : s + 1, :], (ROWS, fibres)).astype(BF16)
        landing = landing + lax.dot_general(
            values, hit.astype(F32).astype(BF16), NT, preferred_element_type=F32
        )
    lane = lax.broadcasted_iota(jnp.int32, (1, total_lanes), 1)
    landing = landing[0:1, :].astype(jnp.int32)
    for h in range(1, pack):
        inside = (lane % lanes >= h * per) & (lane % lanes < (h + 1) * per)
        landing = jnp.where(inside, landing + h * fibres, landing)
    row = lax.broadcasted_iota(jnp.int32, table_ref.shape, 0)
    table_ref[...] = (row == landing).astype(F32).astype(BF16)


def stream_coupling(coupling_ref, expos):
    coupling = coupling_ref[...]
    blocks = coupling.shape[1] // LANES
    return jnp.concatenate(
        [jnp.broadcast_to(coupling[:, h * LANES : (h + 1) * LANES], (expos, LANES)) for h in range(blocks)], 0
    )


def weight_tile(coupling, usable, words, ivars, within, scale_row):
    links = scale_row * coupling
    weights = []
    weight_sum = band_sum = None
    for e, ivar in enumerate(ivars):
        weight = jnp.where(tile_words(words[e], within), ivar * usable[e], 0.0)
        band = weight * inverse_of(ivar + links)
        weights.append(weight)
        weight_sum = weight if e == 0 else weight_sum + weight
        band_sum = band if e == 0 else band_sum + band
    return weights, weight_sum, band_sum * coupling


def write_weights(place_ref, wav_count, which, coupling_v, counts_v, good_v, ivar_of, words_of, sums_ref, weight_ref, beside):
    expos, half, _ = weight_ref.shape
    coupling = coupling_v[...]
    usable = usable_rows(place_ref, counts_v, good_v)
    start = place_ref[1] * (2 * half) + which * half
    tiles = half // ROWS
    tiles_in_group = GROUP // ROWS
    for tile in range(tiles):
        beside(tile, tiles)
        group, within = divmod(tile, tiles_in_group)
        scale_row = 4.0
        if tile in (0, tiles - 1):
            row = start + ROWS * tile + lax.broadcasted_iota(jnp.int32, (ROWS, 1), 0)
            scale_row = jnp.where((row == 0) | (row == wav_count * 2 * half - 1), 2.0, 4.0)
        at = slice(ROWS * tile, ROWS * (tile + 1))
        weights, weight_sum, band_sum = weight_tile(
            coupling,
            usable,
            [words_of(e, group) for e in range(expos)],
            [ivar_of(e, tile) for e in range(expos)],
            within,
            scale_row,
        )
        for e in range(expos):
            weight_ref[e, at, :] = weights[e]
        sums_ref[0, at, :] = weight_sum
        sums_ref[1, at, :] = band_sum


def sent_kernel(
    moves, wav_count, place_ref, slots_ref, coupling_ref, counts_ref, good_ref, bits_ref, ivar_ref,
    sums_ref, weight_ref, table_ref, slots_v, coupling_v, counts_v, good_v, bits_v, ivar_v, sems,
):
    expos, width, _ = ivar_ref.shape
    half = width // 2
    which = 1 - place_ref[2]
    words = GROUP // BITS

    def part(source, target, first):
        at = pl.ds(pl.multiple_of(first, ROWS), GROUP)
        return source.at[:, at, :], target.at[:, at, :]

    waits = in_flight(
        [
            (slots_ref, slots_v),
            (coupling_ref, coupling_v),
            (counts_ref, counts_v),
            (good_ref, good_v),
            (bits_ref, bits_v),
        ]
        + [part(ivar_ref, ivar_v, which * half + g) for g in range(0, half, GROUP)]
        + [part(ivar_ref, ivar_v, (1 - which) * half + g) for g in range(0, half, GROUP)],
        sems,
    )
    waits[0].wait()
    write_send_table(*moves, place_ref[0], slots_v, table_ref)
    for wait in waits[1:5]:
        wait.wait()

    def arrive(tile, tiles):
        if ROWS * tile % GROUP == 0:
            waits[5 + ROWS * tile // GROUP].wait()

    write_weights(
        place_ref, wav_count, which, coupling_v, counts_v, good_v,
        lambda e, tile: ivar_v[e, pl.ds(pl.multiple_of(which * half + ROWS * tile, ROWS), ROWS), :],
        lambda e, group: bits_v[e, pl.ds(pl.multiple_of(which * (half // BITS) + words * group, words), words), :],
        sums_ref, weight_ref, arrive,
    )
    for wait in waits[5 + half // GROUP :]:
        wait.wait()


def sent_weights(moves, wav_count, place, slots, coupling, counts, good, bits, ivar):
    expos, width, fibres = ivar.shape
    half = width // 2
    fib_count, pack, per, _ = moves
    inputs = (slots, coupling, counts, good, bits, ivar)
    return pl.pallas_call(
        functools.partial(sent_kernel, moves, wav_count),
        in_specs=[in_smem] + [in_hbm] * 6,
        out_specs=[in_vmem] * 9,
        out_shape=[
            shaped((2, half, fibres)),
            shaped((expos, half, fibres)),
            shaped((fib_count * pack * per, pack * fibres), BF16),
        ]
        + [shaped(x.shape, x.dtype) for x in inputs],
        scratch_shapes=[pltpu.SemaphoreType.DMA((5 + width // GROUP,))],
        compiler_params=params(),
        cost_estimate=cost(20 * ivar.size, 6 * ivar.size),
        name="sent_weights",
    )(place, *held_in_hbm(*inputs))


def lay_out(source_ref, target_ref, pieces, pitch):
    expos, _, fibres = source_ref.shape
    for h in range(fibres // LANES):
        for e in range(expos):
            for first, length, at in pieces:
                target_ref[pl.ds((h * expos + e) * pitch + at, length), :] = source_ref[
                    e, pl.ds(first, length), pl.ds(h * LANES, LANES)
                ]


def kept_kernel(
    wav_count, place_ref, coupling_ref, counts_ref, good_ref, pixels_ref, ivar_ref, bits_ref,
    sums_ref, weight_ref, up_ref, down_ref, ivar_s, pixel_s,
):
    expos, width, fibres = ivar_ref.shape
    half = width // 2
    streams = expos * fibres // LANES
    count = -(-HALO // ROWS) * ROWS
    pitch = odd(2 * count)
    which = place_ref[2]
    words = GROUP // BITS
    edges = [(0, count, 0), (width - count, count, count)]
    lay_out(ivar_ref, ivar_s, edges, pitch)
    lay_out(pixels_ref, pixel_s, edges, pitch)
    coupling = stream_coupling(coupling_ref, expos)
    back = 1.0 / coupling
    zero = jnp.zeros((streams, LANES), F32)
    states = [(zero, zero + 1.0, zero), (zero, zero + 1.0, zero)]

    def eliminate(tile, tiles):
        for i in range(HALO * tile // tiles, HALO * (tile + 1) // tiles):
            for side, row in enumerate((2 * count - HALO + i, HALO - 1 - i)):
                at = pl.ds(row, streams, stride=pitch)
                states[side] = advance(states[side], ivar_s[at, :], pixel_s[at, :], back)
                if i % 24 == 23:
                    states[side] = rescaled(states[side])

    write_weights(
        place_ref, wav_count, which, coupling_ref, counts_ref, good_ref,
        lambda e, tile: ivar_ref[e, pl.ds(pl.multiple_of(which * half + ROWS * tile, ROWS), ROWS), :],
        lambda e, group: bits_ref[e, pl.ds(pl.multiple_of(which * (half // BITS) + words * group, words), words), :],
        sums_ref, weight_ref, eliminate,
    )
    for (n, d, b), out_ref in zip(states, (up_ref, down_ref)):
        scale = 1.0 / (d + n)
        out_ref[0] = coupling * (n * scale)
        out_ref[1] = b * scale


def kept_weights(wav_count, place, coupling, counts, good, pixels, ivar, bits):
    expos, width, fibres = ivar.shape
    half = width // 2
    streams = expos * fibres // LANES
    count = -(-HALO // ROWS) * ROWS
    edge = shaped((2, streams, LANES))
    edge_scratch = pltpu.VMEM((streams * odd(2 * count), LANES), F32)
    return pl.pallas_call(
        functools.partial(kept_kernel, wav_count),
        in_specs=[in_smem] + [in_vmem] * 6,
        out_specs=[in_vmem] * 4,
        out_shape=[shaped((2, half, fibres)), shaped((expos, half, fibres)), edge, edge],
        scratch_shapes=[edge_scratch, edge_scratch],
        compiler_params=params(),
        cost_estimate=cost(20 * ivar.size, 6 * ivar.size),
        name="kept_weights",
    )(place, coupling, counts, good, pixels, ivar, bits)


def layout_kernel(arrived_ref, pixels_ref, ivar_ref, pixel_out, ivar_out):
    width = ivar_ref.shape[1]
    lay_out(ivar_ref, ivar_out, [(0, width, 0)], odd(width))
    lay_out(pixels_ref, pixel_out, [(0, width, 0)], odd(width))


def stream_layout(arrived, pixels, ivar):
    expos, width, fibres = ivar.shape
    streams = expos * fibres // LANES
    laid = shaped((streams * odd(width), LANES))
    return pl.pallas_call(
        layout_kernel,
        in_specs=[in_vmem] * 3,
        out_specs=[in_vmem] * 2,
        out_shape=[laid, laid],
        compiler_params=params(),
        cost_estimate=cost(0, 16 * ivar.size),
        name="stream_layout",
    )(arrived, pixels, ivar)


def solve_kernel(
    wav_count, place_ref, coupling_ref, left_ref, right_ref, pixel_ref, ivar_ref, weight_ref,
    theirs_ref, solved_s, lead_s, rest_s,
):
    streams = left_ref.shape[1]
    expos, half, fibres = weight_ref.shape
    width = 2 * half
    pitch = odd(width)
    middle = half
    coupling = stream_coupling(coupling_ref, expos)
    back = 1.0 / coupling

    def row_at(i):
        return pl.ds(i, streams, stride=pitch)

    def begin(edge_ref, outermost):
        n = jnp.where(place_ref[1] == outermost, 0.0, edge_ref[0]) * back
        return (n, 1.0 - n, jnp.where(place_ref[1] == outermost, 0.0, edge_ref[1]))

    def keep(side, i, state):
        n, d, b = state
        inverse = inverse_of(d + n)
        lead_s[side, i] = d * inverse
        rest_s[side, i] = b * inverse

    unrolled = divisor_of(middle, 24)

    def eliminate(it, states):
        states = list(states)
        for k in range(unrolled):
            i = it * unrolled + k
            for side, row in enumerate((i, width - 1 - i)):
                keep(side, i, states[side])
                states[side] = advance(states[side], ivar_ref[row_at(row), :], pixel_ref[row_at(row), :], back)
        return tuple(rescaled(state) for state in states)

    states = lax.fori_loop(0, middle // unrolled, eliminate, (begin(left_ref, 0), begin(right_ref, wav_count - 1)))
    for side in range(2):
        keep(side, middle, states[side])
    lead, rest = lead_s[0, middle], rest_s[0, middle]
    lead_r, rest_r = lead_s[1, middle], rest_s[1, middle]
    left = (rest + lead * rest_r) / (1.0 - lead * lead_r)
    right = rest_r + lead_r * left
    several = divisor_of(middle, 48)

    def after_both(near, far):
        return far[0] * near[0], far[1] + far[0] * near[1]

    def step(factors, value):
        return factors[1] + factors[0] * value

    def substitute(it, values):
        values = list(values)
        for k in range(0, several, 4):
            for side in range(2):
                rows = [middle - 1 - (it * several + k + m) for m in range(4)]
                one, two, three, four = [(lead_s[side, i], rest_s[side, i]) for i in rows]
                first_two = after_both(one, two)
                all_four = after_both(first_two, after_both(three, four))
                value = values[side]
                third = step(first_two, value)
                solved = [value, step(one, value), third, step(three, third)]
                values[side] = step(all_four, value)
                for i, x in zip(rows, solved):
                    solved_s[row_at(i if side == 0 else width - 1 - i), :] = x
        return tuple(values)

    lax.fori_loop(0, middle // several, substitute, (left, right))

    add_up(theirs_ref, weight_ref, solved_s, coupling_ref, 1 - place_ref[2])


def add_up(out_ref, weight_ref, solved_ref, coupling_ref, which):
    expos, half, fibres = weight_ref.shape
    pitch = odd(2 * half)
    start = which * half
    back = 1.0 / coupling_ref[...]
    unrolled = divisor_of(half // ROWS, 5)

    def body(g, carry):
        for k in range(unrolled):
            row = pl.multiple_of((g * unrolled + k) * ROWS, ROWS)
            for h in range(fibres // LANES):
                total = None
                for e in range(expos):
                    at = pl.ds((h * expos + e) * pitch + start + row, ROWS)
                    term = weight_ref[e, pl.ds(row, ROWS), pl.ds(h * LANES, LANES)] * solved_ref[at, :]
                    total = term if e == 0 else total + term
                out_ref[0, pl.ds(row, ROWS), pl.ds(h * LANES, LANES)] = total * back[:, h * LANES : (h + 1) * LANES]
        return carry

    lax.fori_loop(0, half // ROWS // unrolled, body, 0)


def flux_sums(wav_count, place, coupling, left, right, pixels, ivar, weight):
    expos, half, fibres = weight.shape
    streams = left.shape[1]
    factor_scratch = pltpu.VMEM((2, half + 1, streams, LANES), F32)
    return pl.pallas_call(
        functools.partial(solve_kernel, wav_count),
        in_specs=[in_smem] + [in_vmem] * 6,
        out_specs=[in_vmem, in_vmem],
        out_shape=[shaped((1, half, fibres)), shaped(pixels.shape)],
        scratch_shapes=[factor_scratch, factor_scratch],
        compiler_params=params(),
        cost_estimate=cost(0, 0),
        name="flux_sums",
    )(place, coupling, left, right, pixels, ivar, weight)


def kept_flux_kernel(place_ref, coupling_ref, solved_ref, weight_ref, out_ref):
    add_up(out_ref, weight_ref, solved_ref, coupling_ref, place_ref[2])


def kept_flux(place, coupling, solved, weight):
    expos, half, fibres = weight.shape
    return pl.pallas_call(
        kept_flux_kernel,
        in_specs=[in_smem] + [in_vmem] * 3,
        out_specs=in_vmem,
        out_shape=shaped((1, half, fibres)),
        compiler_params=params(),
        cost_estimate=cost(2 * weight.size, 8 * weight.size),
        name="kept_flux",
    )(place, coupling, solved, weight)


def split_dot(x, table, dims):
    top = x.astype(BF16)
    low = (x - top.astype(F32)).astype(BF16)
    both = lax.dot_general(jnp.concatenate([top, low], 0), table, dims, preferred_element_type=F32)
    return both[: x.shape[0]] + both[x.shape[0] :]


def sort_kernel(pack, scaled, theirs_ref, mine_ref, table_ref, *refs):
    values, rows, _ = mine_ref.shape
    part = rows // pack
    totals = [mine_ref[v] + theirs_ref[v] for v in range(values)]
    if scaled:
        scale_ref, _, *out_refs = refs
        totals = [t * scale_ref[...] for t in totals]
    else:
        *out_refs, scale_ref = refs
        scale = 1.0 / jnp.maximum(totals[0], 1.0)
        scale_ref[...] = scale
        totals[1] = totals[1] * scale
    x = jnp.concatenate(
        [jnp.concatenate([t[h * part : (h + 1) * part] for h in range(pack)], 1) for t in totals], 0
    )
    moved = split_dot(x, table_ref[...], NT)
    lanes = moved.shape[1] // len(out_refs)
    for d, out_ref in enumerate(out_refs):
        for v in range(values):
            out_ref[v] = moved[v * part : (v + 1) * part, d * lanes : (d + 1) * lanes]


def sort_fibres(theirs, mine, table, pack, pieces, scale=None, ahead=None):
    values, rows, fibres = mine.shape
    lanes = table.shape[0] // pieces
    scaled = scale is not None
    outs = [shaped((values, rows // pack, lanes))] * pieces + ([] if scaled else [shaped((rows, fibres))])
    args = (theirs, mine, table) + ((scale, ahead) if scaled else ())
    return pl.pallas_call(
        functools.partial(sort_kernel, pack, scaled),
        in_specs=[in_vmem] * len(args),
        out_specs=[in_vmem] * len(outs),
        out_shape=outs,
        compiler_params=params(),
        cost_estimate=cost(0, 0),
        name="sort_flux" if scaled else "sort_weights",
    )(*args)


def exchange(pieces, fib_count):
    if len(pieces) == 1:
        return [lax.all_to_all(pieces[0], "fib", split_axis=2, concat_axis=2, tiled=True)]
    swapped = [lax.ppermute(pieces[d], "fib", [(i, i ^ d) for i in range(fib_count)]) for d in range(1, fib_count)]
    return [pieces[0]] + swapped


def landed(refs, table):
    values, part, _ = refs[0].shape
    x = jnp.concatenate(
        [jnp.concatenate([ref[v] for ref in refs], 1) if len(refs) > 1 else refs[0][v] for v in range(values)], 0
    )
    moved = split_dot(x, table, NT)
    return [moved[v * part : (v + 1) * part] for v in range(values)]


def columns_of(table, which, pieces):
    lanes = table.shape[1] // pieces
    return jnp.concatenate([table[:, d * lanes : (d + 1) * lanes] for d in which], 1)


def early_kernel(moves, which, pieces, place_ref, slots_ref, *refs):
    *piece_refs, table_ref, sums_ref = refs
    write_recv_table(*moves, place_ref[0], slots_ref, table_ref)
    for v, moved in enumerate(landed(piece_refs, columns_of(table_ref[...], which, pieces))):
        sums_ref[v] = moved


def place_early(moves, which, place, slots, weight_pieces, fibres):
    fib_count, pack, per, _ = moves
    early = [weight_pieces[d] for d in which]
    values, part, _ = early[0].shape
    return pl.pallas_call(
        functools.partial(early_kernel, moves, which, len(weight_pieces)),
        in_specs=[in_smem] + [in_vmem] * (1 + len(early)),
        out_specs=[in_vmem] * 2,
        out_shape=[
            shaped((pack * fibres, fib_count * pack * per), BF16),
            shaped((values, part, pack * fibres)),
        ],
        compiler_params=params(),
        cost_estimate=cost(0, 0),
        name="place_early",
    )(place, slots, *early)


def weights_end_kernel(pack, total, late, pieces, place_ref, table_ref, sums_ref, *refs):
    *late_refs, ivar_ref, res_ref = refs
    weight, band = sums_ref[0], sums_ref[1]
    if late:
        more_weight, more_band = landed(late_refs, columns_of(table_ref[...], late, pieces))
        weight, band = weight + more_weight, band + more_band
    rows, fibres = ivar_ref.shape
    part = rows // pack
    start = (place_ref[1] * 2 + place_ref[2]) * rows
    for h in range(pack):
        at = slice(h * part, (h + 1) * part)
        cut = slice(h * fibres, (h + 1) * fibres)
        row = start + h * part + lax.broadcasted_iota(jnp.int32, (part, 1), 0)
        w, b = weight[:, cut], band[:, cut]
        before = jnp.where(row == 0, 0.0, b)
        after = jnp.where(row == total - 1, 0.0, b)
        ivar_ref[at, :] = w
        res_ref[0, at, :] = before
        res_ref[1, at, :] = jnp.minimum(w, 1.0) - before - after
        res_ref[2, at, :] = after


def end_weights(place, table, sums, late, weight_pieces, pack, fibres, total):
    rows = sums.shape[1] * pack
    late_pieces = [weight_pieces[d] for d in late]
    return pl.pallas_call(
        functools.partial(weights_end_kernel, pack, total, late, len(weight_pieces)),
        in_specs=[in_smem] + [in_vmem] * (2 + len(late)),
        out_specs=[in_vmem] * 2,
        out_shape=[shaped((rows, fibres)), shaped((3, rows, fibres))],
        compiler_params=params(),
        cost_estimate=cost(0, 0),
        name="end_weights",
    )(place, table, sums, *late_pieces)


def flux_end_kernel(pack, order, table_ref, *refs):
    *piece_refs, flux_ref = refs
    (flux,) = landed([piece_refs[order.index(d)] for d in range(len(order))], table_ref[...])
    rows, fibres = flux_ref.shape
    part = rows // pack
    for h in range(pack):
        flux_ref[h * part : (h + 1) * part, :] = flux[:, h * fibres : (h + 1) * fibres]


def end_flux(table, pieces, pack, fibres):
    rows = pieces[0].shape[1] * pack
    order = [0] + sorted(range(1, len(pieces)), key=lambda d: (d < len(pieces) // 2, d))
    return pl.pallas_call(
        functools.partial(flux_end_kernel, pack, order),
        in_specs=[in_vmem] * (1 + len(pieces)),
        out_specs=in_vmem,
        out_shape=shaped((rows, fibres)),
        compiler_params=params(),
        cost_estimate=cost(2 * rows * table.size, 2 * rows * fibres * 4),
        name="end_flux",
    )(table, *(pieces[d] for d in order))


def after(value, done):
    return lax.optimization_barrier((value, done))[0]


def per_device(pixels, pixel_ivar, clip_bits, coupling, counts, good_flags, owner_slot):
    expos, width, fibres = pixels.shape
    fib_count, wav_count = lax.axis_size("fib"), lax.axis_size("wav")
    total = width * wav_count
    per = fibres // fib_count
    rows = width // 2
    pack = max(1, LANES // per)
    while pack > 1 and rows % (pack * ROWS):
        pack //= 2
    rel = pack * per == LANES and fib_count & (fib_count - 1) == 0
    pieces = fib_count if rel else 1
    place = jnp.stack([lax.axis_index(axis) for axis in ("fib", "wav", "exp")]).astype(jnp.int32)
    coupling, counts, slots = coupling[None], counts[None], owner_slot[None]
    swap = [(0, 1), (1, 0)]
    moves = (fib_count, pack, per, rel)

    theirs, weight_t, send_table, slots, coupling, counts, good, bits, ivar = sent_weights(
        moves, wav_count, place, slots, coupling, counts, good_flags, clip_bits, pixel_ivar
    )
    arriving = lax.ppermute(theirs, "exp", swap)
    mine, weight_m, up, down = kept_weights(
        wav_count, place, coupling, counts, good, pixels, ivar, bits
    )
    upward = [(i, (i + 1) % wav_count) for i in range(wav_count)]
    left = lax.ppermute(up, "wav", upward)
    right = lax.ppermute(down, "wav", [(j, i) for i, j in upward])
    *sorted_pieces, scale = sort_fibres(arriving, mine, send_table, pack, pieces)
    weight_pieces = exchange(sorted_pieces, fib_count)

    pixel_s, ivar_s = stream_layout(left[0] + right[0], pixels, ivar)
    theirs, solved = flux_sums(wav_count, place, coupling, left, right, pixel_s, ivar_s, weight_t)
    early = [0, fib_count // 2] if rel else [0]
    late = [d for d in range(pieces) if d not in early]
    ahead = weight_pieces[early[-1]][0, :ROWS, :] * 0.5
    arriving = lax.ppermute(theirs, "exp", swap)
    mine = kept_flux(after(place, theirs), coupling, solved, weight_m)
    sorted_pieces = sort_fibres(arriving, mine, send_table, pack, pieces, scale, ahead)
    flux_pieces = exchange(sorted_pieces, fib_count)
    recv_table, placed = place_early(moves, early, after(place, sorted_pieces[0]), slots, weight_pieces, fibres)
    ivar, res = end_weights(place, recv_table, placed, late, weight_pieces, pack, fibres, total)
    flux = end_flux(recv_table, flux_pieces, pack, fibres)
    return (flux, ivar, res)


def solution(mesh):
    return jax.shard_map(
        per_device,
        mesh=mesh,
        in_specs=(
            P("exp", "wav", "fib"),
            P("exp", "wav", "fib"),
            P("exp", "wav", "fib"),
            P("fib"),
            P("fib"),
            P("exp", "fib"),
            P(),
        ),
        out_specs=(
            P(("wav", "exp"), "fib"),
            P(("wav", "exp"), "fib"),
            P(None, ("wav", "exp"), "fib"),
        ),
        check_vma=False,
    )
```
